32 devices in a mesh: dp: 4 (over y, core), ctx: 8 (over z, x).
Axes of the slice: x: 2, y: 2, z: 4, core: 2. Of those that a mesh axis runs over, the one named last changes fastest.
Arguments:
- tokens: bfloat16 [4, 1024, 1152], P('dp', 'ctx'), may hold values from -6 to 6
- positions: int32 [4, 1024], P('dp', 'ctx'), may hold values from 0 to 2046, as said below
- block_sizes: int32 [4], P('dp'), may hold values from 128 to 512, as said below
- attn_gain: bfloat16 [1152], P('ctx'), may hold values from 0.099609375 to 1.8984375
- w_query: bfloat16 [1152, 1152], P('ctx', 'dp'), may hold values from -0.25 to 0.25
- w_key: bfloat16 [1152, 384], P('ctx', 'dp'), may hold values from -0.25 to 0.25
- w_value: bfloat16 [1152, 384], P('ctx', 'dp'), may hold values from -0.1875 to 0.1875
- w_out: bfloat16 [1152, 1152], P('ctx', 'dp'), may hold values from -1.5 to 1.5
- mlp_gain: bfloat16 [1152], P('ctx'), may hold values from 0.099609375 to 1.8984375
- w_gate: bfloat16 [1152, 3072], P('ctx', 'dp'), may hold values from -0.1875 to 0.1875
- w_up: bfloat16 [1152, 3072], P('ctx', 'dp'), may hold values from -0.1875 to 0.1875
- w_down: bfloat16 [3072, 1152], P('ctx', 'dp'), may hold values from -0.109375 to 0.109375
- cotangent: bfloat16 [4, 1024, 1152], P('dp', 'ctx'), may hold values from -6 to 6
Outputs:
- output: bfloat16 [4, 1024, 1152], P('dp', 'ctx')
- input_grad: bfloat16 [4, 1024, 1152], P('dp', 'ctx')
- grad_attn_gain: float32 [1152], P('ctx')
- grad_w_query: float32 [1152, 1152], P('ctx', 'dp')
- grad_w_key: float32 [1152, 384], P('ctx', 'dp')
- grad_w_value: float32 [1152, 384], P('ctx', 'dp')
- grad_w_out: float32 [1152, 1152], P('ctx', 'dp')
- grad_mlp_gain: float32 [1152], P('ctx')
- grad_w_gate: float32 [1152, 3072], P('ctx', 'dp')
- grad_w_up: float32 [1152, 3072], P('ctx', 'dp')
- grad_w_down: float32 [3072, 1152], P('ctx', 'dp')
The draws below stay inside these ranges and needn't reach their ends.
Inputs may be any that keep to these rules, and one draw needn't show every extreme that they name: `positions`: strictly increasing along each sequence in steps of 1 to 3, from 0 to 2046. `block_sizes`: every entry is 128, 256 or 512, and each of the three occurs.
All inputs are finite; a program needn't handle non-finite values.
Results may differ from the reference program's by a relative error of at most 0.02.
Values may be sent and summed in bfloat16 or wider, within the bound.
A program may use at most 256 MiB of HBM per device.

```python
import jax
import jax.numpy as jnp
from jax import lax

D = 1152
QUERY_HEADS = 18
KEY_VALUE_HEADS = 6
HEAD_SIZE = 64
FF = 3072
BLK = 256
QW = 1152
KVW = 384
SEQUENCE_TOKENS = 1024
SEQS = 4


def draw_positions(key, part):
    key = jax.random.fold_in(key, 11)
    offsets = jax.random.randint(key, (SEQS, SEQUENCE_TOKENS), 0, 2)
    places = jnp.arange(SEQUENCE_TOKENS, dtype=jnp.int32)
    at_ends = (places == 0) | (places == SEQUENCE_TOKENS - 1)
    offsets = jnp.where(at_ends[None, :], 0, offsets)
    return (2 * places[None, :] - offsets).astype(jnp.int32)


def draw_block_sizes(key, part):
    key = jax.random.fold_in(key, 23)
    first_key, second_key = jax.random.split(key)
    options_tab = jnp.array([BLK // 2, BLK, 2 * BLK], dtype=jnp.int32)
    shift_by = jax.random.randint(first_key, (), 0, 3)
    picked = (jnp.arange(SEQS, dtype=jnp.int32) + shift_by) % 3
    return jax.random.permutation(second_key, options_tab[picked]).astype(jnp.int32)


def shard_levels(own_key, shape, cuts, least, high):
    factor_of = 1.0
    for axis_at, parts in cuts:
        heights = jax.random.uniform(jax.random.fold_in(jax.random.fold_in(own_key, 6), axis_at), (parts,), jnp.float32, least / len(cuts), high / len(cuts))
        factor_of = factor_of * jnp.repeat(jnp.exp(heights), shape[axis_at] // parts).reshape((-1,) + (1,) * (len(shape) - 1 - axis_at))
    return factor_of


def gaussian(key, extent, deviation, bound, cuts=(), held_as=jnp.bfloat16):
    entries = jax.random.normal(key, extent, jnp.float32) * deviation
    if len(cuts) > 0:
        entries = shard_levels(key, extent, cuts, -0.22, 0.18) * entries
    return jnp.clip(entries, min=-bound, max=bound).astype(held_as)


def setup_inputs(seed: int = 0) -> dict:
    arg_keys = jax.random.split(jax.random.key(seed), 14)
    tokens = gaussian(arg_keys[0], (SEQS, SEQUENCE_TOKENS, D), 1.0, 6.0, ((0, 4), (1, 8)))
    positions = draw_positions(jax.random.fold_in(arg_keys[13], 71), 0)
    block_sizes = draw_block_sizes(jax.random.fold_in(arg_keys[13], 71), 0)
    attn_gain = jnp.clip(1.0 + 0.18 * jax.random.normal(arg_keys[3], (D,), jnp.float32), 0.099609375, 1.8984375).astype(jnp.bfloat16)
    w_query = gaussian(arg_keys[4], (D, QW), (D // 2) ** -0.5, 0.25, ((0, 8), (1, 4)))
    w_key = gaussian(arg_keys[5], (D, KVW), (D // 2) ** -0.5, 0.25, ((0, 8), (1, 4)))
    w_value = gaussian(arg_keys[6], (D, KVW), D ** -0.5, 0.1875, ((0, 8), (1, 4)))
    w_out = gaussian(arg_keys[7], (QW, D), (QW // 64) ** -0.5, 1.5, ((0, 8), (1, 4)))
    mlp_gain = jnp.clip(1.0 + 0.18 * jax.random.normal(arg_keys[8], (D,), jnp.float32), 0.099609375, 1.8984375).astype(jnp.bfloat16)
    w_gate = gaussian(arg_keys[9], (D, FF), D ** -0.5, 0.1875, ((0, 8), (1, 4)))
    w_up = gaussian(arg_keys[10], (D, FF), D ** -0.5, 0.1875, ((0, 8), (1, 4)))
    w_down = gaussian(arg_keys[11], (FF, D), FF ** -0.5, 0.109375, ((0, 8), (1, 4)))
    cotangent = gaussian(arg_keys[12], (SEQS, SEQUENCE_TOKENS, D), 1.0, 6.0, ((0, 4), (1, 8)))
    return {"tokens": tokens, "positions": positions, "block_sizes": block_sizes, "attn_gain": attn_gain, "w_query": w_query, "w_key": w_key, "w_value": w_value, "w_out": w_out, "mlp_gain": mlp_gain, "w_gate": w_gate, "w_up": w_up, "w_down": w_down, "cotangent": cotangent}


EPSILON = 1e-05
THETA = 10000.0
VERY_NEGATIVE = -1e+30

@jax.custom_vjp
def low(v):
    return lax.optimization_barrier(v.astype(jnp.bfloat16)).astype(jnp.float32)

@jax.custom_vjp
def low_back(v):
    return v

def low_keep(v):
    return (low(v), None)

def low_pass(kept, grad):
    return (grad,)

def back_keep(v):
    return (v, None)

def back_low(kept, grad):
    return (low(grad),)
low.defvjp(low_keep, low_pass)
low_back.defvjp(back_keep, back_low)

def product(left, right):
    return jnp.dot(left, right, precision=lax.Precision.HIGHEST, preferred_element_type=jnp.float32)

def angles_of(place_ids):
    half_dim = HEAD_SIZE // 2
    frequency = THETA ** (-(jnp.arange(half_dim, dtype=jnp.float32) * 2.0 / HEAD_SIZE))
    return place_ids.astype(jnp.float32)[:, None] * frequency[None, :]

def rotate(values, angles, forward):
    row_total = values.shape[0]
    half_dim = angles.shape[1]
    shaped = values.reshape(row_total, -1, 2 * half_dim)
    first_half = shaped[..., :half_dim]
    second = shaped[..., half_dim:]
    cosine = jnp.cos(angles)[:, None, :]
    sine_vals = jnp.sin(angles)[:, None, :]
    if forward:
        rotated = jnp.concatenate([first_half * cosine - second * sine_vals, second * cosine + first_half * sine_vals], -1)
    else:
        rotated = jnp.concatenate([first_half * cosine + second * sine_vals, second * cosine - first_half * sine_vals], -1)
    return rotated.reshape(row_total, -1)

def rms_norm(values):
    inverse = lax.rsqrt(lax.optimization_barrier(jnp.mean(values * values, -1, keepdims=True)) + EPSILON)
    return values * inverse

def attend(query_matrix, rotated_keys, value_entries, block_len):
    query_group_width = QUERY_HEADS // KEY_VALUE_HEADS
    key_head_rows = rotated_keys.reshape(SEQUENCE_TOKENS, KEY_VALUE_HEADS, HEAD_SIZE)
    value_head_rows = value_entries.reshape(SEQUENCE_TOKENS, KEY_VALUE_HEADS, HEAD_SIZE)
    row_total = 256 if SEQUENCE_TOKENS % 256 == 0 else SEQUENCE_TOKENS
    key_rows = jnp.arange(SEQUENCE_TOKENS, dtype=jnp.int32)
    score_scale = HEAD_SIZE ** (-0.5)

    def one_block(leading_row):
        query_block = lax.dynamic_slice_in_dim(query_matrix, leading_row, row_total, 0).reshape(row_total, KEY_VALUE_HEADS, query_group_width, HEAD_SIZE)
        query_rows = leading_row + jnp.arange(row_total, dtype=jnp.int32)
        scores = jnp.einsum('tkgd,nkd->kgtn', query_block, key_head_rows, precision=lax.Precision.HIGHEST) * score_scale
        scores = low_back(scores)
        allowed = (key_rows // block_len)[None, :] <= (query_rows // block_len)[:, None]
        scores = jnp.where(allowed[None, None], scores, VERY_NEGATIVE)
        row_top = lax.optimization_barrier(jnp.max(scores, -1, keepdims=True))
        exp_vals = jnp.exp(scores - row_top)
        prob_vals = low(exp_vals / lax.optimization_barrier(jnp.sum(exp_vals, -1, keepdims=True)))
        attended = jnp.einsum('kgtn,nkd->tkgd', prob_vals, value_head_rows, precision=lax.Precision.HIGHEST)
        return attended.reshape(row_total, QUERY_HEADS * HEAD_SIZE)
    starts = jnp.arange(SEQUENCE_TOKENS // row_total, dtype=jnp.int32) * row_total
    return lax.map(jax.checkpoint(one_block), starts).reshape(SEQUENCE_TOKENS, QUERY_HEADS * HEAD_SIZE)

def layer_forward(tokens_f, place_ids, block_len, gain_one, query_w, key_w, value_w, out_w, gain_two, gate_w, up_w, down_w):
    angles = angles_of(place_ids)
    hidden_one = low(rms_norm(tokens_f) * gain_one)
    query_matrix = low(rotate(low_back(product(hidden_one, query_w)), angles, True))
    rotated_keys = low(rotate(low_back(product(hidden_one, key_w)), angles, True))
    value_entries = low(low_back(product(hidden_one, value_w)))
    attended = low(low_back(attend(query_matrix, rotated_keys, value_entries, block_len)))
    mixed_rows = tokens_f + low_back(product(attended, out_w))
    hidden_two = low(rms_norm(mixed_rows) * gain_two)
    gate_pre = low_back(product(hidden_two, gate_w))
    up_pre = low_back(product(hidden_two, up_w))
    inner_act = low(jax.nn.silu(gate_pre) * up_pre)
    return mixed_rows + low_back(product(inner_act, down_w))

def reference(tokens, positions, block_sizes, attn_gain, w_query, w_key, w_value, w_out, mlp_gain, w_gate, w_up, w_down, cotangent):
    params = tuple((weight.astype(jnp.float32) for weight in (attn_gain, w_query, w_key, w_value, w_out, mlp_gain, w_gate, w_up, w_down)))
    tokens_f = tokens.astype(jnp.float32)

    def whole_forward(inputs, weights):
        return lax.map(lambda element: layer_forward(element[0], element[1], element[2], *weights), (inputs, positions, block_sizes))
    result, pullback = jax.vjp(whole_forward, tokens_f, params)
    grad_tokens, grad_params = pullback(cotangent.astype(jnp.float32))
    return (result.astype(jnp.bfloat16), grad_tokens.astype(jnp.bfloat16), grad_params[0], grad_params[1], grad_params[2], grad_params[3], grad_params[4], grad_params[5], grad_params[6], grad_params[7], grad_params[8])
```

```python
import jax
import jax.numpy as jnp
from jax import lax
from jax.experimental import pallas as pl
from jax.experimental.pallas import tpu as pltpu
from jax.sharding import PartitionSpec as P

QUERY_HEADS = 18
KEY_VALUE_HEADS = 6
HEAD_SIZE = 64


EPSILON = 1e-05
THETA = 10000.0
VERY_NEGATIVE = -1e30


def product(left, right):
    return jnp.dot(left, right, preferred_element_type=jnp.float32)


def angles_of(place_ids):
    half_dim = HEAD_SIZE // 2
    frequency = THETA ** (-(jnp.arange(half_dim, dtype=jnp.float32) * 2.0 / HEAD_SIZE))
    return place_ids.astype(jnp.float32)[:, None] * frequency[None, :]


def rotate(values, angles, forward):
    row_total = values.shape[0]
    half_dim = angles.shape[1]
    shaped = values.reshape(row_total, -1, 2 * half_dim)
    first_half = shaped[..., :half_dim]
    second = shaped[..., half_dim:]
    cosine = jnp.cos(angles)[:, None, :]
    sine_vals = jnp.sin(angles)[:, None, :]
    if forward:
        rotated = jnp.concatenate(
            [first_half * cosine - second * sine_vals, second * cosine + first_half * sine_vals], -1
        )
    else:
        rotated = jnp.concatenate(
            [first_half * cosine + second * sine_vals, second * cosine - first_half * sine_vals], -1
        )
    return rotated.reshape(row_total, -1)


def norm_back(grad_normed, normed, inverse):
    return inverse * (grad_normed - normed * jnp.mean(grad_normed * normed, -1, keepdims=True))


def visible(query_rows, key_rows, block_len):
    return ((key_rows // block_len)[None, :] <= (query_rows // block_len)[:, None])[None, None]


def attend_forward(query_rows4, complete_keys, complete_values, query_rows, block_len, score_scale):
    key_count = complete_keys.shape[0]
    key_row_width = 512
    block_list = key_count // key_row_width
    query_group_width = QUERY_HEADS // KEY_VALUE_HEADS
    row_total = query_rows4.shape[0]
    key_block_list = complete_keys.reshape(block_list, key_row_width, KEY_VALUE_HEADS, HEAD_SIZE)
    value_block_list = complete_values.reshape(
        block_list, key_row_width, KEY_VALUE_HEADS, HEAD_SIZE
    )
    last_block = query_rows[-1] // block_len

    def advance(carried, inputs):
        key_blk, val_blk, first_key = inputs
        key_rows = first_key + jnp.arange(key_row_width, dtype=jnp.int32)

        def compute(current):
            run_max, run_sum, accum = current
            scores = (
                jnp.einsum(
                    "tkgd,nkd->kgtn", query_rows4, key_blk, preferred_element_type=jnp.float32
                )
                * score_scale
            )
            allowed = visible(query_rows, key_rows, block_len)
            scores = jnp.where(allowed, scores, VERY_NEGATIVE)
            new_max = jnp.maximum(run_max, jnp.max(scores, -1))
            weights = jnp.where(allowed, jnp.exp(scores - new_max[..., None]), 0.0)
            factor = jnp.exp(run_max - new_max)
            new_sum = run_sum * factor + jnp.sum(weights, -1)
            accum = accum * factor[..., None] + jnp.einsum(
                "kgtn,nkd->kgtd",
                weights.astype(jnp.bfloat16),
                val_blk,
                preferred_element_type=jnp.float32,
            )
            return (new_max, new_sum, accum)

        return (
            lax.cond(
                first_key // block_len > last_block, lambda unchanged: unchanged, compute, carried
            ),
            None,
        )

    start_state = (
        jnp.full((KEY_VALUE_HEADS, query_group_width, row_total), VERY_NEGATIVE, jnp.float32),
        jnp.zeros((KEY_VALUE_HEADS, query_group_width, row_total), jnp.float32),
        jnp.zeros((KEY_VALUE_HEADS, query_group_width, row_total, HEAD_SIZE), jnp.float32),
    )
    firsts = jnp.arange(block_list, dtype=jnp.int32) * key_row_width
    final_state, unused = lax.scan(advance, start_state, (key_block_list, value_block_list, firsts))
    run_max, run_sum, accum = final_state
    return (accum / run_sum[..., None], run_max + jnp.log(run_sum))


def attend_backward(
    query_rows4,
    head_gradients,
    log_sums,
    row_delta,
    complete_keys,
    complete_values,
    query_rows,
    block_len,
    score_scale,
):
    key_count = complete_keys.shape[0]
    key_row_width = 512
    block_list = key_count // key_row_width
    query_group_width = QUERY_HEADS // KEY_VALUE_HEADS
    row_total = query_rows4.shape[0]
    key_block_list = complete_keys.reshape(block_list, key_row_width, KEY_VALUE_HEADS, HEAD_SIZE)
    value_block_list = complete_values.reshape(
        block_list, key_row_width, KEY_VALUE_HEADS, HEAD_SIZE
    )
    last_block = query_rows[-1] // block_len

    def advance(grad_query, inputs):
        key_blk, val_blk, first_key = inputs
        key_rows = first_key + jnp.arange(key_row_width, dtype=jnp.int32)

        def compute(current):
            scores = (
                jnp.einsum(
                    "tkgd,nkd->kgtn", query_rows4, key_blk, preferred_element_type=jnp.float32
                )
                * score_scale
            )
            allowed = visible(query_rows, key_rows, block_len)
            prob_vals = jnp.where(allowed, jnp.exp(scores - log_sums[..., None]), 0.0)
            grad_prob = jnp.einsum(
                "tkgd,nkd->kgtn", head_gradients, val_blk, preferred_element_type=jnp.float32
            )
            grad_score = (prob_vals * (grad_prob - row_delta[..., None])).astype(jnp.bfloat16)
            current = current + jnp.einsum(
                "kgtn,nkd->tkgd", grad_score, key_blk, preferred_element_type=jnp.float32
            )
            grad_key = jnp.einsum(
                "kgtn,tkgd->nkd", grad_score, query_rows4, preferred_element_type=jnp.float32
            )
            grad_value = jnp.einsum(
                "kgtn,tkgd->nkd",
                prob_vals.astype(jnp.bfloat16),
                head_gradients,
                preferred_element_type=jnp.float32,
            )
            return (current, (grad_key, grad_value))

        def nothing(current):
            empty_block = jnp.zeros((key_row_width, KEY_VALUE_HEADS, HEAD_SIZE), jnp.float32)
            return (current, (empty_block, empty_block))

        return lax.cond(first_key // block_len > last_block, nothing, compute, grad_query)

    firsts = jnp.arange(block_list, dtype=jnp.int32) * key_row_width
    initial_gradient = jnp.zeros(
        (row_total, KEY_VALUE_HEADS, query_group_width, HEAD_SIZE), jnp.float32
    )
    grad_query, stacked_rows = lax.scan(
        advance, initial_gradient, (key_block_list, value_block_list, firsts)
    )
    key_gradients = stacked_rows[0].reshape(key_count, KEY_VALUE_HEADS * HEAD_SIZE)
    value_gradients = stacked_rows[1].reshape(key_count, KEY_VALUE_HEADS * HEAD_SIZE)
    return (grad_query, key_gradients, value_gradients)


def on_device(
    tokens,
    positions,
    block_sizes,
    attn_gain,
    w_query,
    w_key,
    w_value,
    w_out,
    mlp_gain,
    w_gate,
    w_up,
    w_down,
    cotangent,
):
    row_parts = (
        lax.all_gather(w_query, "ctx", axis=0, tiled=True),
        lax.all_gather(w_key, "ctx", axis=0, tiled=True),
        lax.all_gather(w_value, "ctx", axis=0, tiled=True),
        lax.all_gather(w_out, "ctx", axis=0, tiled=True),
        lax.all_gather(w_gate, "ctx", axis=0, tiled=True),
        lax.all_gather(w_up, "ctx", axis=0, tiled=True),
        lax.all_gather(w_down, "ctx", axis=0, tiled=True),
        lax.all_gather(attn_gain, "ctx", axis=0, tiled=True),
        lax.all_gather(mlp_gain, "ctx", axis=0, tiled=True),
    )
    whole_w = (
        lax.all_gather(row_parts[0], "dp", axis=1, tiled=True),
        lax.all_gather(row_parts[1], "dp", axis=1, tiled=True),
        lax.all_gather(row_parts[2], "dp", axis=1, tiled=True),
        lax.all_gather(row_parts[3], "dp", axis=1, tiled=True),
        lax.all_gather(row_parts[4], "dp", axis=1, tiled=True),
        lax.all_gather(row_parts[5], "dp", axis=1, tiled=True),
        lax.all_gather(row_parts[6], "dp", axis=1, tiled=True),
    )
    query_w, key_w, value_w, out_w, gate_w, up_w, down_w = whole_w
    gain_one = row_parts[7].astype(jnp.float32)
    gain_two = row_parts[8].astype(jnp.float32)
    seq_count = tokens.shape[0]
    seq_rows = tokens.shape[1]
    width = tokens.shape[2]
    inputs = tokens.reshape(seq_count * seq_rows, width).astype(jnp.float32)
    row_total = inputs.shape[0]
    query_group_width = QUERY_HEADS // KEY_VALUE_HEADS
    query_rows = lax.axis_index("ctx") * seq_rows + jnp.arange(seq_rows, dtype=jnp.int32)
    angles = angles_of(positions.reshape(-1))
    score_scale = HEAD_SIZE ** (-0.5)
    inv_one = lax.rsqrt(jnp.mean(inputs * inputs, -1, keepdims=True) + EPSILON)
    normed_one = inputs * inv_one
    hidden_one = (normed_one * gain_one).astype(jnp.bfloat16)
    query_matrix = rotate(product(hidden_one, query_w), angles, True).astype(jnp.bfloat16)
    keys_own = rotate(product(hidden_one, key_w), angles, True).astype(jnp.bfloat16)
    values_own = product(hidden_one, value_w).astype(jnp.bfloat16)
    complete_keys, complete_values = (
        lax.all_gather(keys_own.reshape(seq_count, seq_rows, -1), "ctx", axis=1, tiled=True),
        lax.all_gather(values_own.reshape(seq_count, seq_rows, -1), "ctx", axis=1, tiled=True),
    )
    query_rows4 = query_matrix.reshape(row_total, KEY_VALUE_HEADS, query_group_width, HEAD_SIZE)
    member = 0
    heads_one, lse_one = attend_forward(
        query_rows4,
        complete_keys[member],
        complete_values[member],
        query_rows,
        block_sizes[member],
        score_scale,
    )
    attn_flat = heads_one.transpose(2, 0, 1, 3).reshape(row_total, QUERY_HEADS * HEAD_SIZE)
    attn_low = attn_flat.astype(jnp.bfloat16)
    mixed_rows = inputs + product(attn_low, out_w)
    inv_two = lax.rsqrt(jnp.mean(mixed_rows * mixed_rows, -1, keepdims=True) + EPSILON)
    normed_two = mixed_rows * inv_two
    hidden_two = (normed_two * gain_two).astype(jnp.bfloat16)
    gate_pre = product(hidden_two, gate_w)
    up_pre = product(hidden_two, up_w)
    sigmoid_gate = jax.nn.sigmoid(gate_pre)
    silu_gate = gate_pre * sigmoid_gate
    inner_act = (silu_gate * up_pre).astype(jnp.bfloat16)
    result = mixed_rows + product(inner_act, down_w)
    output = result.astype(jnp.bfloat16).reshape(seq_count, seq_rows, width)
    back_parts = (
        lax.all_gather(w_query, "ctx", axis=0, tiled=True),
        lax.all_gather(w_key, "ctx", axis=0, tiled=True),
        lax.all_gather(w_value, "ctx", axis=0, tiled=True),
        lax.all_gather(w_out, "ctx", axis=0, tiled=True),
        lax.all_gather(w_gate, "ctx", axis=0, tiled=True),
        lax.all_gather(w_up, "ctx", axis=0, tiled=True),
        lax.all_gather(w_down, "ctx", axis=0, tiled=True),
    )
    back_whole = (
        lax.all_gather(back_parts[0], "dp", axis=1, tiled=True),
        lax.all_gather(back_parts[1], "dp", axis=1, tiled=True),
        lax.all_gather(back_parts[2], "dp", axis=1, tiled=True),
        lax.all_gather(back_parts[3], "dp", axis=1, tiled=True),
        lax.all_gather(back_parts[4], "dp", axis=1, tiled=True),
        lax.all_gather(back_parts[5], "dp", axis=1, tiled=True),
        lax.all_gather(back_parts[6], "dp", axis=1, tiled=True),
    )
    back_query, back_key, back_value, back_out, back_gate, back_up, back_down = back_whole
    grad_top = cotangent.reshape(row_total, width)
    grad_down = jnp.einsum("tf,td->fd", inner_act, grad_top, preferred_element_type=jnp.float32)
    grad_inner = jnp.einsum("td,fd->tf", grad_top, back_down, preferred_element_type=jnp.float32)
    grad_gate = (
        grad_inner * up_pre * sigmoid_gate * (1.0 + gate_pre * (1.0 - sigmoid_gate))
    ).astype(jnp.bfloat16)
    grad_upval = (grad_inner * silu_gate).astype(jnp.bfloat16)
    grad_gatew = jnp.einsum("td,tf->df", hidden_two, grad_gate, preferred_element_type=jnp.float32)
    grad_upw = jnp.einsum("td,tf->df", hidden_two, grad_upval, preferred_element_type=jnp.float32)
    grad_hidden_two = jnp.einsum(
        "tf,df->td", grad_gate, back_gate, preferred_element_type=jnp.float32
    ) + jnp.einsum("tf,df->td", grad_upval, back_up, preferred_element_type=jnp.float32)
    grad_gain_two = jnp.sum(grad_hidden_two * normed_two, 0)
    grad_mixed = grad_top.astype(jnp.float32) + norm_back(
        grad_hidden_two * gain_two, normed_two, inv_two
    )
    grad_branch = grad_mixed.astype(jnp.bfloat16)
    grad_outw = jnp.einsum("tq,td->qd", attn_low, grad_branch, preferred_element_type=jnp.float32)
    attention_gradient = jnp.einsum(
        "td,qd->tq", grad_branch, back_out, preferred_element_type=jnp.float32
    ).astype(jnp.bfloat16)
    head_gradients = attention_gradient.reshape(
        row_total, KEY_VALUE_HEADS, query_group_width, HEAD_SIZE
    )
    row_delta = jnp.einsum("tkgd,kgtd->kgt", head_gradients.astype(jnp.float32), heads_one)
    member = 0
    grad_q_one, grad_k_one, grad_v_one = attend_backward(
        query_rows4,
        head_gradients,
        lse_one,
        row_delta,
        complete_keys[member],
        complete_values[member],
        query_rows,
        block_sizes[member],
        score_scale,
    )
    key_grads = [grad_k_one]
    value_grads = [grad_v_one]
    grad_keys_all = jnp.stack(key_grads, 0)
    grad_values_all = jnp.stack(value_grads, 0)
    grad_keys_own, grad_values_own = (
        lax.psum_scatter(grad_keys_all, "ctx", scatter_dimension=1, tiled=True),
        lax.psum_scatter(grad_values_all, "ctx", scatter_dimension=1, tiled=True),
    )
    grad_keys_own = grad_keys_own.reshape(row_total, -1)
    grad_values_own = grad_values_own.reshape(row_total, -1)
    grad_query_raw = rotate(
        grad_q_one.reshape(row_total, QUERY_HEADS * HEAD_SIZE) * score_scale, angles, False
    ).astype(jnp.bfloat16)
    grad_key_raw = rotate(grad_keys_own * score_scale, angles, False).astype(jnp.bfloat16)
    grad_value_raw = grad_values_own.astype(jnp.bfloat16)
    grad_queryw = jnp.einsum(
        "td,tq->dq", hidden_one, grad_query_raw, preferred_element_type=jnp.float32
    )
    grad_keyw = jnp.einsum(
        "td,tq->dq", hidden_one, grad_key_raw, preferred_element_type=jnp.float32
    )
    grad_valuew = jnp.einsum(
        "td,tq->dq", hidden_one, grad_value_raw, preferred_element_type=jnp.float32
    )
    grad_hidden_one = jnp.einsum(
        "tq,dq->td", grad_query_raw, back_query, preferred_element_type=jnp.float32
    )
    grad_hidden_one = grad_hidden_one + jnp.einsum(
        "tq,dq->td", grad_key_raw, back_key, preferred_element_type=jnp.float32
    )
    grad_hidden_one = grad_hidden_one + jnp.einsum(
        "tq,dq->td", grad_value_raw, back_value, preferred_element_type=jnp.float32
    )
    grad_gain_one = jnp.sum(grad_hidden_one * normed_one, 0)
    grad_input = grad_mixed + norm_back(grad_hidden_one * gain_one, normed_one, inv_one)
    input_grad = grad_input.astype(jnp.bfloat16).reshape(seq_count, seq_rows, width)
    summed_rows = (
        lax.psum_scatter(grad_queryw, "ctx", scatter_dimension=0, tiled=True),
        lax.psum_scatter(grad_keyw, "ctx", scatter_dimension=0, tiled=True),
        lax.psum_scatter(grad_valuew, "ctx", scatter_dimension=0, tiled=True),
        lax.psum_scatter(grad_outw, "ctx", scatter_dimension=0, tiled=True),
        lax.psum_scatter(grad_gatew, "ctx", scatter_dimension=0, tiled=True),
        lax.psum_scatter(grad_upw, "ctx", scatter_dimension=0, tiled=True),
        lax.psum_scatter(grad_down, "ctx", scatter_dimension=0, tiled=True),
        lax.psum_scatter(grad_gain_one, "ctx", scatter_dimension=0, tiled=True),
        lax.psum_scatter(grad_gain_two, "ctx", scatter_dimension=0, tiled=True),
    )
    final_w = (
        lax.psum_scatter(
            summed_rows[0].astype(jnp.bfloat16), "dp", scatter_dimension=1, tiled=True
        ).astype(jnp.float32),
        lax.psum_scatter(
            summed_rows[1].astype(jnp.bfloat16), "dp", scatter_dimension=1, tiled=True
        ).astype(jnp.float32),
        lax.psum_scatter(
            summed_rows[2].astype(jnp.bfloat16), "dp", scatter_dimension=1, tiled=True
        ).astype(jnp.float32),
        lax.psum_scatter(
            summed_rows[3].astype(jnp.bfloat16), "dp", scatter_dimension=1, tiled=True
        ).astype(jnp.float32),
        lax.psum_scatter(
            summed_rows[4].astype(jnp.bfloat16), "dp", scatter_dimension=1, tiled=True
        ).astype(jnp.float32),
        lax.psum_scatter(
            summed_rows[5].astype(jnp.bfloat16), "dp", scatter_dimension=1, tiled=True
        ).astype(jnp.float32),
        lax.psum_scatter(
            summed_rows[6].astype(jnp.bfloat16), "dp", scatter_dimension=1, tiled=True
        ).astype(jnp.float32),
    )
    final_gains = lax.psum((summed_rows[7], summed_rows[8]), "dp")
    return (
        output,
        input_grad,
        final_gains[0],
        final_w[0],
        final_w[1],
        final_w[2],
        final_w[3],
        final_gains[1],
        final_w[4],
        final_w[5],
        final_w[6],
    )


MESH = pl.DeviceIdType.MESH
F32 = jnp.float32
BF16 = jnp.bfloat16


def dot_nn(a, b):
    return lax.dot_general(a, b, (((1,), (0,)), ((), ())), preferred_element_type=F32)


def dot_nt(a, b):
    return lax.dot_general(a, b, (((1,), (1,)), ((), ())), preferred_element_type=F32)


def dot_tn(a, b):
    return lax.dot_general(a, b, (((0,), (0,)), ((), ())), preferred_element_type=F32)


class Wires:
    def __init__(self, send_sems, recv_sems):
        self.send_sems, self.recv_sems = send_sems, recv_sems
        self.sends = 0
        self.recvs = 0
        self.pending = []

    def slots(self, count):
        first = self.recvs
        self.recvs += count
        return first

    def send(self, src, dst, slot, device, is_self=None):
        mine = self.sends
        self.sends += 1
        remote = pltpu.make_async_remote_copy(
            src_ref=src,
            dst_ref=dst,
            send_sem=self.send_sems.at[mine],
            recv_sem=self.recv_sems.at[slot],
            device_id=device,
            device_id_type=MESH,
        )
        if is_self is None:
            remote.start()
            finish = remote.wait_send
        else:
            local = pltpu.make_async_copy(src, dst, self.recv_sems.at[slot])

            @pl.when(is_self)
            def _():
                local.start()

            @pl.when(jnp.logical_not(is_self))
            def _():
                remote.start()

            def finish():
                @pl.when(jnp.logical_not(is_self))
                def _():
                    remote.wait_send()

        self.pending.append(finish)
        return finish

    def keep(self, src, dst, slot):
        pltpu.make_async_copy(src, dst, self.recv_sems.at[slot]).start()

    def recv(self, dst, slot):
        pltpu.make_async_copy(dst, dst, self.recv_sems.at[slot]).wait()

    def done(self, finish):
        finish()
        self.pending.remove(finish)

    def drain(self):
        for finish in self.pending:
            finish()
        self.pending = []


N_SEM = 224


def layer_kernel(
    tok, cot, cs, bias, wqkv, wo, wgu, wdt,
    o_out, o_ing, o_gain, o_qkv, o_o, o_gu, o_dt,
    csf, b2, x2, wqz, woz, wq, wok, wg8, wd8, c8, n8, n1, qf, kvf, kv, q6, p6, o6, ab,
    mp, ml, mid, dmid, dmb, dm4, do6, act, pt, l1, s2, l2, l1o, s2o, l2o,
    ggu, lgu, sgu, lf, gdt, lgd, sgd, ld, lo, lq, so, sq, lzo, lzq, dkv, lx, sx, lkz,
    lg, sg, lgz, dqk, send_sems, recv_sems,
):
    net = Wires(send_sems, recv_sems)
    dp = lax.axis_index("dp")
    ctx = lax.axis_index("ctx")
    y, c = dp // 2, lax.rem(dp, 2)
    z, x = ctx // 2, lax.rem(ctx, 2)
    z_hi, z_lo = z // 2, lax.rem(z, 2)
    y_c = y + c - 2 * y * c
    tokens, width = tok.shape
    rows = wqkv.shape[0]
    qcols = wo.shape[1]
    kcols = (wqkv.shape[1] - qcols) // 2
    ff = wdt.shape[1]
    drows = wdt.shape[0]
    qw = 2 * qcols
    kw = 2 * kcols
    groups = kw // HEAD_SIZE
    per = QUERY_HEADS // KEY_VALUE_HEADS
    heads = groups * per
    keys = kv.shape[1]
    n_ctx = keys // tokens
    scale = HEAD_SIZE ** (-0.5)

    def flip(a, h):
        return 1 - a if h else a

    def zat(k):
        return (z, 2 * z_hi + 1 - z_lo, 2 * (1 - z_hi) + z_lo, 3 - z)[k]

    def dev(yy, cc, zz, xx):
        return (2 * yy + cc, 2 * zz + xx)

    def off(value, step):
        return pl.multiple_of(value * step, step)

    partner = dev(y, 1 - c, z, x)

    barrier = pltpu.get_barrier_semaphore()
    for k in range(4):
        for hx in range(2):
            for hy in range(2):
                for hc in range(2):
                    if k + hx + hy + hc:
                        pl.semaphore_signal(
                            barrier, inc=1,
                            device_id=dev(flip(y, hy), flip(c, hc), zat(k), flip(x, hx)),
                            device_id_type=MESH,
                        )
    pl.semaphore_wait(barrier, 31)

    r_tok = net.slots(3)
    net.send(tok, x2, r_tok, partner)
    net.send(cs, csf.at[pl.ds(tokens, tokens)], r_tok + 1, partner)
    net.send(bias, b2.at[1], r_tok + 2, partner)
    r_wqz, r_woz = net.slots(4), net.slots(4)
    r_wq, r_wo = net.slots(16), net.slots(16)

    def spread_qkv(k, src):
        zs = zat(k)
        for hx in range(2):
            for hy in range(2):
                net.send(
                    src,
                    wq.at[c, pl.ds(off(2 * zs + x, rows), rows)],
                    r_wq + k * 4 + hx * 2 + c,
                    dev(flip(y, hy), y, z, flip(x, hx)),
                    is_self=(c == y) if hx + hy == 0 else None,
                )

    def spread_wo(k, src):
        zs = zat(k)
        core = zs // 2
        for hx in range(2):
            for hy in range(2):
                net.send(
                    src,
                    wok.at[dp, pl.ds(off(2 * lax.rem(zs, 2) + x, rows), rows)],
                    r_wo + lax.rem(zs, 2) * 8 + hx * 4 + hy * 2 + c,
                    dev(flip(y, hy), core, z, flip(x, hx)),
                    is_self=(c == core) if hx + hy == 0 else None,
                )

    for k in range(1, 4):
        net.send(wqkv, wqz.at[k - 1], r_wqz + k, dev(y, c, zat(k), x))
    spread_qkv(0, wqkv)
    for k in range(1, 4):
        net.send(wo, woz.at[k - 1], r_woz + k, dev(y, c, zat(k), x))

    csf[0:tokens] = cs[...]
    b2[0] = bias[...]

    def normed(values):
        v = values.astype(F32)
        inv = lax.rsqrt(jnp.mean(v * v, -1, keepdims=True) + EPSILON)
        return v * inv, inv

    n1[0:tokens] = normed(tok[...])[0].astype(BF16)
    net.recv(x2, r_tok)
    n1[tokens : 2 * tokens] = normed(x2[...])[0].astype(BF16)
    net.recv(csf.at[pl.ds(tokens, tokens)], r_tok + 1)
    net.recv(b2.at[1], r_tok + 2)

    for k in range(1, 4):
        net.recv(wqz.at[k - 1], r_wqz + k)
        spread_qkv(k, wqz.at[k - 1])

    r_gu, r_wd = net.slots(8), net.slots(4)
    for k in range(4):
        for hx in range(2):
            net.send(
                wgu.at[:, :, pl.ds(off(flip(x, hx), ff), ff)],
                wg8.at[:, pl.ds(off(ctx, rows), rows)],
                r_gu + k * 2 + hx,
                dev(y_c, c, zat(k), flip(x, hx)),
                is_self=(c == 0) if k + hx == 0 else None,
            )
    wd_c = z_lo
    wd_y = z_hi + wd_c - 2 * z_hi * wd_c
    wd_home = jnp.logical_and(wd_c == c, wd_y == y)
    for k in range(4):
        net.send(
            wdt,
            wd8.at[pl.ds(off(dp, drows), drows)],
            r_wd + dp,
            dev(wd_y, wd_c, zat(k), x),
            is_self=wd_home if k == 0 else None,
        )
    spread_wo(0, wo)
    for k in range(1, 4):
        net.recv(woz.at[k - 1], r_woz + k)
        spread_wo(k, woz.at[k - 1])

    def gather_start(buf, slot):
        for h in range(1, 4):
            net.send(buf.at[0], buf.at[2 * h], slot + h, dev(flip(y, h % 2), c, z, flip(x, h // 2)))
        net.send(buf.at[0], buf.at[1], slot + 4, partner)

    def gather_pass(buf, slot, h):
        net.recv(buf.at[2 * h], slot + h)
        net.send(buf.at[2 * h], buf.at[2 * h + 1], slot + 4 + h, partner)

    c8[0] = cot[...]
    r_c8 = net.slots(8)
    gather_start(c8, r_c8)

    lane = lax.broadcasted_iota(jnp.int32, (2 * tokens, 128), 1)
    low_half = lax.rem(lane, HEAD_SIZE) < HEAD_SIZE // 2

    def turn(tile, forward):
        other = jnp.where(low_half, pltpu.roll(tile, 96, 1), pltpu.roll(tile, 32, 1))
        turned = other * csf[:, 128:256]
        return tile * csf[:, 0:128] + (turned if forward else -turned)

    for k in range(4):
        for hx in range(2):
            for cc in range(2):
                net.recv(
                    wq.at[cc, pl.ds(off(2 * zat(k) + flip(x, hx), rows), rows)],
                    r_wq + k * 4 + hx * 2 + cc,
                )
    qf[:, qw:] = jnp.zeros((2 * tokens, qf.shape[1] - qw), F32)
    for part in range(2):
        got = dot_nn(n1[...], wq[part])
        qf[:, qcols * part : qcols * (part + 1)] = got[:, :qcols]
        kvf[:, kcols * part : kcols * (part + 1)] = got[:, qcols : qcols + kcols]
        kvf[:, kw + kcols * part : kw + kcols * (part + 1)] = got[:, qcols + kcols :]
    for t in range(qf.shape[1] // 128):
        qf[:, 128 * t : 128 * (t + 1)] = turn(qf[:, 128 * t : 128 * (t + 1)], True) * scale

    def turn_keys(forward):
        for t in range(kw // 128 + 1):
            tile = kvf[:, 128 * t : 128 * (t + 1)]
            kvf[:, 128 * t : 128 * (t + 1)] = jnp.where(
                128 * t + lane < kw, turn(tile, forward), tile
            )

    turn_keys(True)
    own_keys = pl.ds(off(ctx, tokens), tokens)
    for s in range(2):
        kv[s, own_keys] = kvf[s * tokens : (s + 1) * tokens].astype(BF16)
    r_kz, r_kx = net.slots(4), net.slots(4)
    for k in range(1, 4):
        net.send(kv.at[:, own_keys], kv.at[:, own_keys], r_kz + k, dev(y, c, zat(k), x))
    net.send(kv.at[:, own_keys], kv.at[:, own_keys], r_kx, dev(y, c, z, 1 - x))
    for s in range(2):
        for h in range(heads):
            q6[s * groups + h // per, (h % per) * tokens : (h % per + 1) * tokens] = qf[
                s * tokens : (s + 1) * tokens, HEAD_SIZE * h : HEAD_SIZE * (h + 1)
            ].astype(BF16)
    for h in range(1, 4):
        gather_pass(c8, r_c8, h)
    for k in range(1, 4):
        part = pl.ds(off(2 * zat(k) + x, tokens), tokens)
        net.recv(kv.at[:, part], r_kz + k)
        net.send(kv.at[:, part], kv.at[:, part], r_kx + k, dev(y, c, z, 1 - x))
    for k in range(4):
        net.recv(kv.at[:, pl.ds(off(2 * zat(k) + 1 - x, tokens), tokens)], r_kx + k)

    def attend(s, carry):
        mask = b2[s][0:1, :]
        for g in range(groups):
            kg = kv[s, :, HEAD_SIZE * g : HEAD_SIZE * (g + 1)]
            vg = kv[s, :, kw + HEAD_SIZE * g : kw + HEAD_SIZE * (g + 1)]
            scores = dot_nt(q6[s * groups + g], kg) + mask
            weights = jnp.exp(scores - jnp.max(scores, -1, keepdims=True))
            probs = (weights * (1.0 / jnp.sum(weights, -1, keepdims=True))).astype(BF16)
            p6[s * groups + g] = probs
            got = dot_nn(probs, vg).astype(BF16)
            o6[s * groups + g] = got
            for i in range(per):
                h = g * per + i
                ab[pl.ds(off(s, tokens), tokens), HEAD_SIZE * h : HEAD_SIZE * (h + 1)] = got[
                    i * tokens : (i + 1) * tokens
                ]
        return carry

    lax.fori_loop(0, 2, attend, 0)

    for zz in range(2):
        for hx in range(2):
            for hy in range(2):
                for cc in range(2):
                    part = 2 * flip(y, hy) + cc
                    net.recv(
                        wok.at[part, pl.ds(off(2 * zz + flip(x, hx), rows), rows)],
                        r_wo + zz * 8 + hx * 4 + hy * 2 + cc,
                    )
    for part in range(4):
        got = dot_nn(ab[:, 0:qw], wok[part])
        for s in range(2):
            mp[s, :, qcols * part : qcols * (part + 1)] = got[s * tokens : (s + 1) * tokens]
    r_ml = net.slots(1)
    mp_sent = net.send(mp.at[1], ml, r_ml, partner)
    net.recv(ml, r_ml)
    mid[...] = tok[...].astype(F32) + mp[0] + ml[...]
    n8[0] = normed(mid[...])[0].astype(BF16)
    r_n8 = net.slots(8)
    gather_start(n8, r_n8)

    for h in range(1, 4):
        net.recv(c8.at[2 * h + 1], r_c8 + 4 + h)
    net.recv(c8.at[1], r_c8 + 4)
    for k in range(4):
        for hx in range(2):
            net.recv(
                wg8.at[:, pl.ds(off(2 * zat(k) + flip(x, hx), rows), rows)], r_gu + k * 2 + hx
            )
    for part in range(4):
        net.recv(wd8.at[pl.ds(drows * part, drows)], r_wd + part)
    for h in range(1, 4):
        gather_pass(n8, r_n8, h)
    net.recv(n8.at[1], r_n8 + 4)
    for h in range(1, 4):
        net.recv(n8.at[2 * h + 1], r_n8 + 4 + h)

    all_tokens = 8 * tokens

    def feed(i, carry):
        pair = pl.ds(2 * i, 2)
        here = n8[pair].reshape(2 * tokens, width)
        grad_inner = dot_nn(c8[pair].reshape(2 * tokens, width), wd8[...])
        gate = dot_nn(here, wg8[0])
        up = dot_nn(here, wg8[1])
        sig = 1.0 / (1.0 + jnp.exp(-gate))
        silu = gate * sig
        dgate = (grad_inner * up * sig * (1.0 + gate * (1.0 - sig))).astype(BF16)
        dup = (grad_inner * silu).astype(BF16)
        at = off(i, 2 * tokens)
        act[pl.ds(at, 2 * tokens)] = (silu * up).astype(BF16)
        act[pl.ds(at + all_tokens, 2 * tokens)] = dgate
        act[pl.ds(at + 2 * all_tokens, 2 * tokens)] = dup
        pt[pair] = (dot_nt(dgate, wg8[0]) + dot_nt(dup, wg8[1])).astype(BF16).reshape(2, tokens, width)
        return carry

    lax.fori_loop(0, 4, feed, 0)

    def reduce_start(part, land, slot):
        return [net.send(part.at[2 * h + 1], land.at[h], slot + h, partner) for h in range(4)]

    def reduce_pass(part, land, out, land2, slot):
        for h in range(1, 4):
            net.recv(land.at[h], slot + h)
            out[h - 1] = (part[2 * h].astype(F32) + land[h].astype(F32)).astype(BF16)
            net.send(
                out.at[h - 1], land2.at[h - 1], slot + 4 + h,
                dev(flip(y, h % 2), c, z, flip(x, h // 2)),
            )
        net.recv(land.at[0], slot)
        return part[0].astype(F32) + land[0].astype(F32)

    def reduce_end(land2, slot):
        total = 0.0
        for h in range(1, 4):
            net.recv(land2.at[h - 1], slot + 4 + h)
            total = total + land2[h - 1].astype(F32)
        return total

    def flat(ref, i):
        return ref[:, :, pl.ds(off(i, 128), 128)].reshape(all_tokens, 128)

    def grad_gu(i, carry):
        left = flat(n8, i)
        at = pl.ds(off(i, 128), 128)
        ggu[0, at] = dot_tn(left, act[pl.ds(all_tokens, all_tokens)]).astype(BF16)
        ggu[1, at] = dot_tn(left, act[pl.ds(2 * all_tokens, all_tokens)]).astype(BF16)
        return carry

    def grad_d(i, carry):
        gdt[pl.ds(off(i, 128), 128)] = dot_tn(flat(c8, i), act[pl.ds(0, all_tokens)]).astype(BF16)
        return carry

    def feed_out(i, carry):
        got = dot_nt(act[pl.ds(off(i, 2 * tokens), 2 * tokens)], wd8[...])
        pt[pl.ds(2 * i, 2)] = got.astype(BF16).reshape(2, tokens, width)
        return carry

    r_dn = net.slots(8)
    pt_sent = reduce_start(pt, l1, r_dn)
    lax.fori_loop(0, width // 128, grad_d, 0)
    dmid[...] = reduce_pass(pt, l1, s2, l2, r_dn)

    gd_z = 2 * y_c + c
    r_gd = net.slots(4)

    def to_home(k):
        return pltpu.make_async_remote_copy(
            src_ref=gdt, dst_ref=lgd.at[k - 1],
            send_sem=send_sems.at[N_SEM - 4 + k], recv_sem=recv_sems.at[r_gd + k],
            device_id=dev(y, c, zat(k), x), device_id_type=MESH,
        )

    for k in range(1, 4):
        @pl.when(zat(k) == gd_z)
        def _(k=k):
            to_home(k).start()

    lax.fori_loop(0, width // 128, grad_gu, 0)
    r_gz = net.slots(4)
    for k in range(1, 4):
        net.send(
            ggu.at[:, pl.ds(off(zat(k), 2 * rows), 2 * rows)], lgu.at[k - 1], r_gz + k,
            dev(y, c, zat(k), x),
        )
    for finish in pt_sent:
        net.done(finish)
    lax.fori_loop(0, 4, feed_out, 0)
    r_out = net.slots(8)
    reduce_start(pt, l1o, r_out)

    total = dmid[...] + reduce_end(l2, r_dn)
    normed_two, inv_two = normed(mid[...])
    sg[0] = jnp.zeros(sg.shape[1:], F32)
    sg[0, 1:2] = jnp.sum(total * normed_two, 0, keepdims=True)
    dmid[...] = cot[...].astype(F32) + inv_two * (
        total - normed_two * jnp.mean(total * normed_two, -1, keepdims=True)
    )
    dmb[0] = dmid[...].astype(BF16)
    r_dm = net.slots(1)
    net.send(dmb.at[0], dmb.at[1], r_dm, partner)
    mid[...] = mid[...] + reduce_pass(pt, l1o, s2o, l2o, r_out)
    net.recv(dmb.at[1], r_dm)

    for part in range(4):
        for s in range(2):
            dm4[part, s * tokens : (s + 1) * tokens] = dmb[s, :, qcols * part : qcols * (part + 1)]
    dattn = dot_nt(dm4[0], wok[0])
    for part in range(1, 4):
        dattn = dattn + dot_nt(dm4[part], wok[part])
    qf[:, 0:qw] = dattn
    for s in range(2):
        for h in range(heads):
            do6[s * groups + h // per, (h % per) * tokens : (h % per + 1) * tokens] = qf[
                s * tokens : (s + 1) * tokens, HEAD_SIZE * h : HEAD_SIZE * (h + 1)
            ].astype(BF16)
    attn_all = ab[:, 0:qw]
    for part in range(4):
        act[qw * part : qw * (part + 1), 0:qcols] = dot_tn(attn_all, dm4[part]).astype(BF16)
    r_go = net.slots(16)
    for zz in range(2):
        for hx in range(2):
            for hy in range(2):
                for hc in range(2):
                    zt = 2 * c + zz
                    to_dp = 2 * flip(y, hy) + flip(c, hc)
                    at = pl.multiple_of(to_dp * qw + (2 * zz + flip(x, hx)) * rows, rows)
                    src = act.at[pl.ds(at, rows)]
                    dst = lo.at[zt, hx * 2 + hy]
                    slot = r_go + zt * 4 + hx * 2 + hy
                    if hx + hy + hc == 0:
                        net.keep(src, dst, slot)
                    else:
                        net.send(src, dst, slot, dev(flip(y, hy), flip(c, hc), z, flip(x, hx)))

    def attend_back(s, carry):
        for g in range(groups):
            at = s * groups + g
            kg = kv[s, :, HEAD_SIZE * g : HEAD_SIZE * (g + 1)]
            vg = kv[s, :, kw + HEAD_SIZE * g : kw + HEAD_SIZE * (g + 1)]
            dout = do6[at]
            delta = jnp.sum(dout.astype(F32) * o6[at].astype(F32), -1, keepdims=True)
            dprob = dot_nt(dout, vg)
            dscore = (p6[at].astype(F32) * (dprob - delta)).astype(BF16)
            dquery = dot_nn(dscore, kg) * scale
            dkeys = dot_tn(q6[at], dscore)
            dvals = dot_tn(dout, p6[at])
            for t in range(n_ctx):
                cols = slice(t * tokens, (t + 1) * tokens)
                dkv[t, s, HEAD_SIZE * g : HEAD_SIZE * (g + 1)] = dkeys[:, cols].astype(BF16)
                dkv[t, s, kw + HEAD_SIZE * g : kw + HEAD_SIZE * (g + 1)] = dvals[:, cols].astype(BF16)
            for i in range(per):
                h = g * per + i
                qf[pl.ds(off(s, tokens), tokens), HEAD_SIZE * h : HEAD_SIZE * (h + 1)] = dquery[
                    i * tokens : (i + 1) * tokens
                ]
        return carry

    lax.fori_loop(0, 2, attend_back, 0)
    r_dx, r_dz = net.slots(4), net.slots(4)
    for k in range(4):
        net.send(dkv.at[2 * zat(k) + 1 - x], lx.at[k], r_dx + k, dev(y, c, z, 1 - x))
    for t in range(qf.shape[1] // 128):
        qf[:, 128 * t : 128 * (t + 1)] = turn(qf[:, 128 * t : 128 * (t + 1)], False)
    for part in range(2):
        dqk[part, :, 0:qcols] = qf[:, qcols * part : qcols * (part + 1)].astype(BF16)
    for k in range(1, 4):
        net.recv(lx.at[k], r_dx + k)
        sx[k - 1] = (dkv[2 * zat(k) + x].astype(F32) + lx[k].astype(F32)).astype(BF16)
        net.send(sx.at[k - 1], lkz.at[k - 1], r_dz + k, dev(y, c, zat(k), x))

    r_gf, r_ld = net.slots(2), net.slots(1)
    mine = ggu[:, pl.ds(off(z, 2 * rows), 2 * rows)].astype(F32)
    for k in range(1, 4):
        net.recv(lgu.at[k - 1], r_gz + k)
        mine = mine + lgu[k - 1].astype(F32)
    sgu[...] = mine.astype(BF16)
    for hx in range(2):
        net.send(
            sgu.at[:, pl.ds(off(flip(x, hx), rows), rows)], lf.at[hx], r_gf + hx,
            dev(y_c, c, z, flip(x, hx)), is_self=(c == 0) if hx == 0 else None,
        )

    def share(hy, hc):
        to_dp = 2 * flip(y, hy) + flip(c, hc)
        return pltpu.make_async_remote_copy(
            src_ref=sgd.at[pl.ds(off(to_dp, drows), drows)], dst_ref=ld,
            send_sem=send_sems.at[N_SEM - 8 + 2 * hy + hc], recv_sem=recv_sems.at[r_ld],
            device_id=dev(flip(y, hy), flip(c, hc), z, x), device_id_type=MESH,
        )

    @pl.when(z == gd_z)
    def _():
        for k in range(1, 4):
            net.recv(lgd.at[k - 1], r_gd + k)

        def add(i, carry):
            at = pl.ds(off(i, 128), 128)
            part = gdt[at].astype(F32)
            for k in range(3):
                part = part + lgd[k, at].astype(F32)
            sgd[at] = part.astype(BF16)
            return carry

        lax.fori_loop(0, width // 128, add, 0)
        net.keep(sgd.at[pl.ds(off(dp, drows), drows)], ld, r_ld)
        for hy, hc in ((0, 1), (1, 0), (1, 1)):
            share(hy, hc).start()

    def attn_pass(land, out, send_at, slot, absolute):
        for k in (1, 2, 3, 0):
            at = zat(k) if absolute else k
            part = 0.0
            for h in range(4):
                net.recv(land.at[at, h], slot + at * 4 + h)
                part = part + land[at, h, :, 0 : out.shape[1]].astype(F32)
            if k == 0:
                out[...] = part
            else:
                send_at[0][k - 1] = part.astype(BF16)
                net.send(send_at[0].at[k - 1], send_at[1].at[k - 1], send_at[2] + k, dev(y, c, zat(k), x))

    r_zo, r_zq = net.slots(4), net.slots(4)
    attn_pass(lo, o_o, (so, lzo, r_zo), r_go, True)

    net.recv(lx.at[0], r_dx)
    total = dkv[2 * z + x].astype(F32) + lx[0].astype(F32)
    for k in range(1, 4):
        net.recv(lkz.at[k - 1], r_dz + k)
        total = total + lkz[k - 1].astype(F32)
    for s in range(2):
        kvf[s * tokens : (s + 1) * tokens] = total[s].T
    turn_keys(False)
    for part in range(2):
        dqk[part, :, qcols : qcols + kcols] = kvf[:, kcols * part : kcols * (part + 1)].astype(BF16)
        dqk[part, :, qcols + kcols :] = kvf[:, kw + kcols * part : kw + kcols * (part + 1)].astype(BF16)
    for part in range(2):
        got = dot_tn(n1[...], dqk[part]).astype(BF16)
        for t in range(n_ctx):
            p6[t // 2, (t % 2) * rows : (t % 2 + 1) * rows, 512 * part : 512 * part + qcols + 2 * kcols] = got[
                rows * t : rows * (t + 1)
            ]
    r_gq = net.slots(16)
    hy_c = y_c
    for k in (1, 2, 3, 0):
        for hx in range(2):
            for ct in range(2):
                net.send(
                    p6.at[zat(k), pl.ds(off(flip(x, hx), rows), rows), pl.ds(512 * ct, 512)],
                    lq.at[k, hx * 2 + hy_c],
                    r_gq + k * 4 + hx * 2 + hy_c,
                    dev(c, ct, z, flip(x, hx)),
                    is_self=jnp.logical_and(y == c, c == ct) if hx == 0 else None,
                )
    net.done(mp_sent)
    got = dot_nt(dqk[0], wq[0]) + dot_nt(dqk[1], wq[1])
    for s in range(2):
        mp[s] = got[s * tokens : (s + 1) * tokens]
    r_dn1 = net.slots(1)
    net.send(mp.at[1], ml, r_dn1, partner)
    net.recv(ml, r_dn1)
    total = mp[0] + ml[...]
    normed_one, inv_one = normed(tok[...])
    sg[0, 0:1] = jnp.sum(total * normed_one, 0, keepdims=True)
    r_lg = net.slots(8)
    for h in range(1, 8):
        net.send(
            sg.at[0], lg.at[h], r_lg + h, dev(flip(y, (h // 2) % 2), flip(c, h % 2), z, flip(x, h // 4))
        )
    o_ing[...] = (
        dmid[...]
        + inv_one * (total - normed_one * jnp.mean(total * normed_one, -1, keepdims=True))
    ).astype(BF16)
    gains = sg[0]
    for h in range(1, 8):
        net.recv(lg.at[h], r_lg + h)
        gains = gains + lg[h]
    sg[1] = gains
    r_lgz = net.slots(4)
    for k in range(1, 4):
        net.send(sg.at[1], lgz.at[k - 1], r_lgz + k, dev(y, c, zat(k), x))

    attn_pass(lq, o_qkv, (sq, lzq, r_zq), r_gq, False)

    o_out[...] = (mid[...] + reduce_end(l2o, r_out)).astype(BF16)
    for hx in range(2):
        net.recv(lf.at[hx], r_gf + hx)
        o_gu[:, :, pl.ds(off(flip(x, hx), ff), ff)] = lf[hx].astype(F32)
    net.recv(ld, r_ld)
    o_dt[...] = ld[...].astype(F32)
    for out, land, slot in ((o_o, lzo, r_zo), (o_qkv, lzq, r_zq)):
        for k in range(1, 4):
            net.recv(land.at[k - 1], slot + k)
            out[...] = out[...] + land[k - 1].astype(F32)
    gains = sg[1]
    for k in range(1, 4):
        net.recv(lgz.at[k - 1], r_lgz + k)
        gains = gains + lgz[k - 1]
    o_gain[...] = gains

    for k in range(1, 4):
        @pl.when(zat(k) == gd_z)
        def _(k=k):
            to_home(k).wait_send()

    @pl.when(z == gd_z)
    def _():
        for hy, hc in ((0, 1), (1, 0), (1, 1)):
            share(hy, hc).wait_send()

    net.drain()


def run_layer(tok, cot, cs, bias, wqkv, wo, wgu, wdt):
    tokens, width = tok.shape
    rows, packed = wqkv.shape
    qcols = wo.shape[1]
    drows, ff = wdt.shape
    keys = bias.shape[1]
    n_ctx = keys // tokens
    qw = 2 * qcols
    kw = packed - qcols
    groups = kw // HEAD_SIZE
    per = QUERY_HEADS // KEY_VALUE_HEADS
    stack = per * tokens
    wide = -(-qw // 128) * 128
    out_shape = [
        jax.ShapeDtypeStruct((tokens, width), BF16),
        jax.ShapeDtypeStruct((tokens, width), BF16),
        jax.ShapeDtypeStruct((8, width), F32),
        jax.ShapeDtypeStruct((rows, packed), F32),
        jax.ShapeDtypeStruct((rows, qcols), F32),
        jax.ShapeDtypeStruct((2, rows, 2 * ff), F32),
        jax.ShapeDtypeStruct((drows, ff), F32),
    ]

    def vm(*shape, dtype=BF16):
        return pltpu.VMEM(shape, dtype)

    scratch = [
        vm(2 * tokens, 256, dtype=F32),
        vm(2, 8, keys, dtype=F32),
        vm(tokens, width),
        vm(3, rows, packed),
        vm(3, rows, qcols),
        vm(2, width, packed),
        vm(4, 4 * rows, qcols),
        vm(2, width, ff),
        vm(width, ff),
        vm(8, tokens, width),
        vm(8, tokens, width),
        vm(2 * tokens, width),
        vm(2 * tokens, wide, dtype=F32),
        vm(2 * tokens, 2 * kw, dtype=F32),
        vm(2, keys, 2 * kw),
        vm(2 * groups, stack, HEAD_SIZE),
        vm(2 * groups, stack, keys),
        vm(2 * groups, stack, HEAD_SIZE),
        vm(2 * tokens, wide),
        vm(2, tokens, width, dtype=F32),
        vm(tokens, width, dtype=F32),
        vm(tokens, width, dtype=F32),
        vm(tokens, width, dtype=F32),
        vm(2, tokens, width),
        vm(4, 2 * tokens, qcols),
        vm(2 * groups, stack, HEAD_SIZE),
        vm(24 * tokens, ff),
        vm(8, tokens, width),
        vm(4, tokens, width),
        vm(3, tokens, width),
        vm(3, tokens, width),
        vm(4, tokens, width),
        vm(3, tokens, width),
        vm(3, tokens, width),
        vm(2, width, ff),
        vm(3, 2, 2 * rows, ff),
        vm(2, 2 * rows, ff),
        vm(2, 2, rows, ff),
        vm(width, ff),
        vm(3, width, ff),
        vm(width, ff),
        vm(drows, ff),
        vm(4, 4, rows, ff),
        vm(4, 4, rows, 512),
        vm(3, rows, qcols),
        vm(3, rows, packed),
        vm(3, rows, qcols),
        vm(3, rows, packed),
        vm(n_ctx, 2, 2 * kw, tokens),
        vm(4, 2, 2 * kw, tokens),
        vm(3, 2, 2 * kw, tokens),
        vm(3, 2, 2 * kw, tokens),
        vm(8, 8, width, dtype=F32),
        vm(2, 8, width, dtype=F32),
        vm(3, 8, width, dtype=F32),
        vm(2, 2 * tokens, packed),
        pltpu.SemaphoreType.DMA((N_SEM,)),
        pltpu.SemaphoreType.DMA((N_SEM,)),
    ]
    inside = pl.BlockSpec(memory_space=pltpu.VMEM)
    return pl.pallas_call(
        layer_kernel,
        out_shape=out_shape,
        in_specs=[inside] * 8,
        out_specs=[inside] * len(out_shape),
        scratch_shapes=scratch,
        compiler_params=pltpu.CompilerParams(
            collective_id=0, has_side_effects=True, vmem_limit_bytes=VMEM_LIMIT
        ),
        name="layer",
    )(tok, cot, cs, bias, wqkv, wo, wgu, wdt)


VMEM_LIMIT = 63 * 1024 * 1024


def on_device_plane(
    tokens, positions, block_sizes, attn_gain, w_query, w_key, w_value, w_out, mlp_gain,
    w_gate, w_up, w_down, cotangent,
):
    seq_rows, width = tokens.shape[1:]
    ctx = lax.axis_index("ctx")
    angles = angles_of(positions[0])
    cosine, sine = jnp.cos(angles), jnp.sin(angles)
    cs = jnp.concatenate([cosine] * 4 + [-sine, sine] * 2, 1)
    keys = seq_rows * lax.axis_size("ctx")
    block = block_sizes[0]
    limit = (ctx * seq_rows // block + 1) * block
    bias = jnp.where(jnp.arange(keys, dtype=jnp.int32) < limit, 0.0, VERY_NEGATIVE).astype(F32)
    bias = jnp.broadcast_to(bias[None, :], (8, keys))
    gain_one = attn_gain.astype(F32)[:, None]
    gain_two = mlp_gain.astype(F32)[:, None]
    wqkv = (jnp.concatenate([w_query, w_key, w_value], 1).astype(F32) * gain_one).astype(BF16)
    wgu = jnp.stack([(w_gate.astype(F32) * gain_two).astype(BF16), (w_up.astype(F32) * gain_two).astype(BF16)])
    output, input_grad, gains, g_qkv, g_o, g_gu, g_dt = run_layer(
        tokens[0], cotangent[0], cs, bias, wqkv, w_out, wgu, w_down.T
    )
    rows, qcols = w_query.shape
    kcols = w_key.shape[1]
    part = lax.dynamic_slice(gains, (0, ctx * rows), (2, rows))
    g_qkv = g_qkv * gain_one
    return (
        output[None],
        input_grad[None],
        part[0] / gain_one[:, 0],
        g_qkv[:, :qcols],
        g_qkv[:, qcols : qcols + kcols],
        g_qkv[:, qcols + kcols :],
        g_o,
        part[1] / gain_two[:, 0],
        g_gu[0] * gain_two,
        g_gu[1] * gain_two,
        g_dt.T,
    )


def solution(mesh):
    placed = (
        P("dp", "ctx", None),
        P("dp", "ctx"),
        P("dp"),
        P("ctx"),
        P("ctx", "dp"),
        P("ctx", "dp"),
        P("ctx", "dp"),
        P("ctx", "dp"),
        P("ctx"),
        P("ctx", "dp"),
        P("ctx", "dp"),
        P("ctx", "dp"),
        P("dp", "ctx", None),
    )
    fits = mesh.shape["dp"] == 4 and mesh.shape["ctx"] == 8
    return jax.shard_map(
        on_device_plane if fits else on_device,
        mesh=mesh,
        in_specs=placed,
        out_specs=(
            P("dp", "ctx", None),
            P("dp", "ctx", None),
            P("ctx"),
            P("ctx", "dp"),
            P("ctx", "dp"),
            P("ctx", "dp"),
            P("ctx", "dp"),
            P("ctx"),
            P("ctx", "dp"),
            P("ctx", "dp"),
            P("ctx", "dp"),
        ),
        check_vma=False,
    )
```

```python
import jax
import jax.numpy as jnp
from jax import lax
from jax.experimental import pallas as pl
from jax.experimental.pallas import tpu as pltpu
from jax.sharding import PartitionSpec as P

QUERY_HEADS = 18
KEY_VALUE_HEADS = 6
HEAD_SIZE = 64


EPSILON = 1e-05
THETA = 10000.0
VERY_NEGATIVE = -1e30


def product(left, right):
    return jnp.dot(left, right, preferred_element_type=jnp.float32)


def angles_of(place_ids):
    half_dim = HEAD_SIZE // 2
    frequency = THETA ** (-(jnp.arange(half_dim, dtype=jnp.float32) * 2.0 / HEAD_SIZE))
    return place_ids.astype(jnp.float32)[:, None] * frequency[None, :]


def rotate(values, angles, forward):
    row_total = values.shape[0]
    half_dim = angles.shape[1]
    shaped = values.reshape(row_total, -1, 2 * half_dim)
    first_half = shaped[..., :half_dim]
    second = shaped[..., half_dim:]
    cosine = jnp.cos(angles)[:, None, :]
    sine_vals = jnp.sin(angles)[:, None, :]
    if forward:
        rotated = jnp.concatenate(
            [first_half * cosine - second * sine_vals, second * cosine + first_half * sine_vals], -1
        )
    else:
        rotated = jnp.concatenate(
            [first_half * cosine + second * sine_vals, second * cosine - first_half * sine_vals], -1
        )
    return rotated.reshape(row_total, -1)


def norm_back(grad_normed, normed, inverse):
    return inverse * (grad_normed - normed * jnp.mean(grad_normed * normed, -1, keepdims=True))


def visible(query_rows, key_rows, block_len):
    return ((key_rows // block_len)[None, :] <= (query_rows // block_len)[:, None])[None, None]


def attend_forward(query_rows4, complete_keys, complete_values, query_rows, block_len, score_scale):
    key_count = complete_keys.shape[0]
    key_row_width = 512
    block_list = key_count // key_row_width
    query_group_width = QUERY_HEADS // KEY_VALUE_HEADS
    row_total = query_rows4.shape[0]
    key_block_list = complete_keys.reshape(block_list, key_row_width, KEY_VALUE_HEADS, HEAD_SIZE)
    value_block_list = complete_values.reshape(
        block_list, key_row_width, KEY_VALUE_HEADS, HEAD_SIZE
    )
    last_block = query_rows[-1] // block_len

    def advance(carried, inputs):
        key_blk, val_blk, first_key = inputs
        key_rows = first_key + jnp.arange(key_row_width, dtype=jnp.int32)

        def compute(current):
            run_max, run_sum, accum = current
            scores = (
                jnp.einsum(
                    "tkgd,nkd->kgtn", query_rows4, key_blk, preferred_element_type=jnp.float32
                )
                * score_scale
            )
            allowed = visible(query_rows, key_rows, block_len)
            scores = jnp.where(allowed, scores, VERY_NEGATIVE)
            new_max = jnp.maximum(run_max, jnp.max(scores, -1))
            weights = jnp.where(allowed, jnp.exp(scores - new_max[..., None]), 0.0)
            factor = jnp.exp(run_max - new_max)
            new_sum = run_sum * factor + jnp.sum(weights, -1)
            accum = accum * factor[..., None] + jnp.einsum(
                "kgtn,nkd->kgtd",
                weights.astype(jnp.bfloat16),
                val_blk,
                preferred_element_type=jnp.float32,
            )
            return (new_max, new_sum, accum)

        return (
            lax.cond(
                first_key // block_len > last_block, lambda unchanged: unchanged, compute, carried
            ),
            None,
        )

    start_state = (
        jnp.full((KEY_VALUE_HEADS, query_group_width, row_total), VERY_NEGATIVE, jnp.float32),
        jnp.zeros((KEY_VALUE_HEADS, query_group_width, row_total), jnp.float32),
        jnp.zeros((KEY_VALUE_HEADS, query_group_width, row_total, HEAD_SIZE), jnp.float32),
    )
    firsts = jnp.arange(block_list, dtype=jnp.int32) * key_row_width
    final_state, unused = lax.scan(advance, start_state, (key_block_list, value_block_list, firsts))
    run_max, run_sum, accum = final_state
    return (accum / run_sum[..., None], run_max + jnp.log(run_sum))


def attend_backward(
    query_rows4,
    head_gradients,
    log_sums,
    row_delta,
    complete_keys,
    complete_values,
    query_rows,
    block_len,
    score_scale,
):
    key_count = complete_keys.shape[0]
    key_row_width = 512
    block_list = key_count // key_row_width
    query_group_width = QUERY_HEADS // KEY_VALUE_HEADS
    row_total = query_rows4.shape[0]
    key_block_list = complete_keys.reshape(block_list, key_row_width, KEY_VALUE_HEADS, HEAD_SIZE)
    value_block_list = complete_values.reshape(
        block_list, key_row_width, KEY_VALUE_HEADS, HEAD_SIZE
    )
    last_block = query_rows[-1] // block_len

    def advance(grad_query, inputs):
        key_blk, val_blk, first_key = inputs
        key_rows = first_key + jnp.arange(key_row_width, dtype=jnp.int32)

        def compute(current):
            scores = (
                jnp.einsum(
                    "tkgd,nkd->kgtn", query_rows4, key_blk, preferred_element_type=jnp.float32
                )
                * score_scale
            )
            allowed = visible(query_rows, key_rows, block_len)
            prob_vals = jnp.where(allowed, jnp.exp(scores - log_sums[..., None]), 0.0)
            grad_prob = jnp.einsum(
                "tkgd,nkd->kgtn", head_gradients, val_blk, preferred_element_type=jnp.float32
            )
            grad_score = (prob_vals * (grad_prob - row_delta[..., None])).astype(jnp.bfloat16)
            current = current + jnp.einsum(
                "kgtn,nkd->tkgd", grad_score, key_blk, preferred_element_type=jnp.float32
            )
            grad_key = jnp.einsum(
                "kgtn,tkgd->nkd", grad_score, query_rows4, preferred_element_type=jnp.float32
            )
            grad_value = jnp.einsum(
                "kgtn,tkgd->nkd",
                prob_vals.astype(jnp.bfloat16),
                head_gradients,
                preferred_element_type=jnp.float32,
            )
            return (current, (grad_key, grad_value))

        def nothing(current):
            empty_block = jnp.zeros((key_row_width, KEY_VALUE_HEADS, HEAD_SIZE), jnp.float32)
            return (current, (empty_block, empty_block))

        return lax.cond(first_key // block_len > last_block, nothing, compute, grad_query)

    firsts = jnp.arange(block_list, dtype=jnp.int32) * key_row_width
    initial_gradient = jnp.zeros(
        (row_total, KEY_VALUE_HEADS, query_group_width, HEAD_SIZE), jnp.float32
    )
    grad_query, stacked_rows = lax.scan(
        advance, initial_gradient, (key_block_list, value_block_list, firsts)
    )
    key_gradients = stacked_rows[0].reshape(key_count, KEY_VALUE_HEADS * HEAD_SIZE)
    value_gradients = stacked_rows[1].reshape(key_count, KEY_VALUE_HEADS * HEAD_SIZE)
    return (grad_query, key_gradients, value_gradients)


def on_device(
    tokens,
    positions,
    block_sizes,
    attn_gain,
    w_query,
    w_key,
    w_value,
    w_out,
    mlp_gain,
    w_gate,
    w_up,
    w_down,
    cotangent,
):
    row_parts = (
        lax.all_gather(w_query, "ctx", axis=0, tiled=True),
        lax.all_gather(w_key, "ctx", axis=0, tiled=True),
        lax.all_gather(w_value, "ctx", axis=0, tiled=True),
        lax.all_gather(w_out, "ctx", axis=0, tiled=True),
        lax.all_gather(w_gate, "ctx", axis=0, tiled=True),
        lax.all_gather(w_up, "ctx", axis=0, tiled=True),
        lax.all_gather(w_down, "ctx", axis=0, tiled=True),
        lax.all_gather(attn_gain, "ctx", axis=0, tiled=True),
        lax.all_gather(mlp_gain, "ctx", axis=0, tiled=True),
    )
    whole_w = (
        lax.all_gather(row_parts[0], "dp", axis=1, tiled=True),
        lax.all_gather(row_parts[1], "dp", axis=1, tiled=True),
        lax.all_gather(row_parts[2], "dp", axis=1, tiled=True),
        lax.all_gather(row_parts[3], "dp", axis=1, tiled=True),
        lax.all_gather(row_parts[4], "dp", axis=1, tiled=True),
        lax.all_gather(row_parts[5], "dp", axis=1, tiled=True),
        lax.all_gather(row_parts[6], "dp", axis=1, tiled=True),
    )
    query_w, key_w, value_w, out_w, gate_w, up_w, down_w = whole_w
    gain_one = row_parts[7].astype(jnp.float32)
    gain_two = row_parts[8].astype(jnp.float32)
    seq_count = tokens.shape[0]
    seq_rows = tokens.shape[1]
    width = tokens.shape[2]
    inputs = tokens.reshape(seq_count * seq_rows, width).astype(jnp.float32)
    row_total = inputs.shape[0]
    query_group_width = QUERY_HEADS // KEY_VALUE_HEADS
    query_rows = lax.axis_index("ctx") * seq_rows + jnp.arange(seq_rows, dtype=jnp.int32)
    angles = angles_of(positions.reshape(-1))
    score_scale = HEAD_SIZE ** (-0.5)
    inv_one = lax.rsqrt(jnp.mean(inputs * inputs, -1, keepdims=True) + EPSILON)
    normed_one = inputs * inv_one
    hidden_one = (normed_one * gain_one).astype(jnp.bfloat16)
    query_matrix = rotate(product(hidden_one, query_w), angles, True).astype(jnp.bfloat16)
    keys_own = rotate(product(hidden_one, key_w), angles, True).astype(jnp.bfloat16)
    values_own = product(hidden_one, value_w).astype(jnp.bfloat16)
    complete_keys, complete_values = (
        lax.all_gather(keys_own.reshape(seq_count, seq_rows, -1), "ctx", axis=1, tiled=True),
        lax.all_gather(values_own.reshape(seq_count, seq_rows, -1), "ctx", axis=1, tiled=True),
    )
    query_rows4 = query_matrix.reshape(row_total, KEY_VALUE_HEADS, query_group_width, HEAD_SIZE)
    member = 0
    heads_one, lse_one = attend_forward(
        query_rows4,
        complete_keys[member],
        complete_values[member],
        query_rows,
        block_sizes[member],
        score_scale,
    )
    attn_flat = heads_one.transpose(2, 0, 1, 3).reshape(row_total, QUERY_HEADS * HEAD_SIZE)
    attn_low = attn_flat.astype(jnp.bfloat16)
    mixed_rows = inputs + product(attn_low, out_w)
    inv_two = lax.rsqrt(jnp.mean(mixed_rows * mixed_rows, -1, keepdims=True) + EPSILON)
    normed_two = mixed_rows * inv_two
    hidden_two = (normed_two * gain_two).astype(jnp.bfloat16)
    gate_pre = product(hidden_two, gate_w)
    up_pre = product(hidden_two, up_w)
    sigmoid_gate = jax.nn.sigmoid(gate_pre)
    silu_gate = gate_pre * sigmoid_gate
    inner_act = (silu_gate * up_pre).astype(jnp.bfloat16)
    result = mixed_rows + product(inner_act, down_w)
    output = result.astype(jnp.bfloat16).reshape(seq_count, seq_rows, width)
    back_parts = (
        lax.all_gather(w_query, "ctx", axis=0, tiled=True),
        lax.all_gather(w_key, "ctx", axis=0, tiled=True),
        lax.all_gather(w_value, "ctx", axis=0, tiled=True),
        lax.all_gather(w_out, "ctx", axis=0, tiled=True),
        lax.all_gather(w_gate, "ctx", axis=0, tiled=True),
        lax.all_gather(w_up, "ctx", axis=0, tiled=True),
        lax.all_gather(w_down, "ctx", axis=0, tiled=True),
    )
    back_whole = (
        lax.all_gather(back_parts[0], "dp", axis=1, tiled=True),
        lax.all_gather(back_parts[1], "dp", axis=1, tiled=True),
        lax.all_gather(back_parts[2], "dp", axis=1, tiled=True),
        lax.all_gather(back_parts[3], "dp", axis=1, tiled=True),
        lax.all_gather(back_parts[4], "dp", axis=1, tiled=True),
        lax.all_gather(back_parts[5], "dp", axis=1, tiled=True),
        lax.all_gather(back_parts[6], "dp", axis=1, tiled=True),
    )
    back_query, back_key, back_value, back_out, back_gate, back_up, back_down = back_whole
    grad_top = cotangent.reshape(row_total, width)
    grad_down = jnp.einsum("tf,td->fd", inner_act, grad_top, preferred_element_type=jnp.float32)
    grad_inner = jnp.einsum("td,fd->tf", grad_top, back_down, preferred_element_type=jnp.float32)
    grad_gate = (
        grad_inner * up_pre * sigmoid_gate * (1.0 + gate_pre * (1.0 - sigmoid_gate))
    ).astype(jnp.bfloat16)
    grad_upval = (grad_inner * silu_gate).astype(jnp.bfloat16)
    grad_gatew = jnp.einsum("td,tf->df", hidden_two, grad_gate, preferred_element_type=jnp.float32)
    grad_upw = jnp.einsum("td,tf->df", hidden_two, grad_upval, preferred_element_type=jnp.float32)
    grad_hidden_two = jnp.einsum(
        "tf,df->td", grad_gate, back_gate, preferred_element_type=jnp.float32
    ) + jnp.einsum("tf,df->td", grad_upval, back_up, preferred_element_type=jnp.float32)
    grad_gain_two = jnp.sum(grad_hidden_two * normed_two, 0)
    grad_mixed = grad_top.astype(jnp.float32) + norm_back(
        grad_hidden_two * gain_two, normed_two, inv_two
    )
    grad_branch = grad_mixed.astype(jnp.bfloat16)
    grad_outw = jnp.einsum("tq,td->qd", attn_low, grad_branch, preferred_element_type=jnp.float32)
    attention_gradient = jnp.einsum(
        "td,qd->tq", grad_branch, back_out, preferred_element_type=jnp.float32
    ).astype(jnp.bfloat16)
    head_gradients = attention_gradient.reshape(
        row_total, KEY_VALUE_HEADS, query_group_width, HEAD_SIZE
    )
    row_delta = jnp.einsum("tkgd,kgtd->kgt", head_gradients.astype(jnp.float32), heads_one)
    member = 0
    grad_q_one, grad_k_one, grad_v_one = attend_backward(
        query_rows4,
        head_gradients,
        lse_one,
        row_delta,
        complete_keys[member],
        complete_values[member],
        query_rows,
        block_sizes[member],
        score_scale,
    )
    key_grads = [grad_k_one]
    value_grads = [grad_v_one]
    grad_keys_all = jnp.stack(key_grads, 0)
    grad_values_all = jnp.stack(value_grads, 0)
    grad_keys_own, grad_values_own = (
        lax.psum_scatter(grad_keys_all, "ctx", scatter_dimension=1, tiled=True),
        lax.psum_scatter(grad_values_all, "ctx", scatter_dimension=1, tiled=True),
    )
    grad_keys_own = grad_keys_own.reshape(row_total, -1)
    grad_values_own = grad_values_own.reshape(row_total, -1)
    grad_query_raw = rotate(
        grad_q_one.reshape(row_total, QUERY_HEADS * HEAD_SIZE) * score_scale, angles, False
    ).astype(jnp.bfloat16)
    grad_key_raw = rotate(grad_keys_own * score_scale, angles, False).astype(jnp.bfloat16)
    grad_value_raw = grad_values_own.astype(jnp.bfloat16)
    grad_queryw = jnp.einsum(
        "td,tq->dq", hidden_one, grad_query_raw, preferred_element_type=jnp.float32
    )
    grad_keyw = jnp.einsum(
        "td,tq->dq", hidden_one, grad_key_raw, preferred_element_type=jnp.float32
    )
    grad_valuew = jnp.einsum(
        "td,tq->dq", hidden_one, grad_value_raw, preferred_element_type=jnp.float32
    )
    grad_hidden_one = jnp.einsum(
        "tq,dq->td", grad_query_raw, back_query, preferred_element_type=jnp.float32
    )
    grad_hidden_one = grad_hidden_one + jnp.einsum(
        "tq,dq->td", grad_key_raw, back_key, preferred_element_type=jnp.float32
    )
    grad_hidden_one = grad_hidden_one + jnp.einsum(
        "tq,dq->td", grad_value_raw, back_value, preferred_element_type=jnp.float32
    )
    grad_gain_one = jnp.sum(grad_hidden_one * normed_one, 0)
    grad_input = grad_mixed + norm_back(grad_hidden_one * gain_one, normed_one, inv_one)
    input_grad = grad_input.astype(jnp.bfloat16).reshape(seq_count, seq_rows, width)
    summed_rows = (
        lax.psum_scatter(grad_queryw, "ctx", scatter_dimension=0, tiled=True),
        lax.psum_scatter(grad_keyw, "ctx", scatter_dimension=0, tiled=True),
        lax.psum_scatter(grad_valuew, "ctx", scatter_dimension=0, tiled=True),
        lax.psum_scatter(grad_outw, "ctx", scatter_dimension=0, tiled=True),
        lax.psum_scatter(grad_gatew, "ctx", scatter_dimension=0, tiled=True),
        lax.psum_scatter(grad_upw, "ctx", scatter_dimension=0, tiled=True),
        lax.psum_scatter(grad_down, "ctx", scatter_dimension=0, tiled=True),
        lax.psum_scatter(grad_gain_one, "ctx", scatter_dimension=0, tiled=True),
        lax.psum_scatter(grad_gain_two, "ctx", scatter_dimension=0, tiled=True),
    )
    final_w = (
        lax.psum_scatter(
            summed_rows[0].astype(jnp.bfloat16), "dp", scatter_dimension=1, tiled=True
        ).astype(jnp.float32),
        lax.psum_scatter(
            summed_rows[1].astype(jnp.bfloat16), "dp", scatter_dimension=1, tiled=True
        ).astype(jnp.float32),
        lax.psum_scatter(
            summed_rows[2].astype(jnp.bfloat16), "dp", scatter_dimension=1, tiled=True
        ).astype(jnp.float32),
        lax.psum_scatter(
            summed_rows[3].astype(jnp.bfloat16), "dp", scatter_dimension=1, tiled=True
        ).astype(jnp.float32),
        lax.psum_scatter(
            summed_rows[4].astype(jnp.bfloat16), "dp", scatter_dimension=1, tiled=True
        ).astype(jnp.float32),
        lax.psum_scatter(
            summed_rows[5].astype(jnp.bfloat16), "dp", scatter_dimension=1, tiled=True
        ).astype(jnp.float32),
        lax.psum_scatter(
            summed_rows[6].astype(jnp.bfloat16), "dp", scatter_dimension=1, tiled=True
        ).astype(jnp.float32),
    )
    final_gains = lax.psum((summed_rows[7], summed_rows[8]), "dp")
    return (
        output,
        input_grad,
        final_gains[0],
        final_w[0],
        final_w[1],
        final_w[2],
        final_w[3],
        final_gains[1],
        final_w[4],
        final_w[5],
        final_w[6],
    )


MESH = pl.DeviceIdType.MESH
F32 = jnp.float32
BF16 = jnp.bfloat16


def dot_nn(a, b):
    return lax.dot_general(a, b, (((1,), (0,)), ((), ())), preferred_element_type=F32)


def dot_nt(a, b):
    return lax.dot_general(a, b, (((1,), (1,)), ((), ())), preferred_element_type=F32)


def dot_tn(a, b):
    return lax.dot_general(a, b, (((0,), (0,)), ((), ())), preferred_element_type=F32)


class Wires:
    def __init__(self, send_sems, recv_sems):
        self.send_sems, self.recv_sems = send_sems, recv_sems
        self.sends = 0
        self.recvs = 0
        self.pending = []

    def slots(self, count):
        first = self.recvs
        self.recvs += count
        return first

    def send(self, src, dst, slot, device, is_self=None, only=None):
        mine = self.sends
        self.sends += 1
        remote = pltpu.make_async_remote_copy(
            src_ref=src,
            dst_ref=dst,
            send_sem=self.send_sems.at[mine],
            recv_sem=self.recv_sems.at[slot],
            device_id=device,
            device_id_type=MESH,
        )
        if only is not None:

            @pl.when(only)
            def _():
                remote.start()

            def finish():
                @pl.when(only)
                def _():
                    remote.wait_send()

        elif is_self is None:
            remote.start()
            finish = remote.wait_send
        else:
            local = pltpu.make_async_copy(src, dst, self.recv_sems.at[slot])

            @pl.when(is_self)
            def _():
                local.start()

            @pl.when(jnp.logical_not(is_self))
            def _():
                remote.start()

            def finish():
                @pl.when(jnp.logical_not(is_self))
                def _():
                    remote.wait_send()

        self.pending.append(finish)
        return finish

    def keep(self, src, dst, slot):
        pltpu.make_async_copy(src, dst, self.recv_sems.at[slot]).start()

    def recv(self, dst, slot):
        pltpu.make_async_copy(dst, dst, self.recv_sems.at[slot]).wait()

    def done(self, finish):
        finish()
        self.pending.remove(finish)

    def drain(self):
        for finish in self.pending:
            finish()
        self.pending = []


N_SEM = 256


def layer_kernel(
    tok, cot, cs, bias, gain, wqkv, wo, wgate, wup, wdt,
    o_out, o_ing, o_gain, o_q, o_k, o_v, o_o, o_gate, o_up, o_d,
    csf, b2, x2, gb, grow, wqz, woz, wq, wok, wg8, wd8, c8, n8, n1, qf, kvf, kv, q6, p6, o6, ab,
    mp, ml, mid, dmid, dmb, dm4, do6, act, pt, l1, s2, l2, l1o, s2o, l2o,
    ggu, lgu, lf, gdt, lgd, sgd, ld, lo, lq, lk, so, sq, sk, lzo, lzq, lzk, kvg, dkv, lx, sx, lkz,
    lg, sg, dqk, send_sems, recv_sems,
):
    net = Wires(send_sems, recv_sems)
    dp = lax.axis_index("dp")
    ctx = lax.axis_index("ctx")
    y, c = dp // 2, lax.rem(dp, 2)
    z, x = ctx // 2, lax.rem(ctx, 2)
    z_hi, z_lo = z // 2, lax.rem(z, 2)
    y_c = y + c - 2 * y * c
    tokens, width = tok.shape
    rows = wqkv.shape[0]
    qcols = wo.shape[1]
    kcols = (wqkv.shape[1] - qcols) // 2
    ff = wdt.shape[1]
    drows = wdt.shape[0]
    qw = 2 * qcols
    kw = 2 * kcols
    groups = kw // HEAD_SIZE
    per = QUERY_HEADS // KEY_VALUE_HEADS
    heads = groups * per
    keys = kv.shape[1]
    n_ctx = keys // tokens
    scale = HEAD_SIZE ** (-0.5)

    def flip(a, h):
        return 1 - a if h else a

    def zat(k):
        return (z, 2 * z_hi + 1 - z_lo, 2 * (1 - z_hi) + z_lo, 3 - z)[k]

    def dev(yy, cc, zz, xx):
        return (2 * yy + cc, 2 * zz + xx)

    def off(value, step):
        return pl.multiple_of(value * step, step)

    partner = dev(y, 1 - c, z, x)

    barrier = pltpu.get_barrier_semaphore()
    for k in range(4):
        for hx in range(2):
            for hy in range(2):
                for hc in range(2):
                    if k + hx + hy + hc:
                        pl.semaphore_signal(
                            barrier, inc=1,
                            device_id=dev(flip(y, hy), flip(c, hc), zat(k), flip(x, hx)),
                            device_id_type=MESH,
                        )
    pl.semaphore_wait(barrier, 31)

    r_tok = net.slots(3)
    net.send(tok, x2, r_tok, partner)
    net.send(cs, csf.at[pl.ds(tokens, tokens)], r_tok + 1, partner)
    net.send(bias, b2.at[1], r_tok + 2, partner)
    r_g = net.slots(8)
    r_wqz, r_wq = net.slots(4), net.slots(16)

    def spread_qkv(k, src):
        zs = zat(k)
        for hx, hy in ((0, 0), (1, 0), (0, 1)):
            net.send(
                src,
                wq.at[c, pl.ds(off(2 * zs + x, rows), rows)],
                r_wq + k * 4 + hx * 2 + c,
                dev(flip(y, hy), y, z, flip(x, hx)),
                is_self=(c == y) if hx + hy == 0 else None,
            )

    for k in range(1, 4):
        net.send(wqkv, wqz.at[k - 1], r_wqz + k, dev(y, c, zat(k), x))
    spread_qkv(0, wqkv)
    for k in range(4):
        for hx in range(2):
            if k + hx:
                net.send(gain, gb.at[ctx], r_g + 2 * k + hx, dev(y, c, zat(k), flip(x, hx)))

    csf[0:tokens] = cs[...]
    b2[0] = bias[...]
    gb[ctx] = gain[...]
    c8[0] = cot[...]

    def normed(values):
        v = values.astype(F32)
        inv = lax.rsqrt(jnp.mean(v * v, -1, keepdims=True) + EPSILON)
        return v * inv, inv

    for k in range(1, 4):
        net.recv(wqz.at[k - 1], r_wqz + k)
        spread_qkv(k, wqz.at[k - 1])

    r_woz, r_wo = net.slots(4), net.slots(16)

    def spread_wo(k, src):
        zs = zat(k)
        core = zs // 2
        for hx, hy in ((0, 0), (1, 0), (0, 1)):
            net.send(
                src,
                wok.at[dp, pl.ds(off(2 * lax.rem(zs, 2) + x, rows), rows)],
                r_wo + lax.rem(zs, 2) * 8 + hx * 4 + hy * 2 + c,
                dev(flip(y, hy), core, z, flip(x, hx)),
                is_self=(c == core) if hx + hy == 0 else None,
            )

    r_gu, r_wd, r_wy = net.slots(16), net.slots(2), net.slots(2)
    home = y_c == z_lo

    def send_ff(m):
        for zh in range(2):
            for hx in range(2):
                net.send(
                    (wgate, wup)[m].at[:, pl.ds(off(flip(x, hx), ff), ff)],
                    wg8.at[m, pl.ds(off(ctx, rows), rows)],
                    r_gu + m * 8 + ctx,
                    dev(y, c, 2 * zh + y_c, flip(x, hx)),
                    is_self=(z == 2 * zh + y_c) if hx == 0 else None,
                )

    ff_passed = []

    def pass_ff(m):
        for i in range(n_ctx):
            part = wg8.at[m, pl.ds(rows * i, rows)]

            @pl.when(home)
            def _():
                net.recv(part, r_gu + m * 8 + i)

            ff_passed.append(
                net.send(part, part, r_gu + m * 8 + i, dev(1 - y, c, z, x), only=home)
            )

    def take_ff(m):
        for i in range(n_ctx):

            @pl.when(jnp.logical_not(home))
            def _():
                net.recv(wg8.at[m, pl.ds(rows * i, rows)], r_gu + m * 8 + i)

    def send_down():
        z_x = z_hi + z_lo - 2 * z_hi * z_lo
        for zh in range(2):
            net.send(
                wdt,
                wd8.at[pl.ds(off(dp, drows), drows)],
                r_wd + c,
                dev(y, z_lo, 2 * zh + z_x, x),
                is_self=jnp.logical_and(z == 2 * zh + z_x, c == z_lo),
            )

    for k in range(1, 4):
        net.send(wo, woz.at[k - 1], r_woz + k, dev(y, c, zat(k), x))
    spread_wo(0, wo)
    send_ff(0)

    for k in range(4):
        for hx in range(2):
            if k + hx:
                net.recv(gb.at[2 * zat(k) + flip(x, hx)], r_g + 2 * k + hx)
    for t in range(n_ctx):
        grow[:, rows * t : rows * (t + 1)] = gb[t]
    n1[0:tokens] = (normed(tok[...])[0] * grow[0:1]).astype(BF16)
    net.recv(x2, r_tok)
    n1[tokens : 2 * tokens] = (normed(x2[...])[0] * grow[0:1]).astype(BF16)
    net.recv(csf.at[pl.ds(tokens, tokens)], r_tok + 1)
    net.recv(b2.at[1], r_tok + 2)

    for k in range(4):
        at_x = pl.ds(off(2 * zat(k) + x, rows), rows)
        at_o = pl.ds(off(2 * zat(k) + 1 - x, rows), rows)
        slot = r_wq + k * 4

        @pl.when(c == y)
        def _():
            net.recv(wq.at[0, at_o], slot + 2)

        net.send(wq.at[0, at_o], wq.at[0, at_o], slot + 2, dev(1 - y, c, z, x), only=(c == y))

        @pl.when(c != y)
        def _():
            net.recv(wq.at[1, at_x], slot + 1)

        net.send(wq.at[1, at_x], wq.at[1, at_x], slot + 3, dev(y, c, z, 1 - x), only=(c != y))
    for k in range(1, 4):
        net.recv(woz.at[k - 1], r_woz + k)
        spread_wo(k, woz.at[k - 1])
    for k in range(4):
        at_x = pl.ds(off(2 * zat(k) + x, rows), rows)
        at_o = pl.ds(off(2 * zat(k) + 1 - x, rows), rows)
        slot = r_wq + k * 4

        @pl.when(c == y)
        def _():
            net.recv(wq.at[1, at_x], slot + 1)

        @pl.when(c != y)
        def _():
            net.recv(wq.at[0, at_o], slot + 2)

        net.recv(wq.at[0, at_x], slot)
        net.recv(wq.at[1, at_o], slot + 3)

    def gather_start(buf, slot):
        net.send(buf.at[0], buf.at[1], slot + 4, partner)
        for h in range(1, 4):
            net.send(buf.at[0], buf.at[2 * h], slot + h, dev(y, c, zat(h % 2), flip(x, h // 2)))

    def gather_pass(buf, slot, h):
        net.recv(buf.at[2 * h], slot + h)
        net.send(buf.at[2 * h], buf.at[2 * h + 1], slot + 4 + h, partner)

    lane = lax.broadcasted_iota(jnp.int32, (2 * tokens, 128), 1)
    low_half = lax.rem(lane, HEAD_SIZE) < HEAD_SIZE // 2

    def turn(tile, forward):
        other = jnp.where(low_half, pltpu.roll(tile, 96, 1), pltpu.roll(tile, 32, 1))
        turned = other * csf[:, 128:256]
        return tile * csf[:, 0:128] + (turned if forward else -turned)

    qf[:, qw:] = jnp.zeros((2 * tokens, qf.shape[1] - qw), F32)
    for part in range(2):
        got = dot_nn(n1[...], wq[part])
        qf[:, qcols * part : qcols * (part + 1)] = got[:, :qcols]
        kvf[:, kcols * part : kcols * (part + 1)] = got[:, qcols : qcols + kcols]
        kvf[:, kw + kcols * part : kw + kcols * (part + 1)] = got[:, qcols + kcols :]

    def turn_keys(forward):
        for t in range(kw // 128 + 1):
            tile = kvf[:, 128 * t : 128 * (t + 1)]
            kvf[:, 128 * t : 128 * (t + 1)] = jnp.where(
                128 * t + lane < kw, turn(tile, forward), tile
            )

    turn_keys(True)
    own_keys = pl.ds(off(ctx, tokens), tokens)
    for s in range(2):
        kv[s, own_keys] = kvf[s * tokens : (s + 1) * tokens].astype(BF16)
    r_kz, r_kx = net.slots(4), net.slots(4)
    for k in range(1, 4):
        net.send(kv.at[:, own_keys], kv.at[:, own_keys], r_kz + k, dev(y, c, zat(k), x))
    net.send(kv.at[:, own_keys], kv.at[:, own_keys], r_kx, dev(y, c, z, 1 - x))
    send_ff(1)
    send_down()

    for t in range(qf.shape[1] // 128):
        qf[:, 128 * t : 128 * (t + 1)] = turn(qf[:, 128 * t : 128 * (t + 1)], True) * scale
    for s in range(2):
        for h in range(heads):
            q6[s * groups + h // per, (h % per) * tokens : (h % per + 1) * tokens] = qf[
                s * tokens : (s + 1) * tokens, HEAD_SIZE * h : HEAD_SIZE * (h + 1)
            ].astype(BF16)
    for k in range(1, 4):
        part = pl.ds(off(2 * zat(k) + x, tokens), tokens)
        net.recv(kv.at[:, part], r_kz + k)
        net.send(kv.at[:, part], kv.at[:, part], r_kx + k, dev(y, c, z, 1 - x))
    r_c8 = net.slots(8)
    gather_start(c8, r_c8)
    for zz in range(2):
        part = wok.at[2 * (1 - y), pl.ds(off(2 * zz + x, rows), rows)]
        net.recv(part, r_wo + zz * 8 + 2)
        net.send(part, part, r_wo + zz * 8 + 6, dev(y, c, z, 1 - x))
        part = wok.at[2 * y + 1, pl.ds(off(2 * zz + 1 - x, rows), rows)]
        net.recv(part, r_wo + zz * 8 + 5)
        net.send(part, part, r_wo + zz * 8 + 7, dev(1 - y, c, z, x))
    pass_ff(0)
    for k in range(4):
        net.recv(kv.at[:, pl.ds(off(2 * zat(k) + 1 - x, tokens), tokens)], r_kx + k)

    def attend(s, carry):
        mask = b2[s][0:1, :]
        for g in range(groups):
            kg = kv[s, :, HEAD_SIZE * g : HEAD_SIZE * (g + 1)]
            vg = kv[s, :, kw + HEAD_SIZE * g : kw + HEAD_SIZE * (g + 1)]
            scores = dot_nt(q6[s * groups + g], kg) + mask
            weights = jnp.exp(scores - jnp.max(scores, -1, keepdims=True))
            probs = (weights * (1.0 / jnp.sum(weights, -1, keepdims=True))).astype(BF16)
            p6[s * groups + g] = probs
            got = dot_nn(probs, vg).astype(BF16)
            o6[s * groups + g] = got
            for i in range(per):
                h = g * per + i
                ab[pl.ds(off(s, tokens), tokens), HEAD_SIZE * h : HEAD_SIZE * (h + 1)] = got[
                    i * tokens : (i + 1) * tokens
                ]
        return carry

    lax.fori_loop(0, 2, attend, 0)

    for hx, hy, cc in ((0, 0, 0), (0, 0, 1), (0, 1, 1), (1, 0, 0), (1, 1, 0), (1, 1, 1)):
        for zz in range(2):
            net.recv(
                wok.at[2 * flip(y, hy) + cc, pl.ds(off(2 * zz + flip(x, hx), rows), rows)],
                r_wo + zz * 8 + hx * 4 + hy * 2 + cc,
            )
    for part in range(4):
        got = dot_nn(ab[:, 0:qw], wok[part])
        for s in range(2):
            mp[s, :, qcols * part : qcols * (part + 1)] = got[s * tokens : (s + 1) * tokens]
    r_ml = net.slots(1)
    mp_sent = net.send(mp.at[1], ml, r_ml, partner)
    pass_ff(1)
    for cc in range(2):
        part = wd8.at[pl.ds(off(2 * y + cc, drows), drows)]
        net.recv(part, r_wd + cc)
        net.send(part, part, r_wy + cc, dev(1 - y, c, z, x))
    for h in range(1, 4):
        gather_pass(c8, r_c8, h)
    net.recv(ml, r_ml)
    mid[...] = tok[...].astype(F32) + mp[0] + ml[...]
    n8[0] = (normed(mid[...])[0] * grow[1:2]).astype(BF16)
    r_n8 = net.slots(8)
    gather_start(n8, r_n8)

    net.recv(c8.at[1], r_c8 + 4)
    for h in range(1, 4):
        net.recv(c8.at[2 * h + 1], r_c8 + 4 + h)
    take_ff(0)
    take_ff(1)
    for cc in range(2):
        net.recv(wd8.at[pl.ds(off(2 * (1 - y) + cc, drows), drows)], r_wy + cc)

    all_tokens = 8 * tokens

    def feed(i):
        pair = slice(2 * i, 2 * i + 2)
        here = n8[pair].reshape(2 * tokens, width)
        grad_inner = dot_nn(c8[pair].reshape(2 * tokens, width), wd8[...])
        gate = dot_nn(here, wg8[0])
        up = dot_nn(here, wg8[1])
        sig = 1.0 / (1.0 + jnp.exp(-gate))
        silu = gate * sig
        dgate = (grad_inner * up * sig * (1.0 + gate * (1.0 - sig))).astype(BF16)
        dup = (grad_inner * silu).astype(BF16)
        at = 2 * tokens * i
        act[at : at + 2 * tokens] = (silu * up).astype(BF16)
        act[at + all_tokens : at + all_tokens + 2 * tokens] = dgate
        act[at + 2 * all_tokens : at + 2 * all_tokens + 2 * tokens] = dup
        pt[pair] = (dot_nt(dgate, wg8[0]) + dot_nt(dup, wg8[1])).astype(BF16).reshape(2, tokens, width)

    def reduce_start(part, land, slot, h):
        return net.send(part.at[2 * h + 1], land.at[h], slot + h, partner)

    def reduce_pass(part, land, out, land2, slot, h):
        net.recv(land.at[h], slot + h)
        out[h - 1] = (part[2 * h].astype(F32) + land[h].astype(F32)).astype(BF16)
        net.send(
            out.at[h - 1], land2.at[h - 1], slot + 4 + h,
            dev(y, c, zat(h % 2), flip(x, h // 2)),
        )

    def reduce_own(part, land, slot):
        net.recv(land.at[0], slot)
        return part[0].astype(F32) + land[0].astype(F32)

    def reduce_end(land2, slot):
        total = 0.0
        for h in range(1, 4):
            net.recv(land2.at[h - 1], slot + 4 + h)
            total = total + land2[h - 1].astype(F32)
        return total

    r_dn = net.slots(8)
    pt_sent = []
    net.recv(n8.at[1], r_n8 + 4)
    for h in range(4):
        if h:
            gather_pass(n8, r_n8, h)
            net.recv(n8.at[2 * h + 1], r_n8 + 4 + h)
        feed(h)
        pt_sent.append(reduce_start(pt, l1, r_dn, h))
        if h > 1:
            reduce_pass(pt, l1, s2, l2, r_dn, h - 1)
    reduce_pass(pt, l1, s2, l2, r_dn, 3)
    dmid[...] = reduce_own(pt, l1, r_dn)

    def flat(ref, i):
        return ref[:, :, pl.ds(off(i, 128), 128)].reshape(all_tokens, 128)

    def grad_gu(i, carry):
        left = flat(n8, i)
        at = pl.ds(off(i, 128), 128)
        ggu[0, at] = dot_tn(left, act[pl.ds(all_tokens, all_tokens)]).astype(BF16)
        ggu[1, at] = dot_tn(left, act[pl.ds(2 * all_tokens, all_tokens)]).astype(BF16)
        return carry

    def grad_d(i, carry):
        gdt[pl.ds(off(i, 128), 128)] = dot_tn(flat(c8, i), act[pl.ds(0, all_tokens)]).astype(BF16)
        return carry

    def feed_out(i, carry):
        got = dot_nt(act[pl.ds(off(i, 2 * tokens), 2 * tokens)], wd8[...])
        pt[pl.ds(2 * i, 2)] = got.astype(BF16).reshape(2, tokens, width)
        return carry

    r_gd, r_gz = net.slots(1), net.slots(4)
    half = 2 * drows
    lax.fori_loop(0, width // 128, grad_d, 0)
    net.send(gdt.at[pl.ds(off(1 - y, half), half)], lgd, r_gd, dev(1 - y, c, z, x))
    lax.fori_loop(0, width // 128, grad_gu, 0)
    for zt in range(4):
        at = pl.ds(2 * rows * zt, 2 * rows)
        net.send(
            ggu.at[:, at], lgu.at[:, at], r_gz + zt, dev(1 - y, c, z, x),
            only=jnp.logical_not(home),
        )
    for finish in pt_sent:
        net.done(finish)
    lax.fori_loop(0, 4, feed_out, 0)
    r_out = net.slots(8)
    for h in range(4):
        reduce_start(pt, l1o, r_out, h)

    total = dmid[...] + reduce_end(l2, r_dn)
    normed_two, inv_two = normed(mid[...])
    total = total * grow[1:2]
    dmid[...] = cot[...].astype(F32) + inv_two * (
        total - normed_two * jnp.mean(total * normed_two, -1, keepdims=True)
    )
    dmb[0] = dmid[...].astype(BF16)
    r_dm = net.slots(1)
    net.send(dmb.at[0], dmb.at[1], r_dm, partner)

    r_ld = net.slots(2)
    net.recv(lgd, r_gd)
    sgd[...] = (gdt[pl.ds(off(y, half), half)].astype(F32) + lgd[...].astype(F32)).astype(BF16)
    gd_z = 2 * (z_lo + c - 2 * z_lo * c) + c
    for cc in range(2):
        net.send(
            sgd.at[pl.ds(cc * drows, drows)], ld.at[z_hi], r_ld + z_hi, dev(y, cc, gd_z, x),
            is_self=jnp.logical_and(z == gd_z, c == cc),
        )
    net.recv(dmb.at[1], r_dm)

    for part in range(4):
        for s in range(2):
            dm4[part, s * tokens : (s + 1) * tokens] = dmb[s, :, qcols * part : qcols * (part + 1)]
    dattn = dot_nt(dm4[0], wok[0])
    for part in range(1, 4):
        dattn = dattn + dot_nt(dm4[part], wok[part])
    qf[:, 0:qw] = dattn
    for s in range(2):
        for h in range(heads):
            do6[s * groups + h // per, (h % per) * tokens : (h % per + 1) * tokens] = qf[
                s * tokens : (s + 1) * tokens, HEAD_SIZE * h : HEAD_SIZE * (h + 1)
            ].astype(BF16)
    attn_all = ab[:, 0:qw]
    for part in range(4):
        act[qw * part : qw * (part + 1), 0:qcols] = dot_tn(attn_all, dm4[part]).astype(BF16)
    r_go = net.slots(16)
    for zz in range(2):
        for hx in range(2):
            for hy in range(2):
                for hc in range(2):
                    zt = 2 * c + zz
                    to_dp = 2 * flip(y, hy) + flip(c, hc)
                    at = pl.multiple_of(to_dp * qw + (2 * zz + flip(x, hx)) * rows, rows)
                    src = act.at[pl.ds(at, rows)]
                    dst = lo.at[zt, hx * 2 + hy]
                    slot = r_go + zt * 4 + hx * 2 + hy
                    if hx + hy + hc == 0:
                        net.keep(src, dst, slot)
                    else:
                        net.send(src, dst, slot, dev(flip(y, hy), flip(c, hc), z, flip(x, hx)))

    def attend_back(s):
        for g in range(groups):
            at = s * groups + g
            kg = kv[s, :, HEAD_SIZE * g : HEAD_SIZE * (g + 1)]
            vg = kv[s, :, kw + HEAD_SIZE * g : kw + HEAD_SIZE * (g + 1)]
            dout = do6[at]
            delta = jnp.sum(dout.astype(F32) * o6[at].astype(F32), -1, keepdims=True)
            dprob = dot_nt(dout, vg)
            dscore = (p6[at].astype(F32) * (dprob - delta)).astype(BF16)
            dquery = dot_nn(dscore, kg) * scale
            dkeys = dot_tn(q6[at], dscore)
            dvals = dot_tn(dout, p6[at])
            for t in range(n_ctx):
                cols = slice(t * tokens, (t + 1) * tokens)
                dkv[t, s, HEAD_SIZE * g : HEAD_SIZE * (g + 1)] = dkeys[:, cols].astype(BF16)
                dkv[t, s, kw + HEAD_SIZE * g : kw + HEAD_SIZE * (g + 1)] = dvals[:, cols].astype(BF16)
            for i in range(per):
                h = g * per + i
                qf[s * tokens : (s + 1) * tokens, HEAD_SIZE * h : HEAD_SIZE * (h + 1)] = dquery[
                    i * tokens : (i + 1) * tokens
                ]

    attend_back(0)
    r_gf = net.slots(4)
    for k in (3, 2, 1, 0):
        at = pl.ds(off(zat(k), 2 * rows), 2 * rows)

        @pl.when(home)
        def _():
            net.recv(lgu.at[:, at], r_gz + zat(k))
            ggu[:, at] = (ggu[:, at].astype(F32) + lgu[:, at].astype(F32)).astype(BF16)

        for hx in range(2):
            src = ggu.at[:, pl.ds(off(2 * zat(k) + flip(x, hx), rows), rows)]
            dst = lf.at[x, z_hi]
            slot = r_gf + x * 2 + z_hi
            if k + hx:
                net.send(src, dst, slot, dev(y, c, zat(k), flip(x, hx)), only=home)
            else:

                @pl.when(home)
                def _():
                    net.keep(src, dst, slot)

    attend_back(1)
    r_dx, r_dz = net.slots(4), net.slots(4)
    for k in (1, 2, 3, 0):
        net.send(dkv.at[2 * zat(k) + 1 - x], lx.at[k], r_dx + k, dev(y, c, z, 1 - x))
    for t in range(qf.shape[1] // 128):
        qf[:, 128 * t : 128 * (t + 1)] = turn(qf[:, 128 * t : 128 * (t + 1)], False)
    for part in range(2):
        dqk[part, :, 0:qcols] = qf[:, qcols * part : qcols * (part + 1)].astype(BF16)
        got = dot_tn(n1[...], dqk[part, :, 0:qcols]).astype(BF16)
        for t in range(n_ctx):
            p6[t // 2, (t % 2) * rows : (t % 2 + 1) * rows, ff * part : ff * part + qcols] = got[
                rows * t : rows * (t + 1)
            ]

    def send_grads(source, land, slot):
        for k in (3, 2, 1, 0):
            for hx in range(2):
                for ct in range(2):
                    net.send(
                        source(zat(k), flip(x, hx), ct),
                        land.at[k, hx * 2 + y_c],
                        slot + k * 4 + hx * 2 + y_c,
                        dev(c, ct, z, flip(x, hx)),
                        is_self=jnp.logical_and(y == c, c == ct) if hx == 0 else None,
                    )

    for k in range(1, 4):
        net.recv(lx.at[k], r_dx + k)
        sx[k - 1] = (dkv[2 * zat(k) + x].astype(F32) + lx[k].astype(F32)).astype(BF16)
        net.send(sx.at[k - 1], lkz.at[k - 1], r_dz + k, dev(y, c, zat(k), x))
    r_gq = net.slots(16)
    send_grads(
        lambda zt, xt, ct: p6.at[zt, pl.ds(off(xt, rows), rows), pl.ds(ff * ct, ff)], lq, r_gq
    )
    for h in range(1, 4):
        reduce_pass(pt, l1o, s2o, l2o, r_out, h)
    mid[...] = mid[...] + reduce_own(pt, l1o, r_out)

    def attn_pass(land, out, staged, arrived, send_slot, slot, absolute):
        for k in (1, 2, 3, 0):
            at = zat(k) if absolute else k
            part = 0.0
            for h in range(4):
                net.recv(land.at[at, h], slot + at * 4 + h)
                part = part + land[at, h, :, 0 : out.shape[1]].astype(F32)
            if k == 0:
                out[...] = part
            else:
                staged[k - 1] = part.astype(BF16)
                net.send(staged.at[k - 1], arrived.at[k - 1], send_slot + k, dev(y, c, zat(k), x))

    def attn_end(out, arrived, slot):
        for k in range(1, 4):
            net.recv(arrived.at[k - 1], slot + k)
            out[...] = out[...] + arrived[k - 1].astype(F32)

    r_zo, r_zq, r_zk = net.slots(4), net.slots(4), net.slots(4)
    attn_pass(lo, o_o, so, lzo, r_zo, r_go, True)

    net.recv(lx.at[0], r_dx)
    total = dkv[2 * z + x].astype(F32) + lx[0].astype(F32)
    for k in range(1, 4):
        net.recv(lkz.at[k - 1], r_dz + k)
        total = total + lkz[k - 1].astype(F32)
    for s in range(2):
        kvf[s * tokens : (s + 1) * tokens] = total[s].T
    turn_keys(False)
    for part in range(2):
        dqk[part, :, qcols : qcols + kcols] = kvf[:, kcols * part : kcols * (part + 1)].astype(BF16)
        dqk[part, :, qcols + kcols :] = kvf[:, kw + kcols * part : kw + kcols * (part + 1)].astype(BF16)
    for finish in ff_passed:
        net.done(finish)
    for part in range(2):
        wg8[part, :, 0 : 2 * kcols] = dot_tn(n1[...], dqk[part, :, qcols:]).astype(BF16)
    r_gk = net.slots(16)
    send_grads(
        lambda zt, xt, ct: wg8.at[ct, pl.ds(off(2 * zt + xt, rows), rows), pl.ds(0, 256)], lk, r_gk
    )
    net.done(mp_sent)
    got = dot_nt(dqk[0], wq[0]) + dot_nt(dqk[1], wq[1])
    for s in range(2):
        mp[s] = got[s * tokens : (s + 1) * tokens]
    r_dn1 = net.slots(1)
    net.send(mp.at[1], ml, r_dn1, partner)
    attn_pass(lq, o_q, sq, lzq, r_zq, r_gq, False)
    net.recv(ml, r_dn1)
    total = mp[0] + ml[...]
    normed_one, inv_one = normed(tok[...])
    total = total * grow[0:1]
    o_ing[...] = (
        dmid[...]
        + inv_one * (total - normed_one * jnp.mean(total * normed_one, -1, keepdims=True))
    ).astype(BF16)
    attn_pass(lk, kvg, sk, lzk, r_zk, r_gk, False)

    o_out[...] = (mid[...] + reduce_end(l2o, r_out)).astype(BF16)
    gains = [0.0, 0.0]
    for h in range(2):
        for zh in range(2):
            net.recv(lf.at[h, zh], r_gf + h * 2 + zh)
        for m in range(2):
            got = lf[h, 0, m].astype(F32) + lf[h, 1, m].astype(F32)
            cols = slice(h * ff, (h + 1) * ff)
            (o_gate, o_up)[m][:, cols] = got
            gains[1] = gains[1] + jnp.sum(
                got * (wgate, wup)[m][:, cols].astype(F32), 1, keepdims=True
            )
    for zh in range(2):
        net.recv(ld.at[zh], r_ld + zh)
    o_d[...] = (ld[0].astype(F32) + ld[1].astype(F32)).T
    attn_end(o_o, lzo, r_zo)
    attn_end(o_q, lzq, r_zq)
    gains[0] = jnp.sum(o_q[...] * wqkv[:, 0:qcols].astype(F32), 1, keepdims=True)
    attn_end(kvg, lzk, r_zk)
    gains[0] = gains[0] + jnp.sum(kvg[...] * wqkv[:, qcols:].astype(F32), 1, keepdims=True)
    o_k[...] = kvg[:, 0:kcols]
    o_v[...] = kvg[:, kcols:]
    column = lax.broadcasted_iota(jnp.int32, (rows, 128), 1)
    both = jnp.where(column == 0, gains[0], jnp.where(column == 1, gains[1], 0.0))
    sg[...] = both.T[0:8]
    r_lg = net.slots(4)
    for h in range(1, 4):
        net.send(sg, lg.at[h - 1], r_lg + h, dev(flip(y, h // 2), flip(c, h % 2), z, x))
    total = sg[...]
    for h in range(1, 4):
        net.recv(lg.at[h - 1], r_lg + h)
        total = total + lg[h - 1]
    o_gain[...] = total / gain[...]
    net.drain()


def run_layer(tok, cot, cs, bias, gain, wqkv, wo, wgate, wup, wdt):
    tokens, width = tok.shape
    rows, packed = wqkv.shape
    qcols = wo.shape[1]
    drows, ff = wdt.shape
    keys = bias.shape[1]
    n_ctx = keys // tokens
    qw = 2 * qcols
    kw = packed - qcols
    groups = kw // HEAD_SIZE
    per = QUERY_HEADS // KEY_VALUE_HEADS
    stack = per * tokens
    wide = -(-qw // 128) * 128
    out_shape = [
        jax.ShapeDtypeStruct((tokens, width), BF16),
        jax.ShapeDtypeStruct((tokens, width), BF16),
        jax.ShapeDtypeStruct((8, rows), F32),
        jax.ShapeDtypeStruct((rows, qcols), F32),
        jax.ShapeDtypeStruct((rows, kw // 2), F32),
        jax.ShapeDtypeStruct((rows, kw // 2), F32),
        jax.ShapeDtypeStruct((rows, qcols), F32),
        jax.ShapeDtypeStruct((rows, 2 * ff), F32),
        jax.ShapeDtypeStruct((rows, 2 * ff), F32),
        jax.ShapeDtypeStruct((ff, drows), F32),
    ]

    def vm(*shape, dtype=BF16):
        return pltpu.VMEM(shape, dtype)

    scratch = [
        vm(2 * tokens, 256, dtype=F32),
        vm(2, 8, keys, dtype=F32),
        vm(tokens, width),
        vm(n_ctx, 8, rows, dtype=F32),
        vm(8, width, dtype=F32),
        vm(3, rows, packed),
        vm(3, rows, qcols),
        vm(2, width, packed),
        vm(4, 4 * rows, qcols),
        vm(2, width, ff),
        vm(width, ff),
        vm(8, tokens, width),
        vm(8, tokens, width),
        vm(2 * tokens, width),
        vm(2 * tokens, wide, dtype=F32),
        vm(2 * tokens, 2 * kw, dtype=F32),
        vm(2, keys, 2 * kw),
        vm(2 * groups, stack, HEAD_SIZE),
        vm(2 * groups, stack, keys),
        vm(2 * groups, stack, HEAD_SIZE),
        vm(2 * tokens, wide),
        vm(2, tokens, width, dtype=F32),
        vm(tokens, width, dtype=F32),
        vm(tokens, width, dtype=F32),
        vm(tokens, width, dtype=F32),
        vm(2, tokens, width),
        vm(4, 2 * tokens, qcols),
        vm(2 * groups, stack, HEAD_SIZE),
        vm(24 * tokens, ff),
        vm(8, tokens, width),
        vm(4, tokens, width),
        vm(3, tokens, width),
        vm(3, tokens, width),
        vm(4, tokens, width),
        vm(3, tokens, width),
        vm(3, tokens, width),
        vm(2, width, ff),
        vm(2, width, ff),
        vm(2, 2, 2, rows, ff),
        vm(width, ff),
        vm(2 * drows, ff),
        vm(2 * drows, ff),
        vm(2, drows, ff),
        vm(4, 4, rows, ff),
        vm(4, 4, rows, ff),
        vm(4, 4, rows, 256),
        vm(3, rows, qcols),
        vm(3, rows, qcols),
        vm(3, rows, kw),
        vm(3, rows, qcols),
        vm(3, rows, qcols),
        vm(3, rows, kw),
        vm(rows, kw, dtype=F32),
        vm(n_ctx, 2, 2 * kw, tokens),
        vm(4, 2, 2 * kw, tokens),
        vm(3, 2, 2 * kw, tokens),
        vm(3, 2, 2 * kw, tokens),
        vm(3, 8, rows, dtype=F32),
        vm(8, rows, dtype=F32),
        vm(2, 2 * tokens, packed),
        pltpu.SemaphoreType.DMA((N_SEM,)),
        pltpu.SemaphoreType.DMA((N_SEM,)),
    ]
    inside = pl.BlockSpec(memory_space=pltpu.VMEM)
    return pl.pallas_call(
        layer_kernel,
        out_shape=out_shape,
        in_specs=[inside] * 10,
        out_specs=[inside] * len(out_shape),
        scratch_shapes=scratch,
        compiler_params=pltpu.CompilerParams(
            collective_id=0, has_side_effects=True, vmem_limit_bytes=VMEM_LIMIT
        ),
        name="layer",
    )(tok, cot, cs, bias, gain, wqkv, wo, wgate, wup, wdt)


VMEM_LIMIT = 63 * 1024 * 1024


def on_device_plane(
    tokens, positions, block_sizes, attn_gain, w_query, w_key, w_value, w_out, mlp_gain,
    w_gate, w_up, w_down, cotangent,
):
    seq_rows, width = tokens.shape[1:]
    ctx = lax.axis_index("ctx")
    angles = angles_of(positions[0])
    cosine, sine = jnp.cos(angles), jnp.sin(angles)
    cs = jnp.concatenate([cosine] * 4 + [-sine, sine] * 2, 1)
    keys = seq_rows * lax.axis_size("ctx")
    block = block_sizes[0]
    limit = (ctx * seq_rows // block + 1) * block
    bias = jnp.where(jnp.arange(keys, dtype=jnp.int32) < limit, 0.0, VERY_NEGATIVE).astype(F32)
    bias = jnp.broadcast_to(bias[None, :], (8, keys))
    rows = w_query.shape[0]
    gain = jnp.concatenate([attn_gain[None], mlp_gain[None], jnp.ones((6, rows), BF16)], 0).astype(F32)
    wqkv = jnp.concatenate([w_query, w_key, w_value], 1)
    output, input_grad, gains, g_q, g_k, g_v, g_o, g_gate, g_up, g_d = run_layer(
        tokens[0], cotangent[0], cs, bias, gain, wqkv, w_out, w_gate, w_up, w_down.T
    )
    return (
        output[None],
        input_grad[None],
        gains[0],
        g_q,
        g_k,
        g_v,
        g_o,
        gains[1],
        g_gate,
        g_up,
        g_d,
    )


def solution(mesh):
    placed = (
        P("dp", "ctx", None),
        P("dp", "ctx"),
        P("dp"),
        P("ctx"),
        P("ctx", "dp"),
        P("ctx", "dp"),
        P("ctx", "dp"),
        P("ctx", "dp"),
        P("ctx"),
        P("ctx", "dp"),
        P("ctx", "dp"),
        P("ctx", "dp"),
        P("dp", "ctx", None),
    )
    fits = mesh.shape["dp"] == 4 and mesh.shape["ctx"] == 8
    return jax.shard_map(
        on_device_plane if fits else on_device,
        mesh=mesh,
        in_specs=placed,
        out_specs=(
            P("dp", "ctx", None),
            P("dp", "ctx", None),
            P("ctx"),
            P("ctx", "dp"),
            P("ctx", "dp"),
            P("ctx", "dp"),
            P("ctx", "dp"),
            P("ctx"),
            P("ctx", "dp"),
            P("ctx", "dp"),
            P("ctx", "dp"),
        ),
        check_vma=False,
    )
```

```python
import jax
import jax.numpy as jnp
from jax import lax
from jax.experimental import pallas as pl
from jax.experimental.pallas import tpu as pltpu
from jax.sharding import PartitionSpec as P

QUERY_HEADS = 18
KEY_VALUE_HEADS = 6
HEAD_SIZE = 64


EPSILON = 1e-05
THETA = 10000.0
VERY_NEGATIVE = -1e30


def product(left, right):
    return jnp.dot(left, right, preferred_element_type=jnp.float32)


def angles_of(place_ids):
    half_dim = HEAD_SIZE // 2
    frequency = THETA ** (-(jnp.arange(half_dim, dtype=jnp.float32) * 2.0 / HEAD_SIZE))
    return place_ids.astype(jnp.float32)[:, None] * frequency[None, :]


def rotate(values, angles, forward):
    row_total = values.shape[0]
    half_dim = angles.shape[1]
    shaped = values.reshape(row_total, -1, 2 * half_dim)
    first_half = shaped[..., :half_dim]
    second = shaped[..., half_dim:]
    cosine = jnp.cos(angles)[:, None, :]
    sine_vals = jnp.sin(angles)[:, None, :]
    if forward:
        rotated = jnp.concatenate(
            [first_half * cosine - second * sine_vals, second * cosine + first_half * sine_vals], -1
        )
    else:
        rotated = jnp.concatenate(
            [first_half * cosine + second * sine_vals, second * cosine - first_half * sine_vals], -1
        )
    return rotated.reshape(row_total, -1)


def norm_back(grad_normed, normed, inverse):
    return inverse * (grad_normed - normed * jnp.mean(grad_normed * normed, -1, keepdims=True))


def visible(query_rows, key_rows, block_len):
    return ((key_rows // block_len)[None, :] <= (query_rows // block_len)[:, None])[None, None]


def attend_forward(query_rows4, complete_keys, complete_values, query_rows, block_len, score_scale):
    key_count = complete_keys.shape[0]
    key_row_width = 512
    block_list = key_count // key_row_width
    query_group_width = QUERY_HEADS // KEY_VALUE_HEADS
    row_total = query_rows4.shape[0]
    key_block_list = complete_keys.reshape(block_list, key_row_width, KEY_VALUE_HEADS, HEAD_SIZE)
    value_block_list = complete_values.reshape(
        block_list, key_row_width, KEY_VALUE_HEADS, HEAD_SIZE
    )
    last_block = query_rows[-1] // block_len

    def advance(carried, inputs):
        key_blk, val_blk, first_key = inputs
        key_rows = first_key + jnp.arange(key_row_width, dtype=jnp.int32)

        def compute(current):
            run_max, run_sum, accum = current
            scores = (
                jnp.einsum(
                    "tkgd,nkd->kgtn", query_rows4, key_blk, preferred_element_type=jnp.float32
                )
                * score_scale
            )
            allowed = visible(query_rows, key_rows, block_len)
            scores = jnp.where(allowed, scores, VERY_NEGATIVE)
            new_max = jnp.maximum(run_max, jnp.max(scores, -1))
            weights = jnp.where(allowed, jnp.exp(scores - new_max[..., None]), 0.0)
            factor = jnp.exp(run_max - new_max)
            new_sum = run_sum * factor + jnp.sum(weights, -1)
            accum = accum * factor[..., None] + jnp.einsum(
                "kgtn,nkd->kgtd",
                weights.astype(jnp.bfloat16),
                val_blk,
                preferred_element_type=jnp.float32,
            )
            return (new_max, new_sum, accum)

        return (
            lax.cond(
                first_key // block_len > last_block, lambda unchanged: unchanged, compute, carried
            ),
            None,
        )

    start_state = (
        jnp.full((KEY_VALUE_HEADS, query_group_width, row_total), VERY_NEGATIVE, jnp.float32),
        jnp.zeros((KEY_VALUE_HEADS, query_group_width, row_total), jnp.float32),
        jnp.zeros((KEY_VALUE_HEADS, query_group_width, row_total, HEAD_SIZE), jnp.float32),
    )
    firsts = jnp.arange(block_list, dtype=jnp.int32) * key_row_width
    final_state, unused = lax.scan(advance, start_state, (key_block_list, value_block_list, firsts))
    run_max, run_sum, accum = final_state
    return (accum / run_sum[..., None], run_max + jnp.log(run_sum))


def attend_backward(
    query_rows4,
    head_gradients,
    log_sums,
    row_delta,
    complete_keys,
    complete_values,
    query_rows,
    block_len,
    score_scale,
):
    key_count = complete_keys.shape[0]
    key_row_width = 512
    block_list = key_count // key_row_width
    query_group_width = QUERY_HEADS // KEY_VALUE_HEADS
    row_total = query_rows4.shape[0]
    key_block_list = complete_keys.reshape(block_list, key_row_width, KEY_VALUE_HEADS, HEAD_SIZE)
    value_block_list = complete_values.reshape(
        block_list, key_row_width, KEY_VALUE_HEADS, HEAD_SIZE
    )
    last_block = query_rows[-1] // block_len

    def advance(grad_query, inputs):
        key_blk, val_blk, first_key = inputs
        key_rows = first_key + jnp.arange(key_row_width, dtype=jnp.int32)

        def compute(current):
            scores = (
                jnp.einsum(
                    "tkgd,nkd->kgtn", query_rows4, key_blk, preferred_element_type=jnp.float32
                )
                * score_scale
            )
            allowed = visible(query_rows, key_rows, block_len)
            prob_vals = jnp.where(allowed, jnp.exp(scores - log_sums[..., None]), 0.0)
            grad_prob = jnp.einsum(
                "tkgd,nkd->kgtn", head_gradients, val_blk, preferred_element_type=jnp.float32
            )
            grad_score = (prob_vals * (grad_prob - row_delta[..., None])).astype(jnp.bfloat16)
            current = current + jnp.einsum(
                "kgtn,nkd->tkgd", grad_score, key_blk, preferred_element_type=jnp.float32
            )
            grad_key = jnp.einsum(
                "kgtn,tkgd->nkd", grad_score, query_rows4, preferred_element_type=jnp.float32
            )
            grad_value = jnp.einsum(
                "kgtn,tkgd->nkd",
                prob_vals.astype(jnp.bfloat16),
                head_gradients,
                preferred_element_type=jnp.float32,
            )
            return (current, (grad_key, grad_value))

        def nothing(current):
            empty_block = jnp.zeros((key_row_width, KEY_VALUE_HEADS, HEAD_SIZE), jnp.float32)
            return (current, (empty_block, empty_block))

        return lax.cond(first_key // block_len > last_block, nothing, compute, grad_query)

    firsts = jnp.arange(block_list, dtype=jnp.int32) * key_row_width
    initial_gradient = jnp.zeros(
        (row_total, KEY_VALUE_HEADS, query_group_width, HEAD_SIZE), jnp.float32
    )
    grad_query, stacked_rows = lax.scan(
        advance, initial_gradient, (key_block_list, value_block_list, firsts)
    )
    key_gradients = stacked_rows[0].reshape(key_count, KEY_VALUE_HEADS * HEAD_SIZE)
    value_gradients = stacked_rows[1].reshape(key_count, KEY_VALUE_HEADS * HEAD_SIZE)
    return (grad_query, key_gradients, value_gradients)


def on_device(
    tokens,
    positions,
    block_sizes,
    attn_gain,
    w_query,
    w_key,
    w_value,
    w_out,
    mlp_gain,
    w_gate,
    w_up,
    w_down,
    cotangent,
):
    row_parts = (
        lax.all_gather(w_query, "ctx", axis=0, tiled=True),
        lax.all_gather(w_key, "ctx", axis=0, tiled=True),
        lax.all_gather(w_value, "ctx", axis=0, tiled=True),
        lax.all_gather(w_out, "ctx", axis=0, tiled=True),
        lax.all_gather(w_gate, "ctx", axis=0, tiled=True),
        lax.all_gather(w_up, "ctx", axis=0, tiled=True),
        lax.all_gather(w_down, "ctx", axis=0, tiled=True),
        lax.all_gather(attn_gain, "ctx", axis=0, tiled=True),
        lax.all_gather(mlp_gain, "ctx", axis=0, tiled=True),
    )
    whole_w = (
        lax.all_gather(row_parts[0], "dp", axis=1, tiled=True),
        lax.all_gather(row_parts[1], "dp", axis=1, tiled=True),
        lax.all_gather(row_parts[2], "dp", axis=1, tiled=True),
        lax.all_gather(row_parts[3], "dp", axis=1, tiled=True),
        lax.all_gather(row_parts[4], "dp", axis=1, tiled=True),
        lax.all_gather(row_parts[5], "dp", axis=1, tiled=True),
        lax.all_gather(row_parts[6], "dp", axis=1, tiled=True),
    )
    query_w, key_w, value_w, out_w, gate_w, up_w, down_w = whole_w
    gain_one = row_parts[7].astype(jnp.float32)
    gain_two = row_parts[8].astype(jnp.float32)
    seq_count = tokens.shape[0]
    seq_rows = tokens.shape[1]
    width = tokens.shape[2]
    inputs = tokens.reshape(seq_count * seq_rows, width).astype(jnp.float32)
    row_total = inputs.shape[0]
    query_group_width = QUERY_HEADS // KEY_VALUE_HEADS
    query_rows = lax.axis_index("ctx") * seq_rows + jnp.arange(seq_rows, dtype=jnp.int32)
    angles = angles_of(positions.reshape(-1))
    score_scale = HEAD_SIZE ** (-0.5)
    inv_one = lax.rsqrt(jnp.mean(inputs * inputs, -1, keepdims=True) + EPSILON)
    normed_one = inputs * inv_one
    hidden_one = (normed_one * gain_one).astype(jnp.bfloat16)
    query_matrix = rotate(product(hidden_one, query_w), angles, True).astype(jnp.bfloat16)
    keys_own = rotate(product(hidden_one, key_w), angles, True).astype(jnp.bfloat16)
    values_own = product(hidden_one, value_w).astype(jnp.bfloat16)
    complete_keys, complete_values = (
        lax.all_gather(keys_own.reshape(seq_count, seq_rows, -1), "ctx", axis=1, tiled=True),
        lax.all_gather(values_own.reshape(seq_count, seq_rows, -1), "ctx", axis=1, tiled=True),
    )
    query_rows4 = query_matrix.reshape(row_total, KEY_VALUE_HEADS, query_group_width, HEAD_SIZE)
    member = 0
    heads_one, lse_one = attend_forward(
        query_rows4,
        complete_keys[member],
        complete_values[member],
        query_rows,
        block_sizes[member],
        score_scale,
    )
    attn_flat = heads_one.transpose(2, 0, 1, 3).reshape(row_total, QUERY_HEADS * HEAD_SIZE)
    attn_low = attn_flat.astype(jnp.bfloat16)
    mixed_rows = inputs + product(attn_low, out_w)
    inv_two = lax.rsqrt(jnp.mean(mixed_rows * mixed_rows, -1, keepdims=True) + EPSILON)
    normed_two = mixed_rows * inv_two
    hidden_two = (normed_two * gain_two).astype(jnp.bfloat16)
    gate_pre = product(hidden_two, gate_w)
    up_pre = product(hidden_two, up_w)
    sigmoid_gate = jax.nn.sigmoid(gate_pre)
    silu_gate = gate_pre * sigmoid_gate
    inner_act = (silu_gate * up_pre).astype(jnp.bfloat16)
    result = mixed_rows + product(inner_act, down_w)
    output = result.astype(jnp.bfloat16).reshape(seq_count, seq_rows, width)
    back_parts = (
        lax.all_gather(w_query, "ctx", axis=0, tiled=True),
        lax.all_gather(w_key, "ctx", axis=0, tiled=True),
        lax.all_gather(w_value, "ctx", axis=0, tiled=True),
        lax.all_gather(w_out, "ctx", axis=0, tiled=True),
        lax.all_gather(w_gate, "ctx", axis=0, tiled=True),
        lax.all_gather(w_up, "ctx", axis=0, tiled=True),
        lax.all_gather(w_down, "ctx", axis=0, tiled=True),
    )
    back_whole = (
        lax.all_gather(back_parts[0], "dp", axis=1, tiled=True),
        lax.all_gather(back_parts[1], "dp", axis=1, tiled=True),
        lax.all_gather(back_parts[2], "dp", axis=1, tiled=True),
        lax.all_gather(back_parts[3], "dp", axis=1, tiled=True),
        lax.all_gather(back_parts[4], "dp", axis=1, tiled=True),
        lax.all_gather(back_parts[5], "dp", axis=1, tiled=True),
        lax.all_gather(back_parts[6], "dp", axis=1, tiled=True),
    )
    back_query, back_key, back_value, back_out, back_gate, back_up, back_down = back_whole
    grad_top = cotangent.reshape(row_total, width)
    grad_down = jnp.einsum("tf,td->fd", inner_act, grad_top, preferred_element_type=jnp.float32)
    grad_inner = jnp.einsum("td,fd->tf", grad_top, back_down, preferred_element_type=jnp.float32)
    grad_gate = (
        grad_inner * up_pre * sigmoid_gate * (1.0 + gate_pre * (1.0 - sigmoid_gate))
    ).astype(jnp.bfloat16)
    grad_upval = (grad_inner * silu_gate).astype(jnp.bfloat16)
    grad_gatew = jnp.einsum("td,tf->df", hidden_two, grad_gate, preferred_element_type=jnp.float32)
    grad_upw = jnp.einsum("td,tf->df", hidden_two, grad_upval, preferred_element_type=jnp.float32)
    grad_hidden_two = jnp.einsum(
        "tf,df->td", grad_gate, back_gate, preferred_element_type=jnp.float32
    ) + jnp.einsum("tf,df->td", grad_upval, back_up, preferred_element_type=jnp.float32)
    grad_gain_two = jnp.sum(grad_hidden_two * normed_two, 0)
    grad_mixed = grad_top.astype(jnp.float32) + norm_back(
        grad_hidden_two * gain_two, normed_two, inv_two
    )
    grad_branch = grad_mixed.astype(jnp.bfloat16)
    grad_outw = jnp.einsum("tq,td->qd", attn_low, grad_branch, preferred_element_type=jnp.float32)
    attention_gradient = jnp.einsum(
        "td,qd->tq", grad_branch, back_out, preferred_element_type=jnp.float32
    ).astype(jnp.bfloat16)
    head_gradients = attention_gradient.reshape(
        row_total, KEY_VALUE_HEADS, query_group_width, HEAD_SIZE
    )
    row_delta = jnp.einsum("tkgd,kgtd->kgt", head_gradients.astype(jnp.float32), heads_one)
    member = 0
    grad_q_one, grad_k_one, grad_v_one = attend_backward(
        query_rows4,
        head_gradients,
        lse_one,
        row_delta,
        complete_keys[member],
        complete_values[member],
        query_rows,
        block_sizes[member],
        score_scale,
    )
    key_grads = [grad_k_one]
    value_grads = [grad_v_one]
    grad_keys_all = jnp.stack(key_grads, 0)
    grad_values_all = jnp.stack(value_grads, 0)
    grad_keys_own, grad_values_own = (
        lax.psum_scatter(grad_keys_all, "ctx", scatter_dimension=1, tiled=True),
        lax.psum_scatter(grad_values_all, "ctx", scatter_dimension=1, tiled=True),
    )
    grad_keys_own = grad_keys_own.reshape(row_total, -1)
    grad_values_own = grad_values_own.reshape(row_total, -1)
    grad_query_raw = rotate(
        grad_q_one.reshape(row_total, QUERY_HEADS * HEAD_SIZE) * score_scale, angles, False
    ).astype(jnp.bfloat16)
    grad_key_raw = rotate(grad_keys_own * score_scale, angles, False).astype(jnp.bfloat16)
    grad_value_raw = grad_values_own.astype(jnp.bfloat16)
    grad_queryw = jnp.einsum(
        "td,tq->dq", hidden_one, grad_query_raw, preferred_element_type=jnp.float32
    )
    grad_keyw = jnp.einsum(
        "td,tq->dq", hidden_one, grad_key_raw, preferred_element_type=jnp.float32
    )
    grad_valuew = jnp.einsum(
        "td,tq->dq", hidden_one, grad_value_raw, preferred_element_type=jnp.float32
    )
    grad_hidden_one = jnp.einsum(
        "tq,dq->td", grad_query_raw, back_query, preferred_element_type=jnp.float32
    )
    grad_hidden_one = grad_hidden_one + jnp.einsum(
        "tq,dq->td", grad_key_raw, back_key, preferred_element_type=jnp.float32
    )
    grad_hidden_one = grad_hidden_one + jnp.einsum(
        "tq,dq->td", grad_value_raw, back_value, preferred_element_type=jnp.float32
    )
    grad_gain_one = jnp.sum(grad_hidden_one * normed_one, 0)
    grad_input = grad_mixed + norm_back(grad_hidden_one * gain_one, normed_one, inv_one)
    input_grad = grad_input.astype(jnp.bfloat16).reshape(seq_count, seq_rows, width)
    summed_rows = (
        lax.psum_scatter(grad_queryw, "ctx", scatter_dimension=0, tiled=True),
        lax.psum_scatter(grad_keyw, "ctx", scatter_dimension=0, tiled=True),
        lax.psum_scatter(grad_valuew, "ctx", scatter_dimension=0, tiled=True),
        lax.psum_scatter(grad_outw, "ctx", scatter_dimension=0, tiled=True),
        lax.psum_scatter(grad_gatew, "ctx", scatter_dimension=0, tiled=True),
        lax.psum_scatter(grad_upw, "ctx", scatter_dimension=0, tiled=True),
        lax.psum_scatter(grad_down, "ctx", scatter_dimension=0, tiled=True),
        lax.psum_scatter(grad_gain_one, "ctx", scatter_dimension=0, tiled=True),
        lax.psum_scatter(grad_gain_two, "ctx", scatter_dimension=0, tiled=True),
    )
    final_w = (
        lax.psum_scatter(
            summed_rows[0].astype(jnp.bfloat16), "dp", scatter_dimension=1, tiled=True
        ).astype(jnp.float32),
        lax.psum_scatter(
            summed_rows[1].astype(jnp.bfloat16), "dp", scatter_dimension=1, tiled=True
        ).astype(jnp.float32),
        lax.psum_scatter(
            summed_rows[2].astype(jnp.bfloat16), "dp", scatter_dimension=1, tiled=True
        ).astype(jnp.float32),
        lax.psum_scatter(
            summed_rows[3].astype(jnp.bfloat16), "dp", scatter_dimension=1, tiled=True
        ).astype(jnp.float32),
        lax.psum_scatter(
            summed_rows[4].astype(jnp.bfloat16), "dp", scatter_dimension=1, tiled=True
        ).astype(jnp.float32),
        lax.psum_scatter(
            summed_rows[5].astype(jnp.bfloat16), "dp", scatter_dimension=1, tiled=True
        ).astype(jnp.float32),
        lax.psum_scatter(
            summed_rows[6].astype(jnp.bfloat16), "dp", scatter_dimension=1, tiled=True
        ).astype(jnp.float32),
    )
    final_gains = lax.psum((summed_rows[7], summed_rows[8]), "dp")
    return (
        output,
        input_grad,
        final_gains[0],
        final_w[0],
        final_w[1],
        final_w[2],
        final_w[3],
        final_gains[1],
        final_w[4],
        final_w[5],
        final_w[6],
    )


MESH = pl.DeviceIdType.MESH
F32 = jnp.float32
BF16 = jnp.bfloat16


def dot_nn(a, b):
    return lax.dot_general(a, b, (((1,), (0,)), ((), ())), preferred_element_type=F32)


def dot_nt(a, b):
    return lax.dot_general(a, b, (((1,), (1,)), ((), ())), preferred_element_type=F32)


def dot_tn(a, b):
    return lax.dot_general(a, b, (((0,), (0,)), ((), ())), preferred_element_type=F32)


class Wires:
    def __init__(self, send_sems, recv_sems):
        self.send_sems, self.recv_sems = send_sems, recv_sems
        self.sends = 0
        self.recvs = 0
        self.pending = []

    def slots(self, count):
        first = self.recvs
        self.recvs += count
        return first

    def send(self, src, dst, slot, device, is_self=None, only=None):
        mine = self.sends
        self.sends += 1
        remote = pltpu.make_async_remote_copy(
            src_ref=src,
            dst_ref=dst,
            send_sem=self.send_sems.at[mine],
            recv_sem=self.recv_sems.at[slot],
            device_id=device,
            device_id_type=MESH,
        )
        if only is not None:

            @pl.when(only)
            def _():
                remote.start()

            def finish():
                @pl.when(only)
                def _():
                    remote.wait_send()

        elif is_self is None:
            remote.start()
            finish = remote.wait_send
        else:
            local = pltpu.make_async_copy(src, dst, self.recv_sems.at[slot])

            @pl.when(is_self)
            def _():
                local.start()

            @pl.when(jnp.logical_not(is_self))
            def _():
                remote.start()

            def finish():
                @pl.when(jnp.logical_not(is_self))
                def _():
                    remote.wait_send()

        self.pending.append(finish)
        return finish

    def keep(self, src, dst, slot):
        pltpu.make_async_copy(src, dst, self.recv_sems.at[slot]).start()

    def recv(self, dst, slot):
        pltpu.make_async_copy(dst, dst, self.recv_sems.at[slot]).wait()

    def done(self, finish):
        finish()
        self.pending.remove(finish)

    def drain(self):
        for finish in self.pending:
            finish()
        self.pending = []


N_SEM = 256


def layer_kernel(
    tok, cot, cs, bias, gain, wqkv, wo, wgate, wup, wdt,
    o_out, o_ing, o_gain, o_q, o_k, o_v, o_o, o_gate, o_up, o_d,
    csf, b2, x2, gb, grow, wqz, woz, wq, wok, wg8, wd8, c8, n8, n1, qf, kvf, kv, q6, p6, o6, ab,
    mp, ml, mid, dmid, dmb, dm4, do6, act, pt, l1, s2, l2, l1o, s2o, l2o,
    ggu, lgu, lf, gdt, lgd, sgd, ld, loy, lo, lqy, lqx, lky, lkx, so, sq, sk, lzo, lzq, lzk, kvg, dkv, lx, sx, lkz,
    lg, sg, dqk, send_sems, recv_sems,
):
    net = Wires(send_sems, recv_sems)
    dp = lax.axis_index("dp")
    ctx = lax.axis_index("ctx")
    y, c = dp // 2, lax.rem(dp, 2)
    z, x = ctx // 2, lax.rem(ctx, 2)
    z_hi, z_lo = z // 2, lax.rem(z, 2)
    y_c = y + c - 2 * y * c
    tokens, width = tok.shape
    rows = wqkv.shape[0]
    qcols = wo.shape[1]
    kcols = (wqkv.shape[1] - qcols) // 2
    ff = wdt.shape[1]
    drows = wdt.shape[0]
    qw = 2 * qcols
    kw = 2 * kcols
    groups = kw // HEAD_SIZE
    per = QUERY_HEADS // KEY_VALUE_HEADS
    heads = groups * per
    keys = kv.shape[1]
    n_ctx = keys // tokens
    scale = HEAD_SIZE ** (-0.5)

    def flip(a, h):
        return 1 - a if h else a

    def zat(k):
        return (z, 2 * z_hi + 1 - z_lo, 2 * (1 - z_hi) + z_lo, 3 - z)[k]

    def dev(yy, cc, zz, xx):
        return (2 * yy + cc, 2 * zz + xx)

    def off(value, step):
        return pl.multiple_of(value * step, step)

    partner = dev(y, 1 - c, z, x)

    barrier = pltpu.get_barrier_semaphore()
    for k in range(4):
        for hx in range(2):
            for hy in range(2):
                for hc in range(2):
                    if k + hx + hy + hc:
                        pl.semaphore_signal(
                            barrier, inc=1,
                            device_id=dev(flip(y, hy), flip(c, hc), zat(k), flip(x, hx)),
                            device_id_type=MESH,
                        )
    pl.semaphore_wait(barrier, 31)

    r_tok = net.slots(3)
    net.send(tok, x2, r_tok, partner)
    net.send(cs, csf.at[pl.ds(tokens, tokens)], r_tok + 1, partner)
    net.send(bias, b2.at[1], r_tok + 2, partner)
    r_g = net.slots(8)
    r_wqz, r_wq = net.slots(4), net.slots(16)

    def spread_qkv(k, src):
        zs = zat(k)
        for hx, hy in ((0, 0), (1, 0), (0, 1)):
            net.send(
                src,
                wq.at[c, pl.ds(off(2 * zs + x, rows), rows)],
                r_wq + k * 4 + hx * 2 + c,
                dev(flip(y, hy), y, z, flip(x, hx)),
                is_self=(c == y) if hx + hy == 0 else None,
            )

    for k in range(1, 4):
        net.send(wqkv, wqz.at[k - 1], r_wqz + k, dev(y, c, zat(k), x))
    spread_qkv(0, wqkv)
    for k in range(4):
        for hx in range(2):
            if k + hx:
                net.send(gain, gb.at[ctx], r_g + 2 * k + hx, dev(y, c, zat(k), flip(x, hx)))

    csf[0:tokens] = cs[...]
    b2[0] = bias[...]
    gb[ctx] = gain[...]
    c8[0] = cot[...]

    def normed(values):
        v = values.astype(F32)
        inv = lax.rsqrt(jnp.mean(v * v, -1, keepdims=True) + EPSILON)
        return v * inv, inv

    def gather_x(buf, slot):
        net.send(buf.at[0], buf.at[4], slot + 2, dev(y, c, z, 1 - x))

    def gather_z(buf, slot):
        net.send(buf.at[0], buf.at[1], slot + 4, partner)
        net.send(buf.at[0], buf.at[2], slot + 1, dev(y, c, zat(1), x))

    def gather_pass(buf, slot, h):
        net.recv(buf.at[2 * h], slot + h)
        net.send(buf.at[2 * h], buf.at[2 * h + 1], slot + 4 + h, partner)
        if h == 1:
            net.send(buf.at[2], buf.at[6], slot + 3, dev(y, c, z, 1 - x))

    r_c8 = net.slots(8)
    for k in range(1, 4):
        net.recv(wqz.at[k - 1], r_wqz + k)
        spread_qkv(k, wqz.at[k - 1])
    gather_x(c8, r_c8)

    r_woz, r_wo = net.slots(4), net.slots(16)

    def spread_wo(k, src):
        zs = zat(k)
        core = zs // 2
        for hx, hy in ((0, 0), (1, 0), (0, 1)):
            net.send(
                src,
                wok.at[dp, pl.ds(off(2 * lax.rem(zs, 2) + x, rows), rows)],
                r_wo + lax.rem(zs, 2) * 8 + hx * 4 + hy * 2 + c,
                dev(flip(y, hy), core, z, flip(x, hx)),
                is_self=(c == core) if hx + hy == 0 else None,
            )

    r_gu, r_wd, r_wy = net.slots(16), net.slots(2), net.slots(2)
    home = y_c == z_lo

    def send_ff(m):
        for zh in range(2):
            for hx in range(2):
                net.send(
                    (wgate, wup)[m].at[:, pl.ds(off(flip(x, hx), ff), ff)],
                    wg8.at[m, pl.ds(off(ctx, rows), rows)],
                    r_gu + m * 8 + ctx,
                    dev(y, c, 2 * zh + y_c, flip(x, hx)),
                    is_self=(z == 2 * zh + y_c) if hx == 0 else None,
                )

    ff_passed = []

    def pass_ff(m):
        for i in range(n_ctx):
            part = wg8.at[m, pl.ds(rows * i, rows)]

            @pl.when(home)
            def _():
                net.recv(part, r_gu + m * 8 + i)

            ff_passed.append(
                net.send(part, part, r_gu + m * 8 + i, dev(1 - y, c, z, x), only=home)
            )

    def take_ff(m):
        for i in range(n_ctx):

            @pl.when(jnp.logical_not(home))
            def _():
                net.recv(wg8.at[m, pl.ds(rows * i, rows)], r_gu + m * 8 + i)

    def send_down():
        z_x = z_hi + z_lo - 2 * z_hi * z_lo
        for zh in range(2):
            net.send(
                wdt,
                wd8.at[pl.ds(off(dp, drows), drows)],
                r_wd + c,
                dev(y, z_lo, 2 * zh + z_x, x),
                is_self=jnp.logical_and(z == 2 * zh + z_x, c == z_lo),
            )

    for k in range(1, 4):
        net.send(wo, woz.at[k - 1], r_woz + k, dev(y, c, zat(k), x))
    spread_wo(0, wo)
    send_ff(0)
    gather_z(c8, r_c8)

    for k in range(4):
        for hx in range(2):
            if k + hx:
                net.recv(gb.at[2 * zat(k) + flip(x, hx)], r_g + 2 * k + hx)
    for t in range(n_ctx):
        grow[:, rows * t : rows * (t + 1)] = gb[t]
    n1[0:tokens] = (normed(tok[...])[0] * grow[0:1]).astype(BF16)
    net.recv(x2, r_tok)
    n1[tokens : 2 * tokens] = (normed(x2[...])[0] * grow[0:1]).astype(BF16)
    net.recv(csf.at[pl.ds(tokens, tokens)], r_tok + 1)
    net.recv(b2.at[1], r_tok + 2)

    for k in range(4):
        at_x = pl.ds(off(2 * zat(k) + x, rows), rows)
        at_o = pl.ds(off(2 * zat(k) + 1 - x, rows), rows)
        slot = r_wq + k * 4

        @pl.when(c == y)
        def _():
            net.recv(wq.at[0, at_o], slot + 2)

        net.send(wq.at[0, at_o], wq.at[0, at_o], slot + 2, dev(1 - y, c, z, x), only=(c == y))

        @pl.when(c != y)
        def _():
            net.recv(wq.at[1, at_x], slot + 1)

        net.send(wq.at[1, at_x], wq.at[1, at_x], slot + 3, dev(y, c, z, 1 - x), only=(c != y))
    for k in range(1, 4):
        net.recv(woz.at[k - 1], r_woz + k)
        spread_wo(k, woz.at[k - 1])
    for k in range(4):
        at_x = pl.ds(off(2 * zat(k) + x, rows), rows)
        at_o = pl.ds(off(2 * zat(k) + 1 - x, rows), rows)
        slot = r_wq + k * 4

        @pl.when(c == y)
        def _():
            net.recv(wq.at[1, at_x], slot + 1)

        @pl.when(c != y)
        def _():
            net.recv(wq.at[0, at_o], slot + 2)

        net.recv(wq.at[0, at_x], slot)
        net.recv(wq.at[1, at_o], slot + 3)

    lane = lax.broadcasted_iota(jnp.int32, (2 * tokens, 128), 1)
    low_half = lax.rem(lane, HEAD_SIZE) < HEAD_SIZE // 2

    def turn(tile, forward):
        other = jnp.where(low_half, pltpu.roll(tile, 96, 1), pltpu.roll(tile, 32, 1))
        turned = other * csf[:, 128:256]
        return tile * csf[:, 0:128] + (turned if forward else -turned)

    qf[:, qw:] = jnp.zeros((2 * tokens, qf.shape[1] - qw), F32)
    for part in range(2):
        got = dot_nn(n1[...], wq[part])
        qf[:, qcols * part : qcols * (part + 1)] = got[:, :qcols]
        kvf[:, kcols * part : kcols * (part + 1)] = got[:, qcols : qcols + kcols]
        kvf[:, kw + kcols * part : kw + kcols * (part + 1)] = got[:, qcols + kcols :]

    def turn_keys(forward):
        for t in range(kw // 128 + 1):
            tile = kvf[:, 128 * t : 128 * (t + 1)]
            kvf[:, 128 * t : 128 * (t + 1)] = jnp.where(
                128 * t + lane < kw, turn(tile, forward), tile
            )

    turn_keys(True)
    own_keys = pl.ds(off(ctx, tokens), tokens)
    for s in range(2):
        kv[s, own_keys] = kvf[s * tokens : (s + 1) * tokens].astype(BF16)
    r_kz, r_kx = net.slots(8), net.slots(8)

    def kv_part(s, k, hx):
        return kv.at[s, pl.ds(off(2 * zat(k) + flip(x, hx), tokens), tokens)]

    for s in range(2):
        part = kv_part(s, 0, 0)
        for k in range(1, 4):
            net.send(part, part, r_kz + 4 * s + k, dev(y, c, zat(k), x))
        net.send(part, part, r_kx + 4 * s, dev(y, c, z, 1 - x))

    def pass_kv(s, k):
        part = kv_part(s, k, 0)
        net.recv(part, r_kz + 4 * s + k)
        net.send(part, part, r_kx + 4 * s + k, dev(y, c, z, 1 - x))

    def take_kv(s):
        for k in range(4):
            net.recv(kv_part(s, k, 1), r_kx + 4 * s + k)

    send_ff(1)
    send_down()

    for t in range(qf.shape[1] // 128):
        qf[:, 128 * t : 128 * (t + 1)] = turn(qf[:, 128 * t : 128 * (t + 1)], True) * scale
    for s in range(2):
        for h in range(heads):
            q6[s * groups + h // per, (h % per) * tokens : (h % per + 1) * tokens] = qf[
                s * tokens : (s + 1) * tokens, HEAD_SIZE * h : HEAD_SIZE * (h + 1)
            ].astype(BF16)
    for k in range(1, 4):
        pass_kv(0, k)
    pass_kv(1, 1)
    pass_kv(1, 2)
    for zz in range(2):
        for cc in range(2):
            part = wok.at[2 * y + cc, pl.ds(off(2 * zz + 1 - x, rows), rows)]
            slot = r_wo + zz * 8 + 4 + cc
            net.recv(part, slot)
            net.send(part, part, slot + 2, dev(1 - y, c, z, x))
    pass_ff(0)
    take_kv(0)

    def attend(s, g):
        kg = kv[s, :, HEAD_SIZE * g : HEAD_SIZE * (g + 1)]
        vg = kv[s, :, kw + HEAD_SIZE * g : kw + HEAD_SIZE * (g + 1)]
        scores = dot_nt(q6[s * groups + g], kg) + b2[s, 0:1, :]
        weights = jnp.exp(scores - jnp.max(scores, -1, keepdims=True))
        probs = (weights * (1.0 / jnp.sum(weights, -1, keepdims=True))).astype(BF16)
        p6[s * groups + g] = probs
        got = dot_nn(probs, vg).astype(BF16)
        o6[s * groups + g] = got
        for i in range(per):
            h = g * per + i
            ab[s * tokens : (s + 1) * tokens, HEAD_SIZE * h : HEAD_SIZE * (h + 1)] = got[
                i * tokens : (i + 1) * tokens
            ]

    attend(0, 0)
    pass_kv(1, 3)
    attend(0, 1)
    gather_pass(c8, r_c8, 1)
    attend(0, 2)
    take_kv(1)
    for g in range(groups):
        attend(1, g)

    for hx, hy, cc in ((0, 0, 0), (0, 0, 1), (0, 1, 0), (0, 1, 1), (1, 1, 0), (1, 1, 1)):
        for zz in range(2):
            net.recv(
                wok.at[2 * flip(y, hy) + cc, pl.ds(off(2 * zz + flip(x, hx), rows), rows)],
                r_wo + zz * 8 + hx * 4 + hy * 2 + cc,
            )
    for part in range(4):
        got = dot_nn(ab[:, 0:qw], wok[part])
        for s in range(2):
            mp[s, :, qcols * part : qcols * (part + 1)] = got[s * tokens : (s + 1) * tokens]
    r_ml = net.slots(1)
    mp_sent = net.send(mp.at[1], ml, r_ml, partner)
    pass_ff(1)
    for cc in range(2):
        part = wd8.at[pl.ds(off(2 * y + cc, drows), drows)]
        net.recv(part, r_wd + cc)
        net.send(part, part, r_wy + cc, dev(1 - y, c, z, x))
    gather_pass(c8, r_c8, 2)
    gather_pass(c8, r_c8, 3)
    net.recv(ml, r_ml)
    mid[...] = tok[...].astype(F32) + mp[0] + ml[...]
    n8[0] = (normed(mid[...])[0] * grow[1:2]).astype(BF16)
    r_n8 = net.slots(8)
    gather_z(n8, r_n8)
    gather_x(n8, r_n8)

    net.recv(c8.at[1], r_c8 + 4)
    for h in range(1, 4):
        net.recv(c8.at[2 * h + 1], r_c8 + 4 + h)
    take_ff(0)
    take_ff(1)
    for cc in range(2):
        net.recv(wd8.at[pl.ds(off(2 * (1 - y) + cc, drows), drows)], r_wy + cc)

    all_tokens = 8 * tokens

    def feed(i):
        pair = slice(2 * i, 2 * i + 2)
        here = n8[pair].reshape(2 * tokens, width)
        grad_inner = dot_nn(c8[pair].reshape(2 * tokens, width), wd8[...])
        gate = dot_nn(here, wg8[0])
        up = dot_nn(here, wg8[1])
        sig = 1.0 / (1.0 + jnp.exp(-gate))
        silu = gate * sig
        dgate = (grad_inner * up * sig * (1.0 + gate * (1.0 - sig))).astype(BF16)
        dup = (grad_inner * silu).astype(BF16)
        at = 2 * tokens * i
        act[at : at + 2 * tokens] = (silu * up).astype(BF16)
        act[at + all_tokens : at + all_tokens + 2 * tokens] = dgate
        act[at + 2 * all_tokens : at + 2 * all_tokens + 2 * tokens] = dup
        pt[pair] = (dot_nt(dgate, wg8[0]) + dot_nt(dup, wg8[1])).astype(BF16).reshape(2, tokens, width)

    def reduce_start(part, land, slot, h):
        return net.send(part.at[2 * h + 1], land.at[h], slot + h, partner)

    def reduce_pass(part, land, out, land2, slot, h):
        net.recv(land.at[h], slot + h)
        out[h - 1] = (part[2 * h].astype(F32) + land[h].astype(F32)).astype(BF16)
        net.send(
            out.at[h - 1], land2.at[h - 1], slot + 4 + h,
            dev(y, c, zat(h % 2), flip(x, h // 2)),
        )

    def reduce_own(part, land, slot):
        net.recv(land.at[0], slot)
        return part[0].astype(F32) + land[0].astype(F32)

    def reduce_end(land2, slot):
        total = 0.0
        for h in range(1, 4):
            net.recv(land2.at[h - 1], slot + 4 + h)
            total = total + land2[h - 1].astype(F32)
        return total

    r_dn = net.slots(8)
    pt_sent = []
    net.recv(n8.at[1], r_n8 + 4)
    for h in range(4):
        if h:
            gather_pass(n8, r_n8, h)
            net.recv(n8.at[2 * h + 1], r_n8 + 4 + h)
        feed(h)
        pt_sent.append(reduce_start(pt, l1, r_dn, h))
        if h > 1:
            reduce_pass(pt, l1, s2, l2, r_dn, h - 1)
    reduce_pass(pt, l1, s2, l2, r_dn, 3)
    dmid[...] = reduce_own(pt, l1, r_dn)

    def flat(ref, i):
        return ref[:, :, pl.ds(off(i, 128), 128)].reshape(all_tokens, 128)

    def grad_gu(i, carry):
        left = flat(n8, i)
        at = pl.ds(off(i, 128), 128)
        ggu[0, at] = dot_tn(left, act[pl.ds(all_tokens, all_tokens)]).astype(BF16)
        ggu[1, at] = dot_tn(left, act[pl.ds(2 * all_tokens, all_tokens)]).astype(BF16)
        return carry

    def grad_d(i, carry):
        gdt[pl.ds(off(i, 128), 128)] = dot_tn(flat(c8, i), act[pl.ds(0, all_tokens)]).astype(BF16)
        return carry

    def feed_out(i, carry):
        got = dot_nt(act[pl.ds(off(i, 2 * tokens), 2 * tokens)], wd8[...])
        pt[pl.ds(2 * i, 2)] = got.astype(BF16).reshape(2, tokens, width)
        return carry

    r_gd, r_gz = net.slots(1), net.slots(4)
    half = 2 * drows
    lax.fori_loop(0, width // 128, grad_d, 0)
    net.send(gdt.at[pl.ds(off(1 - y, half), half)], lgd, r_gd, dev(1 - y, c, z, x))
    lax.fori_loop(0, width // 128, grad_gu, 0)
    for zt in range(4):
        at = pl.ds(2 * rows * zt, 2 * rows)
        net.send(
            ggu.at[:, at], lgu.at[:, at], r_gz + zt, dev(1 - y, c, z, x),
            only=jnp.logical_not(home),
        )
    for finish in pt_sent:
        net.done(finish)
    lax.fori_loop(0, 4, feed_out, 0)
    r_out = net.slots(8)
    for h in range(4):
        reduce_start(pt, l1o, r_out, h)

    total = dmid[...] + reduce_end(l2, r_dn)
    normed_two, inv_two = normed(mid[...])
    total = total * grow[1:2]
    dmid[...] = cot[...].astype(F32) + inv_two * (
        total - normed_two * jnp.mean(total * normed_two, -1, keepdims=True)
    )
    dmb[0] = dmid[...].astype(BF16)
    r_dm = net.slots(1)
    net.send(dmb.at[0], dmb.at[1], r_dm, partner)

    r_ld = net.slots(2)
    net.recv(lgd, r_gd)
    sgd[...] = (gdt[pl.ds(off(y, half), half)].astype(F32) + lgd[...].astype(F32)).astype(BF16)
    gd_z = 2 * (z_lo + c - 2 * z_lo * c) + c
    for cc in range(2):
        net.send(
            sgd.at[pl.ds(cc * drows, drows)], ld.at[z_hi], r_ld + z_hi, dev(y, cc, gd_z, x),
            is_self=jnp.logical_and(z == gd_z, c == cc),
        )
    net.recv(dmb.at[1], r_dm)

    for part in range(4):
        for s in range(2):
            dm4[part, s * tokens : (s + 1) * tokens] = dmb[s, :, qcols * part : qcols * (part + 1)]
    dattn = dot_nt(dm4[0], wok[0])
    for part in range(1, 4):
        dattn = dattn + dot_nt(dm4[part], wok[part])
    qf[:, 0:qw] = dattn
    for s in range(2):
        for h in range(heads):
            do6[s * groups + h // per, (h % per) * tokens : (h % per + 1) * tokens] = qf[
                s * tokens : (s + 1) * tokens, HEAD_SIZE * h : HEAD_SIZE * (h + 1)
            ].astype(BF16)
    attn_all = ab[:, 0:qw]
    for part in range(4):
        act[qw * part : qw * (part + 1), 0:qcols] = dot_tn(attn_all, dm4[part]).astype(BF16)
    r_gy, r_go = net.slots(2), net.slots(8)
    for cc in range(2):
        net.send(
            act.at[pl.ds(off(2 * (1 - y) + cc, qw), qw)], loy.at[cc], r_gy + cc, dev(1 - y, c, z, x)
        )

    def pass_go():
        for cc in range(2):
            net.recv(loy.at[cc], r_gy + cc)
            at = pl.ds(off(2 * y + cc, qw), qw)
            act[at] = (act[at].astype(F32) + loy[cc].astype(F32)).astype(BF16)
        for hx in (1, 0):
            for hc in range(2):
                for zz in range(2):
                    at = pl.multiple_of((2 * y + flip(c, hc)) * qw + (2 * zz + flip(x, hx)) * rows, rows)
                    src = act.at[pl.ds(at, rows)]
                    dst = lo.at[2 * c + zz, hx]
                    slot = r_go + (2 * c + zz) * 2 + hx
                    if hx + hc == 0:
                        net.keep(src, dst, slot)
                    else:
                        net.send(src, dst, slot, dev(y, flip(c, hc), z, flip(x, hx)))

    def attend_back(s, g):
        at = s * groups + g
        kg = kv[s, :, HEAD_SIZE * g : HEAD_SIZE * (g + 1)]
        vg = kv[s, :, kw + HEAD_SIZE * g : kw + HEAD_SIZE * (g + 1)]
        dout = do6[at]
        delta = jnp.sum(dout.astype(F32) * o6[at].astype(F32), -1, keepdims=True)
        dprob = dot_nt(dout, vg)
        dscore = (p6[at].astype(F32) * (dprob - delta)).astype(BF16)
        dquery = dot_nn(dscore, kg) * scale
        dkeys = dot_tn(q6[at], dscore)
        dvals = dot_tn(dout, p6[at])
        for t in range(n_ctx):
            cols = slice(t * tokens, (t + 1) * tokens)
            dkv[t, s, HEAD_SIZE * g : HEAD_SIZE * (g + 1)] = dkeys[:, cols].astype(BF16)
            dkv[t, s, kw + HEAD_SIZE * g : kw + HEAD_SIZE * (g + 1)] = dvals[:, cols].astype(BF16)
        for i in range(per):
            h = g * per + i
            qf[s * tokens : (s + 1) * tokens, HEAD_SIZE * h : HEAD_SIZE * (h + 1)] = dquery[
                i * tokens : (i + 1) * tokens
            ]

    r_dx, r_dz = net.slots(8), net.slots(8)

    def send_dkv(s):
        for k in (1, 2, 3, 0):
            net.send(
                dkv.at[2 * zat(k) + 1 - x, s], lx.at[k, s], r_dx + 4 * s + k, dev(y, c, z, 1 - x)
            )

    def pass_dkv(s):
        for k in range(1, 4):
            net.recv(lx.at[k, s], r_dx + 4 * s + k)
            sx[k - 1, s] = (dkv[2 * zat(k) + x, s].astype(F32) + lx[k, s].astype(F32)).astype(BF16)
            net.send(sx.at[k - 1, s], lkz.at[k - 1, s], r_dz + 4 * s + k, dev(y, c, zat(k), x))

    for g in range(groups):
        attend_back(0, g)
    send_dkv(0)
    r_gf = net.slots(4)
    for k in (3, 2, 1, 0):
        at = pl.ds(off(zat(k), 2 * rows), 2 * rows)

        @pl.when(home)
        def _():
            net.recv(lgu.at[:, at], r_gz + zat(k))
            ggu[:, at] = (ggu[:, at].astype(F32) + lgu[:, at].astype(F32)).astype(BF16)

        for hx in range(2):
            src = ggu.at[:, pl.ds(off(2 * zat(k) + flip(x, hx), rows), rows)]
            dst = lf.at[x, z_hi]
            slot = r_gf + x * 2 + z_hi
            if k + hx:
                net.send(src, dst, slot, dev(y, c, zat(k), flip(x, hx)), only=home)
            else:

                @pl.when(home)
                def _():
                    net.keep(src, dst, slot)

    attend_back(1, 0)
    pass_go()
    attend_back(1, 1)
    pass_dkv(0)
    attend_back(1, 2)
    send_dkv(1)
    for t in range(qf.shape[1] // 128):
        qf[:, 128 * t : 128 * (t + 1)] = turn(qf[:, 128 * t : 128 * (t + 1)], False)
    grad = dot_tn(n1[...], qf[:, 0:qw].astype(BF16)).astype(BF16)
    for t in range(n_ctx):
        p6[t // 2, (t % 2) * rows : (t % 2 + 1) * rows, 0:qw] = grad[rows * t : rows * (t + 1)]
    for part in range(2):
        dqk[part, :, 0:qcols] = qf[:, qcols * part : qcols * (part + 1)].astype(BF16)
    r_qy, r_qx, r_zq = net.slots(4), net.slots(4), net.slots(4)
    mine = c == y

    def send_grads(source, land, slot):
        for k in range(4):
            net.send(
                source(zat(k), slice(0, 2)), land.at[zat(k)], slot + k, dev(1 - y, c, z, x),
                only=jnp.logical_not(mine),
            )

    def add_y(source, land, slot, land_x, slot_x):
        for k in range(4):

            @pl.when(mine)
            def _():
                net.recv(land.at[zat(k)], slot + k)
                here = source(zat(k), slice(0, 2))
                here[...] = (here[...].astype(F32) + land[zat(k)].astype(F32)).astype(BF16)

            net.send(
                source(zat(k), 1 - x), land_x.at[k], slot_x + k, dev(y, c, z, 1 - x), only=mine
            )

    def add_x(source, land_x, slot_x, staged, arrived, slot_z):
        wide_part = arrived.shape[2]
        for k in (1, 2, 3, 0):

            @pl.when(mine)
            def _():
                net.recv(land_x.at[k], slot_x + k)
                staged[k] = (source(zat(k), x)[...].astype(F32) + land_x[k].astype(F32)).astype(BF16)

            for cc in range(2):
                first = cc * (staged.shape[2] - wide_part)
                src = staged.at[k, :, pl.ds(first, wide_part)]
                if k:
                    net.send(src, arrived.at[k], slot_z + k, dev(y, cc, zat(k), x), only=mine)
                else:

                    @pl.when(jnp.logical_and(mine, c == cc))
                    def _():
                        net.keep(src, arrived.at[k], slot_z)

                    net.send(
                        src, arrived.at[k], slot_z, dev(y, cc, z, x),
                        only=jnp.logical_and(mine, c != cc),
                    )

    def add_z(out, arrived, slot_z, staged):
        total = 0.0
        for k in (1, 2, 3, 0):
            net.recv(arrived.at[k], slot_z + k)
            total = total + arrived[k].astype(F32)
        count = out.shape[1]
        skip = count - (staged.shape[2] - arrived.shape[2])
        out[...] = jnp.where(c == 0, total[:, 0:count], total[:, skip : skip + count])

    def in_p6(zt, xt):
        at = pl.ds(0, 2 * rows) if isinstance(xt, slice) else pl.ds(off(xt, rows), rows)
        return p6.at[zt, at, pl.ds(0, qf.shape[1])]

    def in_wg8(zt, xt):
        at = pl.ds(off(zt, 2 * rows), 2 * rows) if isinstance(xt, slice) else pl.ds(off(2 * zt + xt, rows), rows)
        return wg8.at[0, at]

    send_grads(in_p6, lqy, r_qy)
    pass_dkv(1)
    for h in range(1, 4):
        reduce_pass(pt, l1o, s2o, l2o, r_out, h)
    mid[...] = mid[...] + reduce_own(pt, l1o, r_out)

    def attn_pass(land, out, staged, arrived, send_slot, slot, absolute):
        for k in (1, 2, 3, 0):
            at = zat(k) if absolute else k
            part = 0.0
            for h in range(2):
                net.recv(land.at[at, h], slot + at * 2 + h)
                part = part + land[at, h, :, 0 : out.shape[1]].astype(F32)
            if k == 0:
                out[...] = part
            else:
                staged[k - 1] = part.astype(BF16)
                net.send(staged.at[k - 1], arrived.at[k - 1], send_slot + k, dev(y, c, zat(k), x))

    def attn_end(out, arrived, slot):
        for k in range(1, 4):
            net.recv(arrived.at[k - 1], slot + k)
            out[...] = out[...] + arrived[k - 1].astype(F32)

    r_zo = net.slots(4)
    attn_pass(lo, o_o, so, lzo, r_zo, r_go, True)
    add_y(in_p6, lqy, r_qy, lqx, r_qx)

    for s in range(2):
        net.recv(lx.at[0, s], r_dx + 4 * s)
        total = dkv[2 * z + x, s].astype(F32) + lx[0, s].astype(F32)
        for k in range(1, 4):
            net.recv(lkz.at[k - 1, s], r_dz + 4 * s + k)
            total = total + lkz[k - 1, s].astype(F32)
        kvf[s * tokens : (s + 1) * tokens] = total.T
    turn_keys(False)
    for part in range(2):
        dqk[part, :, qcols : qcols + kcols] = kvf[:, kcols * part : kcols * (part + 1)].astype(BF16)
        dqk[part, :, qcols + kcols :] = kvf[:, kw + kcols * part : kw + kcols * (part + 1)].astype(BF16)
    for finish in ff_passed:
        net.done(finish)
    for part in range(2):
        wg8[0, :, 2 * kcols * part : 2 * kcols * (part + 1)] = dot_tn(
            n1[...], dqk[part, :, qcols:]
        ).astype(BF16)
    r_ky, r_kx2, r_zk = net.slots(4), net.slots(4), net.slots(4)
    send_grads(in_wg8, lky, r_ky)
    net.done(mp_sent)
    got = dot_nt(dqk[0], wq[0]) + dot_nt(dqk[1], wq[1])
    for s in range(2):
        mp[s] = got[s * tokens : (s + 1) * tokens]
    r_dn1 = net.slots(1)
    net.send(mp.at[1], ml, r_dn1, partner)
    add_x(in_p6, lqx, r_qx, sq, lzq, r_zq)
    add_y(in_wg8, lky, r_ky, lkx, r_kx2)
    net.recv(ml, r_dn1)
    total = mp[0] + ml[...]
    normed_one, inv_one = normed(tok[...])
    total = total * grow[0:1]
    o_ing[...] = (
        dmid[...]
        + inv_one * (total - normed_one * jnp.mean(total * normed_one, -1, keepdims=True))
    ).astype(BF16)
    add_x(in_wg8, lkx, r_kx2, sk, lzk, r_zk)

    o_out[...] = (mid[...] + reduce_end(l2o, r_out)).astype(BF16)
    gains = [0.0, 0.0]
    for h in range(2):
        for zh in range(2):
            net.recv(lf.at[h, zh], r_gf + h * 2 + zh)
        for m in range(2):
            got = lf[h, 0, m].astype(F32) + lf[h, 1, m].astype(F32)
            cols = slice(h * ff, (h + 1) * ff)
            (o_gate, o_up)[m][:, cols] = got
            gains[1] = gains[1] + jnp.sum(
                got * (wgate, wup)[m][:, cols].astype(F32), 1, keepdims=True
            )
    for zh in range(2):
        net.recv(ld.at[zh], r_ld + zh)
    o_d[...] = (ld[0].astype(F32) + ld[1].astype(F32)).T
    attn_end(o_o, lzo, r_zo)
    add_z(o_q, lzq, r_zq, sq)
    gains[0] = jnp.sum(o_q[...] * wqkv[:, 0:qcols].astype(F32), 1, keepdims=True)
    add_z(kvg, lzk, r_zk, sk)
    gains[0] = gains[0] + jnp.sum(kvg[...] * wqkv[:, qcols:].astype(F32), 1, keepdims=True)
    o_k[...] = kvg[:, 0:kcols]
    o_v[...] = kvg[:, kcols:]
    column = lax.broadcasted_iota(jnp.int32, (rows, 128), 1)
    both = jnp.where(column == 0, gains[0], jnp.where(column == 1, gains[1], 0.0))
    sg[...] = both.T[0:8]
    r_lg = net.slots(4)
    for h in range(1, 4):
        net.send(sg, lg.at[h - 1], r_lg + h, dev(flip(y, h // 2), flip(c, h % 2), z, x))
    total = sg[...]
    for h in range(1, 4):
        net.recv(lg.at[h - 1], r_lg + h)
        total = total + lg[h - 1]
    o_gain[...] = total / gain[...]
    net.drain()


def run_layer(tok, cot, cs, bias, gain, wqkv, wo, wgate, wup, wdt):
    tokens, width = tok.shape
    rows, packed = wqkv.shape
    qcols = wo.shape[1]
    drows, ff = wdt.shape
    keys = bias.shape[1]
    n_ctx = keys // tokens
    qw = 2 * qcols
    kw = packed - qcols
    groups = kw // HEAD_SIZE
    per = QUERY_HEADS // KEY_VALUE_HEADS
    stack = per * tokens
    wide = -(-qw // 128) * 128
    out_shape = [
        jax.ShapeDtypeStruct((tokens, width), BF16),
        jax.ShapeDtypeStruct((tokens, width), BF16),
        jax.ShapeDtypeStruct((8, rows), F32),
        jax.ShapeDtypeStruct((rows, qcols), F32),
        jax.ShapeDtypeStruct((rows, kw // 2), F32),
        jax.ShapeDtypeStruct((rows, kw // 2), F32),
        jax.ShapeDtypeStruct((rows, qcols), F32),
        jax.ShapeDtypeStruct((rows, 2 * ff), F32),
        jax.ShapeDtypeStruct((rows, 2 * ff), F32),
        jax.ShapeDtypeStruct((ff, drows), F32),
    ]

    def vm(*shape, dtype=BF16):
        return pltpu.VMEM(shape, dtype)

    scratch = [
        vm(2 * tokens, 256, dtype=F32),
        vm(2, 8, keys, dtype=F32),
        vm(tokens, width),
        vm(n_ctx, 8, rows, dtype=F32),
        vm(8, width, dtype=F32),
        vm(3, rows, packed),
        vm(3, rows, qcols),
        vm(2, width, packed),
        vm(4, 4 * rows, qcols),
        vm(2, width, ff),
        vm(width, ff),
        vm(8, tokens, width),
        vm(8, tokens, width),
        vm(2 * tokens, width),
        vm(2 * tokens, wide, dtype=F32),
        vm(2 * tokens, 2 * kw, dtype=F32),
        vm(2, keys, 2 * kw),
        vm(2 * groups, stack, HEAD_SIZE),
        vm(2 * groups, stack, keys),
        vm(2 * groups, stack, HEAD_SIZE),
        vm(2 * tokens, wide),
        vm(2, tokens, width, dtype=F32),
        vm(tokens, width, dtype=F32),
        vm(tokens, width, dtype=F32),
        vm(tokens, width, dtype=F32),
        vm(2, tokens, width),
        vm(4, 2 * tokens, qcols),
        vm(2 * groups, stack, HEAD_SIZE),
        vm(24 * tokens, ff),
        vm(8, tokens, width),
        vm(4, tokens, width),
        vm(3, tokens, width),
        vm(3, tokens, width),
        vm(4, tokens, width),
        vm(3, tokens, width),
        vm(3, tokens, width),
        vm(2, width, ff),
        vm(2, width, ff),
        vm(2, 2, 2, rows, ff),
        vm(width, ff),
        vm(2 * drows, ff),
        vm(2 * drows, ff),
        vm(2, drows, ff),
        vm(2, qw, ff),
        vm(4, 2, rows, ff),
        vm(4, 2 * rows, wide),
        vm(4, rows, wide),
        vm(4, 2 * rows, ff),
        vm(4, rows, ff),
        vm(3, rows, qcols),
        vm(4, rows, wide),
        vm(4, rows, ff),
        vm(3, rows, qcols),
        vm(4, rows, ff),
        vm(4, rows, 256),
        vm(rows, kw, dtype=F32),
        vm(n_ctx, 2, 2 * kw, tokens),
        vm(4, 2, 2 * kw, tokens),
        vm(3, 2, 2 * kw, tokens),
        vm(3, 2, 2 * kw, tokens),
        vm(3, 8, rows, dtype=F32),
        vm(8, rows, dtype=F32),
        vm(2, 2 * tokens, packed),
        pltpu.SemaphoreType.DMA((N_SEM,)),
        pltpu.SemaphoreType.DMA((N_SEM,)),
    ]
    inside = pl.BlockSpec(memory_space=pltpu.VMEM)
    return pl.pallas_call(
        layer_kernel,
        out_shape=out_shape,
        in_specs=[inside] * 10,
        out_specs=[inside] * len(out_shape),
        scratch_shapes=scratch,
        compiler_params=pltpu.CompilerParams(
            collective_id=0, has_side_effects=True, vmem_limit_bytes=VMEM_LIMIT
        ),
        name="layer",
    )(tok, cot, cs, bias, gain, wqkv, wo, wgate, wup, wdt)


VMEM_LIMIT = 63 * 1024 * 1024


def on_device_plane(
    tokens, positions, block_sizes, attn_gain, w_query, w_key, w_value, w_out, mlp_gain,
    w_gate, w_up, w_down, cotangent,
):
    seq_rows, width = tokens.shape[1:]
    ctx = lax.axis_index("ctx")
    angles = angles_of(positions[0])
    cosine, sine = jnp.cos(angles), jnp.sin(angles)
    cs = jnp.concatenate([cosine] * 4 + [-sine, sine] * 2, 1)
    keys = seq_rows * lax.axis_size("ctx")
    block = block_sizes[0]
    limit = (ctx * seq_rows // block + 1) * block
    bias = jnp.where(jnp.arange(keys, dtype=jnp.int32) < limit, 0.0, VERY_NEGATIVE).astype(F32)
    bias = jnp.broadcast_to(bias[None, :], (8, keys))
    rows = w_query.shape[0]
    gain = jnp.concatenate([attn_gain[None], mlp_gain[None], jnp.ones((6, rows), BF16)], 0).astype(F32)
    wqkv = jnp.concatenate([w_query, w_key, w_value], 1)
    output, input_grad, gains, g_q, g_k, g_v, g_o, g_gate, g_up, g_d = run_layer(
        tokens[0], cotangent[0], cs, bias, gain, wqkv, w_out, w_gate, w_up, w_down.T
    )
    return (
        output[None],
        input_grad[None],
        gains[0],
        g_q,
        g_k,
        g_v,
        g_o,
        gains[1],
        g_gate,
        g_up,
        g_d,
    )


def solution(mesh):
    placed = (
        P("dp", "ctx", None),
        P("dp", "ctx"),
        P("dp"),
        P("ctx"),
        P("ctx", "dp"),
        P("ctx", "dp"),
        P("ctx", "dp"),
        P("ctx", "dp"),
        P("ctx"),
        P("ctx", "dp"),
        P("ctx", "dp"),
        P("ctx", "dp"),
        P("dp", "ctx", None),
    )
    fits = mesh.shape["dp"] == 4 and mesh.shape["ctx"] == 8
    return jax.shard_map(
        on_device_plane if fits else on_device,
        mesh=mesh,
        in_specs=placed,
        out_specs=(
            P("dp", "ctx", None),
            P("dp", "ctx", None),
            P("ctx"),
            P("ctx", "dp"),
            P("ctx", "dp"),
            P("ctx", "dp"),
            P("ctx", "dp"),
            P("ctx"),
            P("ctx", "dp"),
            P("ctx", "dp"),
            P("ctx", "dp"),
        ),
        check_vma=False,
    )
```

```python
import jax
import jax.numpy as jnp
import numpy as np
from jax import lax
from jax.experimental import pallas as pl
from jax.experimental.pallas import tpu as pltpu
from jax.sharding import PartitionSpec as P

QUERY_HEADS = 18
KEY_VALUE_HEADS = 6
HEAD_SIZE = 64


EPSILON = 1e-05
THETA = 10000.0
VERY_NEGATIVE = -1e30


def product(left, right):
    return jnp.dot(left, right, preferred_element_type=jnp.float32)


def angles_of(place_ids):
    half_dim = HEAD_SIZE // 2
    frequency = THETA ** (-(jnp.arange(half_dim, dtype=jnp.float32) * 2.0 / HEAD_SIZE))
    return place_ids.astype(jnp.float32)[:, None] * frequency[None, :]


def rotate(values, angles, forward):
    row_total = values.shape[0]
    half_dim = angles.shape[1]
    shaped = values.reshape(row_total, -1, 2 * half_dim)
    first_half = shaped[..., :half_dim]
    second = shaped[..., half_dim:]
    cosine = jnp.cos(angles)[:, None, :]
    sine_vals = jnp.sin(angles)[:, None, :]
    if forward:
        rotated = jnp.concatenate(
            [first_half * cosine - second * sine_vals, second * cosine + first_half * sine_vals], -1
        )
    else:
        rotated = jnp.concatenate(
            [first_half * cosine + second * sine_vals, second * cosine - first_half * sine_vals], -1
        )
    return rotated.reshape(row_total, -1)


def norm_back(grad_normed, normed, inverse):
    return inverse * (grad_normed - normed * jnp.mean(grad_normed * normed, -1, keepdims=True))


def visible(query_rows, key_rows, block_len):
    return ((key_rows // block_len)[None, :] <= (query_rows // block_len)[:, None])[None, None]


def attend_forward(query_rows4, complete_keys, complete_values, query_rows, block_len, score_scale):
    key_count = complete_keys.shape[0]
    key_row_width = 512
    block_list = key_count // key_row_width
    query_group_width = QUERY_HEADS // KEY_VALUE_HEADS
    row_total = query_rows4.shape[0]
    key_block_list = complete_keys.reshape(block_list, key_row_width, KEY_VALUE_HEADS, HEAD_SIZE)
    value_block_list = complete_values.reshape(
        block_list, key_row_width, KEY_VALUE_HEADS, HEAD_SIZE
    )
    last_block = query_rows[-1] // block_len

    def advance(carried, inputs):
        key_blk, val_blk, first_key = inputs
        key_rows = first_key + jnp.arange(key_row_width, dtype=jnp.int32)

        def compute(current):
            run_max, run_sum, accum = current
            scores = (
                jnp.einsum(
                    "tkgd,nkd->kgtn", query_rows4, key_blk, preferred_element_type=jnp.float32
                )
                * score_scale
            )
            allowed = visible(query_rows, key_rows, block_len)
            scores = jnp.where(allowed, scores, VERY_NEGATIVE)
            new_max = jnp.maximum(run_max, jnp.max(scores, -1))
            weights = jnp.where(allowed, jnp.exp(scores - new_max[..., None]), 0.0)
            factor = jnp.exp(run_max - new_max)
            new_sum = run_sum * factor + jnp.sum(weights, -1)
            accum = accum * factor[..., None] + jnp.einsum(
                "kgtn,nkd->kgtd",
                weights.astype(jnp.bfloat16),
                val_blk,
                preferred_element_type=jnp.float32,
            )
            return (new_max, new_sum, accum)

        return (
            lax.cond(
                first_key // block_len > last_block, lambda unchanged: unchanged, compute, carried
            ),
            None,
        )

    start_state = (
        jnp.full((KEY_VALUE_HEADS, query_group_width, row_total), VERY_NEGATIVE, jnp.float32),
        jnp.zeros((KEY_VALUE_HEADS, query_group_width, row_total), jnp.float32),
        jnp.zeros((KEY_VALUE_HEADS, query_group_width, row_total, HEAD_SIZE), jnp.float32),
    )
    firsts = jnp.arange(block_list, dtype=jnp.int32) * key_row_width
    final_state, unused = lax.scan(advance, start_state, (key_block_list, value_block_list, firsts))
    run_max, run_sum, accum = final_state
    return (accum / run_sum[..., None], run_max + jnp.log(run_sum))


def attend_backward(
    query_rows4,
    head_gradients,
    log_sums,
    row_delta,
    complete_keys,
    complete_values,
    query_rows,
    block_len,
    score_scale,
):
    key_count = complete_keys.shape[0]
    key_row_width = 512
    block_list = key_count // key_row_width
    query_group_width = QUERY_HEADS // KEY_VALUE_HEADS
    row_total = query_rows4.shape[0]
    key_block_list = complete_keys.reshape(block_list, key_row_width, KEY_VALUE_HEADS, HEAD_SIZE)
    value_block_list = complete_values.reshape(
        block_list, key_row_width, KEY_VALUE_HEADS, HEAD_SIZE
    )
    last_block = query_rows[-1] // block_len

    def advance(grad_query, inputs):
        key_blk, val_blk, first_key = inputs
        key_rows = first_key + jnp.arange(key_row_width, dtype=jnp.int32)

        def compute(current):
            scores = (
                jnp.einsum(
                    "tkgd,nkd->kgtn", query_rows4, key_blk, preferred_element_type=jnp.float32
                )
                * score_scale
            )
            allowed = visible(query_rows, key_rows, block_len)
            prob_vals = jnp.where(allowed, jnp.exp(scores - log_sums[..., None]), 0.0)
            grad_prob = jnp.einsum(
                "tkgd,nkd->kgtn", head_gradients, val_blk, preferred_element_type=jnp.float32
            )
            grad_score = (prob_vals * (grad_prob - row_delta[..., None])).astype(jnp.bfloat16)
            current = current + jnp.einsum(
                "kgtn,nkd->tkgd", grad_score, key_blk, preferred_element_type=jnp.float32
            )
            grad_key = jnp.einsum(
                "kgtn,tkgd->nkd", grad_score, query_rows4, preferred_element_type=jnp.float32
            )
            grad_value = jnp.einsum(
                "kgtn,tkgd->nkd",
                prob_vals.astype(jnp.bfloat16),
                head_gradients,
                preferred_element_type=jnp.float32,
            )
            return (current, (grad_key, grad_value))

        def nothing(current):
            empty_block = jnp.zeros((key_row_width, KEY_VALUE_HEADS, HEAD_SIZE), jnp.float32)
            return (current, (empty_block, empty_block))

        return lax.cond(first_key // block_len > last_block, nothing, compute, grad_query)

    firsts = jnp.arange(block_list, dtype=jnp.int32) * key_row_width
    initial_gradient = jnp.zeros(
        (row_total, KEY_VALUE_HEADS, query_group_width, HEAD_SIZE), jnp.float32
    )
    grad_query, stacked_rows = lax.scan(
        advance, initial_gradient, (key_block_list, value_block_list, firsts)
    )
    key_gradients = stacked_rows[0].reshape(key_count, KEY_VALUE_HEADS * HEAD_SIZE)
    value_gradients = stacked_rows[1].reshape(key_count, KEY_VALUE_HEADS * HEAD_SIZE)
    return (grad_query, key_gradients, value_gradients)


def on_device(
    tokens,
    positions,
    block_sizes,
    attn_gain,
    w_query,
    w_key,
    w_value,
    w_out,
    mlp_gain,
    w_gate,
    w_up,
    w_down,
    cotangent,
):
    row_parts = (
        lax.all_gather(w_query, "ctx", axis=0, tiled=True),
        lax.all_gather(w_key, "ctx", axis=0, tiled=True),
        lax.all_gather(w_value, "ctx", axis=0, tiled=True),
        lax.all_gather(w_out, "ctx", axis=0, tiled=True),
        lax.all_gather(w_gate, "ctx", axis=0, tiled=True),
        lax.all_gather(w_up, "ctx", axis=0, tiled=True),
        lax.all_gather(w_down, "ctx", axis=0, tiled=True),
        lax.all_gather(attn_gain, "ctx", axis=0, tiled=True),
        lax.all_gather(mlp_gain, "ctx", axis=0, tiled=True),
    )
    whole_w = (
        lax.all_gather(row_parts[0], "dp", axis=1, tiled=True),
        lax.all_gather(row_parts[1], "dp", axis=1, tiled=True),
        lax.all_gather(row_parts[2], "dp", axis=1, tiled=True),
        lax.all_gather(row_parts[3], "dp", axis=1, tiled=True),
        lax.all_gather(row_parts[4], "dp", axis=1, tiled=True),
        lax.all_gather(row_parts[5], "dp", axis=1, tiled=True),
        lax.all_gather(row_parts[6], "dp", axis=1, tiled=True),
    )
    query_w, key_w, value_w, out_w, gate_w, up_w, down_w = whole_w
    gain_one = row_parts[7].astype(jnp.float32)
    gain_two = row_parts[8].astype(jnp.float32)
    seq_count = tokens.shape[0]
    seq_rows = tokens.shape[1]
    width = tokens.shape[2]
    inputs = tokens.reshape(seq_count * seq_rows, width).astype(jnp.float32)
    row_total = inputs.shape[0]
    query_group_width = QUERY_HEADS // KEY_VALUE_HEADS
    query_rows = lax.axis_index("ctx") * seq_rows + jnp.arange(seq_rows, dtype=jnp.int32)
    angles = angles_of(positions.reshape(-1))
    score_scale = HEAD_SIZE ** (-0.5)
    inv_one = lax.rsqrt(jnp.mean(inputs * inputs, -1, keepdims=True) + EPSILON)
    normed_one = inputs * inv_one
    hidden_one = (normed_one * gain_one).astype(jnp.bfloat16)
    query_matrix = rotate(product(hidden_one, query_w), angles, True).astype(jnp.bfloat16)
    keys_own = rotate(product(hidden_one, key_w), angles, True).astype(jnp.bfloat16)
    values_own = product(hidden_one, value_w).astype(jnp.bfloat16)
    complete_keys, complete_values = (
        lax.all_gather(keys_own.reshape(seq_count, seq_rows, -1), "ctx", axis=1, tiled=True),
        lax.all_gather(values_own.reshape(seq_count, seq_rows, -1), "ctx", axis=1, tiled=True),
    )
    query_rows4 = query_matrix.reshape(row_total, KEY_VALUE_HEADS, query_group_width, HEAD_SIZE)
    member = 0
    heads_one, lse_one = attend_forward(
        query_rows4,
        complete_keys[member],
        complete_values[member],
        query_rows,
        block_sizes[member],
        score_scale,
    )
    attn_flat = heads_one.transpose(2, 0, 1, 3).reshape(row_total, QUERY_HEADS * HEAD_SIZE)
    attn_low = attn_flat.astype(jnp.bfloat16)
    mixed_rows = inputs + product(attn_low, out_w)
    inv_two = lax.rsqrt(jnp.mean(mixed_rows * mixed_rows, -1, keepdims=True) + EPSILON)
    normed_two = mixed_rows * inv_two
    hidden_two = (normed_two * gain_two).astype(jnp.bfloat16)
    gate_pre = product(hidden_two, gate_w)
    up_pre = product(hidden_two, up_w)
    sigmoid_gate = jax.nn.sigmoid(gate_pre)
    silu_gate = gate_pre * sigmoid_gate
    inner_act = (silu_gate * up_pre).astype(jnp.bfloat16)
    result = mixed_rows + product(inner_act, down_w)
    output = result.astype(jnp.bfloat16).reshape(seq_count, seq_rows, width)
    back_parts = (
        lax.all_gather(w_query, "ctx", axis=0, tiled=True),
        lax.all_gather(w_key, "ctx", axis=0, tiled=True),
        lax.all_gather(w_value, "ctx", axis=0, tiled=True),
        lax.all_gather(w_out, "ctx", axis=0, tiled=True),
        lax.all_gather(w_gate, "ctx", axis=0, tiled=True),
        lax.all_gather(w_up, "ctx", axis=0, tiled=True),
        lax.all_gather(w_down, "ctx", axis=0, tiled=True),
    )
    back_whole = (
        lax.all_gather(back_parts[0], "dp", axis=1, tiled=True),
        lax.all_gather(back_parts[1], "dp", axis=1, tiled=True),
        lax.all_gather(back_parts[2], "dp", axis=1, tiled=True),
        lax.all_gather(back_parts[3], "dp", axis=1, tiled=True),
        lax.all_gather(back_parts[4], "dp", axis=1, tiled=True),
        lax.all_gather(back_parts[5], "dp", axis=1, tiled=True),
        lax.all_gather(back_parts[6], "dp", axis=1, tiled=True),
    )
    back_query, back_key, back_value, back_out, back_gate, back_up, back_down = back_whole
    grad_top = cotangent.reshape(row_total, width)
    grad_down = jnp.einsum("tf,td->fd", inner_act, grad_top, preferred_element_type=jnp.float32)
    grad_inner = jnp.einsum("td,fd->tf", grad_top, back_down, preferred_element_type=jnp.float32)
    grad_gate = (
        grad_inner * up_pre * sigmoid_gate * (1.0 + gate_pre * (1.0 - sigmoid_gate))
    ).astype(jnp.bfloat16)
    grad_upval = (grad_inner * silu_gate).astype(jnp.bfloat16)
    grad_gatew = jnp.einsum("td,tf->df", hidden_two, grad_gate, preferred_element_type=jnp.float32)
    grad_upw = jnp.einsum("td,tf->df", hidden_two, grad_upval, preferred_element_type=jnp.float32)
    grad_hidden_two = jnp.einsum(
        "tf,df->td", grad_gate, back_gate, preferred_element_type=jnp.float32
    ) + jnp.einsum("tf,df->td", grad_upval, back_up, preferred_element_type=jnp.float32)
    grad_gain_two = jnp.sum(grad_hidden_two * normed_two, 0)
    grad_mixed = grad_top.astype(jnp.float32) + norm_back(
        grad_hidden_two * gain_two, normed_two, inv_two
    )
    grad_branch = grad_mixed.astype(jnp.bfloat16)
    grad_outw = jnp.einsum("tq,td->qd", attn_low, grad_branch, preferred_element_type=jnp.float32)
    attention_gradient = jnp.einsum(
        "td,qd->tq", grad_branch, back_out, preferred_element_type=jnp.float32
    ).astype(jnp.bfloat16)
    head_gradients = attention_gradient.reshape(
        row_total, KEY_VALUE_HEADS, query_group_width, HEAD_SIZE
    )
    row_delta = jnp.einsum("tkgd,kgtd->kgt", head_gradients.astype(jnp.float32), heads_one)
    member = 0
    grad_q_one, grad_k_one, grad_v_one = attend_backward(
        query_rows4,
        head_gradients,
        lse_one,
        row_delta,
        complete_keys[member],
        complete_values[member],
        query_rows,
        block_sizes[member],
        score_scale,
    )
    key_grads = [grad_k_one]
    value_grads = [grad_v_one]
    grad_keys_all = jnp.stack(key_grads, 0)
    grad_values_all = jnp.stack(value_grads, 0)
    grad_keys_own, grad_values_own = (
        lax.psum_scatter(grad_keys_all, "ctx", scatter_dimension=1, tiled=True),
        lax.psum_scatter(grad_values_all, "ctx", scatter_dimension=1, tiled=True),
    )
    grad_keys_own = grad_keys_own.reshape(row_total, -1)
    grad_values_own = grad_values_own.reshape(row_total, -1)
    grad_query_raw = rotate(
        grad_q_one.reshape(row_total, QUERY_HEADS * HEAD_SIZE) * score_scale, angles, False
    ).astype(jnp.bfloat16)
    grad_key_raw = rotate(grad_keys_own * score_scale, angles, False).astype(jnp.bfloat16)
    grad_value_raw = grad_values_own.astype(jnp.bfloat16)
    grad_queryw = jnp.einsum(
        "td,tq->dq", hidden_one, grad_query_raw, preferred_element_type=jnp.float32
    )
    grad_keyw = jnp.einsum(
        "td,tq->dq", hidden_one, grad_key_raw, preferred_element_type=jnp.float32
    )
    grad_valuew = jnp.einsum(
        "td,tq->dq", hidden_one, grad_value_raw, preferred_element_type=jnp.float32
    )
    grad_hidden_one = jnp.einsum(
        "tq,dq->td", grad_query_raw, back_query, preferred_element_type=jnp.float32
    )
    grad_hidden_one = grad_hidden_one + jnp.einsum(
        "tq,dq->td", grad_key_raw, back_key, preferred_element_type=jnp.float32
    )
    grad_hidden_one = grad_hidden_one + jnp.einsum(
        "tq,dq->td", grad_value_raw, back_value, preferred_element_type=jnp.float32
    )
    grad_gain_one = jnp.sum(grad_hidden_one * normed_one, 0)
    grad_input = grad_mixed + norm_back(grad_hidden_one * gain_one, normed_one, inv_one)
    input_grad = grad_input.astype(jnp.bfloat16).reshape(seq_count, seq_rows, width)
    summed_rows = (
        lax.psum_scatter(grad_queryw, "ctx", scatter_dimension=0, tiled=True),
        lax.psum_scatter(grad_keyw, "ctx", scatter_dimension=0, tiled=True),
        lax.psum_scatter(grad_valuew, "ctx", scatter_dimension=0, tiled=True),
        lax.psum_scatter(grad_outw, "ctx", scatter_dimension=0, tiled=True),
        lax.psum_scatter(grad_gatew, "ctx", scatter_dimension=0, tiled=True),
        lax.psum_scatter(grad_upw, "ctx", scatter_dimension=0, tiled=True),
        lax.psum_scatter(grad_down, "ctx", scatter_dimension=0, tiled=True),
        lax.psum_scatter(grad_gain_one, "ctx", scatter_dimension=0, tiled=True),
        lax.psum_scatter(grad_gain_two, "ctx", scatter_dimension=0, tiled=True),
    )
    final_w = (
        lax.psum_scatter(
            summed_rows[0].astype(jnp.bfloat16), "dp", scatter_dimension=1, tiled=True
        ).astype(jnp.float32),
        lax.psum_scatter(
            summed_rows[1].astype(jnp.bfloat16), "dp", scatter_dimension=1, tiled=True
        ).astype(jnp.float32),
        lax.psum_scatter(
            summed_rows[2].astype(jnp.bfloat16), "dp", scatter_dimension=1, tiled=True
        ).astype(jnp.float32),
        lax.psum_scatter(
            summed_rows[3].astype(jnp.bfloat16), "dp", scatter_dimension=1, tiled=True
        ).astype(jnp.float32),
        lax.psum_scatter(
            summed_rows[4].astype(jnp.bfloat16), "dp", scatter_dimension=1, tiled=True
        ).astype(jnp.float32),
        lax.psum_scatter(
            summed_rows[5].astype(jnp.bfloat16), "dp", scatter_dimension=1, tiled=True
        ).astype(jnp.float32),
        lax.psum_scatter(
            summed_rows[6].astype(jnp.bfloat16), "dp", scatter_dimension=1, tiled=True
        ).astype(jnp.float32),
    )
    final_gains = lax.psum((summed_rows[7], summed_rows[8]), "dp")
    return (
        output,
        input_grad,
        final_gains[0],
        final_w[0],
        final_w[1],
        final_w[2],
        final_w[3],
        final_gains[1],
        final_w[4],
        final_w[5],
        final_w[6],
    )


MESH = pl.DeviceIdType.MESH
F32 = jnp.float32
BF16 = jnp.bfloat16


def dot_nn(a, b):
    return lax.dot_general(a, b, (((1,), (0,)), ((), ())), preferred_element_type=F32)


def dot_nt(a, b):
    return lax.dot_general(a, b, (((1,), (1,)), ((), ())), preferred_element_type=F32)


def dot_tn(a, b):
    return lax.dot_general(a, b, (((0,), (0,)), ((), ())), preferred_element_type=F32)


class Wires:
    def __init__(self, send_sems, recv_sems):
        self.send_sems, self.recv_sems = send_sems, recv_sems
        self.sends = 0
        self.recvs = 0
        self.pending = []

    def slots(self, count):
        first = self.recvs
        self.recvs += count
        return first

    def send(self, src, dst, slot, device, is_self=None, only=None):
        mine = self.sends
        self.sends += 1
        remote = pltpu.make_async_remote_copy(
            src_ref=src,
            dst_ref=dst,
            send_sem=self.send_sems.at[mine],
            recv_sem=self.recv_sems.at[slot],
            device_id=device,
            device_id_type=MESH,
        )
        if only is not None:

            @pl.when(only)
            def _():
                remote.start()

            def finish():
                @pl.when(only)
                def _():
                    remote.wait_send()

        elif is_self is None:
            remote.start()
            finish = remote.wait_send
        else:
            local = pltpu.make_async_copy(src, dst, self.recv_sems.at[slot])

            @pl.when(is_self)
            def _():
                local.start()

            @pl.when(jnp.logical_not(is_self))
            def _():
                remote.start()

            def finish():
                @pl.when(jnp.logical_not(is_self))
                def _():
                    remote.wait_send()

        self.pending.append(finish)
        return finish

    def keep(self, src, dst, slot):
        pltpu.make_async_copy(src, dst, self.recv_sems.at[slot]).start()

    def recv(self, dst, slot):
        pltpu.make_async_copy(dst, dst, self.recv_sems.at[slot]).wait()

    def done(self, finish):
        finish()
        self.pending.remove(finish)

    def drain(self):
        for finish in self.pending:
            finish()
        self.pending = []


N_SEM = 288
FREQUENCY = np.float32(THETA) ** (-(np.arange(HEAD_SIZE // 2, dtype=np.float32) * 2.0 / HEAD_SIZE)).astype(np.float32)


def layer_kernel(
    tok, cot, pos, blk, gain_one, gain_two, wquery, wkey, wvalue, wo, wgate, wup, wdt,
    o_out, o_ing, o_gain_one, o_gain_two, o_q, o_k, o_v, o_o, o_gate, o_up, o_d,
    wqkv, gain, csf, b2, x2, gb, grow, wqz, woz, wq, wok, wg8, wd8, c8, n8, n1, qf, kvf, kv, q6, p6, o6, ab,
    mp, ml, mid, dmid, dmb, dm4, do6, act, pt, l1, s2, l2, l1o, s2o, l2o,
    ggu, lgu, lf, gdt, lgd, sgd, ld, loy, lo, lqy, lqx, lky, lkx, so, sq, sk, lzo, lzq, lzk, kvg, dkv, lx, sx, lkz,
    lg, sg, dqk, send_sems, recv_sems,
):
    net = Wires(send_sems, recv_sems)
    dp = lax.axis_index("dp")
    ctx = lax.axis_index("ctx")
    y, c = dp // 2, lax.rem(dp, 2)
    z, x = ctx // 2, lax.rem(ctx, 2)
    z_hi, z_lo = z // 2, lax.rem(z, 2)
    y_c = y + c - 2 * y * c
    tokens, width = tok.shape
    rows = wquery.shape[0]
    qcols = wo.shape[1]
    kcols = wkey.shape[1]
    ff = wdt.shape[1]
    drows = wdt.shape[0]
    qw = 2 * qcols
    kw = 2 * kcols
    groups = kw // HEAD_SIZE
    per = QUERY_HEADS // KEY_VALUE_HEADS
    heads = groups * per
    keys = kv.shape[1]
    n_ctx = keys // tokens
    scale = HEAD_SIZE ** (-0.5)

    def flip(a, h):
        return 1 - a if h else a

    def zat(k):
        return (z, 2 * z_hi + 1 - z_lo, 2 * (1 - z_hi) + z_lo, 3 - z)[k]

    def dev(yy, cc, zz, xx):
        return (2 * yy + cc, 2 * zz + xx)

    def off(value, step):
        return pl.multiple_of(value * step, step)

    partner = dev(y, 1 - c, z, x)
    middle = z_hi != z_lo

    wqkv[:, 0:qcols] = wquery[...]
    wqkv[:, qcols : qcols + kcols] = wkey[...]
    wqkv[:, qcols + kcols :] = wvalue[...]
    row = lax.broadcasted_iota(jnp.int32, gain.shape, 0)
    gain[...] = jnp.where(
        row == 0, gain_one[...].astype(F32).reshape(1, rows), jnp.where(row == 1, gain_two[...].astype(F32).reshape(1, rows), 1.0)
    )

    barrier = pltpu.get_barrier_semaphore()
    for k in range(4):
        for hx in range(2):
            for hy in range(2):
                for hc in range(2):
                    if k + hx + hy + hc:
                        pl.semaphore_signal(
                            barrier, inc=1,
                            device_id=dev(flip(y, hy), flip(c, hc), zat(k), flip(x, hx)),
                            device_id_type=MESH,
                        )
    pl.semaphore_wait(barrier, 31)

    r_tok = net.slots(3)
    net.send(tok, x2, r_tok, partner)
    r_g = net.slots(8)
    r_wqz, r_wq = net.slots(4), net.slots(16)

    def spread_qkv(k, src):
        zs = zat(k)
        for hx, hy in ((0, 0), (1, 0), (0, 1)):
            net.send(
                src,
                wq.at[c, pl.ds(off(2 * zs + x, rows), rows)],
                r_wq + k * 4 + hx * 2 + c,
                dev(flip(y, hy), y, z, flip(x, hx)),
                is_self=(c == y) if hx + hy == 0 else None,
            )

    def z_start(src, land, slot):
        for k in range(1, 4):
            net.send(src, land(k), slot + k, dev(y, c, zat(k), x), only=middle if k == 3 else None)

    def z_relay(here, there, slot):
        net.send(here, there, slot + 3, dev(y, c, zat(1), x), only=middle)

    z_start(wqkv, lambda k: wqz.at[k - 1], r_wqz)
    spread_qkv(0, wqkv)
    for k in range(4):
        for hx in range(2):
            if k + hx:
                net.send(gain, gb.at[ctx], r_g + 2 * k + hx, dev(y, c, zat(k), flip(x, hx)))

    across = lax.broadcasted_iota(jnp.int32, (tokens, 128), 1)
    entry = lax.rem(across, HEAD_SIZE // 2)
    frequency = jnp.zeros((tokens, 128), F32)
    for i in range(HEAD_SIZE // 2):
        frequency = jnp.where(entry == i, float(FREQUENCY[i]), frequency)
    places = jnp.broadcast_to(pos[...].astype(F32), (tokens, tokens)).T
    angles = places * frequency
    sine = jnp.sin(angles)
    csf[0:tokens, 0:128] = jnp.cos(angles)
    csf[0:tokens, 128:256] = jnp.where(lax.rem(across, HEAD_SIZE) < HEAD_SIZE // 2, -sine, sine)
    inverse = 1.0 / blk[0].astype(F32)
    key = lax.broadcasted_iota(jnp.int32, (8, keys), 1).astype(F32)
    own_block = jnp.floor(jnp.full((8, keys), ctx * tokens, jnp.int32).astype(F32) * inverse)
    b2[0] = jnp.where(jnp.floor(key * inverse) <= own_block, 0.0, VERY_NEGATIVE)
    net.send(csf.at[pl.ds(0, tokens)], csf.at[pl.ds(tokens, tokens)], r_tok + 1, partner)
    net.send(b2.at[0], b2.at[1], r_tok + 2, partner)
    gb[ctx] = gain[...]
    c8[0] = cot[...]

    def normed(values):
        v = values.astype(F32)
        inv = lax.rsqrt(jnp.mean(v * v, -1, keepdims=True) + EPSILON)
        return v * inv, inv

    def gather_x(buf, slot):
        net.send(buf.at[0], buf.at[4], slot + 2, dev(y, c, z, 1 - x))

    def gather_z(buf, slot):
        net.send(buf.at[0], buf.at[1], slot + 4, partner)
        net.send(buf.at[0], buf.at[2], slot + 1, dev(y, c, zat(1), x))

    def gather_pass(buf, slot, h):
        net.recv(buf.at[2 * h], slot + h)
        net.send(buf.at[2 * h], buf.at[2 * h + 1], slot + 4 + h, partner)
        if h == 1:
            net.send(buf.at[2], buf.at[6], slot + 3, dev(y, c, z, 1 - x))

    r_c8 = net.slots(8)
    for k in (1, 2, 3):
        net.recv(wqz.at[k - 1], r_wqz + k)
        if k == 2:
            z_relay(wqz.at[1], wqz.at[2], r_wqz)
        spread_qkv(k, wqz.at[k - 1])
    gather_x(c8, r_c8)

    r_woz, r_wo = net.slots(4), net.slots(16)

    def spread_wo(k, src):
        zs = zat(k)
        core = zs // 2
        for hx, hy in ((0, 0), (1, 0), (0, 1)):
            net.send(
                src,
                wok.at[dp, pl.ds(off(2 * lax.rem(zs, 2) + x, rows), rows)],
                r_wo + lax.rem(zs, 2) * 8 + hx * 4 + hy * 2 + c,
                dev(flip(y, hy), core, z, flip(x, hx)),
                is_self=(c == core) if hx + hy == 0 else None,
            )

    r_gu, r_wd, r_wy = net.slots(16), net.slots(2), net.slots(2)
    home = y_c == z_lo

    def send_ff(m):
        for zh in range(2):
            for hx in range(2):
                net.send(
                    (wgate, wup)[m].at[:, pl.ds(off(flip(x, hx), ff), ff)],
                    wg8.at[m, pl.ds(off(ctx, rows), rows)],
                    r_gu + m * 8 + ctx,
                    dev(y, c, 2 * zh + y_c, flip(x, hx)),
                    is_self=(z == 2 * zh + y_c) if hx == 0 else None,
                )

    ff_passed = []

    def pass_ff(m):
        for i in range(n_ctx):
            at = 2 * zat(i // 2) + flip(x, i % 2)
            part = wg8.at[m, pl.ds(off(at, rows), rows)]
            slot = r_gu + m * 8 + at

            @pl.when(home)
            def _():
                net.recv(part, slot)

            ff_passed.append(net.send(part, part, slot, dev(1 - y, c, z, x), only=home))

    def take_ff(m):
        for i in range(n_ctx):

            @pl.when(jnp.logical_not(home))
            def _():
                net.recv(wg8.at[m, pl.ds(rows * i, rows)], r_gu + m * 8 + i)

    def send_down():
        z_x = z_hi + z_lo - 2 * z_hi * z_lo
        for zh in range(2):
            net.send(
                wdt,
                wd8.at[pl.ds(off(dp, drows), drows)],
                r_wd + c,
                dev(y, z_lo, 2 * zh + z_x, x),
                is_self=jnp.logical_and(z == 2 * zh + z_x, c == z_lo),
            )

    z_start(wo, lambda k: woz.at[k - 1], r_woz)
    spread_wo(0, wo)
    send_ff(0)
    gather_z(c8, r_c8)

    for k in range(4):
        for hx in range(2):
            if k + hx:
                net.recv(gb.at[2 * zat(k) + flip(x, hx)], r_g + 2 * k + hx)
    for t in range(n_ctx):
        grow[:, rows * t : rows * (t + 1)] = gb[t]
    n1[0:tokens] = (normed(tok[...])[0] * grow[0:1]).astype(BF16)
    net.recv(x2, r_tok)
    n1[tokens : 2 * tokens] = (normed(x2[...])[0] * grow[0:1]).astype(BF16)
    net.recv(csf.at[pl.ds(tokens, tokens)], r_tok + 1)
    net.recv(b2.at[1], r_tok + 2)

    for k in range(4):
        at_x = pl.ds(off(2 * zat(k) + x, rows), rows)
        at_o = pl.ds(off(2 * zat(k) + 1 - x, rows), rows)
        slot = r_wq + k * 4

        @pl.when(c == y)
        def _():
            net.recv(wq.at[0, at_o], slot + 2)

        net.send(wq.at[0, at_o], wq.at[0, at_o], slot + 2, dev(1 - y, c, z, x), only=(c == y))

        @pl.when(c != y)
        def _():
            net.recv(wq.at[1, at_x], slot + 1)

        net.send(wq.at[1, at_x], wq.at[1, at_x], slot + 3, dev(y, c, z, 1 - x), only=(c != y))
    for k in range(1, 4):
        net.recv(woz.at[k - 1], r_woz + k)
        if k == 2:
            z_relay(woz.at[1], woz.at[2], r_woz)
        spread_wo(k, woz.at[k - 1])
    for k in range(4):
        at_x = pl.ds(off(2 * zat(k) + x, rows), rows)
        at_o = pl.ds(off(2 * zat(k) + 1 - x, rows), rows)
        slot = r_wq + k * 4

        @pl.when(c == y)
        def _():
            net.recv(wq.at[1, at_x], slot + 1)

        @pl.when(c != y)
        def _():
            net.recv(wq.at[0, at_o], slot + 2)

        net.recv(wq.at[0, at_x], slot)
        net.recv(wq.at[1, at_o], slot + 3)

    lane = lax.broadcasted_iota(jnp.int32, (2 * tokens, 128), 1)
    low_half = lax.rem(lane, HEAD_SIZE) < HEAD_SIZE // 2

    def turn(tile, forward):
        other = jnp.where(low_half, pltpu.roll(tile, 96, 1), pltpu.roll(tile, 32, 1))
        turned = other * csf[:, 128:256]
        return tile * csf[:, 0:128] + (turned if forward else -turned)

    qf[:, qw:] = jnp.zeros((2 * tokens, qf.shape[1] - qw), F32)
    for part in range(2):
        got = dot_nn(n1[...], wq[part])
        qf[:, qcols * part : qcols * (part + 1)] = got[:, :qcols]
        kvf[:, kcols * part : kcols * (part + 1)] = got[:, qcols : qcols + kcols]
        kvf[:, kw + kcols * part : kw + kcols * (part + 1)] = got[:, qcols + kcols :]

    def turn_keys(forward):
        for t in range(kw // 128 + 1):
            tile = kvf[:, 128 * t : 128 * (t + 1)]
            kvf[:, 128 * t : 128 * (t + 1)] = jnp.where(
                128 * t + lane < kw, turn(tile, forward), tile
            )

    turn_keys(True)
    own_keys = pl.ds(off(ctx, tokens), tokens)
    for s in range(2):
        kv[s, own_keys] = kvf[s * tokens : (s + 1) * tokens].astype(BF16)
    r_kz, r_kx = net.slots(8), net.slots(8)

    def kv_part(s, k, hx):
        return kv.at[s, pl.ds(off(2 * zat(k) + flip(x, hx), tokens), tokens)]

    for s in range(2):
        part = kv_part(s, 0, 0)
        z_start(part, lambda k: part, r_kz + 4 * s)
        net.send(part, part, r_kx + 4 * s, dev(y, c, z, 1 - x))

    def pass_kv(s, k):
        part = kv_part(s, k, 0)
        net.recv(part, r_kz + 4 * s + k)
        if k == 2:
            z_relay(part, part, r_kz + 4 * s)
        net.send(part, part, r_kx + 4 * s + k, dev(y, c, z, 1 - x))

    def take_kv(s):
        for k in range(4):
            net.recv(kv_part(s, k, 1), r_kx + 4 * s + k)

    send_ff(1)
    send_down()

    for t in range(qf.shape[1] // 128):
        qf[:, 128 * t : 128 * (t + 1)] = turn(qf[:, 128 * t : 128 * (t + 1)], True) * scale
    for s in range(2):
        for h in range(heads):
            q6[s * groups + h // per, (h % per) * tokens : (h % per + 1) * tokens] = qf[
                s * tokens : (s + 1) * tokens, HEAD_SIZE * h : HEAD_SIZE * (h + 1)
            ].astype(BF16)
    for k in range(1, 4):
        pass_kv(0, k)
    pass_kv(1, 1)
    pass_kv(1, 2)
    for zz in range(2):
        part = wok.at[2 * (1 - y), pl.ds(off(2 * zz + x, rows), rows)]
        net.recv(part, r_wo + zz * 8 + 2)
        net.send(part, part, r_wo + zz * 8 + 6, dev(y, c, z, 1 - x))
        part = wok.at[2 * y + 1, pl.ds(off(2 * zz + 1 - x, rows), rows)]
        net.recv(part, r_wo + zz * 8 + 5)
        net.send(part, part, r_wo + zz * 8 + 7, dev(1 - y, c, z, x))
    pass_ff(0)
    take_kv(0)

    def attend(s, g):
        kg = kv[s, :, HEAD_SIZE * g : HEAD_SIZE * (g + 1)]
        vg = kv[s, :, kw + HEAD_SIZE * g : kw + HEAD_SIZE * (g + 1)]
        scores = dot_nt(q6[s * groups + g], kg) + b2[s, 0:1, :]
        weights = jnp.exp(scores - jnp.max(scores, -1, keepdims=True))
        probs = (weights * (1.0 / jnp.sum(weights, -1, keepdims=True))).astype(BF16)
        p6[s * groups + g] = probs
        got = dot_nn(probs, vg).astype(BF16)
        o6[s * groups + g] = got
        for i in range(per):
            h = g * per + i
            ab[s * tokens : (s + 1) * tokens, HEAD_SIZE * h : HEAD_SIZE * (h + 1)] = got[
                i * tokens : (i + 1) * tokens
            ]

    attend(0, 0)
    pass_kv(1, 3)
    attend(0, 1)
    gather_pass(c8, r_c8, 1)
    attend(0, 2)
    take_kv(1)
    for g in range(groups):
        attend(1, g)

    for hx, hy, cc in ((0, 0, 0), (0, 0, 1), (0, 1, 1), (1, 0, 0), (1, 1, 0), (1, 1, 1)):
        for zz in range(2):
            net.recv(
                wok.at[2 * flip(y, hy) + cc, pl.ds(off(2 * zz + flip(x, hx), rows), rows)],
                r_wo + zz * 8 + hx * 4 + hy * 2 + cc,
            )
    for part in range(4):
        got = dot_nn(ab[:, 0:qw], wok[part])
        for s in range(2):
            mp[s, :, qcols * part : qcols * (part + 1)] = got[s * tokens : (s + 1) * tokens]
    r_ml = net.slots(1)
    mp_sent = net.send(mp.at[1], ml, r_ml, partner)
    pass_ff(1)
    for cc in range(2):
        part = wd8.at[pl.ds(off(2 * y + cc, drows), drows)]
        net.recv(part, r_wd + cc)
        net.send(part, part, r_wy + cc, dev(1 - y, c, z, x))
    gather_pass(c8, r_c8, 2)
    gather_pass(c8, r_c8, 3)
    net.recv(ml, r_ml)
    mid[...] = tok[...].astype(F32) + mp[0] + ml[...]
    n8[0] = (normed(mid[...])[0] * grow[1:2]).astype(BF16)
    r_n8 = net.slots(8)
    gather_z(n8, r_n8)
    gather_x(n8, r_n8)

    net.recv(c8.at[1], r_c8 + 4)
    for h in range(1, 4):
        net.recv(c8.at[2 * h + 1], r_c8 + 4 + h)
    take_ff(0)
    take_ff(1)
    for cc in range(2):
        net.recv(wd8.at[pl.ds(off(2 * (1 - y) + cc, drows), drows)], r_wy + cc)

    all_tokens = 8 * tokens

    def feed(i):
        pair = slice(2 * i, 2 * i + 2)
        here = n8[pair].reshape(2 * tokens, width)
        grad_inner = dot_nn(c8[pair].reshape(2 * tokens, width), wd8[...])
        gate = dot_nn(here, wg8[0])
        up = dot_nn(here, wg8[1])
        sig = 1.0 / (1.0 + jnp.exp(-gate))
        silu = gate * sig
        dgate = (grad_inner * up * sig * (1.0 + gate * (1.0 - sig))).astype(BF16)
        dup = (grad_inner * silu).astype(BF16)
        at = 2 * tokens * i
        act[at : at + 2 * tokens] = (silu * up).astype(BF16)
        act[at + all_tokens : at + all_tokens + 2 * tokens] = dgate
        act[at + 2 * all_tokens : at + 2 * all_tokens + 2 * tokens] = dup
        pt[pair] = (dot_nt(dgate, wg8[0]) + dot_nt(dup, wg8[1])).astype(BF16).reshape(2, tokens, width)

    def reduce_start(part, land, slot, h):
        return net.send(part.at[2 * h + 1], land.at[h], slot + h, partner)

    def reduce_pass(part, land, out, land2, slot, h):
        net.recv(land.at[h], slot + h)
        out[h - 1] = (part[2 * h].astype(F32) + land[h].astype(F32)).astype(BF16)
        net.send(
            out.at[h - 1], land2.at[h - 1], slot + 4 + h,
            dev(y, c, zat(h % 2), flip(x, h // 2)),
        )

    def reduce_own(part, land, slot):
        net.recv(land.at[0], slot)
        return part[0].astype(F32) + land[0].astype(F32)

    def reduce_end(land2, slot):
        total = 0.0
        for h in range(1, 4):
            net.recv(land2.at[h - 1], slot + 4 + h)
            total = total + land2[h - 1].astype(F32)
        return total

    r_dn = net.slots(8)
    pt_sent = []
    net.recv(n8.at[1], r_n8 + 4)
    for h in range(4):
        if h:
            gather_pass(n8, r_n8, h)
            net.recv(n8.at[2 * h + 1], r_n8 + 4 + h)
        feed(h)
        pt_sent.append(reduce_start(pt, l1, r_dn, h))
        if h > 1:
            reduce_pass(pt, l1, s2, l2, r_dn, h - 1)
    reduce_pass(pt, l1, s2, l2, r_dn, 3)
    dmid[...] = reduce_own(pt, l1, r_dn)

    def flat(ref, i):
        return ref[:, :, pl.ds(off(i, 128), 128)].reshape(all_tokens, 128)

    def grad_gu(i, carry):
        left = flat(n8, i)
        at = pl.ds(off(i, 128), 128)
        ggu[0, at] = dot_tn(left, act[pl.ds(all_tokens, all_tokens)]).astype(BF16)
        ggu[1, at] = dot_tn(left, act[pl.ds(2 * all_tokens, all_tokens)]).astype(BF16)
        return carry

    def grad_d(i, carry):
        gdt[pl.ds(off(i, 128), 128)] = dot_tn(flat(c8, i), act[pl.ds(0, all_tokens)]).astype(BF16)
        return carry

    def feed_out(i, carry):
        got = dot_nt(act[pl.ds(off(i, 2 * tokens), 2 * tokens)], wd8[...])
        pt[pl.ds(2 * i, 2)] = got.astype(BF16).reshape(2, tokens, width)
        return carry

    r_gd, r_gz = net.slots(1), net.slots(4)
    half = 2 * drows
    lax.fori_loop(0, width // 128, grad_d, 0)
    net.send(gdt.at[pl.ds(off(1 - y, half), half)], lgd, r_gd, dev(1 - y, c, z, x))
    lax.fori_loop(0, width // 128, grad_gu, 0)
    for zt in range(4):
        at = pl.ds(2 * rows * zt, 2 * rows)
        net.send(
            ggu.at[:, at], lgu.at[:, at], r_gz + zt, dev(1 - y, c, z, x),
            only=jnp.logical_not(home),
        )
    for finish in pt_sent:
        net.done(finish)
    lax.fori_loop(0, 4, feed_out, 0)
    r_out = net.slots(8)
    for h in range(4):
        reduce_start(pt, l1o, r_out, h)

    total = dmid[...] + reduce_end(l2, r_dn)
    normed_two, inv_two = normed(mid[...])
    total = total * grow[1:2]
    dmid[...] = cot[...].astype(F32) + inv_two * (
        total - normed_two * jnp.mean(total * normed_two, -1, keepdims=True)
    )
    dmb[0] = dmid[...].astype(BF16)
    r_dm = net.slots(1)
    net.send(dmb.at[0], dmb.at[1], r_dm, partner)

    r_ld = net.slots(2)
    net.recv(lgd, r_gd)
    sgd[...] = (gdt[pl.ds(off(y, half), half)].astype(F32) + lgd[...].astype(F32)).astype(BF16)
    gd_z = 2 * (z_lo + c - 2 * z_lo * c) + c
    for cc in range(2):
        net.send(
            sgd.at[pl.ds(cc * drows, drows)], ld.at[z_hi], r_ld + z_hi, dev(y, cc, gd_z, x),
            is_self=jnp.logical_and(z == gd_z, c == cc),
        )
    net.recv(dmb.at[1], r_dm)

    for part in range(4):
        for s in range(2):
            dm4[part, s * tokens : (s + 1) * tokens] = dmb[s, :, qcols * part : qcols * (part + 1)]
    dattn = dot_nt(dm4[0], wok[0])
    for part in range(1, 4):
        dattn = dattn + dot_nt(dm4[part], wok[part])
    qf[:, 0:qw] = dattn
    for s in range(2):
        for h in range(heads):
            do6[s * groups + h // per, (h % per) * tokens : (h % per + 1) * tokens] = qf[
                s * tokens : (s + 1) * tokens, HEAD_SIZE * h : HEAD_SIZE * (h + 1)
            ].astype(BF16)
    attn_all = ab[:, 0:qw]
    for part in range(4):
        act[qw * part : qw * (part + 1), 0:qcols] = dot_tn(attn_all, dm4[part]).astype(BF16)
    r_gy, r_go = net.slots(2), net.slots(8)
    for cc in range(2):
        net.send(
            act.at[pl.ds(off(2 * (1 - y) + cc, qw), qw)], loy.at[cc], r_gy + cc, dev(1 - y, c, z, x)
        )

    def pass_go():
        for cc in range(2):
            net.recv(loy.at[cc], r_gy + cc)
            at = pl.ds(off(2 * y + cc, qw), qw)
            act[at] = (act[at].astype(F32) + loy[cc].astype(F32)).astype(BF16)
        for hx in (1, 0):
            for hc in range(2):
                for zz in range(2):
                    at = pl.multiple_of((2 * y + flip(c, hc)) * qw + (2 * zz + flip(x, hx)) * rows, rows)
                    src = act.at[pl.ds(at, rows)]
                    dst = lo.at[2 * c + zz, hx]
                    slot = r_go + (2 * c + zz) * 2 + hx
                    if hx + hc == 0:
                        net.keep(src, dst, slot)
                    else:
                        net.send(src, dst, slot, dev(y, flip(c, hc), z, flip(x, hx)))

    def attend_back(s, g):
        at = s * groups + g
        kg = kv[s, :, HEAD_SIZE * g : HEAD_SIZE * (g + 1)]
        vg = kv[s, :, kw + HEAD_SIZE * g : kw + HEAD_SIZE * (g + 1)]
        dout = do6[at]
        delta = jnp.sum(dout.astype(F32) * o6[at].astype(F32), -1, keepdims=True)
        dprob = dot_nt(dout, vg)
        dscore = (p6[at].astype(F32) * (dprob - delta)).astype(BF16)
        dquery = dot_nn(dscore, kg) * scale
        dkeys = dot_tn(q6[at], dscore)
        dvals = dot_tn(dout, p6[at])
        for t in range(n_ctx):
            cols = slice(t * tokens, (t + 1) * tokens)
            dkv[t, s, HEAD_SIZE * g : HEAD_SIZE * (g + 1)] = dkeys[:, cols].astype(BF16)
            dkv[t, s, kw + HEAD_SIZE * g : kw + HEAD_SIZE * (g + 1)] = dvals[:, cols].astype(BF16)
        for i in range(per):
            h = g * per + i
            qf[s * tokens : (s + 1) * tokens, HEAD_SIZE * h : HEAD_SIZE * (h + 1)] = dquery[
                i * tokens : (i + 1) * tokens
            ]

    r_dx, r_dz = net.slots(8), net.slots(8)

    def send_dkv(s):
        for k in (1, 2, 3, 0):
            net.send(
                dkv.at[2 * zat(k) + 1 - x, s], lx.at[k, s], r_dx + 4 * s + k, dev(y, c, z, 1 - x)
            )

    def pass_dkv(s):
        for k in range(1, 4):
            net.recv(lx.at[k, s], r_dx + 4 * s + k)
            sx[k - 1, s] = (dkv[2 * zat(k) + x, s].astype(F32) + lx[k, s].astype(F32)).astype(BF16)
            net.send(sx.at[k - 1, s], lkz.at[k - 1, s], r_dz + 4 * s + k, dev(y, c, zat(k), x))

    for g in range(groups):
        attend_back(0, g)
    send_dkv(0)
    r_gf = net.slots(4)
    for k in (3, 2, 1, 0):
        at = pl.ds(off(zat(k), 2 * rows), 2 * rows)

        @pl.when(home)
        def _():
            net.recv(lgu.at[:, at], r_gz + zat(k))
            ggu[:, at] = (ggu[:, at].astype(F32) + lgu[:, at].astype(F32)).astype(BF16)

        for hx in range(2):
            src = ggu.at[:, pl.ds(off(2 * zat(k) + flip(x, hx), rows), rows)]
            dst = lf.at[x, z_hi]
            slot = r_gf + x * 2 + z_hi
            if k + hx:
                net.send(src, dst, slot, dev(y, c, zat(k), flip(x, hx)), only=home)
            else:

                @pl.when(home)
                def _():
                    net.keep(src, dst, slot)

    attend_back(1, 0)
    pass_go()
    attend_back(1, 1)
    pass_dkv(0)
    attend_back(1, 2)
    send_dkv(1)
    for t in range(qf.shape[1] // 128):
        qf[:, 128 * t : 128 * (t + 1)] = turn(qf[:, 128 * t : 128 * (t + 1)], False)
    grad = dot_tn(n1[...], qf[:, 0:qw].astype(BF16)).astype(BF16)
    for t in range(n_ctx):
        p6[t // 2, (t % 2) * rows : (t % 2 + 1) * rows, 0:qw] = grad[rows * t : rows * (t + 1)]
    for part in range(2):
        dqk[part, :, 0:qcols] = qf[:, qcols * part : qcols * (part + 1)].astype(BF16)
    r_qy, r_qx, r_zq = net.slots(4), net.slots(4), net.slots(4)
    mine = c == y

    def send_grads(source, land, slot):
        for k in range(4):
            net.send(
                source(zat(k), slice(0, 2)), land.at[zat(k)], slot + k, dev(1 - y, c, z, x),
                only=jnp.logical_not(mine),
            )

    def add_y(source, land, slot, land_x, slot_x):
        for k in range(4):

            @pl.when(mine)
            def _():
                net.recv(land.at[zat(k)], slot + k)
                here = source(zat(k), slice(0, 2))
                here[...] = (here[...].astype(F32) + land[zat(k)].astype(F32)).astype(BF16)

            net.send(
                source(zat(k), 1 - x), land_x.at[k], slot_x + k, dev(y, c, z, 1 - x), only=mine
            )

    def add_x(source, land_x, slot_x, staged, arrived, slot_z):
        wide_part = arrived.shape[2]
        for k in (1, 2, 3, 0):

            @pl.when(mine)
            def _():
                net.recv(land_x.at[k], slot_x + k)
                staged[k] = (source(zat(k), x)[...].astype(F32) + land_x[k].astype(F32)).astype(BF16)

            for cc in range(2):
                first = cc * (staged.shape[2] - wide_part)
                src = staged.at[k, :, pl.ds(first, wide_part)]
                if k:
                    net.send(src, arrived.at[k], slot_z + k, dev(y, cc, zat(k), x), only=mine)
                else:

                    @pl.when(jnp.logical_and(mine, c == cc))
                    def _():
                        net.keep(src, arrived.at[k], slot_z)

                    net.send(
                        src, arrived.at[k], slot_z, dev(y, cc, z, x),
                        only=jnp.logical_and(mine, c != cc),
                    )

    def add_z(out, arrived, slot_z, staged):
        total = 0.0
        for k in (1, 2, 3, 0):
            net.recv(arrived.at[k], slot_z + k)
            total = total + arrived[k].astype(F32)
        count = out.shape[1]
        skip = count - (staged.shape[2] - arrived.shape[2])
        out[...] = jnp.where(c == 0, total[:, 0:count], total[:, skip : skip + count])

    def in_p6(zt, xt):
        at = pl.ds(0, 2 * rows) if isinstance(xt, slice) else pl.ds(off(xt, rows), rows)
        return p6.at[zt, at, pl.ds(0, qf.shape[1])]

    def in_wg8(zt, xt):
        at = pl.ds(off(zt, 2 * rows), 2 * rows) if isinstance(xt, slice) else pl.ds(off(2 * zt + xt, rows), rows)
        return wg8.at[0, at]

    send_grads(in_p6, lqy, r_qy)
    pass_dkv(1)
    for h in range(1, 4):
        reduce_pass(pt, l1o, s2o, l2o, r_out, h)
    mid[...] = mid[...] + reduce_own(pt, l1o, r_out)

    def attn_pass(land, out, staged, arrived, send_slot, slot, absolute):
        for k in (1, 2, 3, 0):
            at = zat(k) if absolute else k
            part = 0.0
            for h in range(2):
                net.recv(land.at[at, h], slot + at * 2 + h)
                part = part + land[at, h, :, 0 : out.shape[1]].astype(F32)
            if k == 0:
                out[...] = part
            else:
                staged[k - 1] = part.astype(BF16)
                net.send(staged.at[k - 1], arrived.at[k - 1], send_slot + k, dev(y, c, zat(k), x))

    def attn_end(out, arrived, slot):
        for k in range(1, 4):
            net.recv(arrived.at[k - 1], slot + k)
            out[...] = out[...] + arrived[k - 1].astype(F32)

    r_zo = net.slots(4)
    attn_pass(lo, o_o, so, lzo, r_zo, r_go, True)
    add_y(in_p6, lqy, r_qy, lqx, r_qx)

    for s in range(2):
        net.recv(lx.at[0, s], r_dx + 4 * s)
        total = dkv[2 * z + x, s].astype(F32) + lx[0, s].astype(F32)
        for k in range(1, 4):
            net.recv(lkz.at[k - 1, s], r_dz + 4 * s + k)
            total = total + lkz[k - 1, s].astype(F32)
        kvf[s * tokens : (s + 1) * tokens] = total.T
    turn_keys(False)
    for part in range(2):
        dqk[part, :, qcols : qcols + kcols] = kvf[:, kcols * part : kcols * (part + 1)].astype(BF16)
        dqk[part, :, qcols + kcols :] = kvf[:, kw + kcols * part : kw + kcols * (part + 1)].astype(BF16)
    for finish in ff_passed:
        net.done(finish)
    for part in range(2):
        wg8[0, :, 2 * kcols * part : 2 * kcols * (part + 1)] = dot_tn(
            n1[...], dqk[part, :, qcols:]
        ).astype(BF16)
    r_ky, r_kx2, r_zk = net.slots(4), net.slots(4), net.slots(4)
    send_grads(in_wg8, lky, r_ky)
    net.done(mp_sent)
    got = dot_nt(dqk[0], wq[0]) + dot_nt(dqk[1], wq[1])
    for s in range(2):
        mp[s] = got[s * tokens : (s + 1) * tokens]
    r_dn1 = net.slots(1)
    net.send(mp.at[1], ml, r_dn1, partner)
    add_x(in_p6, lqx, r_qx, sq, lzq, r_zq)
    add_y(in_wg8, lky, r_ky, lkx, r_kx2)
    net.recv(ml, r_dn1)
    total = mp[0] + ml[...]
    normed_one, inv_one = normed(tok[...])
    total = total * grow[0:1]
    o_ing[...] = (
        dmid[...]
        + inv_one * (total - normed_one * jnp.mean(total * normed_one, -1, keepdims=True))
    ).astype(BF16)
    add_x(in_wg8, lkx, r_kx2, sk, lzk, r_zk)

    o_out[...] = (mid[...] + reduce_end(l2o, r_out)).astype(BF16)
    gains = [0.0, 0.0]
    for h in range(2):
        for zh in range(2):
            net.recv(lf.at[h, zh], r_gf + h * 2 + zh)
        for m in range(2):
            got = lf[h, 0, m].astype(F32) + lf[h, 1, m].astype(F32)
            cols = slice(h * ff, (h + 1) * ff)
            (o_gate, o_up)[m][:, cols] = got
            gains[1] = gains[1] + jnp.sum(
                got * (wgate, wup)[m][:, cols].astype(F32), 1, keepdims=True
            )
    for zh in range(2):
        net.recv(ld.at[zh], r_ld + zh)
    o_d[...] = ld[0].astype(F32) + ld[1].astype(F32)
    attn_end(o_o, lzo, r_zo)
    add_z(o_q, lzq, r_zq, sq)
    gains[0] = jnp.sum(o_q[...] * wqkv[:, 0:qcols].astype(F32), 1, keepdims=True)
    add_z(kvg, lzk, r_zk, sk)
    gains[0] = gains[0] + jnp.sum(kvg[...] * wqkv[:, qcols:].astype(F32), 1, keepdims=True)
    o_k[...] = kvg[:, 0:kcols]
    o_v[...] = kvg[:, kcols:]
    column = lax.broadcasted_iota(jnp.int32, (rows, 128), 1)
    both = jnp.where(column == 0, gains[0], jnp.where(column == 1, gains[1], 0.0))
    sg[...] = both.T[0:8]
    r_lg = net.slots(4)
    for h in range(1, 4):
        net.send(sg, lg.at[h - 1], r_lg + h, dev(flip(y, h // 2), flip(c, h % 2), z, x))
    total = sg[...]
    for h in range(1, 4):
        net.recv(lg.at[h - 1], r_lg + h)
        total = total + lg[h - 1]
    total = total / gain[...]
    o_gain_one[...] = total[0:1]
    o_gain_two[...] = total[1:2]
    net.drain()


def hand_over(*refs):
    count = len(refs) // 2
    copies = [pltpu.make_async_copy(refs[i], refs[count + i], refs[-1].at[i]) for i in range(count)]
    for copy in copies:
        copy.start()
    for copy in copies:
        copy.wait()


def run_layer(n_ctx, tok, cot, pos, blk, gain_one, gain_two, wquery, wkey, wvalue, wo, wgate, wup, wdt):
    tokens, width = tok.shape
    rows, qcols = wquery.shape
    packed = qcols + 2 * wkey.shape[1]
    drows, ff = wdt.shape
    keys = n_ctx * tokens
    qw = 2 * qcols
    kw = packed - qcols
    groups = kw // HEAD_SIZE
    per = QUERY_HEADS // KEY_VALUE_HEADS
    stack = per * tokens
    wide = -(-qw // 128) * 128
    out_shape = [
        jax.ShapeDtypeStruct((tokens, width), BF16),
        jax.ShapeDtypeStruct((tokens, width), BF16),
        jax.ShapeDtypeStruct((1, rows), F32),
        jax.ShapeDtypeStruct((1, rows), F32),
        jax.ShapeDtypeStruct((rows, qcols), F32),
        jax.ShapeDtypeStruct((rows, kw // 2), F32),
        jax.ShapeDtypeStruct((rows, kw // 2), F32),
        jax.ShapeDtypeStruct((rows, qcols), F32),
        jax.ShapeDtypeStruct((rows, 2 * ff), F32),
        jax.ShapeDtypeStruct((rows, 2 * ff), F32),
        jax.ShapeDtypeStruct((drows, ff), F32),
    ]

    def vm(*shape, dtype=BF16):
        return pltpu.VMEM(shape, dtype)

    scratch = [
        vm(rows, packed),
        vm(8, rows, dtype=F32),
        vm(2 * tokens, 256, dtype=F32),
        vm(2, 8, keys, dtype=F32),
        vm(tokens, width),
        vm(n_ctx, 8, rows, dtype=F32),
        vm(8, width, dtype=F32),
        vm(3, rows, packed),
        vm(3, rows, qcols),
        vm(2, width, packed),
        vm(4, 4 * rows, qcols),
        vm(2, width, ff),
        vm(width, ff),
        vm(8, tokens, width),
        vm(8, tokens, width),
        vm(2 * tokens, width),
        vm(2 * tokens, wide, dtype=F32),
        vm(2 * tokens, 2 * kw, dtype=F32),
        vm(2, keys, 2 * kw),
        vm(2 * groups, stack, HEAD_SIZE),
        vm(2 * groups, stack, keys),
        vm(2 * groups, stack, HEAD_SIZE),
        vm(2 * tokens, wide),
        vm(2, tokens, width, dtype=F32),
        vm(tokens, width, dtype=F32),
        vm(tokens, width, dtype=F32),
        vm(tokens, width, dtype=F32),
        vm(2, tokens, width),
        vm(4, 2 * tokens, qcols),
        vm(2 * groups, stack, HEAD_SIZE),
        vm(24 * tokens, ff),
        vm(8, tokens, width),
        vm(4, tokens, width),
        vm(3, tokens, width),
        vm(3, tokens, width),
        vm(4, tokens, width),
        vm(3, tokens, width),
        vm(3, tokens, width),
        vm(2, width, ff),
        vm(2, width, ff),
        vm(2, 2, 2, rows, ff),
        vm(width, ff),
        vm(2 * drows, ff),
        vm(2 * drows, ff),
        vm(2, drows, ff),
        vm(2, qw, ff),
        vm(4, 2, rows, ff),
        vm(4, 2 * rows, wide),
        vm(4, rows, wide),
        vm(4, 2 * rows, ff),
        vm(4, rows, ff),
        vm(3, rows, qcols),
        vm(4, rows, wide),
        vm(4, rows, ff),
        vm(3, rows, qcols),
        vm(4, rows, ff),
        vm(4, rows, 256),
        vm(rows, kw, dtype=F32),
        vm(n_ctx, 2, 2 * kw, tokens),
        vm(4, 2, 2 * kw, tokens),
        vm(3, 2, 2 * kw, tokens),
        vm(3, 2, 2 * kw, tokens),
        vm(3, 8, rows, dtype=F32),
        vm(8, rows, dtype=F32),
        vm(2, 2 * tokens, packed),
        pltpu.SemaphoreType.DMA((N_SEM,)),
        pltpu.SemaphoreType.DMA((N_SEM,)),
    ]
    inside = pl.BlockSpec(memory_space=pltpu.VMEM)
    outs = pl.pallas_call(
        layer_kernel,
        out_shape=out_shape,
        in_specs=[inside] * 3 + [pl.BlockSpec(memory_space=pltpu.SMEM)] + [inside] * 9,
        out_specs=[inside] * len(out_shape),
        scratch_shapes=scratch,
        compiler_params=pltpu.CompilerParams(
            collective_id=0, has_side_effects=True, vmem_limit_bytes=VMEM_LIMIT
        ),
        name="layer",
    )(tok, cot, pos, blk, gain_one, gain_two, wquery, wkey, wvalue, wo, wgate, wup, wdt)
    anywhere = pl.BlockSpec(memory_space=pl.ANY)
    return pl.pallas_call(
        hand_over,
        out_shape=out_shape,
        in_specs=[inside] * len(out_shape),
        out_specs=[anywhere] * len(out_shape),
        scratch_shapes=[pltpu.SemaphoreType.DMA((len(out_shape),))],
        name="hand_over",
    )(*outs)


VMEM_LIMIT = 63 * 1024 * 1024


def on_device_plane(
    tokens, positions, block_sizes, attn_gain, w_query, w_key, w_value, w_out, mlp_gain,
    w_gate, w_up, w_down, cotangent,
):
    output, input_grad, g_one, g_two, g_q, g_k, g_v, g_o, g_gate, g_up, g_d = run_layer(
        lax.axis_size("ctx"), tokens[0], cotangent[0], positions, block_sizes, attn_gain,
        mlp_gain, w_query, w_key, w_value, w_out, w_gate, w_up, w_down.T,
    )
    return (
        output[None],
        input_grad[None],
        g_one[0],
        g_q,
        g_k,
        g_v,
        g_o,
        g_two[0],
        g_gate,
        g_up,
        g_d.T,
    )


def solution(mesh):
    placed = (
        P("dp", "ctx", None),
        P("dp", "ctx"),
        P("dp"),
        P("ctx"),
        P("ctx", "dp"),
        P("ctx", "dp"),
        P("ctx", "dp"),
        P("ctx", "dp"),
        P("ctx"),
        P("ctx", "dp"),
        P("ctx", "dp"),
        P("ctx", "dp"),
        P("dp", "ctx", None),
    )
    fits = mesh.shape["dp"] == 4 and mesh.shape["ctx"] == 8
    return jax.shard_map(
        on_device_plane if fits else on_device,
        mesh=mesh,
        in_specs=placed,
        out_specs=(
            P("dp", "ctx", None),
            P("dp", "ctx", None),
            P("ctx"),
            P("ctx", "dp"),
            P("ctx", "dp"),
            P("ctx", "dp"),
            P("ctx", "dp"),
            P("ctx"),
            P("ctx", "dp"),
            P("ctx", "dp"),
            P("ctx", "dp"),
        ),
        check_vma=False,
    )
```

```python
import jax
import jax.numpy as jnp
import numpy as np
from jax import lax
from jax.experimental import pallas as pl
from jax.experimental.pallas import tpu as pltpu
from jax.sharding import PartitionSpec as P

QUERY_HEADS = 18
KEY_VALUE_HEADS = 6
HEAD_SIZE = 64


EPSILON = 1e-05
THETA = 10000.0
VERY_NEGATIVE = -1e30


def product(left, right):
    return jnp.dot(left, right, preferred_element_type=jnp.float32)


def angles_of(place_ids):
    half_dim = HEAD_SIZE // 2
    frequency = THETA ** (-(jnp.arange(half_dim, dtype=jnp.float32) * 2.0 / HEAD_SIZE))
    return place_ids.astype(jnp.float32)[:, None] * frequency[None, :]


def rotate(values, angles, forward):
    row_total = values.shape[0]
    half_dim = angles.shape[1]
    shaped = values.reshape(row_total, -1, 2 * half_dim)
    first_half = shaped[..., :half_dim]
    second = shaped[..., half_dim:]
    cosine = jnp.cos(angles)[:, None, :]
    sine_vals = jnp.sin(angles)[:, None, :]
    if forward:
        rotated = jnp.concatenate(
            [first_half * cosine - second * sine_vals, second * cosine + first_half * sine_vals], -1
        )
    else:
        rotated = jnp.concatenate(
            [first_half * cosine + second * sine_vals, second * cosine - first_half * sine_vals], -1
        )
    return rotated.reshape(row_total, -1)


def norm_back(grad_normed, normed, inverse):
    return inverse * (grad_normed - normed * jnp.mean(grad_normed * normed, -1, keepdims=True))


def visible(query_rows, key_rows, block_len):
    return ((key_rows // block_len)[None, :] <= (query_rows // block_len)[:, None])[None, None]


def attend_forward(query_rows4, complete_keys, complete_values, query_rows, block_len, score_scale):
    key_count = complete_keys.shape[0]
    key_row_width = 512
    block_list = key_count // key_row_width
    query_group_width = QUERY_HEADS // KEY_VALUE_HEADS
    row_total = query_rows4.shape[0]
    key_block_list = complete_keys.reshape(block_list, key_row_width, KEY_VALUE_HEADS, HEAD_SIZE)
    value_block_list = complete_values.reshape(
        block_list, key_row_width, KEY_VALUE_HEADS, HEAD_SIZE
    )
    last_block = query_rows[-1] // block_len

    def advance(carried, inputs):
        key_blk, val_blk, first_key = inputs
        key_rows = first_key + jnp.arange(key_row_width, dtype=jnp.int32)

        def compute(current):
            run_max, run_sum, accum = current
            scores = (
                jnp.einsum(
                    "tkgd,nkd->kgtn", query_rows4, key_blk, preferred_element_type=jnp.float32
                )
                * score_scale
            )
            allowed = visible(query_rows, key_rows, block_len)
            scores = jnp.where(allowed, scores, VERY_NEGATIVE)
            new_max = jnp.maximum(run_max, jnp.max(scores, -1))
            weights = jnp.where(allowed, jnp.exp(scores - new_max[..., None]), 0.0)
            factor = jnp.exp(run_max - new_max)
            new_sum = run_sum * factor + jnp.sum(weights, -1)
            accum = accum * factor[..., None] + jnp.einsum(
                "kgtn,nkd->kgtd",
                weights.astype(jnp.bfloat16),
                val_blk,
                preferred_element_type=jnp.float32,
            )
            return (new_max, new_sum, accum)

        return (
            lax.cond(
                first_key // block_len > last_block, lambda unchanged: unchanged, compute, carried
            ),
            None,
        )

    start_state = (
        jnp.full((KEY_VALUE_HEADS, query_group_width, row_total), VERY_NEGATIVE, jnp.float32),
        jnp.zeros((KEY_VALUE_HEADS, query_group_width, row_total), jnp.float32),
        jnp.zeros((KEY_VALUE_HEADS, query_group_width, row_total, HEAD_SIZE), jnp.float32),
    )
    firsts = jnp.arange(block_list, dtype=jnp.int32) * key_row_width
    final_state, unused = lax.scan(advance, start_state, (key_block_list, value_block_list, firsts))
    run_max, run_sum, accum = final_state
    return (accum / run_sum[..., None], run_max + jnp.log(run_sum))


def attend_backward(
    query_rows4,
    head_gradients,
    log_sums,
    row_delta,
    complete_keys,
    complete_values,
    query_rows,
    block_len,
    score_scale,
):
    key_count = complete_keys.shape[0]
    key_row_width = 512
    block_list = key_count // key_row_width
    query_group_width = QUERY_HEADS // KEY_VALUE_HEADS
    row_total = query_rows4.shape[0]
    key_block_list = complete_keys.reshape(block_list, key_row_width, KEY_VALUE_HEADS, HEAD_SIZE)
    value_block_list = complete_values.reshape(
        block_list, key_row_width, KEY_VALUE_HEADS, HEAD_SIZE
    )
    last_block = query_rows[-1] // block_len

    def advance(grad_query, inputs):
        key_blk, val_blk, first_key = inputs
        key_rows = first_key + jnp.arange(key_row_width, dtype=jnp.int32)

        def compute(current):
            scores = (
                jnp.einsum(
                    "tkgd,nkd->kgtn", query_rows4, key_blk, preferred_element_type=jnp.float32
                )
                * score_scale
            )
            allowed = visible(query_rows, key_rows, block_len)
            prob_vals = jnp.where(allowed, jnp.exp(scores - log_sums[..., None]), 0.0)
            grad_prob = jnp.einsum(
                "tkgd,nkd->kgtn", head_gradients, val_blk, preferred_element_type=jnp.float32
            )
            grad_score = (prob_vals * (grad_prob - row_delta[..., None])).astype(jnp.bfloat16)
            current = current + jnp.einsum(
                "kgtn,nkd->tkgd", grad_score, key_blk, preferred_element_type=jnp.float32
            )
            grad_key = jnp.einsum(
                "kgtn,tkgd->nkd", grad_score, query_rows4, preferred_element_type=jnp.float32
            )
            grad_value = jnp.einsum(
                "kgtn,tkgd->nkd",
                prob_vals.astype(jnp.bfloat16),
                head_gradients,
                preferred_element_type=jnp.float32,
            )
            return (current, (grad_key, grad_value))

        def nothing(current):
            empty_block = jnp.zeros((key_row_width, KEY_VALUE_HEADS, HEAD_SIZE), jnp.float32)
            return (current, (empty_block, empty_block))

        return lax.cond(first_key // block_len > last_block, nothing, compute, grad_query)

    firsts = jnp.arange(block_list, dtype=jnp.int32) * key_row_width
    initial_gradient = jnp.zeros(
        (row_total, KEY_VALUE_HEADS, query_group_width, HEAD_SIZE), jnp.float32
    )
    grad_query, stacked_rows = lax.scan(
        advance, initial_gradient, (key_block_list, value_block_list, firsts)
    )
    key_gradients = stacked_rows[0].reshape(key_count, KEY_VALUE_HEADS * HEAD_SIZE)
    value_gradients = stacked_rows[1].reshape(key_count, KEY_VALUE_HEADS * HEAD_SIZE)
    return (grad_query, key_gradients, value_gradients)


def on_device(
    tokens,
    positions,
    block_sizes,
    attn_gain,
    w_query,
    w_key,
    w_value,
    w_out,
    mlp_gain,
    w_gate,
    w_up,
    w_down,
    cotangent,
):
    row_parts = (
        lax.all_gather(w_query, "ctx", axis=0, tiled=True),
        lax.all_gather(w_key, "ctx", axis=0, tiled=True),
        lax.all_gather(w_value, "ctx", axis=0, tiled=True),
        lax.all_gather(w_out, "ctx", axis=0, tiled=True),
        lax.all_gather(w_gate, "ctx", axis=0, tiled=True),
        lax.all_gather(w_up, "ctx", axis=0, tiled=True),
        lax.all_gather(w_down, "ctx", axis=0, tiled=True),
        lax.all_gather(attn_gain, "ctx", axis=0, tiled=True),
        lax.all_gather(mlp_gain, "ctx", axis=0, tiled=True),
    )
    whole_w = (
        lax.all_gather(row_parts[0], "dp", axis=1, tiled=True),
        lax.all_gather(row_parts[1], "dp", axis=1, tiled=True),
        lax.all_gather(row_parts[2], "dp", axis=1, tiled=True),
        lax.all_gather(row_parts[3], "dp", axis=1, tiled=True),
        lax.all_gather(row_parts[4], "dp", axis=1, tiled=True),
        lax.all_gather(row_parts[5], "dp", axis=1, tiled=True),
        lax.all_gather(row_parts[6], "dp", axis=1, tiled=True),
    )
    query_w, key_w, value_w, out_w, gate_w, up_w, down_w = whole_w
    gain_one = row_parts[7].astype(jnp.float32)
    gain_two = row_parts[8].astype(jnp.float32)
    seq_count = tokens.shape[0]
    seq_rows = tokens.shape[1]
    width = tokens.shape[2]
    inputs = tokens.reshape(seq_count * seq_rows, width).astype(jnp.float32)
    row_total = inputs.shape[0]
    query_group_width = QUERY_HEADS // KEY_VALUE_HEADS
    query_rows = lax.axis_index("ctx") * seq_rows + jnp.arange(seq_rows, dtype=jnp.int32)
    angles = angles_of(positions.reshape(-1))
    score_scale = HEAD_SIZE ** (-0.5)
    inv_one = lax.rsqrt(jnp.mean(inputs * inputs, -1, keepdims=True) + EPSILON)
    normed_one = inputs * inv_one
    hidden_one = (normed_one * gain_one).astype(jnp.bfloat16)
    query_matrix = rotate(product(hidden_one, query_w), angles, True).astype(jnp.bfloat16)
    keys_own = rotate(product(hidden_one, key_w), angles, True).astype(jnp.bfloat16)
    values_own = product(hidden_one, value_w).astype(jnp.bfloat16)
    complete_keys, complete_values = (
        lax.all_gather(keys_own.reshape(seq_count, seq_rows, -1), "ctx", axis=1, tiled=True),
        lax.all_gather(values_own.reshape(seq_count, seq_rows, -1), "ctx", axis=1, tiled=True),
    )
    query_rows4 = query_matrix.reshape(row_total, KEY_VALUE_HEADS, query_group_width, HEAD_SIZE)
    member = 0
    heads_one, lse_one = attend_forward(
        query_rows4,
        complete_keys[member],
        complete_values[member],
        query_rows,
        block_sizes[member],
        score_scale,
    )
    attn_flat = heads_one.transpose(2, 0, 1, 3).reshape(row_total, QUERY_HEADS * HEAD_SIZE)
    attn_low = attn_flat.astype(jnp.bfloat16)
    mixed_rows = inputs + product(attn_low, out_w)
    inv_two = lax.rsqrt(jnp.mean(mixed_rows * mixed_rows, -1, keepdims=True) + EPSILON)
    normed_two = mixed_rows * inv_two
    hidden_two = (normed_two * gain_two).astype(jnp.bfloat16)
    gate_pre = product(hidden_two, gate_w)
    up_pre = product(hidden_two, up_w)
    sigmoid_gate = jax.nn.sigmoid(gate_pre)
    silu_gate = gate_pre * sigmoid_gate
    inner_act = (silu_gate * up_pre).astype(jnp.bfloat16)
    result = mixed_rows + product(inner_act, down_w)
    output = result.astype(jnp.bfloat16).reshape(seq_count, seq_rows, width)
    back_parts = (
        lax.all_gather(w_query, "ctx", axis=0, tiled=True),
        lax.all_gather(w_key, "ctx", axis=0, tiled=True),
        lax.all_gather(w_value, "ctx", axis=0, tiled=True),
        lax.all_gather(w_out, "ctx", axis=0, tiled=True),
        lax.all_gather(w_gate, "ctx", axis=0, tiled=True),
        lax.all_gather(w_up, "ctx", axis=0, tiled=True),
        lax.all_gather(w_down, "ctx", axis=0, tiled=True),
    )
    back_whole = (
        lax.all_gather(back_parts[0], "dp", axis=1, tiled=True),
        lax.all_gather(back_parts[1], "dp", axis=1, tiled=True),
        lax.all_gather(back_parts[2], "dp", axis=1, tiled=True),
        lax.all_gather(back_parts[3], "dp", axis=1, tiled=True),
        lax.all_gather(back_parts[4], "dp", axis=1, tiled=True),
        lax.all_gather(back_parts[5], "dp", axis=1, tiled=True),
        lax.all_gather(back_parts[6], "dp", axis=1, tiled=True),
    )
    back_query, back_key, back_value, back_out, back_gate, back_up, back_down = back_whole
    grad_top = cotangent.reshape(row_total, width)
    grad_down = jnp.einsum("tf,td->fd", inner_act, grad_top, preferred_element_type=jnp.float32)
    grad_inner = jnp.einsum("td,fd->tf", grad_top, back_down, preferred_element_type=jnp.float32)
    grad_gate = (
        grad_inner * up_pre * sigmoid_gate * (1.0 + gate_pre * (1.0 - sigmoid_gate))
    ).astype(jnp.bfloat16)
    grad_upval = (grad_inner * silu_gate).astype(jnp.bfloat16)
    grad_gatew = jnp.einsum("td,tf->df", hidden_two, grad_gate, preferred_element_type=jnp.float32)
    grad_upw = jnp.einsum("td,tf->df", hidden_two, grad_upval, preferred_element_type=jnp.float32)
    grad_hidden_two = jnp.einsum(
        "tf,df->td", grad_gate, back_gate, preferred_element_type=jnp.float32
    ) + jnp.einsum("tf,df->td", grad_upval, back_up, preferred_element_type=jnp.float32)
    grad_gain_two = jnp.sum(grad_hidden_two * normed_two, 0)
    grad_mixed = grad_top.astype(jnp.float32) + norm_back(
        grad_hidden_two * gain_two, normed_two, inv_two
    )
    grad_branch = grad_mixed.astype(jnp.bfloat16)
    grad_outw = jnp.einsum("tq,td->qd", attn_low, grad_branch, preferred_element_type=jnp.float32)
    attention_gradient = jnp.einsum(
        "td,qd->tq", grad_branch, back_out, preferred_element_type=jnp.float32
    ).astype(jnp.bfloat16)
    head_gradients = attention_gradient.reshape(
        row_total, KEY_VALUE_HEADS, query_group_width, HEAD_SIZE
    )
    row_delta = jnp.einsum("tkgd,kgtd->kgt", head_gradients.astype(jnp.float32), heads_one)
    member = 0
    grad_q_one, grad_k_one, grad_v_one = attend_backward(
        query_rows4,
        head_gradients,
        lse_one,
        row_delta,
        complete_keys[member],
        complete_values[member],
        query_rows,
        block_sizes[member],
        score_scale,
    )
    key_grads = [grad_k_one]
    value_grads = [grad_v_one]
    grad_keys_all = jnp.stack(key_grads, 0)
    grad_values_all = jnp.stack(value_grads, 0)
    grad_keys_own, grad_values_own = (
        lax.psum_scatter(grad_keys_all, "ctx", scatter_dimension=1, tiled=True),
        lax.psum_scatter(grad_values_all, "ctx", scatter_dimension=1, tiled=True),
    )
    grad_keys_own = grad_keys_own.reshape(row_total, -1)
    grad_values_own = grad_values_own.reshape(row_total, -1)
    grad_query_raw = rotate(
        grad_q_one.reshape(row_total, QUERY_HEADS * HEAD_SIZE) * score_scale, angles, False
    ).astype(jnp.bfloat16)
    grad_key_raw = rotate(grad_keys_own * score_scale, angles, False).astype(jnp.bfloat16)
    grad_value_raw = grad_values_own.astype(jnp.bfloat16)
    grad_queryw = jnp.einsum(
        "td,tq->dq", hidden_one, grad_query_raw, preferred_element_type=jnp.float32
    )
    grad_keyw = jnp.einsum(
        "td,tq->dq", hidden_one, grad_key_raw, preferred_element_type=jnp.float32
    )
    grad_valuew = jnp.einsum(
        "td,tq->dq", hidden_one, grad_value_raw, preferred_element_type=jnp.float32
    )
    grad_hidden_one = jnp.einsum(
        "tq,dq->td", grad_query_raw, back_query, preferred_element_type=jnp.float32
    )
    grad_hidden_one = grad_hidden_one + jnp.einsum(
        "tq,dq->td", grad_key_raw, back_key, preferred_element_type=jnp.float32
    )
    grad_hidden_one = grad_hidden_one + jnp.einsum(
        "tq,dq->td", grad_value_raw, back_value, preferred_element_type=jnp.float32
    )
    grad_gain_one = jnp.sum(grad_hidden_one * normed_one, 0)
    grad_input = grad_mixed + norm_back(grad_hidden_one * gain_one, normed_one, inv_one)
    input_grad = grad_input.astype(jnp.bfloat16).reshape(seq_count, seq_rows, width)
    summed_rows = (
        lax.psum_scatter(grad_queryw, "ctx", scatter_dimension=0, tiled=True),
        lax.psum_scatter(grad_keyw, "ctx", scatter_dimension=0, tiled=True),
        lax.psum_scatter(grad_valuew, "ctx", scatter_dimension=0, tiled=True),
        lax.psum_scatter(grad_outw, "ctx", scatter_dimension=0, tiled=True),
        lax.psum_scatter(grad_gatew, "ctx", scatter_dimension=0, tiled=True),
        lax.psum_scatter(grad_upw, "ctx", scatter_dimension=0, tiled=True),
        lax.psum_scatter(grad_down, "ctx", scatter_dimension=0, tiled=True),
        lax.psum_scatter(grad_gain_one, "ctx", scatter_dimension=0, tiled=True),
        lax.psum_scatter(grad_gain_two, "ctx", scatter_dimension=0, tiled=True),
    )
    final_w = (
        lax.psum_scatter(
            summed_rows[0].astype(jnp.bfloat16), "dp", scatter_dimension=1, tiled=True
        ).astype(jnp.float32),
        lax.psum_scatter(
            summed_rows[1].astype(jnp.bfloat16), "dp", scatter_dimension=1, tiled=True
        ).astype(jnp.float32),
        lax.psum_scatter(
            summed_rows[2].astype(jnp.bfloat16), "dp", scatter_dimension=1, tiled=True
        ).astype(jnp.float32),
        lax.psum_scatter(
            summed_rows[3].astype(jnp.bfloat16), "dp", scatter_dimension=1, tiled=True
        ).astype(jnp.float32),
        lax.psum_scatter(
            summed_rows[4].astype(jnp.bfloat16), "dp", scatter_dimension=1, tiled=True
        ).astype(jnp.float32),
        lax.psum_scatter(
            summed_rows[5].astype(jnp.bfloat16), "dp", scatter_dimension=1, tiled=True
        ).astype(jnp.float32),
        lax.psum_scatter(
            summed_rows[6].astype(jnp.bfloat16), "dp", scatter_dimension=1, tiled=True
        ).astype(jnp.float32),
    )
    final_gains = lax.psum((summed_rows[7], summed_rows[8]), "dp")
    return (
        output,
        input_grad,
        final_gains[0],
        final_w[0],
        final_w[1],
        final_w[2],
        final_w[3],
        final_gains[1],
        final_w[4],
        final_w[5],
        final_w[6],
    )


MESH = pl.DeviceIdType.MESH
F32 = jnp.float32
BF16 = jnp.bfloat16


def dot_nn(a, b):
    return lax.dot_general(a, b, (((1,), (0,)), ((), ())), preferred_element_type=F32)


def dot_nt(a, b):
    return lax.dot_general(a, b, (((1,), (1,)), ((), ())), preferred_element_type=F32)


def dot_tn(a, b):
    return lax.dot_general(a, b, (((0,), (0,)), ((), ())), preferred_element_type=F32)


class Wires:
    def __init__(self, send_sems, recv_sems):
        self.send_sems, self.recv_sems = send_sems, recv_sems
        self.sends = 0
        self.recvs = 0
        self.pending = []

    def slots(self, count):
        first = self.recvs
        self.recvs += count
        return first

    def send(self, src, dst, slot, device, is_self=None, only=None):
        mine = self.sends
        self.sends += 1
        remote = pltpu.make_async_remote_copy(
            src_ref=src,
            dst_ref=dst,
            send_sem=self.send_sems.at[mine],
            recv_sem=self.recv_sems.at[slot],
            device_id=device,
            device_id_type=MESH,
        )
        if only is not None:

            @pl.when(only)
            def _():
                remote.start()

            def finish():
                @pl.when(only)
                def _():
                    remote.wait_send()

        elif is_self is None:
            remote.start()
            finish = remote.wait_send
        else:
            local = pltpu.make_async_copy(src, dst, self.recv_sems.at[slot])

            @pl.when(is_self)
            def _():
                local.start()

            @pl.when(jnp.logical_not(is_self))
            def _():
                remote.start()

            def finish():
                @pl.when(jnp.logical_not(is_self))
                def _():
                    remote.wait_send()

        self.pending.append(finish)
        return finish

    def keep(self, src, dst, slot):
        pltpu.make_async_copy(src, dst, self.recv_sems.at[slot]).start()

    def recv(self, dst, slot):
        pltpu.make_async_copy(dst, dst, self.recv_sems.at[slot]).wait()

    def done(self, finish):
        finish()
        self.pending.remove(finish)

    def drain(self):
        for finish in self.pending:
            finish()
        self.pending = []


N_SEM = 288
FREQUENCY = np.float32(THETA) ** (-(np.arange(HEAD_SIZE // 2, dtype=np.float32) * 2.0 / HEAD_SIZE)).astype(np.float32)


def layer_kernel(
    tok, cot, pos, blk, gain_one, gain_two, wquery, wkey, wvalue, wo, wgate, wup, wdt,
    o_out, o_ing, o_gain_one, o_gain_two, o_q, o_k, o_v, o_o, o_gate, o_up, o_d,
    wqkv, gain, csf, b2, x2, gb, grow, wqz, woz, wq, wok, wg8, wd8, c8, n8, n1, qf, kvf, kv, q6, p6, o6, ab,
    mp, ml, mid, dmid, dmb, dm4, do6, act, pt, l1, s2, l2, l1o, s2o, l2o,
    ggu, lgu, lf, gdt, lgd, sgd, ld, loy, lo, lqy, lqx, lky, lkx, so, sq, sk, lzo, lzq, lzk, kvg, dkv, lx, sx, lkz,
    lg, sg, dqk, send_sems, recv_sems,
):
    net = Wires(send_sems, recv_sems)
    dp = lax.axis_index("dp")
    ctx = lax.axis_index("ctx")
    y, c = dp // 2, lax.rem(dp, 2)
    z, x = ctx // 2, lax.rem(ctx, 2)
    z_hi, z_lo = z // 2, lax.rem(z, 2)
    y_c = y + c - 2 * y * c
    tokens, width = tok.shape
    rows = wquery.shape[0]
    qcols = wo.shape[1]
    kcols = wkey.shape[1]
    ff = wdt.shape[1]
    drows = wdt.shape[0]
    qw = 2 * qcols
    kw = 2 * kcols
    groups = kw // HEAD_SIZE
    per = QUERY_HEADS // KEY_VALUE_HEADS
    heads = groups * per
    keys = kv.shape[1]
    n_ctx = keys // tokens
    scale = HEAD_SIZE ** (-0.5)

    def flip(a, h):
        return 1 - a if h else a

    def zat(k):
        return (z, 2 * z_hi + 1 - z_lo, 2 * (1 - z_hi) + z_lo, 3 - z)[k]

    def dev(yy, cc, zz, xx):
        return (2 * yy + cc, 2 * zz + xx)

    def off(value, step):
        return pl.multiple_of(value * step, step)

    partner = dev(y, 1 - c, z, x)
    middle = z_hi != z_lo

    wqkv[:, 0:qcols] = wquery[...]
    wqkv[:, qcols : qcols + kcols] = wkey[...]
    wqkv[:, qcols + kcols :] = wvalue[...]
    row = lax.broadcasted_iota(jnp.int32, gain.shape, 0)
    gain[...] = jnp.where(
        row == 0, gain_one[...].astype(F32).reshape(1, rows), jnp.where(row == 1, gain_two[...].astype(F32).reshape(1, rows), 1.0)
    )

    barrier = pltpu.get_barrier_semaphore()
    for k in range(4):
        for hx in range(2):
            for hy in range(2):
                for hc in range(2):
                    if k + hx + hy + hc:
                        pl.semaphore_signal(
                            barrier, inc=1,
                            device_id=dev(flip(y, hy), flip(c, hc), zat(k), flip(x, hx)),
                            device_id_type=MESH,
                        )
    pl.semaphore_wait(barrier, 31)

    r_tok = net.slots(3)
    net.send(tok, x2, r_tok, partner)
    r_g = net.slots(8)
    r_wqz, r_wq = net.slots(4), net.slots(16)

    def spread_qkv(k, src):
        zs = zat(k)
        for hx, hy in ((0, 0), (1, 0), (0, 1)):
            net.send(
                src,
                wq.at[c, pl.ds(off(2 * zs + x, rows), rows)],
                r_wq + k * 4 + hx * 2 + c,
                dev(flip(y, hy), y, z, flip(x, hx)),
                is_self=(c == y) if hx + hy == 0 else None,
            )

    def z_start(src, land, slot):
        for k in range(1, 4):
            net.send(src, land(k), slot + k, dev(y, c, zat(k), x), only=middle if k == 3 else None)

    def z_relay(here, there, slot):
        net.send(here, there, slot + 3, dev(y, c, zat(1), x), only=middle)

    z_start(wqkv, lambda k: wqz.at[k - 1], r_wqz)
    spread_qkv(0, wqkv)
    for k in range(4):
        for hx in range(2):
            if k + hx:
                net.send(gain, gb.at[ctx], r_g + 2 * k + hx, dev(y, c, zat(k), flip(x, hx)))

    across = lax.broadcasted_iota(jnp.int32, (tokens, 128), 1)
    entry = lax.rem(across, HEAD_SIZE // 2)
    frequency = jnp.zeros((tokens, 128), F32)
    for i in range(HEAD_SIZE // 2):
        frequency = jnp.where(entry == i, float(FREQUENCY[i]), frequency)
    places = jnp.broadcast_to(pos[...].astype(F32), (tokens, tokens)).T
    angles = places * frequency
    sine = jnp.sin(angles)
    csf[0:tokens, 0:128] = jnp.cos(angles)
    csf[0:tokens, 128:256] = jnp.where(lax.rem(across, HEAD_SIZE) < HEAD_SIZE // 2, -sine, sine)
    inverse = 1.0 / blk[0].astype(F32)
    key = lax.broadcasted_iota(jnp.int32, (8, keys), 1).astype(F32)
    own_block = jnp.floor(jnp.full((8, keys), ctx * tokens, jnp.int32).astype(F32) * inverse)
    b2[0] = jnp.where(jnp.floor(key * inverse) <= own_block, 0.0, VERY_NEGATIVE)
    net.send(csf.at[pl.ds(0, tokens)], csf.at[pl.ds(tokens, tokens)], r_tok + 1, partner)
    net.send(b2.at[0], b2.at[1], r_tok + 2, partner)
    gb[ctx] = gain[...]
    c8[0] = cot[...]

    def normed(values):
        v = values.astype(F32)
        inv = lax.rsqrt(jnp.mean(v * v, -1, keepdims=True) + EPSILON)
        return v * inv, inv

    def gather_x(buf, slot):
        net.send(buf.at[0], buf.at[4], slot + 2, dev(y, c, z, 1 - x))

    def gather_z(buf, slot):
        net.send(buf.at[0], buf.at[1], slot + 4, partner)
        net.send(buf.at[0], buf.at[2], slot + 1, dev(y, c, zat(1), x))

    def gather_pass(buf, slot, h):
        net.recv(buf.at[2 * h], slot + h)
        net.send(buf.at[2 * h], buf.at[2 * h + 1], slot + 4 + h, partner)
        if h == 1:
            net.send(buf.at[2], buf.at[6], slot + 3, dev(y, c, z, 1 - x))

    r_c8 = net.slots(8)
    for k in (1, 2, 3):
        net.recv(wqz.at[k - 1], r_wqz + k)
        if k == 2:
            z_relay(wqz.at[1], wqz.at[2], r_wqz)
        spread_qkv(k, wqz.at[k - 1])
    gather_x(c8, r_c8)

    r_woz, r_wo = net.slots(4), net.slots(16)

    def spread_wo(k, src):
        zs = zat(k)
        core = zs // 2
        for hx, hy in ((0, 0), (1, 0), (0, 1)):
            net.send(
                src,
                wok.at[dp, pl.ds(off(2 * lax.rem(zs, 2) + x, rows), rows)],
                r_wo + lax.rem(zs, 2) * 8 + hx * 4 + hy * 2 + c,
                dev(flip(y, hy), core, z, flip(x, hx)),
                is_self=(c == core) if hx + hy == 0 else None,
            )

    r_gu, r_wd, r_wy = net.slots(16), net.slots(2), net.slots(2)
    home = y_c == z_lo

    def send_ff(m):
        for zh in range(2):
            for hx in range(2):
                net.send(
                    (wgate, wup)[m].at[:, pl.ds(off(flip(x, hx), ff), ff)],
                    wg8.at[m, pl.ds(off(ctx, rows), rows)],
                    r_gu + m * 8 + ctx,
                    dev(y, c, 2 * zh + y_c, flip(x, hx)),
                    is_self=(z == 2 * zh + y_c) if hx == 0 else None,
                )

    ff_passed = []

    def pass_ff(m):
        for i in range(n_ctx):
            at = 2 * zat(i // 2) + flip(x, i % 2)
            part = wg8.at[m, pl.ds(off(at, rows), rows)]
            slot = r_gu + m * 8 + at

            @pl.when(home)
            def _():
                net.recv(part, slot)

            ff_passed.append(net.send(part, part, slot, dev(1 - y, c, z, x), only=home))

    def take_ff(m):
        for i in range(n_ctx):

            @pl.when(jnp.logical_not(home))
            def _():
                net.recv(wg8.at[m, pl.ds(rows * i, rows)], r_gu + m * 8 + i)

    def send_down():
        z_x = z_hi + z_lo - 2 * z_hi * z_lo
        for zh in range(2):
            net.send(
                wdt,
                wd8.at[pl.ds(off(dp, drows), drows)],
                r_wd + c,
                dev(y, z_lo, 2 * zh + z_x, x),
                is_self=jnp.logical_and(z == 2 * zh + z_x, c == z_lo),
            )

    z_start(wo, lambda k: woz.at[k - 1], r_woz)
    spread_wo(0, wo)
    send_ff(0)
    send_ff(1)
    gather_z(c8, r_c8)

    for k in range(4):
        for hx in range(2):
            if k + hx:
                net.recv(gb.at[2 * zat(k) + flip(x, hx)], r_g + 2 * k + hx)
    for t in range(n_ctx):
        grow[:, rows * t : rows * (t + 1)] = gb[t]
    n1[0:tokens] = (normed(tok[...])[0] * grow[0:1]).astype(BF16)
    net.recv(x2, r_tok)
    n1[tokens : 2 * tokens] = (normed(x2[...])[0] * grow[0:1]).astype(BF16)
    net.recv(csf.at[pl.ds(tokens, tokens)], r_tok + 1)
    net.recv(b2.at[1], r_tok + 2)

    for k in range(4):
        at_x = pl.ds(off(2 * zat(k) + x, rows), rows)
        at_o = pl.ds(off(2 * zat(k) + 1 - x, rows), rows)
        slot = r_wq + k * 4

        @pl.when(c == y)
        def _():
            net.recv(wq.at[0, at_o], slot + 2)

        net.send(wq.at[0, at_o], wq.at[0, at_o], slot + 2, dev(1 - y, c, z, x), only=(c == y))

        @pl.when(c != y)
        def _():
            net.recv(wq.at[1, at_x], slot + 1)

        net.send(wq.at[1, at_x], wq.at[1, at_x], slot + 3, dev(y, c, z, 1 - x), only=(c != y))
    for k in range(1, 4):
        net.recv(woz.at[k - 1], r_woz + k)
        if k == 2:
            z_relay(woz.at[1], woz.at[2], r_woz)
        spread_wo(k, woz.at[k - 1])
    for k in range(4):
        at_x = pl.ds(off(2 * zat(k) + x, rows), rows)
        at_o = pl.ds(off(2 * zat(k) + 1 - x, rows), rows)
        slot = r_wq + k * 4

        @pl.when(c == y)
        def _():
            net.recv(wq.at[1, at_x], slot + 1)

        @pl.when(c != y)
        def _():
            net.recv(wq.at[0, at_o], slot + 2)

        net.recv(wq.at[0, at_x], slot)
        net.recv(wq.at[1, at_o], slot + 3)

    lane = lax.broadcasted_iota(jnp.int32, (2 * tokens, 128), 1)
    low_half = lax.rem(lane, HEAD_SIZE) < HEAD_SIZE // 2

    def turn(tile, forward):
        other = jnp.where(low_half, pltpu.roll(tile, 96, 1), pltpu.roll(tile, 32, 1))
        turned = other * csf[:, 128:256]
        return tile * csf[:, 0:128] + (turned if forward else -turned)

    qf[:, qw:] = jnp.zeros((2 * tokens, qf.shape[1] - qw), F32)
    for part in range(2):
        got = dot_nn(n1[...], wq[part])
        qf[:, qcols * part : qcols * (part + 1)] = got[:, :qcols]
        kvf[:, kcols * part : kcols * (part + 1)] = got[:, qcols : qcols + kcols]
        kvf[:, kw + kcols * part : kw + kcols * (part + 1)] = got[:, qcols + kcols :]

    def turn_keys(forward):
        for t in range(kw // 128 + 1):
            tile = kvf[:, 128 * t : 128 * (t + 1)]
            kvf[:, 128 * t : 128 * (t + 1)] = jnp.where(
                128 * t + lane < kw, turn(tile, forward), tile
            )

    turn_keys(True)
    own_keys = pl.ds(off(ctx, tokens), tokens)
    for s in range(2):
        kv[s, own_keys] = kvf[s * tokens : (s + 1) * tokens].astype(BF16)
    r_kz, r_kx = net.slots(8), net.slots(8)

    def kv_part(s, k, hx):
        return kv.at[s, pl.ds(off(2 * zat(k) + flip(x, hx), tokens), tokens)]

    for s in range(2):
        part = kv_part(s, 0, 0)
        z_start(part, lambda k: part, r_kz + 4 * s)
        net.send(part, part, r_kx + 4 * s, dev(y, c, z, 1 - x))

    def pass_kv(s, k):
        part = kv_part(s, k, 0)
        net.recv(part, r_kz + 4 * s + k)
        if k == 2:
            z_relay(part, part, r_kz + 4 * s)
        net.send(part, part, r_kx + 4 * s + k, dev(y, c, z, 1 - x))

    def take_kv(s):
        for k in range(4):
            net.recv(kv_part(s, k, 1), r_kx + 4 * s + k)

    send_down()

    for t in range(qf.shape[1] // 128):
        qf[:, 128 * t : 128 * (t + 1)] = turn(qf[:, 128 * t : 128 * (t + 1)], True) * scale
    for s in range(2):
        for h in range(heads):
            q6[s * groups + h // per, (h % per) * tokens : (h % per + 1) * tokens] = qf[
                s * tokens : (s + 1) * tokens, HEAD_SIZE * h : HEAD_SIZE * (h + 1)
            ].astype(BF16)
    for k in range(1, 4):
        pass_kv(0, k)
    pass_kv(1, 1)
    pass_kv(1, 2)
    for zz in range(2):
        part = wok.at[2 * (1 - y), pl.ds(off(2 * zz + x, rows), rows)]
        net.recv(part, r_wo + zz * 8 + 2)
        net.send(part, part, r_wo + zz * 8 + 6, dev(y, c, z, 1 - x))
        part = wok.at[2 * y + 1, pl.ds(off(2 * zz + 1 - x, rows), rows)]
        net.recv(part, r_wo + zz * 8 + 5)
        net.send(part, part, r_wo + zz * 8 + 7, dev(1 - y, c, z, x))
    pass_ff(0)
    take_kv(0)

    def attend(s, g):
        kg = kv[s, :, HEAD_SIZE * g : HEAD_SIZE * (g + 1)]
        vg = kv[s, :, kw + HEAD_SIZE * g : kw + HEAD_SIZE * (g + 1)]
        scores = dot_nt(q6[s * groups + g], kg) + b2[s, 0:1, :]
        weights = jnp.exp(scores - jnp.max(scores, -1, keepdims=True))
        probs = (weights * (1.0 / jnp.sum(weights, -1, keepdims=True))).astype(BF16)
        p6[s * groups + g] = probs
        got = dot_nn(probs, vg).astype(BF16)
        o6[s * groups + g] = got
        for i in range(per):
            h = g * per + i
            ab[s * tokens : (s + 1) * tokens, HEAD_SIZE * h : HEAD_SIZE * (h + 1)] = got[
                i * tokens : (i + 1) * tokens
            ]

    attend(0, 0)
    pass_kv(1, 3)
    attend(0, 1)
    gather_pass(c8, r_c8, 1)
    attend(0, 2)
    take_kv(1)
    attend(1, 0)
    pass_ff(1)
    attend(1, 1)
    for cc in range(2):
        part = wd8.at[pl.ds(off(2 * y + cc, drows), drows)]
        net.recv(part, r_wd + cc)
        net.send(part, part, r_wy + cc, dev(1 - y, c, z, x))
    attend(1, 2)

    for hx, hy, cc in ((0, 0, 0), (0, 0, 1), (0, 1, 1), (1, 0, 0), (1, 1, 0), (1, 1, 1)):
        for zz in range(2):
            net.recv(
                wok.at[2 * flip(y, hy) + cc, pl.ds(off(2 * zz + flip(x, hx), rows), rows)],
                r_wo + zz * 8 + hx * 4 + hy * 2 + cc,
            )
    for part in range(4):
        got = dot_nn(ab[:, 0:qw], wok[part])
        for s in range(2):
            mp[s, :, qcols * part : qcols * (part + 1)] = got[s * tokens : (s + 1) * tokens]
    r_ml = net.slots(1)
    mp_sent = net.send(mp.at[1], ml, r_ml, partner)
    gather_pass(c8, r_c8, 2)
    gather_pass(c8, r_c8, 3)
    net.recv(ml, r_ml)
    mid[...] = tok[...].astype(F32) + mp[0] + ml[...]
    n8[0] = (normed(mid[...])[0] * grow[1:2]).astype(BF16)
    r_n8 = net.slots(8)
    gather_z(n8, r_n8)
    gather_x(n8, r_n8)

    net.recv(c8.at[1], r_c8 + 4)
    for h in range(1, 4):
        net.recv(c8.at[2 * h + 1], r_c8 + 4 + h)
    take_ff(0)
    take_ff(1)
    for cc in range(2):
        net.recv(wd8.at[pl.ds(off(2 * (1 - y) + cc, drows), drows)], r_wy + cc)

    all_tokens = 8 * tokens

    def feed(i):
        pair = slice(2 * i, 2 * i + 2)
        here = n8[pair].reshape(2 * tokens, width)
        grad_inner = dot_nn(c8[pair].reshape(2 * tokens, width), wd8[...])
        gate = dot_nn(here, wg8[0])
        up = dot_nn(here, wg8[1])
        sig = 1.0 / (1.0 + jnp.exp(-gate))
        silu = gate * sig
        dgate = (grad_inner * up * sig * (1.0 + gate * (1.0 - sig))).astype(BF16)
        dup = (grad_inner * silu).astype(BF16)
        at = 2 * tokens * i
        act[at : at + 2 * tokens] = (silu * up).astype(BF16)
        act[at + all_tokens : at + all_tokens + 2 * tokens] = dgate
        act[at + 2 * all_tokens : at + 2 * all_tokens + 2 * tokens] = dup
        pt[pair] = (dot_nt(dgate, wg8[0]) + dot_nt(dup, wg8[1])).astype(BF16).reshape(2, tokens, width)

    def reduce_start(part, land, slot, h):
        return net.send(part.at[2 * h + 1], land.at[h], slot + h, partner)

    def reduce_pass(part, land, out, land2, slot, h):
        net.recv(land.at[h], slot + h)
        out[h - 1] = (part[2 * h].astype(F32) + land[h].astype(F32)).astype(BF16)
        net.send(
            out.at[h - 1], land2.at[h - 1], slot + 4 + h,
            dev(y, c, zat(h % 2), flip(x, h // 2)),
        )

    def reduce_own(part, land, slot):
        net.recv(land.at[0], slot)
        return part[0].astype(F32) + land[0].astype(F32)

    def reduce_end(land2, slot):
        total = 0.0
        for h in range(1, 4):
            net.recv(land2.at[h - 1], slot + 4 + h)
            total = total + land2[h - 1].astype(F32)
        return total

    r_dn = net.slots(8)
    pt_sent = []
    net.recv(n8.at[1], r_n8 + 4)
    for h in range(4):
        if h:
            gather_pass(n8, r_n8, h)
            net.recv(n8.at[2 * h + 1], r_n8 + 4 + h)
        feed(h)
        pt_sent.append(reduce_start(pt, l1, r_dn, h))
        if h > 1:
            reduce_pass(pt, l1, s2, l2, r_dn, h - 1)
    reduce_pass(pt, l1, s2, l2, r_dn, 3)
    dmid[...] = reduce_own(pt, l1, r_dn)

    def flat(ref, i):
        return ref[:, :, pl.ds(off(i, 128), 128)].reshape(all_tokens, 128)

    def grad_gu(i, carry):
        left = flat(n8, i)
        at = pl.ds(off(i, 128), 128)
        ggu[0, at] = dot_tn(left, act[pl.ds(all_tokens, all_tokens)]).astype(BF16)
        ggu[1, at] = dot_tn(left, act[pl.ds(2 * all_tokens, all_tokens)]).astype(BF16)
        return carry

    def grad_d(i, carry):
        gdt[pl.ds(off(i, 128), 128)] = dot_tn(flat(c8, i), act[pl.ds(0, all_tokens)]).astype(BF16)
        return carry

    def feed_out(i, carry):
        got = dot_nt(act[pl.ds(off(i, 2 * tokens), 2 * tokens)], wd8[...])
        pt[pl.ds(2 * i, 2)] = got.astype(BF16).reshape(2, tokens, width)
        return carry

    r_gd, r_gz = net.slots(1), net.slots(4)
    half = 2 * drows
    lax.fori_loop(0, width // 128, grad_d, 0)
    net.send(gdt.at[pl.ds(off(1 - y, half), half)], lgd, r_gd, dev(1 - y, c, z, x))
    lax.fori_loop(0, width // 128, grad_gu, 0)
    for zt in range(4):
        at = pl.ds(2 * rows * zt, 2 * rows)
        net.send(
            ggu.at[:, at], lgu.at[:, at], r_gz + zt, dev(1 - y, c, z, x),
            only=jnp.logical_not(home),
        )
    for finish in pt_sent:
        net.done(finish)
    lax.fori_loop(0, 4, feed_out, 0)
    r_out = net.slots(8)
    for h in range(4):
        reduce_start(pt, l1o, r_out, h)

    total = dmid[...] + reduce_end(l2, r_dn)
    normed_two, inv_two = normed(mid[...])
    total = total * grow[1:2]
    dmid[...] = cot[...].astype(F32) + inv_two * (
        total - normed_two * jnp.mean(total * normed_two, -1, keepdims=True)
    )
    dmb[0] = dmid[...].astype(BF16)
    r_dm = net.slots(1)
    net.send(dmb.at[0], dmb.at[1], r_dm, partner)

    r_ld = net.slots(2)
    net.recv(lgd, r_gd)
    sgd[...] = (gdt[pl.ds(off(y, half), half)].astype(F32) + lgd[...].astype(F32)).astype(BF16)
    gd_z = 2 * (z_lo + c - 2 * z_lo * c) + c
    for cc in range(2):
        net.send(
            sgd.at[pl.ds(cc * drows, drows)], ld.at[z_hi], r_ld + z_hi, dev(y, cc, gd_z, x),
            is_self=jnp.logical_and(z == gd_z, c == cc),
        )
    net.recv(dmb.at[1], r_dm)

    for part in range(4):
        for s in range(2):
            dm4[part, s * tokens : (s + 1) * tokens] = dmb[s, :, qcols * part : qcols * (part + 1)]
    dattn = dot_nt(dm4[0], wok[0])
    for part in range(1, 4):
        dattn = dattn + dot_nt(dm4[part], wok[part])
    qf[:, 0:qw] = dattn
    for s in range(2):
        for h in range(heads):
            do6[s * groups + h // per, (h % per) * tokens : (h % per + 1) * tokens] = qf[
                s * tokens : (s + 1) * tokens, HEAD_SIZE * h : HEAD_SIZE * (h + 1)
            ].astype(BF16)
    attn_all = ab[:, 0:qw]
    for part in range(4):
        act[qw * part : qw * (part + 1), 0:qcols] = dot_tn(attn_all, dm4[part]).astype(BF16)
    r_gy, r_go = net.slots(2), net.slots(8)
    for cc in range(2):
        net.send(
            act.at[pl.ds(off(2 * (1 - y) + cc, qw), qw)], loy.at[cc], r_gy + cc, dev(1 - y, c, z, x)
        )

    def pass_go():
        for cc in range(2):
            net.recv(loy.at[cc], r_gy + cc)
            at = pl.ds(off(2 * y + cc, qw), qw)
            act[at] = (act[at].astype(F32) + loy[cc].astype(F32)).astype(BF16)
        for hx in (1, 0):
            for hc in range(2):
                for zz in range(2):
                    at = pl.multiple_of((2 * y + flip(c, hc)) * qw + (2 * zz + flip(x, hx)) * rows, rows)
                    src = act.at[pl.ds(at, rows)]
                    dst = lo.at[2 * c + zz, hx]
                    slot = r_go + (2 * c + zz) * 2 + hx
                    if hx + hc == 0:
                        net.keep(src, dst, slot)
                    else:
                        net.send(src, dst, slot, dev(y, flip(c, hc), z, flip(x, hx)))

    def attend_back(s, g):
        at = s * groups + g
        kg = kv[s, :, HEAD_SIZE * g : HEAD_SIZE * (g + 1)]
        vg = kv[s, :, kw + HEAD_SIZE * g : kw + HEAD_SIZE * (g + 1)]
        dout = do6[at]
        delta = jnp.sum(dout.astype(F32) * o6[at].astype(F32), -1, keepdims=True)
        dprob = dot_nt(dout, vg)
        dscore = (p6[at].astype(F32) * (dprob - delta)).astype(BF16)
        dquery = dot_nn(dscore, kg) * scale
        dkeys = dot_tn(q6[at], dscore)
        dvals = dot_tn(dout, p6[at])
        for t in range(n_ctx):
            cols = slice(t * tokens, (t + 1) * tokens)
            dkv[t, s, HEAD_SIZE * g : HEAD_SIZE * (g + 1)] = dkeys[:, cols].astype(BF16)
            dkv[t, s, kw + HEAD_SIZE * g : kw + HEAD_SIZE * (g + 1)] = dvals[:, cols].astype(BF16)
        for i in range(per):
            h = g * per + i
            qf[s * tokens : (s + 1) * tokens, HEAD_SIZE * h : HEAD_SIZE * (h + 1)] = dquery[
                i * tokens : (i + 1) * tokens
            ]

    r_dx, r_dz = net.slots(8), net.slots(8)

    def send_dkv(s):
        for k in (1, 2, 3, 0):
            net.send(
                dkv.at[2 * zat(k) + 1 - x, s], lx.at[k, s], r_dx + 4 * s + k, dev(y, c, z, 1 - x)
            )

    def pass_dkv(s):
        for k in range(1, 4):
            net.recv(lx.at[k, s], r_dx + 4 * s + k)
            sx[k - 1, s] = (dkv[2 * zat(k) + x, s].astype(F32) + lx[k, s].astype(F32)).astype(BF16)
            net.send(sx.at[k - 1, s], lkz.at[k - 1, s], r_dz + 4 * s + k, dev(y, c, zat(k), x))

    for g in range(groups):
        attend_back(0, g)
    send_dkv(0)
    r_gf = net.slots(4)
    for k in (3, 2, 1, 0):
        at = pl.ds(off(zat(k), 2 * rows), 2 * rows)

        @pl.when(home)
        def _():
            net.recv(lgu.at[:, at], r_gz + zat(k))
            ggu[:, at] = (ggu[:, at].astype(F32) + lgu[:, at].astype(F32)).astype(BF16)

        for hx in range(2):
            src = ggu.at[:, pl.ds(off(2 * zat(k) + flip(x, hx), rows), rows)]
            dst = lf.at[x, z_hi]
            slot = r_gf + x * 2 + z_hi
            if k + hx:
                net.send(src, dst, slot, dev(y, c, zat(k), flip(x, hx)), only=home)
            else:

                @pl.when(home)
                def _():
                    net.keep(src, dst, slot)

    attend_back(1, 0)
    pass_go()
    attend_back(1, 1)
    pass_dkv(0)
    attend_back(1, 2)
    send_dkv(1)
    for t in range(qf.shape[1] // 128):
        qf[:, 128 * t : 128 * (t + 1)] = turn(qf[:, 128 * t : 128 * (t + 1)], False)
    grad = dot_tn(n1[...], qf[:, 0:qw].astype(BF16)).astype(BF16)
    for t in range(n_ctx):
        p6[t // 2, (t % 2) * rows : (t % 2 + 1) * rows, 0:qw] = grad[rows * t : rows * (t + 1)]
    for part in range(2):
        dqk[part, :, 0:qcols] = qf[:, qcols * part : qcols * (part + 1)].astype(BF16)
    r_qy, r_qx, r_zq = net.slots(4), net.slots(4), net.slots(4)
    mine = c == y

    def send_grads(source, land, slot):
        for k in range(4):
            net.send(
                source(zat(k), slice(0, 2)), land.at[zat(k)], slot + k, dev(1 - y, c, z, x),
                only=jnp.logical_not(mine),
            )

    def add_y(source, land, slot, land_x, slot_x):
        for k in range(4):

            @pl.when(mine)
            def _():
                net.recv(land.at[zat(k)], slot + k)
                here = source(zat(k), slice(0, 2))
                here[...] = (here[...].astype(F32) + land[zat(k)].astype(F32)).astype(BF16)

            net.send(
                source(zat(k), 1 - x), land_x.at[k], slot_x + k, dev(y, c, z, 1 - x), only=mine
            )

    def add_x(source, land_x, slot_x, staged, arrived, slot_z):
        wide_part = arrived.shape[2]
        for k in (1, 2, 3, 0):

            @pl.when(mine)
            def _():
                net.recv(land_x.at[k], slot_x + k)
                staged[k] = (source(zat(k), x)[...].astype(F32) + land_x[k].astype(F32)).astype(BF16)

            for cc in range(2):
                first = cc * (staged.shape[2] - wide_part)
                src = staged.at[k, :, pl.ds(first, wide_part)]
                if k:
                    net.send(src, arrived.at[k], slot_z + k, dev(y, cc, zat(k), x), only=mine)
                else:

                    @pl.when(jnp.logical_and(mine, c == cc))
                    def _():
                        net.keep(src, arrived.at[k], slot_z)

                    net.send(
                        src, arrived.at[k], slot_z, dev(y, cc, z, x),
                        only=jnp.logical_and(mine, c != cc),
                    )

    def add_z(out, arrived, slot_z, staged):
        total = 0.0
        for k in (1, 2, 3, 0):
            net.recv(arrived.at[k], slot_z + k)
            total = total + arrived[k].astype(F32)
        count = out.shape[1]
        skip = count - (staged.shape[2] - arrived.shape[2])
        out[...] = jnp.where(c == 0, total[:, 0:count], total[:, skip : skip + count])

    def in_p6(zt, xt):
        at = pl.ds(0, 2 * rows) if isinstance(xt, slice) else pl.ds(off(xt, rows), rows)
        return p6.at[zt, at, pl.ds(0, qf.shape[1])]

    def in_wg8(zt, xt):
        at = pl.ds(off(zt, 2 * rows), 2 * rows) if isinstance(xt, slice) else pl.ds(off(2 * zt + xt, rows), rows)
        return wg8.at[0, at]

    send_grads(in_p6, lqy, r_qy)
    pass_dkv(1)
    for h in range(1, 4):
        reduce_pass(pt, l1o, s2o, l2o, r_out, h)
    mid[...] = mid[...] + reduce_own(pt, l1o, r_out)

    def attn_pass(land, out, staged, arrived, send_slot, slot, absolute):
        for k in (1, 2, 3, 0):
            at = zat(k) if absolute else k
            part = 0.0
            for h in range(2):
                net.recv(land.at[at, h], slot + at * 2 + h)
                part = part + land[at, h, :, 0 : out.shape[1]].astype(F32)
            if k == 0:
                out[...] = part
            else:
                staged[k - 1] = part.astype(BF16)
                net.send(staged.at[k - 1], arrived.at[k - 1], send_slot + k, dev(y, c, zat(k), x))

    def attn_end(out, arrived, slot):
        for k in range(1, 4):
            net.recv(arrived.at[k - 1], slot + k)
            out[...] = out[...] + arrived[k - 1].astype(F32)

    r_zo = net.slots(4)
    attn_pass(lo, o_o, so, lzo, r_zo, r_go, True)
    add_y(in_p6, lqy, r_qy, lqx, r_qx)

    for s in range(2):
        net.recv(lx.at[0, s], r_dx + 4 * s)
        total = dkv[2 * z + x, s].astype(F32) + lx[0, s].astype(F32)
        for k in range(1, 4):
            net.recv(lkz.at[k - 1, s], r_dz + 4 * s + k)
            total = total + lkz[k - 1, s].astype(F32)
        kvf[s * tokens : (s + 1) * tokens] = total.T
    turn_keys(False)
    for part in range(2):
        dqk[part, :, qcols : qcols + kcols] = kvf[:, kcols * part : kcols * (part + 1)].astype(BF16)
        dqk[part, :, qcols + kcols :] = kvf[:, kw + kcols * part : kw + kcols * (part + 1)].astype(BF16)
    for finish in ff_passed:
        net.done(finish)
    for part in range(2):
        wg8[0, :, 2 * kcols * part : 2 * kcols * (part + 1)] = dot_tn(
            n1[...], dqk[part, :, qcols:]
        ).astype(BF16)
    r_ky, r_kx2, r_zk = net.slots(4), net.slots(4), net.slots(4)
    send_grads(in_wg8, lky, r_ky)
    net.done(mp_sent)
    got = dot_nt(dqk[0], wq[0]) + dot_nt(dqk[1], wq[1])
    for s in range(2):
        mp[s] = got[s * tokens : (s + 1) * tokens]
    r_dn1 = net.slots(1)
    net.send(mp.at[1], ml, r_dn1, partner)
    add_x(in_p6, lqx, r_qx, sq, lzq, r_zq)
    add_y(in_wg8, lky, r_ky, lkx, r_kx2)
    net.recv(ml, r_dn1)
    total = mp[0] + ml[...]
    normed_one, inv_one = normed(tok[...])
    total = total * grow[0:1]
    o_ing[...] = (
        dmid[...]
        + inv_one * (total - normed_one * jnp.mean(total * normed_one, -1, keepdims=True))
    ).astype(BF16)
    add_x(in_wg8, lkx, r_kx2, sk, lzk, r_zk)

    o_out[...] = (mid[...] + reduce_end(l2o, r_out)).astype(BF16)
    gains = [0.0, 0.0]
    for h in range(2):
        for zh in range(2):
            net.recv(lf.at[h, zh], r_gf + h * 2 + zh)
        for m in range(2):
            got = lf[h, 0, m].astype(F32) + lf[h, 1, m].astype(F32)
            cols = slice(h * ff, (h + 1) * ff)
            (o_gate, o_up)[m][:, cols] = got
            gains[1] = gains[1] + jnp.sum(
                got * (wgate, wup)[m][:, cols].astype(F32), 1, keepdims=True
            )
    for zh in range(2):
        net.recv(ld.at[zh], r_ld + zh)
    o_d[...] = ld[0].astype(F32) + ld[1].astype(F32)
    attn_end(o_o, lzo, r_zo)
    add_z(o_q, lzq, r_zq, sq)
    gains[0] = jnp.sum(o_q[...] * wqkv[:, 0:qcols].astype(F32), 1, keepdims=True)
    add_z(kvg, lzk, r_zk, sk)
    gains[0] = gains[0] + jnp.sum(kvg[...] * wqkv[:, qcols:].astype(F32), 1, keepdims=True)
    o_k[...] = kvg[:, 0:kcols]
    o_v[...] = kvg[:, kcols:]
    column = lax.broadcasted_iota(jnp.int32, (rows, 128), 1)
    both = jnp.where(column == 0, gains[0], jnp.where(column == 1, gains[1], 0.0))
    sg[...] = both.T[0:8]
    r_lg = net.slots(4)
    for h in range(1, 4):
        net.send(sg, lg.at[h - 1], r_lg + h, dev(flip(y, h // 2), flip(c, h % 2), z, x))
    total = sg[...]
    for h in range(1, 4):
        net.recv(lg.at[h - 1], r_lg + h)
        total = total + lg[h - 1]
    total = total / gain[...]
    o_gain_one[...] = total[0:1]
    o_gain_two[...] = total[1:2]
    net.drain()


def hand_over(*refs):
    count = len(refs) // 2
    copies = [pltpu.make_async_copy(refs[i], refs[count + i], refs[-1].at[i]) for i in range(count)]
    for copy in copies:
        copy.start()
    for copy in copies:
        copy.wait()


def run_layer(n_ctx, tok, cot, pos, blk, gain_one, gain_two, wquery, wkey, wvalue, wo, wgate, wup, wdt):
    tokens, width = tok.shape
    rows, qcols = wquery.shape
    packed = qcols + 2 * wkey.shape[1]
    drows, ff = wdt.shape
    keys = n_ctx * tokens
    qw = 2 * qcols
    kw = packed - qcols
    groups = kw // HEAD_SIZE
    per = QUERY_HEADS // KEY_VALUE_HEADS
    stack = per * tokens
    wide = -(-qw // 128) * 128
    out_shape = [
        jax.ShapeDtypeStruct((tokens, width), BF16),
        jax.ShapeDtypeStruct((tokens, width), BF16),
        jax.ShapeDtypeStruct((1, rows), F32),
        jax.ShapeDtypeStruct((1, rows), F32),
        jax.ShapeDtypeStruct((rows, qcols), F32),
        jax.ShapeDtypeStruct((rows, kw // 2), F32),
        jax.ShapeDtypeStruct((rows, kw // 2), F32),
        jax.ShapeDtypeStruct((rows, qcols), F32),
        jax.ShapeDtypeStruct((rows, 2 * ff), F32),
        jax.ShapeDtypeStruct((rows, 2 * ff), F32),
        jax.ShapeDtypeStruct((drows, ff), F32),
    ]

    def vm(*shape, dtype=BF16):
        return pltpu.VMEM(shape, dtype)

    scratch = [
        vm(rows, packed),
        vm(8, rows, dtype=F32),
        vm(2 * tokens, 256, dtype=F32),
        vm(2, 8, keys, dtype=F32),
        vm(tokens, width),
        vm(n_ctx, 8, rows, dtype=F32),
        vm(8, width, dtype=F32),
        vm(3, rows, packed),
        vm(3, rows, qcols),
        vm(2, width, packed),
        vm(4, 4 * rows, qcols),
        vm(2, width, ff),
        vm(width, ff),
        vm(8, tokens, width),
        vm(8, tokens, width),
        vm(2 * tokens, width),
        vm(2 * tokens, wide, dtype=F32),
        vm(2 * tokens, 2 * kw, dtype=F32),
        vm(2, keys, 2 * kw),
        vm(2 * groups, stack, HEAD_SIZE),
        vm(2 * groups, stack, keys),
        vm(2 * groups, stack, HEAD_SIZE),
        vm(2 * tokens, wide),
        vm(2, tokens, width, dtype=F32),
        vm(tokens, width, dtype=F32),
        vm(tokens, width, dtype=F32),
        vm(tokens, width, dtype=F32),
        vm(2, tokens, width),
        vm(4, 2 * tokens, qcols),
        vm(2 * groups, stack, HEAD_SIZE),
        vm(24 * tokens, ff),
        vm(8, tokens, width),
        vm(4, tokens, width),
        vm(3, tokens, width),
        vm(3, tokens, width),
        vm(4, tokens, width),
        vm(3, tokens, width),
        vm(3, tokens, width),
        vm(2, width, ff),
        vm(2, width, ff),
        vm(2, 2, 2, rows, ff),
        vm(width, ff),
        vm(2 * drows, ff),
        vm(2 * drows, ff),
        vm(2, drows, ff),
        vm(2, qw, ff),
        vm(4, 2, rows, ff),
        vm(4, 2 * rows, wide),
        vm(4, rows, wide),
        vm(4, 2 * rows, ff),
        vm(4, rows, ff),
        vm(3, rows, qcols),
        vm(4, rows, wide),
        vm(4, rows, ff),
        vm(3, rows, qcols),
        vm(4, rows, ff),
        vm(4, rows, 256),
        vm(rows, kw, dtype=F32),
        vm(n_ctx, 2, 2 * kw, tokens),
        vm(4, 2, 2 * kw, tokens),
        vm(3, 2, 2 * kw, tokens),
        vm(3, 2, 2 * kw, tokens),
        vm(3, 8, rows, dtype=F32),
        vm(8, rows, dtype=F32),
        vm(2, 2 * tokens, packed),
        pltpu.SemaphoreType.DMA((N_SEM,)),
        pltpu.SemaphoreType.DMA((N_SEM,)),
    ]
    inside = pl.BlockSpec(memory_space=pltpu.VMEM)
    outs = pl.pallas_call(
        layer_kernel,
        out_shape=out_shape,
        in_specs=[inside] * 3 + [pl.BlockSpec(memory_space=pltpu.SMEM)] + [inside] * 9,
        out_specs=[inside] * len(out_shape),
        scratch_shapes=scratch,
        compiler_params=pltpu.CompilerParams(
            collective_id=0, has_side_effects=True, vmem_limit_bytes=VMEM_LIMIT
        ),
        name="layer",
    )(tok, cot, pos, blk, gain_one, gain_two, wquery, wkey, wvalue, wo, wgate, wup, wdt)
    anywhere = pl.BlockSpec(memory_space=pl.ANY)
    return pl.pallas_call(
        hand_over,
        out_shape=out_shape,
        in_specs=[inside] * len(out_shape),
        out_specs=[anywhere] * len(out_shape),
        scratch_shapes=[pltpu.SemaphoreType.DMA((len(out_shape),))],
        name="hand_over",
    )(*outs)


VMEM_LIMIT = 63 * 1024 * 1024


def on_device_plane(
    tokens, positions, block_sizes, attn_gain, w_query, w_key, w_value, w_out, mlp_gain,
    w_gate, w_up, w_down, cotangent,
):
    output, input_grad, g_one, g_two, g_q, g_k, g_v, g_o, g_gate, g_up, g_d = run_layer(
        lax.axis_size("ctx"), tokens[0], cotangent[0], positions, block_sizes, attn_gain,
        mlp_gain, w_query, w_key, w_value, w_out, w_gate, w_up, w_down.T,
    )
    return (
        output[None],
        input_grad[None],
        g_one[0],
        g_q,
        g_k,
        g_v,
        g_o,
        g_two[0],
        g_gate,
        g_up,
        g_d.T,
    )


def solution(mesh):
    placed = (
        P("dp", "ctx", None),
        P("dp", "ctx"),
        P("dp"),
        P("ctx"),
        P("ctx", "dp"),
        P("ctx", "dp"),
        P("ctx", "dp"),
        P("ctx", "dp"),
        P("ctx"),
        P("ctx", "dp"),
        P("ctx", "dp"),
        P("ctx", "dp"),
        P("dp", "ctx", None),
    )
    fits = mesh.shape["dp"] == 4 and mesh.shape["ctx"] == 8
    return jax.shard_map(
        on_device_plane if fits else on_device,
        mesh=mesh,
        in_specs=placed,
        out_specs=(
            P("dp", "ctx", None),
            P("dp", "ctx", None),
            P("ctx"),
            P("ctx", "dp"),
            P("ctx", "dp"),
            P("ctx", "dp"),
            P("ctx", "dp"),
            P("ctx"),
            P("ctx", "dp"),
            P("ctx", "dp"),
            P("ctx", "dp"),
        ),
        check_vma=False,
    )
```

```python
import jax
import jax.numpy as jnp
import numpy as np
from jax import lax
from jax.experimental import pallas as pl
from jax.experimental.pallas import tpu as pltpu
from jax.sharding import PartitionSpec as P

QUERY_HEADS = 18
KEY_VALUE_HEADS = 6
HEAD_SIZE = 64


EPSILON = 1e-05
THETA = 10000.0
VERY_NEGATIVE = -1e30


def product(left, right):
    return jnp.dot(left, right, preferred_element_type=jnp.float32)


def angles_of(place_ids):
    half_dim = HEAD_SIZE // 2
    frequency = THETA ** (-(jnp.arange(half_dim, dtype=jnp.float32) * 2.0 / HEAD_SIZE))
    return place_ids.astype(jnp.float32)[:, None] * frequency[None, :]


def rotate(values, angles, forward):
    row_total = values.shape[0]
    half_dim = angles.shape[1]
    shaped = values.reshape(row_total, -1, 2 * half_dim)
    first_half = shaped[..., :half_dim]
    second = shaped[..., half_dim:]
    cosine = jnp.cos(angles)[:, None, :]
    sine_vals = jnp.sin(angles)[:, None, :]
    if forward:
        rotated = jnp.concatenate(
            [first_half * cosine - second * sine_vals, second * cosine + first_half * sine_vals], -1
        )
    else:
        rotated = jnp.concatenate(
            [first_half * cosine + second * sine_vals, second * cosine - first_half * sine_vals], -1
        )
    return rotated.reshape(row_total, -1)


def norm_back(grad_normed, normed, inverse):
    return inverse * (grad_normed - normed * jnp.mean(grad_normed * normed, -1, keepdims=True))


def visible(query_rows, key_rows, block_len):
    return ((key_rows // block_len)[None, :] <= (query_rows // block_len)[:, None])[None, None]


def attend_forward(query_rows4, complete_keys, complete_values, query_rows, block_len, score_scale):
    key_count = complete_keys.shape[0]
    key_row_width = 512
    block_list = key_count // key_row_width
    query_group_width = QUERY_HEADS // KEY_VALUE_HEADS
    row_total = query_rows4.shape[0]
    key_block_list = complete_keys.reshape(block_list, key_row_width, KEY_VALUE_HEADS, HEAD_SIZE)
    value_block_list = complete_values.reshape(
        block_list, key_row_width, KEY_VALUE_HEADS, HEAD_SIZE
    )
    last_block = query_rows[-1] // block_len

    def advance(carried, inputs):
        key_blk, val_blk, first_key = inputs
        key_rows = first_key + jnp.arange(key_row_width, dtype=jnp.int32)

        def compute(current):
            run_max, run_sum, accum = current
            scores = (
                jnp.einsum(
                    "tkgd,nkd->kgtn", query_rows4, key_blk, preferred_element_type=jnp.float32
                )
                * score_scale
            )
            allowed = visible(query_rows, key_rows, block_len)
            scores = jnp.where(allowed, scores, VERY_NEGATIVE)
            new_max = jnp.maximum(run_max, jnp.max(scores, -1))
            weights = jnp.where(allowed, jnp.exp(scores - new_max[..., None]), 0.0)
            factor = jnp.exp(run_max - new_max)
            new_sum = run_sum * factor + jnp.sum(weights, -1)
            accum = accum * factor[..., None] + jnp.einsum(
                "kgtn,nkd->kgtd",
                weights.astype(jnp.bfloat16),
                val_blk,
                preferred_element_type=jnp.float32,
            )
            return (new_max, new_sum, accum)

        return (
            lax.cond(
                first_key // block_len > last_block, lambda unchanged: unchanged, compute, carried
            ),
            None,
        )

    start_state = (
        jnp.full((KEY_VALUE_HEADS, query_group_width, row_total), VERY_NEGATIVE, jnp.float32),
        jnp.zeros((KEY_VALUE_HEADS, query_group_width, row_total), jnp.float32),
        jnp.zeros((KEY_VALUE_HEADS, query_group_width, row_total, HEAD_SIZE), jnp.float32),
    )
    firsts = jnp.arange(block_list, dtype=jnp.int32) * key_row_width
    final_state, unused = lax.scan(advance, start_state, (key_block_list, value_block_list, firsts))
    run_max, run_sum, accum = final_state
    return (accum / run_sum[..., None], run_max + jnp.log(run_sum))


def attend_backward(
    query_rows4,
    head_gradients,
    log_sums,
    row_delta,
    complete_keys,
    complete_values,
    query_rows,
    block_len,
    score_scale,
):
    key_count = complete_keys.shape[0]
    key_row_width = 512
    block_list = key_count // key_row_width
    query_group_width = QUERY_HEADS // KEY_VALUE_HEADS
    row_total = query_rows4.shape[0]
    key_block_list = complete_keys.reshape(block_list, key_row_width, KEY_VALUE_HEADS, HEAD_SIZE)
    value_block_list = complete_values.reshape(
        block_list, key_row_width, KEY_VALUE_HEADS, HEAD_SIZE
    )
    last_block = query_rows[-1] // block_len

    def advance(grad_query, inputs):
        key_blk, val_blk, first_key = inputs
        key_rows = first_key + jnp.arange(key_row_width, dtype=jnp.int32)

        def compute(current):
            scores = (
                jnp.einsum(
                    "tkgd,nkd->kgtn", query_rows4, key_blk, preferred_element_type=jnp.float32
                )
                * score_scale
            )
            allowed = visible(query_rows, key_rows, block_len)
            prob_vals = jnp.where(allowed, jnp.exp(scores - log_sums[..., None]), 0.0)
            grad_prob = jnp.einsum(
                "tkgd,nkd->kgtn", head_gradients, val_blk, preferred_element_type=jnp.float32
            )
            grad_score = (prob_vals * (grad_prob - row_delta[..., None])).astype(jnp.bfloat16)
            current = current + jnp.einsum(
                "kgtn,nkd->tkgd", grad_score, key_blk, preferred_element_type=jnp.float32
            )
            grad_key = jnp.einsum(
                "kgtn,tkgd->nkd", grad_score, query_rows4, preferred_element_type=jnp.float32
            )
            grad_value = jnp.einsum(
                "kgtn,tkgd->nkd",
                prob_vals.astype(jnp.bfloat16),
                head_gradients,
                preferred_element_type=jnp.float32,
            )
            return (current, (grad_key, grad_value))

        def nothing(current):
            empty_block = jnp.zeros((key_row_width, KEY_VALUE_HEADS, HEAD_SIZE), jnp.float32)
            return (current, (empty_block, empty_block))

        return lax.cond(first_key // block_len > last_block, nothing, compute, grad_query)

    firsts = jnp.arange(block_list, dtype=jnp.int32) * key_row_width
    initial_gradient = jnp.zeros(
        (row_total, KEY_VALUE_HEADS, query_group_width, HEAD_SIZE), jnp.float32
    )
    grad_query, stacked_rows = lax.scan(
        advance, initial_gradient, (key_block_list, value_block_list, firsts)
    )
    key_gradients = stacked_rows[0].reshape(key_count, KEY_VALUE_HEADS * HEAD_SIZE)
    value_gradients = stacked_rows[1].reshape(key_count, KEY_VALUE_HEADS * HEAD_SIZE)
    return (grad_query, key_gradients, value_gradients)


def on_device(
    tokens,
    positions,
    block_sizes,
    attn_gain,
    w_query,
    w_key,
    w_value,
    w_out,
    mlp_gain,
    w_gate,
    w_up,
    w_down,
    cotangent,
):
    row_parts = (
        lax.all_gather(w_query, "ctx", axis=0, tiled=True),
        lax.all_gather(w_key, "ctx", axis=0, tiled=True),
        lax.all_gather(w_value, "ctx", axis=0, tiled=True),
        lax.all_gather(w_out, "ctx", axis=0, tiled=True),
        lax.all_gather(w_gate, "ctx", axis=0, tiled=True),
        lax.all_gather(w_up, "ctx", axis=0, tiled=True),
        lax.all_gather(w_down, "ctx", axis=0, tiled=True),
        lax.all_gather(attn_gain, "ctx", axis=0, tiled=True),
        lax.all_gather(mlp_gain, "ctx", axis=0, tiled=True),
    )
    whole_w = (
        lax.all_gather(row_parts[0], "dp", axis=1, tiled=True),
        lax.all_gather(row_parts[1], "dp", axis=1, tiled=True),
        lax.all_gather(row_parts[2], "dp", axis=1, tiled=True),
        lax.all_gather(row_parts[3], "dp", axis=1, tiled=True),
        lax.all_gather(row_parts[4], "dp", axis=1, tiled=True),
        lax.all_gather(row_parts[5], "dp", axis=1, tiled=True),
        lax.all_gather(row_parts[6], "dp", axis=1, tiled=True),
    )
    query_w, key_w, value_w, out_w, gate_w, up_w, down_w = whole_w
    gain_one = row_parts[7].astype(jnp.float32)
    gain_two = row_parts[8].astype(jnp.float32)
    seq_count = tokens.shape[0]
    seq_rows = tokens.shape[1]
    width = tokens.shape[2]
    inputs = tokens.reshape(seq_count * seq_rows, width).astype(jnp.float32)
    row_total = inputs.shape[0]
    query_group_width = QUERY_HEADS // KEY_VALUE_HEADS
    query_rows = lax.axis_index("ctx") * seq_rows + jnp.arange(seq_rows, dtype=jnp.int32)
    angles = angles_of(positions.reshape(-1))
    score_scale = HEAD_SIZE ** (-0.5)
    inv_one = lax.rsqrt(jnp.mean(inputs * inputs, -1, keepdims=True) + EPSILON)
    normed_one = inputs * inv_one
    hidden_one = (normed_one * gain_one).astype(jnp.bfloat16)
    query_matrix = rotate(product(hidden_one, query_w), angles, True).astype(jnp.bfloat16)
    keys_own = rotate(product(hidden_one, key_w), angles, True).astype(jnp.bfloat16)
    values_own = product(hidden_one, value_w).astype(jnp.bfloat16)
    complete_keys, complete_values = (
        lax.all_gather(keys_own.reshape(seq_count, seq_rows, -1), "ctx", axis=1, tiled=True),
        lax.all_gather(values_own.reshape(seq_count, seq_rows, -1), "ctx", axis=1, tiled=True),
    )
    query_rows4 = query_matrix.reshape(row_total, KEY_VALUE_HEADS, query_group_width, HEAD_SIZE)
    member = 0
    heads_one, lse_one = attend_forward(
        query_rows4,
        complete_keys[member],
        complete_values[member],
        query_rows,
        block_sizes[member],
        score_scale,
    )
    attn_flat = heads_one.transpose(2, 0, 1, 3).reshape(row_total, QUERY_HEADS * HEAD_SIZE)
    attn_low = attn_flat.astype(jnp.bfloat16)
    mixed_rows = inputs + product(attn_low, out_w)
    inv_two = lax.rsqrt(jnp.mean(mixed_rows * mixed_rows, -1, keepdims=True) + EPSILON)
    normed_two = mixed_rows * inv_two
    hidden_two = (normed_two * gain_two).astype(jnp.bfloat16)
    gate_pre = product(hidden_two, gate_w)
    up_pre = product(hidden_two, up_w)
    sigmoid_gate = jax.nn.sigmoid(gate_pre)
    silu_gate = gate_pre * sigmoid_gate
    inner_act = (silu_gate * up_pre).astype(jnp.bfloat16)
    result = mixed_rows + product(inner_act, down_w)
    output = result.astype(jnp.bfloat16).reshape(seq_count, seq_rows, width)
    back_parts = (
        lax.all_gather(w_query, "ctx", axis=0, tiled=True),
        lax.all_gather(w_key, "ctx", axis=0, tiled=True),
        lax.all_gather(w_value, "ctx", axis=0, tiled=True),
        lax.all_gather(w_out, "ctx", axis=0, tiled=True),
        lax.all_gather(w_gate, "ctx", axis=0, tiled=True),
        lax.all_gather(w_up, "ctx", axis=0, tiled=True),
        lax.all_gather(w_down, "ctx", axis=0, tiled=True),
    )
    back_whole = (
        lax.all_gather(back_parts[0], "dp", axis=1, tiled=True),
        lax.all_gather(back_parts[1], "dp", axis=1, tiled=True),
        lax.all_gather(back_parts[2], "dp", axis=1, tiled=True),
        lax.all_gather(back_parts[3], "dp", axis=1, tiled=True),
        lax.all_gather(back_parts[4], "dp", axis=1, tiled=True),
        lax.all_gather(back_parts[5], "dp", axis=1, tiled=True),
        lax.all_gather(back_parts[6], "dp", axis=1, tiled=True),
    )
    back_query, back_key, back_value, back_out, back_gate, back_up, back_down = back_whole
    grad_top = cotangent.reshape(row_total, width)
    grad_down = jnp.einsum("tf,td->fd", inner_act, grad_top, preferred_element_type=jnp.float32)
    grad_inner = jnp.einsum("td,fd->tf", grad_top, back_down, preferred_element_type=jnp.float32)
    grad_gate = (
        grad_inner * up_pre * sigmoid_gate * (1.0 + gate_pre * (1.0 - sigmoid_gate))
    ).astype(jnp.bfloat16)
    grad_upval = (grad_inner * silu_gate).astype(jnp.bfloat16)
    grad_gatew = jnp.einsum("td,tf->df", hidden_two, grad_gate, preferred_element_type=jnp.float32)
    grad_upw = jnp.einsum("td,tf->df", hidden_two, grad_upval, preferred_element_type=jnp.float32)
    grad_hidden_two = jnp.einsum(
        "tf,df->td", grad_gate, back_gate, preferred_element_type=jnp.float32
    ) + jnp.einsum("tf,df->td", grad_upval, back_up, preferred_element_type=jnp.float32)
    grad_gain_two = jnp.sum(grad_hidden_two * normed_two, 0)
    grad_mixed = grad_top.astype(jnp.float32) + norm_back(
        grad_hidden_two * gain_two, normed_two, inv_two
    )
    grad_branch = grad_mixed.astype(jnp.bfloat16)
    grad_outw = jnp.einsum("tq,td->qd", attn_low, grad_branch, preferred_element_type=jnp.float32)
    attention_gradient = jnp.einsum(
        "td,qd->tq", grad_branch, back_out, preferred_element_type=jnp.float32
    ).astype(jnp.bfloat16)
    head_gradients = attention_gradient.reshape(
        row_total, KEY_VALUE_HEADS, query_group_width, HEAD_SIZE
    )
    row_delta = jnp.einsum("tkgd,kgtd->kgt", head_gradients.astype(jnp.float32), heads_one)
    member = 0
    grad_q_one, grad_k_one, grad_v_one = attend_backward(
        query_rows4,
        head_gradients,
        lse_one,
        row_delta,
        complete_keys[member],
        complete_values[member],
        query_rows,
        block_sizes[member],
        score_scale,
    )
    key_grads = [grad_k_one]
    value_grads = [grad_v_one]
    grad_keys_all = jnp.stack(key_grads, 0)
    grad_values_all = jnp.stack(value_grads, 0)
    grad_keys_own, grad_values_own = (
        lax.psum_scatter(grad_keys_all, "ctx", scatter_dimension=1, tiled=True),
        lax.psum_scatter(grad_values_all, "ctx", scatter_dimension=1, tiled=True),
    )
    grad_keys_own = grad_keys_own.reshape(row_total, -1)
    grad_values_own = grad_values_own.reshape(row_total, -1)
    grad_query_raw = rotate(
        grad_q_one.reshape(row_total, QUERY_HEADS * HEAD_SIZE) * score_scale, angles, False
    ).astype(jnp.bfloat16)
    grad_key_raw = rotate(grad_keys_own * score_scale, angles, False).astype(jnp.bfloat16)
    grad_value_raw = grad_values_own.astype(jnp.bfloat16)
    grad_queryw = jnp.einsum(
        "td,tq->dq", hidden_one, grad_query_raw, preferred_element_type=jnp.float32
    )
    grad_keyw = jnp.einsum(
        "td,tq->dq", hidden_one, grad_key_raw, preferred_element_type=jnp.float32
    )
    grad_valuew = jnp.einsum(
        "td,tq->dq", hidden_one, grad_value_raw, preferred_element_type=jnp.float32
    )
    grad_hidden_one = jnp.einsum(
        "tq,dq->td", grad_query_raw, back_query, preferred_element_type=jnp.float32
    )
    grad_hidden_one = grad_hidden_one + jnp.einsum(
        "tq,dq->td", grad_key_raw, back_key, preferred_element_type=jnp.float32
    )
    grad_hidden_one = grad_hidden_one + jnp.einsum(
        "tq,dq->td", grad_value_raw, back_value, preferred_element_type=jnp.float32
    )
    grad_gain_one = jnp.sum(grad_hidden_one * normed_one, 0)
    grad_input = grad_mixed + norm_back(grad_hidden_one * gain_one, normed_one, inv_one)
    input_grad = grad_input.astype(jnp.bfloat16).reshape(seq_count, seq_rows, width)
    summed_rows = (
        lax.psum_scatter(grad_queryw, "ctx", scatter_dimension=0, tiled=True),
        lax.psum_scatter(grad_keyw, "ctx", scatter_dimension=0, tiled=True),
        lax.psum_scatter(grad_valuew, "ctx", scatter_dimension=0, tiled=True),
        lax.psum_scatter(grad_outw, "ctx", scatter_dimension=0, tiled=True),
        lax.psum_scatter(grad_gatew, "ctx", scatter_dimension=0, tiled=True),
        lax.psum_scatter(grad_upw, "ctx", scatter_dimension=0, tiled=True),
        lax.psum_scatter(grad_down, "ctx", scatter_dimension=0, tiled=True),
        lax.psum_scatter(grad_gain_one, "ctx", scatter_dimension=0, tiled=True),
        lax.psum_scatter(grad_gain_two, "ctx", scatter_dimension=0, tiled=True),
    )
    final_w = (
        lax.psum_scatter(
            summed_rows[0].astype(jnp.bfloat16), "dp", scatter_dimension=1, tiled=True
        ).astype(jnp.float32),
        lax.psum_scatter(
            summed_rows[1].astype(jnp.bfloat16), "dp", scatter_dimension=1, tiled=True
        ).astype(jnp.float32),
        lax.psum_scatter(
            summed_rows[2].astype(jnp.bfloat16), "dp", scatter_dimension=1, tiled=True
        ).astype(jnp.float32),
        lax.psum_scatter(
            summed_rows[3].astype(jnp.bfloat16), "dp", scatter_dimension=1, tiled=True
        ).astype(jnp.float32),
        lax.psum_scatter(
            summed_rows[4].astype(jnp.bfloat16), "dp", scatter_dimension=1, tiled=True
        ).astype(jnp.float32),
        lax.psum_scatter(
            summed_rows[5].astype(jnp.bfloat16), "dp", scatter_dimension=1, tiled=True
        ).astype(jnp.float32),
        lax.psum_scatter(
            summed_rows[6].astype(jnp.bfloat16), "dp", scatter_dimension=1, tiled=True
        ).astype(jnp.float32),
    )
    final_gains = lax.psum((summed_rows[7], summed_rows[8]), "dp")
    return (
        output,
        input_grad,
        final_gains[0],
        final_w[0],
        final_w[1],
        final_w[2],
        final_w[3],
        final_gains[1],
        final_w[4],
        final_w[5],
        final_w[6],
    )


MESH = pl.DeviceIdType.MESH
F32 = jnp.float32
BF16 = jnp.bfloat16


def dot_nn(a, b):
    return lax.dot_general(a, b, (((1,), (0,)), ((), ())), preferred_element_type=F32)


def dot_nt(a, b):
    return lax.dot_general(a, b, (((1,), (1,)), ((), ())), preferred_element_type=F32)


def dot_tn(a, b):
    return lax.dot_general(a, b, (((0,), (0,)), ((), ())), preferred_element_type=F32)


class Wires:
    def __init__(self, send_sems, recv_sems):
        self.send_sems, self.recv_sems = send_sems, recv_sems
        self.sends = 0
        self.recvs = 0
        self.pending = []

    def slots(self, count):
        first = self.recvs
        self.recvs += count
        return first

    def send(self, src, dst, slot, device, is_self=None, only=None):
        mine = self.sends
        self.sends += 1
        remote = pltpu.make_async_remote_copy(
            src_ref=src,
            dst_ref=dst,
            send_sem=self.send_sems.at[mine],
            recv_sem=self.recv_sems.at[slot],
            device_id=device,
            device_id_type=MESH,
        )
        if only is not None:

            @pl.when(only)
            def _():
                remote.start()

            def finish():
                @pl.when(only)
                def _():
                    remote.wait_send()

        elif is_self is None:
            remote.start()
            finish = remote.wait_send
        else:
            local = pltpu.make_async_copy(src, dst, self.recv_sems.at[slot])

            @pl.when(is_self)
            def _():
                local.start()

            @pl.when(jnp.logical_not(is_self))
            def _():
                remote.start()

            def finish():
                @pl.when(jnp.logical_not(is_self))
                def _():
                    remote.wait_send()

        self.pending.append(finish)
        return finish

    def keep(self, src, dst, slot):
        pltpu.make_async_copy(src, dst, self.recv_sems.at[slot]).start()

    def recv(self, dst, slot):
        pltpu.make_async_copy(dst, dst, self.recv_sems.at[slot]).wait()

    def done(self, finish):
        finish()
        self.pending.remove(finish)

    def drain(self):
        for finish in self.pending:
            finish()
        self.pending = []


N_SEM = 288
FREQUENCY = np.float32(THETA) ** (-(np.arange(HEAD_SIZE // 2, dtype=np.float32) * 2.0 / HEAD_SIZE)).astype(np.float32)


def layer_kernel(
    tok, cot, pos, blk, gain_one, gain_two, wquery, wkey, wvalue, wo, wgate, wup, wdt,
    o_out, o_ing, o_gain_one, o_gain_two, o_q, o_k, o_v, o_o, o_gate, o_up, o_d,
    wqkv, gain, csf, b2, x2, gb, grow, wqz, woz, wq, wok, wg8, wd8, c8, n8, n1, qf, kvf, kv, q6, p6, o6, ab,
    mp, ml, mid, dmid, dmb, dm4, do6, act, pt, l1, s2, l2, l1o, s2o, l2o,
    ggu, lgu, lf, gdt, lgd, sgd, ld, loy, lo, lqy, lqx, lky, lkx, so, sq, sk, lzo, lzq, lzk, kvg, dkv, lx, sx, lkz,
    lg, sg, dqk, send_sems, recv_sems,
):
    net = Wires(send_sems, recv_sems)
    dp = lax.axis_index("dp")
    ctx = lax.axis_index("ctx")
    y, c = dp // 2, lax.rem(dp, 2)
    z, x = ctx // 2, lax.rem(ctx, 2)
    z_hi, z_lo = z // 2, lax.rem(z, 2)
    y_c = y + c - 2 * y * c
    tokens, width = tok.shape
    rows = wquery.shape[0]
    qcols = wo.shape[1]
    kcols = wkey.shape[1]
    ff = wdt.shape[1]
    drows = wdt.shape[0]
    qw = 2 * qcols
    kw = 2 * kcols
    groups = kw // HEAD_SIZE
    per = QUERY_HEADS // KEY_VALUE_HEADS
    heads = groups * per
    keys = kv.shape[1]
    n_ctx = keys // tokens
    scale = HEAD_SIZE ** (-0.5)

    def flip(a, h):
        return 1 - a if h else a

    def zat(k):
        return (z, 2 * z_hi + 1 - z_lo, 2 * (1 - z_hi) + z_lo, 3 - z)[k]

    def dev(yy, cc, zz, xx):
        return (2 * yy + cc, 2 * zz + xx)

    def off(value, step):
        return pl.multiple_of(value * step, step)

    partner = dev(y, 1 - c, z, x)
    middle = z_hi != z_lo

    wqkv[:, 0:qcols] = wquery[...]
    wqkv[:, qcols : qcols + kcols] = wkey[...]
    wqkv[:, qcols + kcols :] = wvalue[...]
    row = lax.broadcasted_iota(jnp.int32, gain.shape, 0)
    gain[...] = jnp.where(
        row == 0, gain_one[...].astype(F32).reshape(1, rows), jnp.where(row == 1, gain_two[...].astype(F32).reshape(1, rows), 1.0)
    )

    barrier = pltpu.get_barrier_semaphore()
    for k in range(4):
        for hx in range(2):
            for hy in range(2):
                for hc in range(2):
                    if k + hx + hy + hc:
                        pl.semaphore_signal(
                            barrier, inc=1,
                            device_id=dev(flip(y, hy), flip(c, hc), zat(k), flip(x, hx)),
                            device_id_type=MESH,
                        )
    pl.semaphore_wait(barrier, 31)

    r_tok = net.slots(3)
    net.send(tok, x2, r_tok, partner)
    r_g = net.slots(8)
    r_wqz, r_wq = net.slots(4), net.slots(16)

    def spread_qkv(k, src):
        zs = zat(k)
        for hx, hy in ((0, 0), (1, 0), (0, 1)):
            net.send(
                src,
                wq.at[c, pl.ds(off(2 * zs + x, rows), rows)],
                r_wq + k * 4 + hx * 2 + c,
                dev(flip(y, hy), y, z, flip(x, hx)),
                is_self=(c == y) if hx + hy == 0 else None,
            )

    def z_start(src, land, slot):
        for k in range(1, 4):
            net.send(src, land(k), slot + k, dev(y, c, zat(k), x), only=middle if k == 3 else None)

    def z_relay(here, there, slot):
        net.send(here, there, slot + 3, dev(y, c, zat(1), x), only=middle)

    z_start(wqkv, lambda k: wqz.at[k - 1], r_wqz)
    spread_qkv(0, wqkv)
    for k in range(4):
        for hx in range(2):
            if k + hx:
                net.send(gain, gb.at[ctx], r_g + 2 * k + hx, dev(y, c, zat(k), flip(x, hx)))

    across = lax.broadcasted_iota(jnp.int32, (tokens, 128), 1)
    entry = lax.rem(across, HEAD_SIZE // 2)
    frequency = jnp.zeros((tokens, 128), F32)
    for i in range(HEAD_SIZE // 2):
        frequency = jnp.where(entry == i, float(FREQUENCY[i]), frequency)
    places = jnp.broadcast_to(pos[...].astype(F32), (tokens, tokens)).T
    angles = places * frequency
    sine = jnp.sin(angles)
    csf[0:tokens, 0:128] = jnp.cos(angles)
    csf[0:tokens, 128:256] = jnp.where(lax.rem(across, HEAD_SIZE) < HEAD_SIZE // 2, -sine, sine)
    inverse = 1.0 / blk[0].astype(F32)
    key = lax.broadcasted_iota(jnp.int32, (8, keys), 1).astype(F32)
    own_block = jnp.floor(jnp.full((8, keys), ctx * tokens, jnp.int32).astype(F32) * inverse)
    b2[0] = jnp.where(jnp.floor(key * inverse) <= own_block, 0.0, VERY_NEGATIVE)
    net.send(csf.at[pl.ds(0, tokens)], csf.at[pl.ds(tokens, tokens)], r_tok + 1, partner)
    net.send(b2.at[0], b2.at[1], r_tok + 2, partner)
    gb[ctx] = gain[...]
    c8[0] = cot[...]

    def normed(values):
        v = values.astype(F32)
        inv = lax.rsqrt(jnp.mean(v * v, -1, keepdims=True) + EPSILON)
        return v * inv, inv

    def gather_x(buf, slot):
        net.send(buf.at[0], buf.at[4], slot + 2, dev(y, c, z, 1 - x))

    def gather_z(buf, slot):
        net.send(buf.at[0], buf.at[1], slot + 4, partner)
        net.send(buf.at[0], buf.at[2], slot + 1, dev(y, c, zat(1), x))

    def gather_pass(buf, slot, h):
        net.recv(buf.at[2 * h], slot + h)
        net.send(buf.at[2 * h], buf.at[2 * h + 1], slot + 4 + h, partner)
        if h == 1:
            net.send(buf.at[2], buf.at[6], slot + 3, dev(y, c, z, 1 - x))

    r_c8 = net.slots(8)
    for k in (1, 2, 3):
        net.recv(wqz.at[k - 1], r_wqz + k)
        if k == 2:
            z_relay(wqz.at[1], wqz.at[2], r_wqz)
        spread_qkv(k, wqz.at[k - 1])
    gather_x(c8, r_c8)

    r_woz, r_wo = net.slots(4), net.slots(16)

    def spread_wo(k, src):
        zs = zat(k)
        core = zs // 2
        for hx, hy in ((0, 0), (1, 0), (0, 1)):
            net.send(
                src,
                wok.at[dp, pl.ds(off(2 * lax.rem(zs, 2) + x, rows), rows)],
                r_wo + lax.rem(zs, 2) * 8 + hx * 4 + hy * 2 + c,
                dev(flip(y, hy), core, z, flip(x, hx)),
                is_self=(c == core) if hx + hy == 0 else None,
            )

    r_gu, r_wd, r_wy = net.slots(16), net.slots(2), net.slots(2)
    home = y_c == z_lo

    def send_ff(m):
        for zh in range(2):
            for hx in range(2):
                net.send(
                    (wgate, wup)[m].at[:, pl.ds(off(flip(x, hx), ff), ff)],
                    wg8.at[m, pl.ds(off(ctx, rows), rows)],
                    r_gu + m * 8 + ctx,
                    dev(y, c, 2 * zh + y_c, flip(x, hx)),
                    is_self=(z == 2 * zh + y_c) if hx == 0 else None,
                )

    ff_passed = []

    def pass_ff(m):
        for i in range(n_ctx):
            at = 2 * zat(i // 2) + flip(x, i % 2)
            part = wg8.at[m, pl.ds(off(at, rows), rows)]
            slot = r_gu + m * 8 + at

            @pl.when(home)
            def _():
                net.recv(part, slot)

            ff_passed.append(net.send(part, part, slot, dev(1 - y, c, z, x), only=home))

    def take_ff(m):
        for i in range(n_ctx):

            @pl.when(jnp.logical_not(home))
            def _():
                net.recv(wg8.at[m, pl.ds(rows * i, rows)], r_gu + m * 8 + i)

    def send_down():
        z_x = z_hi + z_lo - 2 * z_hi * z_lo
        for zh in range(2):
            net.send(
                wdt,
                wd8.at[pl.ds(off(dp, drows), drows)],
                r_wd + c,
                dev(y, z_lo, 2 * zh + z_x, x),
                is_self=jnp.logical_and(z == 2 * zh + z_x, c == z_lo),
            )

    z_start(wo, lambda k: woz.at[k - 1], r_woz)
    spread_wo(0, wo)
    send_ff(0)
    send_ff(1)
    gather_z(c8, r_c8)

    for k in range(4):
        for hx in range(2):
            if k + hx:
                net.recv(gb.at[2 * zat(k) + flip(x, hx)], r_g + 2 * k + hx)
    for t in range(n_ctx):
        grow[:, rows * t : rows * (t + 1)] = gb[t]
    n1[0:tokens] = (normed(tok[...])[0] * grow[0:1]).astype(BF16)
    net.recv(x2, r_tok)
    n1[tokens : 2 * tokens] = (normed(x2[...])[0] * grow[0:1]).astype(BF16)
    net.recv(csf.at[pl.ds(tokens, tokens)], r_tok + 1)
    net.recv(b2.at[1], r_tok + 2)

    for k in range(4):
        at_x = pl.ds(off(2 * zat(k) + x, rows), rows)
        at_o = pl.ds(off(2 * zat(k) + 1 - x, rows), rows)
        slot = r_wq + k * 4

        @pl.when(c == y)
        def _():
            net.recv(wq.at[0, at_o], slot + 2)

        net.send(wq.at[0, at_o], wq.at[0, at_o], slot + 2, dev(1 - y, c, z, x), only=(c == y))

        @pl.when(c != y)
        def _():
            net.recv(wq.at[1, at_x], slot + 1)

        net.send(wq.at[1, at_x], wq.at[1, at_x], slot + 3, dev(y, c, z, 1 - x), only=(c != y))
    for k in range(1, 4):
        net.recv(woz.at[k - 1], r_woz + k)
        if k == 2:
            z_relay(woz.at[1], woz.at[2], r_woz)
        spread_wo(k, woz.at[k - 1])
    for k in range(4):
        at_x = pl.ds(off(2 * zat(k) + x, rows), rows)
        at_o = pl.ds(off(2 * zat(k) + 1 - x, rows), rows)
        slot = r_wq + k * 4

        @pl.when(c == y)
        def _():
            net.recv(wq.at[1, at_x], slot + 1)

        @pl.when(c != y)
        def _():
            net.recv(wq.at[0, at_o], slot + 2)

        net.recv(wq.at[0, at_x], slot)
        net.recv(wq.at[1, at_o], slot + 3)

    lane = lax.broadcasted_iota(jnp.int32, (2 * tokens, 128), 1)
    low_half = lax.rem(lane, HEAD_SIZE) < HEAD_SIZE // 2

    def turn(tile, forward):
        other = jnp.where(low_half, pltpu.roll(tile, 96, 1), pltpu.roll(tile, 32, 1))
        turned = other * csf[:, 128:256]
        return tile * csf[:, 0:128] + (turned if forward else -turned)

    qf[:, qw:] = jnp.zeros((2 * tokens, qf.shape[1] - qw), F32)
    for part in range(2):
        got = dot_nn(n1[...], wq[part])
        qf[:, qcols * part : qcols * (part + 1)] = got[:, :qcols]
        kvf[:, kcols * part : kcols * (part + 1)] = got[:, qcols : qcols + kcols]
        kvf[:, kw + kcols * part : kw + kcols * (part + 1)] = got[:, qcols + kcols :]

    def turn_keys(forward):
        for t in range(kw // 128 + 1):
            tile = kvf[:, 128 * t : 128 * (t + 1)]
            kvf[:, 128 * t : 128 * (t + 1)] = jnp.where(
                128 * t + lane < kw, turn(tile, forward), tile
            )

    turn_keys(True)
    own_keys = pl.ds(off(ctx, tokens), tokens)
    for s in range(2):
        kv[s, own_keys] = kvf[s * tokens : (s + 1) * tokens].astype(BF16)
    r_kz, r_kx = net.slots(8), net.slots(8)

    def kv_part(s, k, hx):
        return kv.at[s, pl.ds(off(2 * zat(k) + flip(x, hx), tokens), tokens)]

    for s in range(2):
        part = kv_part(s, 0, 0)
        z_start(part, lambda k: part, r_kz + 4 * s)
        net.send(part, part, r_kx + 4 * s, dev(y, c, z, 1 - x))

    def pass_kv(s, k):
        part = kv_part(s, k, 0)
        net.recv(part, r_kz + 4 * s + k)
        if k == 2:
            z_relay(part, part, r_kz + 4 * s)
        net.send(part, part, r_kx + 4 * s + k, dev(y, c, z, 1 - x))

    def take_kv(s):
        for k in range(4):
            net.recv(kv_part(s, k, 1), r_kx + 4 * s + k)

    send_down()

    for t in range(qf.shape[1] // 128):
        qf[:, 128 * t : 128 * (t + 1)] = turn(qf[:, 128 * t : 128 * (t + 1)], True) * scale
    for s in range(2):
        for h in range(heads):
            q6[s * groups + h // per, (h % per) * tokens : (h % per + 1) * tokens] = qf[
                s * tokens : (s + 1) * tokens, HEAD_SIZE * h : HEAD_SIZE * (h + 1)
            ].astype(BF16)
    for k in range(1, 4):
        pass_kv(0, k)
    pass_kv(1, 1)
    pass_kv(1, 2)
    for zz in range(2):
        part = wok.at[2 * (1 - y), pl.ds(off(2 * zz + x, rows), rows)]
        net.recv(part, r_wo + zz * 8 + 2)
        net.send(part, part, r_wo + zz * 8 + 6, dev(y, c, z, 1 - x))
        part = wok.at[2 * y + 1, pl.ds(off(2 * zz + 1 - x, rows), rows)]
        net.recv(part, r_wo + zz * 8 + 5)
        net.send(part, part, r_wo + zz * 8 + 7, dev(1 - y, c, z, x))
    pass_ff(0)
    take_kv(0)

    def attend(s, g):
        kg = kv[s, :, HEAD_SIZE * g : HEAD_SIZE * (g + 1)]
        vg = kv[s, :, kw + HEAD_SIZE * g : kw + HEAD_SIZE * (g + 1)]
        scores = dot_nt(q6[s * groups + g], kg) + b2[s, 0:1, :]
        weights = jnp.exp(scores - jnp.max(scores, -1, keepdims=True))
        probs = (weights * (1.0 / jnp.sum(weights, -1, keepdims=True))).astype(BF16)
        p6[s * groups + g] = probs
        got = dot_nn(probs, vg).astype(BF16)
        o6[s * groups + g] = got
        for i in range(per):
            h = g * per + i
            ab[s * tokens : (s + 1) * tokens, HEAD_SIZE * h : HEAD_SIZE * (h + 1)] = got[
                i * tokens : (i + 1) * tokens
            ]

    attend(0, 0)
    pass_kv(1, 3)
    attend(0, 1)
    gather_pass(c8, r_c8, 1)
    attend(0, 2)
    pass_ff(1)
    take_kv(1)
    attend(1, 0)
    attend(1, 1)
    for cc in range(2):
        part = wd8.at[pl.ds(off(2 * y + cc, drows), drows)]
        net.recv(part, r_wd + cc)
        net.send(part, part, r_wy + cc, dev(1 - y, c, z, x))
    attend(1, 2)

    for hx, hy, cc in ((0, 0, 0), (0, 0, 1), (0, 1, 1), (1, 0, 0), (1, 1, 0), (1, 1, 1)):
        for zz in range(2):
            net.recv(
                wok.at[2 * flip(y, hy) + cc, pl.ds(off(2 * zz + flip(x, hx), rows), rows)],
                r_wo + zz * 8 + hx * 4 + hy * 2 + cc,
            )
    for part in range(4):
        got = dot_nn(ab[:, 0:qw], wok[part])
        for s in range(2):
            mp[s, :, qcols * part : qcols * (part + 1)] = got[s * tokens : (s + 1) * tokens]
    r_ml = net.slots(1)
    mp_sent = net.send(mp.at[1], ml, r_ml, partner)
    gather_pass(c8, r_c8, 2)
    gather_pass(c8, r_c8, 3)
    net.recv(ml, r_ml)
    mid[...] = tok[...].astype(F32) + mp[0] + ml[...]
    n8[0] = (normed(mid[...])[0] * grow[1:2]).astype(BF16)
    r_n8 = net.slots(8)
    gather_z(n8, r_n8)
    gather_x(n8, r_n8)

    net.recv(c8.at[1], r_c8 + 4)
    for h in range(1, 4):
        net.recv(c8.at[2 * h + 1], r_c8 + 4 + h)
    take_ff(0)
    take_ff(1)
    for cc in range(2):
        net.recv(wd8.at[pl.ds(off(2 * (1 - y) + cc, drows), drows)], r_wy + cc)

    all_tokens = 8 * tokens

    def feed(i):
        pair = slice(2 * i, 2 * i + 2)
        here = n8[pair].reshape(2 * tokens, width)
        grad_inner = dot_nn(c8[pair].reshape(2 * tokens, width), wd8[...])
        gate = dot_nn(here, wg8[0])
        up = dot_nn(here, wg8[1])
        sig = 1.0 / (1.0 + jnp.exp(-gate))
        silu = gate * sig
        dgate = (grad_inner * up * sig * (1.0 + gate * (1.0 - sig))).astype(BF16)
        dup = (grad_inner * silu).astype(BF16)
        at = 2 * tokens * i
        act[at : at + 2 * tokens] = (silu * up).astype(BF16)
        act[at + all_tokens : at + all_tokens + 2 * tokens] = dgate
        act[at + 2 * all_tokens : at + 2 * all_tokens + 2 * tokens] = dup
        pt[pair] = (dot_nt(dgate, wg8[0]) + dot_nt(dup, wg8[1])).astype(BF16).reshape(2, tokens, width)

    def reduce_start(part, land, slot, h):
        return net.send(part.at[2 * h + 1], land.at[h], slot + h, partner)

    def reduce_pass(part, land, out, land2, slot, h):
        net.recv(land.at[h], slot + h)
        out[h - 1] = (part[2 * h].astype(F32) + land[h].astype(F32)).astype(BF16)
        net.send(
            out.at[h - 1], land2.at[h - 1], slot + 4 + h,
            dev(y, c, zat(h % 2), flip(x, h // 2)),
        )

    def reduce_own(part, land, slot):
        net.recv(land.at[0], slot)
        return part[0].astype(F32) + land[0].astype(F32)

    def reduce_end(land2, slot):
        total = 0.0
        for h in range(1, 4):
            net.recv(land2.at[h - 1], slot + 4 + h)
            total = total + land2[h - 1].astype(F32)
        return total

    r_dn = net.slots(8)
    pt_sent = []
    net.recv(n8.at[1], r_n8 + 4)
    for h in range(4):
        if h:
            gather_pass(n8, r_n8, h)
            net.recv(n8.at[2 * h + 1], r_n8 + 4 + h)
        feed(h)
        pt_sent.append(reduce_start(pt, l1, r_dn, h))
        if h > 1:
            reduce_pass(pt, l1, s2, l2, r_dn, h - 1)
    reduce_pass(pt, l1, s2, l2, r_dn, 3)
    dmid[...] = reduce_own(pt, l1, r_dn)

    def flat(ref, i):
        return ref[:, :, pl.ds(off(i, 128), 128)].reshape(all_tokens, 128)

    def grad_gu(i, carry):
        left = flat(n8, i)
        at = pl.ds(off(i, 128), 128)
        ggu[0, at] = dot_tn(left, act[pl.ds(all_tokens, all_tokens)]).astype(BF16)
        ggu[1, at] = dot_tn(left, act[pl.ds(2 * all_tokens, all_tokens)]).astype(BF16)
        return carry

    def grad_d(i, carry):
        gdt[pl.ds(off(i, 128), 128)] = dot_tn(flat(c8, i), act[pl.ds(0, all_tokens)]).astype(BF16)
        return carry

    def feed_out(i, carry):
        got = dot_nt(act[pl.ds(off(i, 2 * tokens), 2 * tokens)], wd8[...])
        pt[pl.ds(2 * i, 2)] = got.astype(BF16).reshape(2, tokens, width)
        return carry

    r_gd, r_gz = net.slots(1), net.slots(4)
    half = 2 * drows
    lax.fori_loop(0, width // 128, grad_d, 0)
    net.send(gdt.at[pl.ds(off(1 - y, half), half)], lgd, r_gd, dev(1 - y, c, z, x))
    lax.fori_loop(0, width // 128, grad_gu, 0)
    for zt in range(4):
        at = pl.ds(2 * rows * zt, 2 * rows)
        net.send(
            ggu.at[:, at], lgu.at[:, at], r_gz + zt, dev(1 - y, c, z, x),
            only=jnp.logical_not(home),
        )

    total = dmid[...] + reduce_end(l2, r_dn)
    normed_two, inv_two = normed(mid[...])
    total = total * grow[1:2]
    dmid[...] = cot[...].astype(F32) + inv_two * (
        total - normed_two * jnp.mean(total * normed_two, -1, keepdims=True)
    )
    dmb[0] = dmid[...].astype(BF16)
    r_dm = net.slots(1)
    net.send(dmb.at[0], dmb.at[1], r_dm, partner)
    for finish in pt_sent:
        net.done(finish)
    lax.fori_loop(0, 4, feed_out, 0)
    r_out = net.slots(8)
    for h in range(4):
        reduce_start(pt, l1o, r_out, h)

    r_ld = net.slots(2)
    net.recv(lgd, r_gd)
    sgd[...] = (gdt[pl.ds(off(y, half), half)].astype(F32) + lgd[...].astype(F32)).astype(BF16)
    gd_z = 2 * (z_lo + c - 2 * z_lo * c) + c
    for cc in range(2):
        net.send(
            sgd.at[pl.ds(cc * drows, drows)], ld.at[z_hi], r_ld + z_hi, dev(y, cc, gd_z, x),
            is_self=jnp.logical_and(z == gd_z, c == cc),
        )
    net.recv(dmb.at[1], r_dm)

    for part in range(4):
        for s in range(2):
            dm4[part, s * tokens : (s + 1) * tokens] = dmb[s, :, qcols * part : qcols * (part + 1)]
    dattn = dot_nt(dm4[0], wok[0])
    for part in range(1, 4):
        dattn = dattn + dot_nt(dm4[part], wok[part])
    qf[:, 0:qw] = dattn
    for s in range(2):
        for h in range(heads):
            do6[s * groups + h // per, (h % per) * tokens : (h % per + 1) * tokens] = qf[
                s * tokens : (s + 1) * tokens, HEAD_SIZE * h : HEAD_SIZE * (h + 1)
            ].astype(BF16)
    attn_all = ab[:, 0:qw]
    for part in range(4):
        act[qw * part : qw * (part + 1), 0:qcols] = dot_tn(attn_all, dm4[part]).astype(BF16)
    r_gy, r_go = net.slots(2), net.slots(8)
    for cc in range(2):
        net.send(
            act.at[pl.ds(off(2 * (1 - y) + cc, qw), qw)], loy.at[cc], r_gy + cc, dev(1 - y, c, z, x)
        )

    def pass_go():
        for cc in range(2):
            net.recv(loy.at[cc], r_gy + cc)
            at = pl.ds(off(2 * y + cc, qw), qw)
            act[at] = (act[at].astype(F32) + loy[cc].astype(F32)).astype(BF16)
        for hx in (1, 0):
            for hc in range(2):
                for zz in range(2):
                    at = pl.multiple_of((2 * y + flip(c, hc)) * qw + (2 * zz + flip(x, hx)) * rows, rows)
                    src = act.at[pl.ds(at, rows)]
                    dst = lo.at[2 * c + zz, hx]
                    slot = r_go + (2 * c + zz) * 2 + hx
                    if hx + hc == 0:
                        net.keep(src, dst, slot)
                    else:
                        net.send(src, dst, slot, dev(y, flip(c, hc), z, flip(x, hx)))

    def attend_back(s, g):
        at = s * groups + g
        kg = kv[s, :, HEAD_SIZE * g : HEAD_SIZE * (g + 1)]
        vg = kv[s, :, kw + HEAD_SIZE * g : kw + HEAD_SIZE * (g + 1)]
        dout = do6[at]
        delta = jnp.sum(dout.astype(F32) * o6[at].astype(F32), -1, keepdims=True)
        dprob = dot_nt(dout, vg)
        dscore = (p6[at].astype(F32) * (dprob - delta)).astype(BF16)
        dquery = dot_nn(dscore, kg) * scale
        dkeys = dot_tn(q6[at], dscore)
        dvals = dot_tn(dout, p6[at])
        for t in range(n_ctx):
            cols = slice(t * tokens, (t + 1) * tokens)
            dkv[t, s, HEAD_SIZE * g : HEAD_SIZE * (g + 1)] = dkeys[:, cols].astype(BF16)
            dkv[t, s, kw + HEAD_SIZE * g : kw + HEAD_SIZE * (g + 1)] = dvals[:, cols].astype(BF16)
        for i in range(per):
            h = g * per + i
            qf[s * tokens : (s + 1) * tokens, HEAD_SIZE * h : HEAD_SIZE * (h + 1)] = dquery[
                i * tokens : (i + 1) * tokens
            ]

    r_dx, r_dz = net.slots(8), net.slots(8)

    def send_dkv(s):
        for k in (1, 2, 3, 0):
            net.send(
                dkv.at[2 * zat(k) + 1 - x, s], lx.at[k, s], r_dx + 4 * s + k, dev(y, c, z, 1 - x)
            )

    def pass_dkv(s):
        for k in range(1, 4):
            net.recv(lx.at[k, s], r_dx + 4 * s + k)
            sx[k - 1, s] = (dkv[2 * zat(k) + x, s].astype(F32) + lx[k, s].astype(F32)).astype(BF16)
            net.send(sx.at[k - 1, s], lkz.at[k - 1, s], r_dz + 4 * s + k, dev(y, c, zat(k), x))

    for g in range(groups):
        attend_back(0, g)
    send_dkv(0)
    attend_back(1, 0)
    attend_back(1, 1)
    pass_dkv(0)
    attend_back(1, 2)
    send_dkv(1)
    pass_go()
    for t in range(qf.shape[1] // 128):
        qf[:, 128 * t : 128 * (t + 1)] = turn(qf[:, 128 * t : 128 * (t + 1)], False)
    grad = dot_tn(n1[...], qf[:, 0:qw].astype(BF16)).astype(BF16)
    for t in range(n_ctx):
        p6[t // 2, (t % 2) * rows : (t % 2 + 1) * rows, 0:qw] = grad[rows * t : rows * (t + 1)]
    for part in range(2):
        dqk[part, :, 0:qcols] = qf[:, qcols * part : qcols * (part + 1)].astype(BF16)
    r_qy, r_qx, r_zq = net.slots(4), net.slots(4), net.slots(4)
    mine = c == y

    def send_grads(source, land, slot):
        for k in range(4):
            net.send(
                source(zat(k), slice(0, 2)), land.at[zat(k)], slot + k, dev(1 - y, c, z, x),
                only=jnp.logical_not(mine),
            )

    def add_y(source, land, slot, land_x, slot_x):
        for k in range(4):

            @pl.when(mine)
            def _():
                net.recv(land.at[zat(k)], slot + k)
                here = source(zat(k), slice(0, 2))
                here[...] = (here[...].astype(F32) + land[zat(k)].astype(F32)).astype(BF16)

            net.send(
                source(zat(k), 1 - x), land_x.at[k], slot_x + k, dev(y, c, z, 1 - x), only=mine
            )

    def add_x(source, land_x, slot_x, staged, arrived, slot_z):
        wide_part = arrived.shape[2]
        for k in (1, 2, 3, 0):

            @pl.when(mine)
            def _():
                net.recv(land_x.at[k], slot_x + k)
                staged[k] = (source(zat(k), x)[...].astype(F32) + land_x[k].astype(F32)).astype(BF16)

            for cc in range(2):
                first = cc * (staged.shape[2] - wide_part)
                src = staged.at[k, :, pl.ds(first, wide_part)]
                if k:
                    net.send(src, arrived.at[k], slot_z + k, dev(y, cc, zat(k), x), only=mine)
                else:

                    @pl.when(jnp.logical_and(mine, c == cc))
                    def _():
                        net.keep(src, arrived.at[k], slot_z)

                    net.send(
                        src, arrived.at[k], slot_z, dev(y, cc, z, x),
                        only=jnp.logical_and(mine, c != cc),
                    )

    def add_z(out, arrived, slot_z, staged):
        total = 0.0
        for k in (1, 2, 3, 0):
            net.recv(arrived.at[k], slot_z + k)
            total = total + arrived[k].astype(F32)
        count = out.shape[1]
        skip = count - (staged.shape[2] - arrived.shape[2])
        out[...] = jnp.where(c == 0, total[:, 0:count], total[:, skip : skip + count])

    def in_p6(zt, xt):
        at = pl.ds(0, 2 * rows) if isinstance(xt, slice) else pl.ds(off(xt, rows), rows)
        return p6.at[zt, at, pl.ds(0, qf.shape[1])]

    def in_wg8(zt, xt):
        at = pl.ds(off(zt, 2 * rows), 2 * rows) if isinstance(xt, slice) else pl.ds(off(2 * zt + xt, rows), rows)
        return wg8.at[0, at]

    send_grads(in_p6, lqy, r_qy)
    pass_dkv(1)
    r_gf = net.slots(4)
    for k in (3, 2, 1, 0):
        at = pl.ds(off(zat(k), 2 * rows), 2 * rows)

        @pl.when(home)
        def _():
            net.recv(lgu.at[:, at], r_gz + zat(k))
            ggu[:, at] = (ggu[:, at].astype(F32) + lgu[:, at].astype(F32)).astype(BF16)

        for hx in range(2):
            src = ggu.at[:, pl.ds(off(2 * zat(k) + flip(x, hx), rows), rows)]
            dst = lf.at[x, z_hi]
            slot = r_gf + x * 2 + z_hi
            if k + hx:
                net.send(src, dst, slot, dev(y, c, zat(k), flip(x, hx)), only=home)
            else:

                @pl.when(home)
                def _():
                    net.keep(src, dst, slot)

    for h in range(1, 4):
        reduce_pass(pt, l1o, s2o, l2o, r_out, h)
    mid[...] = mid[...] + reduce_own(pt, l1o, r_out)

    def attn_pass(land, out, staged, arrived, send_slot, slot, absolute):
        for k in (1, 2, 3, 0):
            at = zat(k) if absolute else k
            part = 0.0
            for h in range(2):
                net.recv(land.at[at, h], slot + at * 2 + h)
                part = part + land[at, h, :, 0 : out.shape[1]].astype(F32)
            if k == 0:
                out[...] = part
            else:
                staged[k - 1] = part.astype(BF16)
                net.send(staged.at[k - 1], arrived.at[k - 1], send_slot + k, dev(y, c, zat(k), x))

    def attn_end(out, arrived, slot):
        for k in range(1, 4):
            net.recv(arrived.at[k - 1], slot + k)
            out[...] = out[...] + arrived[k - 1].astype(F32)

    r_zo = net.slots(4)
    attn_pass(lo, o_o, so, lzo, r_zo, r_go, True)
    add_y(in_p6, lqy, r_qy, lqx, r_qx)

    for s in range(2):
        net.recv(lx.at[0, s], r_dx + 4 * s)
        total = dkv[2 * z + x, s].astype(F32) + lx[0, s].astype(F32)
        for k in range(1, 4):
            net.recv(lkz.at[k - 1, s], r_dz + 4 * s + k)
            total = total + lkz[k - 1, s].astype(F32)
        kvf[s * tokens : (s + 1) * tokens] = total.T
    turn_keys(False)
    for part in range(2):
        dqk[part, :, qcols : qcols + kcols] = kvf[:, kcols * part : kcols * (part + 1)].astype(BF16)
        dqk[part, :, qcols + kcols :] = kvf[:, kw + kcols * part : kw + kcols * (part + 1)].astype(BF16)
    for finish in ff_passed:
        net.done(finish)
    for part in range(2):
        wg8[0, :, 2 * kcols * part : 2 * kcols * (part + 1)] = dot_tn(
            n1[...], dqk[part, :, qcols:]
        ).astype(BF16)
    r_ky, r_kx2, r_zk = net.slots(4), net.slots(4), net.slots(4)
    send_grads(in_wg8, lky, r_ky)
    net.done(mp_sent)
    got = dot_nt(dqk[0], wq[0]) + dot_nt(dqk[1], wq[1])
    for s in range(2):
        mp[s] = got[s * tokens : (s + 1) * tokens]
    r_dn1 = net.slots(1)
    net.send(mp.at[1], ml, r_dn1, partner)
    add_x(in_p6, lqx, r_qx, sq, lzq, r_zq)
    add_y(in_wg8, lky, r_ky, lkx, r_kx2)
    net.recv(ml, r_dn1)
    total = mp[0] + ml[...]
    normed_one, inv_one = normed(tok[...])
    total = total * grow[0:1]
    o_ing[...] = (
        dmid[...]
        + inv_one * (total - normed_one * jnp.mean(total * normed_one, -1, keepdims=True))
    ).astype(BF16)
    add_x(in_wg8, lkx, r_kx2, sk, lzk, r_zk)

    o_out[...] = (mid[...] + reduce_end(l2o, r_out)).astype(BF16)
    gains = [0.0, 0.0]
    for h in range(2):
        for zh in range(2):
            net.recv(lf.at[h, zh], r_gf + h * 2 + zh)
        for m in range(2):
            got = lf[h, 0, m].astype(F32) + lf[h, 1, m].astype(F32)
            cols = slice(h * ff, (h + 1) * ff)
            (o_gate, o_up)[m][:, cols] = got
            gains[1] = gains[1] + jnp.sum(
                got * (wgate, wup)[m][:, cols].astype(F32), 1, keepdims=True
            )
    for zh in range(2):
        net.recv(ld.at[zh], r_ld + zh)
    o_d[...] = ld[0].astype(F32) + ld[1].astype(F32)
    attn_end(o_o, lzo, r_zo)
    add_z(o_q, lzq, r_zq, sq)
    gains[0] = jnp.sum(o_q[...] * wqkv[:, 0:qcols].astype(F32), 1, keepdims=True)
    add_z(kvg, lzk, r_zk, sk)
    gains[0] = gains[0] + jnp.sum(kvg[...] * wqkv[:, qcols:].astype(F32), 1, keepdims=True)
    o_k[...] = kvg[:, 0:kcols]
    o_v[...] = kvg[:, kcols:]
    column = lax.broadcasted_iota(jnp.int32, (rows, 128), 1)
    both = jnp.where(column == 0, gains[0], jnp.where(column == 1, gains[1], 0.0))
    sg[...] = both.T[0:8]
    r_lg = net.slots(4)
    for h in range(1, 4):
        net.send(sg, lg.at[h - 1], r_lg + h, dev(flip(y, h // 2), flip(c, h % 2), z, x))
    total = sg[...]
    for h in range(1, 4):
        net.recv(lg.at[h - 1], r_lg + h)
        total = total + lg[h - 1]
    total = total / gain[...]
    o_gain_one[...] = total[0:1]
    o_gain_two[...] = total[1:2]
    net.drain()


def hand_over(*refs):
    count = len(refs) // 2
    copies = [pltpu.make_async_copy(refs[i], refs[count + i], refs[-1].at[i]) for i in range(count)]
    for copy in copies:
        copy.start()
    for copy in copies:
        copy.wait()


def run_layer(n_ctx, tok, cot, pos, blk, gain_one, gain_two, wquery, wkey, wvalue, wo, wgate, wup, wdt):
    tokens, width = tok.shape
    rows, qcols = wquery.shape
    packed = qcols + 2 * wkey.shape[1]
    drows, ff = wdt.shape
    keys = n_ctx * tokens
    qw = 2 * qcols
    kw = packed - qcols
    groups = kw // HEAD_SIZE
    per = QUERY_HEADS // KEY_VALUE_HEADS
    stack = per * tokens
    wide = -(-qw // 128) * 128
    out_shape = [
        jax.ShapeDtypeStruct((tokens, width), BF16),
        jax.ShapeDtypeStruct((tokens, width), BF16),
        jax.ShapeDtypeStruct((1, rows), F32),
        jax.ShapeDtypeStruct((1, rows), F32),
        jax.ShapeDtypeStruct((rows, qcols), F32),
        jax.ShapeDtypeStruct((rows, kw // 2), F32),
        jax.ShapeDtypeStruct((rows, kw // 2), F32),
        jax.ShapeDtypeStruct((rows, qcols), F32),
        jax.ShapeDtypeStruct((rows, 2 * ff), F32),
        jax.ShapeDtypeStruct((rows, 2 * ff), F32),
        jax.ShapeDtypeStruct((drows, ff), F32),
    ]

    def vm(*shape, dtype=BF16):
        return pltpu.VMEM(shape, dtype)

    scratch = [
        vm(rows, packed),
        vm(8, rows, dtype=F32),
        vm(2 * tokens, 256, dtype=F32),
        vm(2, 8, keys, dtype=F32),
        vm(tokens, width),
        vm(n_ctx, 8, rows, dtype=F32),
        vm(8, width, dtype=F32),
        vm(3, rows, packed),
        vm(3, rows, qcols),
        vm(2, width, packed),
        vm(4, 4 * rows, qcols),
        vm(2, width, ff),
        vm(width, ff),
        vm(8, tokens, width),
        vm(8, tokens, width),
        vm(2 * tokens, width),
        vm(2 * tokens, wide, dtype=F32),
        vm(2 * tokens, 2 * kw, dtype=F32),
        vm(2, keys, 2 * kw),
        vm(2 * groups, stack, HEAD_SIZE),
        vm(2 * groups, stack, keys),
        vm(2 * groups, stack, HEAD_SIZE),
        vm(2 * tokens, wide),
        vm(2, tokens, width, dtype=F32),
        vm(tokens, width, dtype=F32),
        vm(tokens, width, dtype=F32),
        vm(tokens, width, dtype=F32),
        vm(2, tokens, width),
        vm(4, 2 * tokens, qcols),
        vm(2 * groups, stack, HEAD_SIZE),
        vm(24 * tokens, ff),
        vm(8, tokens, width),
        vm(4, tokens, width),
        vm(3, tokens, width),
        vm(3, tokens, width),
        vm(4, tokens, width),
        vm(3, tokens, width),
        vm(3, tokens, width),
        vm(2, width, ff),
        vm(2, width, ff),
        vm(2, 2, 2, rows, ff),
        vm(width, ff),
        vm(2 * drows, ff),
        vm(2 * drows, ff),
        vm(2, drows, ff),
        vm(2, qw, ff),
        vm(4, 2, rows, ff),
        vm(4, 2 * rows, wide),
        vm(4, rows, wide),
        vm(4, 2 * rows, ff),
        vm(4, rows, ff),
        vm(3, rows, qcols),
        vm(4, rows, wide),
        vm(4, rows, ff),
        vm(3, rows, qcols),
        vm(4, rows, ff),
        vm(4, rows, 256),
        vm(rows, kw, dtype=F32),
        vm(n_ctx, 2, 2 * kw, tokens),
        vm(4, 2, 2 * kw, tokens),
        vm(3, 2, 2 * kw, tokens),
        vm(3, 2, 2 * kw, tokens),
        vm(3, 8, rows, dtype=F32),
        vm(8, rows, dtype=F32),
        vm(2, 2 * tokens, packed),
        pltpu.SemaphoreType.DMA((N_SEM,)),
        pltpu.SemaphoreType.DMA((N_SEM,)),
    ]
    inside = pl.BlockSpec(memory_space=pltpu.VMEM)
    outs = pl.pallas_call(
        layer_kernel,
        out_shape=out_shape,
        in_specs=[inside] * 3 + [pl.BlockSpec(memory_space=pltpu.SMEM)] + [inside] * 9,
        out_specs=[inside] * len(out_shape),
        scratch_shapes=scratch,
        compiler_params=pltpu.CompilerParams(
            collective_id=0, has_side_effects=True, vmem_limit_bytes=VMEM_LIMIT
        ),
        name="layer",
    )(tok, cot, pos, blk, gain_one, gain_two, wquery, wkey, wvalue, wo, wgate, wup, wdt)
    anywhere = pl.BlockSpec(memory_space=pl.ANY)
    return pl.pallas_call(
        hand_over,
        out_shape=out_shape,
        in_specs=[inside] * len(out_shape),
        out_specs=[anywhere] * len(out_shape),
        scratch_shapes=[pltpu.SemaphoreType.DMA((len(out_shape),))],
        name="hand_over",
    )(*outs)


VMEM_LIMIT = 63 * 1024 * 1024


def on_device_plane(
    tokens, positions, block_sizes, attn_gain, w_query, w_key, w_value, w_out, mlp_gain,
    w_gate, w_up, w_down, cotangent,
):
    output, input_grad, g_one, g_two, g_q, g_k, g_v, g_o, g_gate, g_up, g_d = run_layer(
        lax.axis_size("ctx"), tokens[0], cotangent[0], positions, block_sizes, attn_gain,
        mlp_gain, w_query, w_key, w_value, w_out, w_gate, w_up, w_down.T,
    )
    return (
        output[None],
        input_grad[None],
        g_one[0],
        g_q,
        g_k,
        g_v,
        g_o,
        g_two[0],
        g_gate,
        g_up,
        g_d.T,
    )


def solution(mesh):
    placed = (
        P("dp", "ctx", None),
        P("dp", "ctx"),
        P("dp"),
        P("ctx"),
        P("ctx", "dp"),
        P("ctx", "dp"),
        P("ctx", "dp"),
        P("ctx", "dp"),
        P("ctx"),
        P("ctx", "dp"),
        P("ctx", "dp"),
        P("ctx", "dp"),
        P("dp", "ctx", None),
    )
    fits = mesh.shape["dp"] == 4 and mesh.shape["ctx"] == 8
    return jax.shard_map(
        on_device_plane if fits else on_device,
        mesh=mesh,
        in_specs=placed,
        out_specs=(
            P("dp", "ctx", None),
            P("dp", "ctx", None),
            P("ctx"),
            P("ctx", "dp"),
            P("ctx", "dp"),
            P("ctx", "dp"),
            P("ctx", "dp"),
            P("ctx"),
            P("ctx", "dp"),
            P("ctx", "dp"),
            P("ctx", "dp"),
        ),
        check_vma=False,
    )
```

```python
import jax
import jax.numpy as jnp
import numpy as np
from jax import lax
from jax.experimental import pallas as pl
from jax.experimental.pallas import tpu as pltpu
from jax.sharding import PartitionSpec as P

QUERY_HEADS = 18
KEY_VALUE_HEADS = 6
HEAD_SIZE = 64


EPSILON = 1e-05
THETA = 10000.0
VERY_NEGATIVE = -1e30


def product(left, right):
    return jnp.dot(left, right, preferred_element_type=jnp.float32)


def angles_of(place_ids):
    half_dim = HEAD_SIZE // 2
    frequency = THETA ** (-(jnp.arange(half_dim, dtype=jnp.float32) * 2.0 / HEAD_SIZE))
    return place_ids.astype(jnp.float32)[:, None] * frequency[None, :]


def rotate(values, angles, forward):
    row_total = values.shape[0]
    half_dim = angles.shape[1]
    shaped = values.reshape(row_total, -1, 2 * half_dim)
    first_half = shaped[..., :half_dim]
    second = shaped[..., half_dim:]
    cosine = jnp.cos(angles)[:, None, :]
    sine_vals = jnp.sin(angles)[:, None, :]
    if forward:
        rotated = jnp.concatenate(
            [first_half * cosine - second * sine_vals, second * cosine + first_half * sine_vals], -1
        )
    else:
        rotated = jnp.concatenate(
            [first_half * cosine + second * sine_vals, second * cosine - first_half * sine_vals], -1
        )
    return rotated.reshape(row_total, -1)


def norm_back(grad_normed, normed, inverse):
    return inverse * (grad_normed - normed * jnp.mean(grad_normed * normed, -1, keepdims=True))


def visible(query_rows, key_rows, block_len):
    return ((key_rows // block_len)[None, :] <= (query_rows // block_len)[:, None])[None, None]


def attend_forward(query_rows4, complete_keys, complete_values, query_rows, block_len, score_scale):
    key_count = complete_keys.shape[0]
    key_row_width = 512
    block_list = key_count // key_row_width
    query_group_width = QUERY_HEADS // KEY_VALUE_HEADS
    row_total = query_rows4.shape[0]
    key_block_list = complete_keys.reshape(block_list, key_row_width, KEY_VALUE_HEADS, HEAD_SIZE)
    value_block_list = complete_values.reshape(
        block_list, key_row_width, KEY_VALUE_HEADS, HEAD_SIZE
    )
    last_block = query_rows[-1] // block_len

    def advance(carried, inputs):
        key_blk, val_blk, first_key = inputs
        key_rows = first_key + jnp.arange(key_row_width, dtype=jnp.int32)

        def compute(current):
            run_max, run_sum, accum = current
            scores = (
                jnp.einsum(
                    "tkgd,nkd->kgtn", query_rows4, key_blk, preferred_element_type=jnp.float32
                )
                * score_scale
            )
            allowed = visible(query_rows, key_rows, block_len)
            scores = jnp.where(allowed, scores, VERY_NEGATIVE)
            new_max = jnp.maximum(run_max, jnp.max(scores, -1))
            weights = jnp.where(allowed, jnp.exp(scores - new_max[..., None]), 0.0)
            factor = jnp.exp(run_max - new_max)
            new_sum = run_sum * factor + jnp.sum(weights, -1)
            accum = accum * factor[..., None] + jnp.einsum(
                "kgtn,nkd->kgtd",
                weights.astype(jnp.bfloat16),
                val_blk,
                preferred_element_type=jnp.float32,
            )
            return (new_max, new_sum, accum)

        return (
            lax.cond(
                first_key // block_len > last_block, lambda unchanged: unchanged, compute, carried
            ),
            None,
        )

    start_state = (
        jnp.full((KEY_VALUE_HEADS, query_group_width, row_total), VERY_NEGATIVE, jnp.float32),
        jnp.zeros((KEY_VALUE_HEADS, query_group_width, row_total), jnp.float32),
        jnp.zeros((KEY_VALUE_HEADS, query_group_width, row_total, HEAD_SIZE), jnp.float32),
    )
    firsts = jnp.arange(block_list, dtype=jnp.int32) * key_row_width
    final_state, unused = lax.scan(advance, start_state, (key_block_list, value_block_list, firsts))
    run_max, run_sum, accum = final_state
    return (accum / run_sum[..., None], run_max + jnp.log(run_sum))


def attend_backward(
    query_rows4,
    head_gradients,
    log_sums,
    row_delta,
    complete_keys,
    complete_values,
    query_rows,
    block_len,
    score_scale,
):
    key_count = complete_keys.shape[0]
    key_row_width = 512
    block_list = key_count // key_row_width
    query_group_width = QUERY_HEADS // KEY_VALUE_HEADS
    row_total = query_rows4.shape[0]
    key_block_list = complete_keys.reshape(block_list, key_row_width, KEY_VALUE_HEADS, HEAD_SIZE)
    value_block_list = complete_values.reshape(
        block_list, key_row_width, KEY_VALUE_HEADS, HEAD_SIZE
    )
    last_block = query_rows[-1] // block_len

    def advance(grad_query, inputs):
        key_blk, val_blk, first_key = inputs
        key_rows = first_key + jnp.arange(key_row_width, dtype=jnp.int32)

        def compute(current):
            scores = (
                jnp.einsum(
                    "tkgd,nkd->kgtn", query_rows4, key_blk, preferred_element_type=jnp.float32
                )
                * score_scale
            )
            allowed = visible(query_rows, key_rows, block_len)
            prob_vals = jnp.where(allowed, jnp.exp(scores - log_sums[..., None]), 0.0)
            grad_prob = jnp.einsum(
                "tkgd,nkd->kgtn", head_gradients, val_blk, preferred_element_type=jnp.float32
            )
            grad_score = (prob_vals * (grad_prob - row_delta[..., None])).astype(jnp.bfloat16)
            current = current + jnp.einsum(
                "kgtn,nkd->tkgd", grad_score, key_blk, preferred_element_type=jnp.float32
            )
            grad_key = jnp.einsum(
                "kgtn,tkgd->nkd", grad_score, query_rows4, preferred_element_type=jnp.float32
            )
            grad_value = jnp.einsum(
                "kgtn,tkgd->nkd",
                prob_vals.astype(jnp.bfloat16),
                head_gradients,
                preferred_element_type=jnp.float32,
            )
            return (current, (grad_key, grad_value))

        def nothing(current):
            empty_block = jnp.zeros((key_row_width, KEY_VALUE_HEADS, HEAD_SIZE), jnp.float32)
            return (current, (empty_block, empty_block))

        return lax.cond(first_key // block_len > last_block, nothing, compute, grad_query)

    firsts = jnp.arange(block_list, dtype=jnp.int32) * key_row_width
    initial_gradient = jnp.zeros(
        (row_total, KEY_VALUE_HEADS, query_group_width, HEAD_SIZE), jnp.float32
    )
    grad_query, stacked_rows = lax.scan(
        advance, initial_gradient, (key_block_list, value_block_list, firsts)
    )
    key_gradients = stacked_rows[0].reshape(key_count, KEY_VALUE_HEADS * HEAD_SIZE)
    value_gradients = stacked_rows[1].reshape(key_count, KEY_VALUE_HEADS * HEAD_SIZE)
    return (grad_query, key_gradients, value_gradients)


def on_device(
    tokens,
    positions,
    block_sizes,
    attn_gain,
    w_query,
    w_key,
    w_value,
    w_out,
    mlp_gain,
    w_gate,
    w_up,
    w_down,
    cotangent,
):
    row_parts = (
        lax.all_gather(w_query, "ctx", axis=0, tiled=True),
        lax.all_gather(w_key, "ctx", axis=0, tiled=True),
        lax.all_gather(w_value, "ctx", axis=0, tiled=True),
        lax.all_gather(w_out, "ctx", axis=0, tiled=True),
        lax.all_gather(w_gate, "ctx", axis=0, tiled=True),
        lax.all_gather(w_up, "ctx", axis=0, tiled=True),
        lax.all_gather(w_down, "ctx", axis=0, tiled=True),
        lax.all_gather(attn_gain, "ctx", axis=0, tiled=True),
        lax.all_gather(mlp_gain, "ctx", axis=0, tiled=True),
    )
    whole_w = (
        lax.all_gather(row_parts[0], "dp", axis=1, tiled=True),
        lax.all_gather(row_parts[1], "dp", axis=1, tiled=True),
        lax.all_gather(row_parts[2], "dp", axis=1, tiled=True),
        lax.all_gather(row_parts[3], "dp", axis=1, tiled=True),
        lax.all_gather(row_parts[4], "dp", axis=1, tiled=True),
        lax.all_gather(row_parts[5], "dp", axis=1, tiled=True),
        lax.all_gather(row_parts[6], "dp", axis=1, tiled=True),
    )
    query_w, key_w, value_w, out_w, gate_w, up_w, down_w = whole_w
    gain_one = row_parts[7].astype(jnp.float32)
    gain_two = row_parts[8].astype(jnp.float32)
    seq_count = tokens.shape[0]
    seq_rows = tokens.shape[1]
    width = tokens.shape[2]
    inputs = tokens.reshape(seq_count * seq_rows, width).astype(jnp.float32)
    row_total = inputs.shape[0]
    query_group_width = QUERY_HEADS // KEY_VALUE_HEADS
    query_rows = lax.axis_index("ctx") * seq_rows + jnp.arange(seq_rows, dtype=jnp.int32)
    angles = angles_of(positions.reshape(-1))
    score_scale = HEAD_SIZE ** (-0.5)
    inv_one = lax.rsqrt(jnp.mean(inputs * inputs, -1, keepdims=True) + EPSILON)
    normed_one = inputs * inv_one
    hidden_one = (normed_one * gain_one).astype(jnp.bfloat16)
    query_matrix = rotate(product(hidden_one, query_w), angles, True).astype(jnp.bfloat16)
    keys_own = rotate(product(hidden_one, key_w), angles, True).astype(jnp.bfloat16)
    values_own = product(hidden_one, value_w).astype(jnp.bfloat16)
    complete_keys, complete_values = (
        lax.all_gather(keys_own.reshape(seq_count, seq_rows, -1), "ctx", axis=1, tiled=True),
        lax.all_gather(values_own.reshape(seq_count, seq_rows, -1), "ctx", axis=1, tiled=True),
    )
    query_rows4 = query_matrix.reshape(row_total, KEY_VALUE_HEADS, query_group_width, HEAD_SIZE)
    member = 0
    heads_one, lse_one = attend_forward(
        query_rows4,
        complete_keys[member],
        complete_values[member],
        query_rows,
        block_sizes[member],
        score_scale,
    )
    attn_flat = heads_one.transpose(2, 0, 1, 3).reshape(row_total, QUERY_HEADS * HEAD_SIZE)
    attn_low = attn_flat.astype(jnp.bfloat16)
    mixed_rows = inputs + product(attn_low, out_w)
    inv_two = lax.rsqrt(jnp.mean(mixed_rows * mixed_rows, -1, keepdims=True) + EPSILON)
    normed_two = mixed_rows * inv_two
    hidden_two = (normed_two * gain_two).astype(jnp.bfloat16)
    gate_pre = product(hidden_two, gate_w)
    up_pre = product(hidden_two, up_w)
    sigmoid_gate = jax.nn.sigmoid(gate_pre)
    silu_gate = gate_pre * sigmoid_gate
    inner_act = (silu_gate * up_pre).astype(jnp.bfloat16)
    result = mixed_rows + product(inner_act, down_w)
    output = result.astype(jnp.bfloat16).reshape(seq_count, seq_rows, width)
    back_parts = (
        lax.all_gather(w_query, "ctx", axis=0, tiled=True),
        lax.all_gather(w_key, "ctx", axis=0, tiled=True),
        lax.all_gather(w_value, "ctx", axis=0, tiled=True),
        lax.all_gather(w_out, "ctx", axis=0, tiled=True),
        lax.all_gather(w_gate, "ctx", axis=0, tiled=True),
        lax.all_gather(w_up, "ctx", axis=0, tiled=True),
        lax.all_gather(w_down, "ctx", axis=0, tiled=True),
    )
    back_whole = (
        lax.all_gather(back_parts[0], "dp", axis=1, tiled=True),
        lax.all_gather(back_parts[1], "dp", axis=1, tiled=True),
        lax.all_gather(back_parts[2], "dp", axis=1, tiled=True),
        lax.all_gather(back_parts[3], "dp", axis=1, tiled=True),
        lax.all_gather(back_parts[4], "dp", axis=1, tiled=True),
        lax.all_gather(back_parts[5], "dp", axis=1, tiled=True),
        lax.all_gather(back_parts[6], "dp", axis=1, tiled=True),
    )
    back_query, back_key, back_value, back_out, back_gate, back_up, back_down = back_whole
    grad_top = cotangent.reshape(row_total, width)
    grad_down = jnp.einsum("tf,td->fd", inner_act, grad_top, preferred_element_type=jnp.float32)
    grad_inner = jnp.einsum("td,fd->tf", grad_top, back_down, preferred_element_type=jnp.float32)
    grad_gate = (
        grad_inner * up_pre * sigmoid_gate * (1.0 + gate_pre * (1.0 - sigmoid_gate))
    ).astype(jnp.bfloat16)
    grad_upval = (grad_inner * silu_gate).astype(jnp.bfloat16)
    grad_gatew = jnp.einsum("td,tf->df", hidden_two, grad_gate, preferred_element_type=jnp.float32)
    grad_upw = jnp.einsum("td,tf->df", hidden_two, grad_upval, preferred_element_type=jnp.float32)
    grad_hidden_two = jnp.einsum(
        "tf,df->td", grad_gate, back_gate, preferred_element_type=jnp.float32
    ) + jnp.einsum("tf,df->td", grad_upval, back_up, preferred_element_type=jnp.float32)
    grad_gain_two = jnp.sum(grad_hidden_two * normed_two, 0)
    grad_mixed = grad_top.astype(jnp.float32) + norm_back(
        grad_hidden_two * gain_two, normed_two, inv_two
    )
    grad_branch = grad_mixed.astype(jnp.bfloat16)
    grad_outw = jnp.einsum("tq,td->qd", attn_low, grad_branch, preferred_element_type=jnp.float32)
    attention_gradient = jnp.einsum(
        "td,qd->tq", grad_branch, back_out, preferred_element_type=jnp.float32
    ).astype(jnp.bfloat16)
    head_gradients = attention_gradient.reshape(
        row_total, KEY_VALUE_HEADS, query_group_width, HEAD_SIZE
    )
    row_delta = jnp.einsum("tkgd,kgtd->kgt", head_gradients.astype(jnp.float32), heads_one)
    member = 0
    grad_q_one, grad_k_one, grad_v_one = attend_backward(
        query_rows4,
        head_gradients,
        lse_one,
        row_delta,
        complete_keys[member],
        complete_values[member],
        query_rows,
        block_sizes[member],
        score_scale,
    )
    key_grads = [grad_k_one]
    value_grads = [grad_v_one]
    grad_keys_all = jnp.stack(key_grads, 0)
    grad_values_all = jnp.stack(value_grads, 0)
    grad_keys_own, grad_values_own = (
        lax.psum_scatter(grad_keys_all, "ctx", scatter_dimension=1, tiled=True),
        lax.psum_scatter(grad_values_all, "ctx", scatter_dimension=1, tiled=True),
    )
    grad_keys_own = grad_keys_own.reshape(row_total, -1)
    grad_values_own = grad_values_own.reshape(row_total, -1)
    grad_query_raw = rotate(
        grad_q_one.reshape(row_total, QUERY_HEADS * HEAD_SIZE) * score_scale, angles, False
    ).astype(jnp.bfloat16)
    grad_key_raw = rotate(grad_keys_own * score_scale, angles, False).astype(jnp.bfloat16)
    grad_value_raw = grad_values_own.astype(jnp.bfloat16)
    grad_queryw = jnp.einsum(
        "td,tq->dq", hidden_one, grad_query_raw, preferred_element_type=jnp.float32
    )
    grad_keyw = jnp.einsum(
        "td,tq->dq", hidden_one, grad_key_raw, preferred_element_type=jnp.float32
    )
    grad_valuew = jnp.einsum(
        "td,tq->dq", hidden_one, grad_value_raw, preferred_element_type=jnp.float32
    )
    grad_hidden_one = jnp.einsum(
        "tq,dq->td", grad_query_raw, back_query, preferred_element_type=jnp.float32
    )
    grad_hidden_one = grad_hidden_one + jnp.einsum(
        "tq,dq->td", grad_key_raw, back_key, preferred_element_type=jnp.float32
    )
    grad_hidden_one = grad_hidden_one + jnp.einsum(
        "tq,dq->td", grad_value_raw, back_value, preferred_element_type=jnp.float32
    )
    grad_gain_one = jnp.sum(grad_hidden_one * normed_one, 0)
    grad_input = grad_mixed + norm_back(grad_hidden_one * gain_one, normed_one, inv_one)
    input_grad = grad_input.astype(jnp.bfloat16).reshape(seq_count, seq_rows, width)
    summed_rows = (
        lax.psum_scatter(grad_queryw, "ctx", scatter_dimension=0, tiled=True),
        lax.psum_scatter(grad_keyw, "ctx", scatter_dimension=0, tiled=True),
        lax.psum_scatter(grad_valuew, "ctx", scatter_dimension=0, tiled=True),
        lax.psum_scatter(grad_outw, "ctx", scatter_dimension=0, tiled=True),
        lax.psum_scatter(grad_gatew, "ctx", scatter_dimension=0, tiled=True),
        lax.psum_scatter(grad_upw, "ctx", scatter_dimension=0, tiled=True),
        lax.psum_scatter(grad_down, "ctx", scatter_dimension=0, tiled=True),
        lax.psum_scatter(grad_gain_one, "ctx", scatter_dimension=0, tiled=True),
        lax.psum_scatter(grad_gain_two, "ctx", scatter_dimension=0, tiled=True),
    )
    final_w = (
        lax.psum_scatter(
            summed_rows[0].astype(jnp.bfloat16), "dp", scatter_dimension=1, tiled=True
        ).astype(jnp.float32),
        lax.psum_scatter(
            summed_rows[1].astype(jnp.bfloat16), "dp", scatter_dimension=1, tiled=True
        ).astype(jnp.float32),
        lax.psum_scatter(
            summed_rows[2].astype(jnp.bfloat16), "dp", scatter_dimension=1, tiled=True
        ).astype(jnp.float32),
        lax.psum_scatter(
            summed_rows[3].astype(jnp.bfloat16), "dp", scatter_dimension=1, tiled=True
        ).astype(jnp.float32),
        lax.psum_scatter(
            summed_rows[4].astype(jnp.bfloat16), "dp", scatter_dimension=1, tiled=True
        ).astype(jnp.float32),
        lax.psum_scatter(
            summed_rows[5].astype(jnp.bfloat16), "dp", scatter_dimension=1, tiled=True
        ).astype(jnp.float32),
        lax.psum_scatter(
            summed_rows[6].astype(jnp.bfloat16), "dp", scatter_dimension=1, tiled=True
        ).astype(jnp.float32),
    )
    final_gains = lax.psum((summed_rows[7], summed_rows[8]), "dp")
    return (
        output,
        input_grad,
        final_gains[0],
        final_w[0],
        final_w[1],
        final_w[2],
        final_w[3],
        final_gains[1],
        final_w[4],
        final_w[5],
        final_w[6],
    )


MESH = pl.DeviceIdType.MESH
F32 = jnp.float32
BF16 = jnp.bfloat16


def dot_nn(a, b):
    return lax.dot_general(a, b, (((1,), (0,)), ((), ())), preferred_element_type=F32)


def dot_nt(a, b):
    return lax.dot_general(a, b, (((1,), (1,)), ((), ())), preferred_element_type=F32)


def dot_tn(a, b):
    return lax.dot_general(a, b, (((0,), (0,)), ((), ())), preferred_element_type=F32)


class Wires:
    def __init__(self, send_sems, recv_sems):
        self.send_sems, self.recv_sems = send_sems, recv_sems
        self.sends = 0
        self.recvs = 0
        self.pending = []

    def slots(self, count):
        first = self.recvs
        self.recvs += count
        return first

    def send(self, src, dst, slot, device, is_self=None, only=None):
        mine = self.sends
        self.sends += 1
        remote = pltpu.make_async_remote_copy(
            src_ref=src,
            dst_ref=dst,
            send_sem=self.send_sems.at[mine],
            recv_sem=self.recv_sems.at[slot],
            device_id=device,
            device_id_type=MESH,
        )
        if only is not None:

            @pl.when(only)
            def _():
                remote.start()

            def finish():
                @pl.when(only)
                def _():
                    remote.wait_send()

        elif is_self is None:
            remote.start()
            finish = remote.wait_send
        else:
            local = pltpu.make_async_copy(src, dst, self.recv_sems.at[slot])

            @pl.when(is_self)
            def _():
                local.start()

            @pl.when(jnp.logical_not(is_self))
            def _():
                remote.start()

            def finish():
                @pl.when(jnp.logical_not(is_self))
                def _():
                    remote.wait_send()

        self.pending.append(finish)
        return finish

    def keep(self, src, dst, slot):
        pltpu.make_async_copy(src, dst, self.recv_sems.at[slot]).start()

    def recv(self, dst, slot):
        pltpu.make_async_copy(dst, dst, self.recv_sems.at[slot]).wait()

    def done(self, finish):
        finish()
        self.pending.remove(finish)

    def drain(self):
        for finish in self.pending:
            finish()
        self.pending = []


N_SEM = 288
FREQUENCY = np.float32(THETA) ** (-(np.arange(HEAD_SIZE // 2, dtype=np.float32) * 2.0 / HEAD_SIZE)).astype(np.float32)


def layer_kernel(
    tok, cot, pos, blk, gain_one, gain_two, wquery, wkey, wvalue, wo, wgate, wup, wdt,
    o_out, o_ing, o_gain_one, o_gain_two, o_q, o_k, o_v, o_o, o_gate, o_up, o_d,
    wqkv, gain, csf, b2, x2, gb, grow, wqz, woz, wq, wok, wg8, wd8, c8, n8, n1, qf, kvf, kv, q6, p6, o6, ab,
    mp, ml, mid, dmid, dmb, dm4, do6, act, pt, l1, s2, l2, l1o, s2o, l2o,
    ggu, lgu, lf, gdt, lgd, sgd, ld, loy, lo, lqy, lqx, lky, lkx, so, sq, sk, lzo, lzq, lzk, kvg, dkv, lx, sx, lkz,
    lg, sg, dqk, send_sems, recv_sems,
):
    net = Wires(send_sems, recv_sems)
    dp = lax.axis_index("dp")
    ctx = lax.axis_index("ctx")
    y, c = dp // 2, lax.rem(dp, 2)
    z, x = ctx // 2, lax.rem(ctx, 2)
    z_hi, z_lo = z // 2, lax.rem(z, 2)
    y_c = y + c - 2 * y * c
    tokens, width = tok.shape
    rows = wquery.shape[0]
    qcols = wo.shape[1]
    kcols = wkey.shape[1]
    ff = wdt.shape[1]
    drows = wdt.shape[0]
    qw = 2 * qcols
    kw = 2 * kcols
    groups = kw // HEAD_SIZE
    per = QUERY_HEADS // KEY_VALUE_HEADS
    heads = groups * per
    keys = kv.shape[1]
    n_ctx = keys // tokens
    scale = HEAD_SIZE ** (-0.5)

    def flip(a, h):
        return 1 - a if h else a

    def zat(k):
        return (z, 2 * z_hi + 1 - z_lo, 2 * (1 - z_hi) + z_lo, 3 - z)[k]

    def dev(yy, cc, zz, xx):
        return (2 * yy + cc, 2 * zz + xx)

    def off(value, step):
        return pl.multiple_of(value * step, step)

    partner = dev(y, 1 - c, z, x)
    middle = z_hi != z_lo

    wqkv[:, 0:qcols] = wquery[...]
    wqkv[:, qcols : qcols + kcols] = wkey[...]
    wqkv[:, qcols + kcols :] = wvalue[...]
    row = lax.broadcasted_iota(jnp.int32, gain.shape, 0)
    gain[...] = jnp.where(
        row == 0, gain_one[...].astype(F32).reshape(1, rows), jnp.where(row == 1, gain_two[...].astype(F32).reshape(1, rows), 1.0)
    )

    barrier = pltpu.get_barrier_semaphore()
    for k in range(4):
        for hx in range(2):
            for hy in range(2):
                for hc in range(2):
                    if k + hx + hy + hc:
                        pl.semaphore_signal(
                            barrier, inc=1,
                            device_id=dev(flip(y, hy), flip(c, hc), zat(k), flip(x, hx)),
                            device_id_type=MESH,
                        )
    pl.semaphore_wait(barrier, 31)

    r_tok = net.slots(3)
    net.send(tok, x2, r_tok, partner)
    r_g = net.slots(8)
    r_wqz, r_wq = net.slots(4), net.slots(16)

    def spread_qkv(k, src):
        zs = zat(k)
        for hx, hy in ((0, 0), (1, 0), (0, 1)):
            net.send(
                src,
                wq.at[c, pl.ds(off(2 * zs + x, rows), rows)],
                r_wq + k * 4 + hx * 2 + c,
                dev(flip(y, hy), y, z, flip(x, hx)),
                is_self=(c == y) if hx + hy == 0 else None,
            )

    def z_start(src, land, slot):
        for k in range(1, 4):
            net.send(src, land(k), slot + k, dev(y, c, zat(k), x), only=middle if k == 3 else None)

    def z_relay(here, there, slot):
        net.send(here, there, slot + 3, dev(y, c, zat(1), x), only=middle)

    z_start(wqkv, lambda k: wqz.at[k - 1], r_wqz)
    spread_qkv(0, wqkv)
    for k in range(4):
        for hx in range(2):
            if k + hx:
                net.send(gain, gb.at[ctx], r_g + 2 * k + hx, dev(y, c, zat(k), flip(x, hx)))

    across = lax.broadcasted_iota(jnp.int32, (tokens, 128), 1)
    entry = lax.rem(across, HEAD_SIZE // 2)
    frequency = jnp.zeros((tokens, 128), F32)
    for i in range(HEAD_SIZE // 2):
        frequency = jnp.where(entry == i, float(FREQUENCY[i]), frequency)
    places = jnp.broadcast_to(pos[...].astype(F32), (tokens, tokens)).T
    angles = places * frequency
    sine = jnp.sin(angles)
    csf[0:tokens, 0:128] = jnp.cos(angles)
    csf[0:tokens, 128:256] = jnp.where(lax.rem(across, HEAD_SIZE) < HEAD_SIZE // 2, -sine, sine)
    inverse = 1.0 / blk[0].astype(F32)
    key = lax.broadcasted_iota(jnp.int32, (8, keys), 1).astype(F32)
    own_block = jnp.floor(jnp.full((8, keys), ctx * tokens, jnp.int32).astype(F32) * inverse)
    b2[0] = jnp.where(jnp.floor(key * inverse) <= own_block, 0.0, VERY_NEGATIVE)
    net.send(csf.at[pl.ds(0, tokens)], csf.at[pl.ds(tokens, tokens)], r_tok + 1, partner)
    net.send(b2.at[0], b2.at[1], r_tok + 2, partner)
    gb[ctx] = gain[...]
    c8[0] = cot[...]

    def normed(values):
        v = values.astype(F32)
        inv = lax.rsqrt(jnp.mean(v * v, -1, keepdims=True) + EPSILON)
        return v * inv, inv

    def gather_x(buf, slot):
        net.send(buf.at[0], buf.at[4], slot + 2, dev(y, c, z, 1 - x))

    def gather_z(buf, slot):
        net.send(buf.at[0], buf.at[1], slot + 4, partner)
        net.send(buf.at[0], buf.at[2], slot + 1, dev(y, c, zat(1), x))

    def gather_pass(buf, slot, h):
        net.recv(buf.at[2 * h], slot + h)
        net.send(buf.at[2 * h], buf.at[2 * h + 1], slot + 4 + h, partner)
        if h == 1:
            net.send(buf.at[2], buf.at[6], slot + 3, dev(y, c, z, 1 - x))

    r_c8 = net.slots(8)
    for k in (1, 2, 3):
        net.recv(wqz.at[k - 1], r_wqz + k)
        if k == 2:
            z_relay(wqz.at[1], wqz.at[2], r_wqz)
        spread_qkv(k, wqz.at[k - 1])
    gather_x(c8, r_c8)

    r_woz, r_wo = net.slots(4), net.slots(16)

    def spread_wo(k, src):
        zs = zat(k)
        core = zs // 2
        for hx, hy in ((0, 0), (1, 0), (0, 1)):
            net.send(
                src,
                wok.at[dp, pl.ds(off(2 * lax.rem(zs, 2) + x, rows), rows)],
                r_wo + lax.rem(zs, 2) * 8 + hx * 4 + hy * 2 + c,
                dev(flip(y, hy), core, z, flip(x, hx)),
                is_self=(c == core) if hx + hy == 0 else None,
            )

    r_gu, r_wd, r_wy = net.slots(16), net.slots(2), net.slots(2)
    home = y_c == z_lo

    def send_ff(m):
        for zh in range(2):
            for hx in range(2):
                net.send(
                    (wgate, wup)[m].at[:, pl.ds(off(flip(x, hx), ff), ff)],
                    wg8.at[m, pl.ds(off(ctx, rows), rows)],
                    r_gu + m * 8 + ctx,
                    dev(y, c, 2 * zh + y_c, flip(x, hx)),
                    is_self=(z == 2 * zh + y_c) if hx == 0 else None,
                )

    ff_passed = []

    def pass_ff(m):
        for i in range(n_ctx):
            at = 2 * zat(i // 2) + flip(x, i % 2)
            part = wg8.at[m, pl.ds(off(at, rows), rows)]
            slot = r_gu + m * 8 + at

            @pl.when(home)
            def _():
                net.recv(part, slot)

            ff_passed.append(net.send(part, part, slot, dev(1 - y, c, z, x), only=home))

    def take_ff(m):
        for i in range(n_ctx):

            @pl.when(jnp.logical_not(home))
            def _():
                net.recv(wg8.at[m, pl.ds(rows * i, rows)], r_gu + m * 8 + i)

    def send_down():
        z_x = z_hi + z_lo - 2 * z_hi * z_lo
        for zh in range(2):
            net.send(
                wdt,
                wd8.at[pl.ds(off(dp, drows), drows)],
                r_wd + c,
                dev(y, z_lo, 2 * zh + z_x, x),
                is_self=jnp.logical_and(z == 2 * zh + z_x, c == z_lo),
            )

    z_start(wo, lambda k: woz.at[k - 1], r_woz)
    spread_wo(0, wo)
    send_ff(0)
    send_ff(1)
    gather_z(c8, r_c8)

    for k in range(4):
        for hx in range(2):
            if k + hx:
                net.recv(gb.at[2 * zat(k) + flip(x, hx)], r_g + 2 * k + hx)
    for t in range(n_ctx):
        grow[:, rows * t : rows * (t + 1)] = gb[t]
    n1[0:tokens] = (normed(tok[...])[0] * grow[0:1]).astype(BF16)
    net.recv(x2, r_tok)
    n1[tokens : 2 * tokens] = (normed(x2[...])[0] * grow[0:1]).astype(BF16)
    net.recv(csf.at[pl.ds(tokens, tokens)], r_tok + 1)
    net.recv(b2.at[1], r_tok + 2)

    for k in range(4):
        at_x = pl.ds(off(2 * zat(k) + x, rows), rows)
        at_o = pl.ds(off(2 * zat(k) + 1 - x, rows), rows)
        slot = r_wq + k * 4

        @pl.when(c == y)
        def _():
            net.recv(wq.at[0, at_o], slot + 2)

        net.send(wq.at[0, at_o], wq.at[0, at_o], slot + 2, dev(1 - y, c, z, x), only=(c == y))

        @pl.when(c != y)
        def _():
            net.recv(wq.at[1, at_x], slot + 1)

        net.send(wq.at[1, at_x], wq.at[1, at_x], slot + 3, dev(y, c, z, 1 - x), only=(c != y))
    for k in range(1, 4):
        net.recv(woz.at[k - 1], r_woz + k)
        if k == 2:
            z_relay(woz.at[1], woz.at[2], r_woz)
        spread_wo(k, woz.at[k - 1])
    for k in range(4):
        at_x = pl.ds(off(2 * zat(k) + x, rows), rows)
        at_o = pl.ds(off(2 * zat(k) + 1 - x, rows), rows)
        slot = r_wq + k * 4

        @pl.when(c == y)
        def _():
            net.recv(wq.at[1, at_x], slot + 1)

        @pl.when(c != y)
        def _():
            net.recv(wq.at[0, at_o], slot + 2)

        net.recv(wq.at[0, at_x], slot)
        net.recv(wq.at[1, at_o], slot + 3)

    lane = lax.broadcasted_iota(jnp.int32, (2 * tokens, 128), 1)
    low_half = lax.rem(lane, HEAD_SIZE) < HEAD_SIZE // 2

    def turn(tile, forward):
        other = jnp.where(low_half, pltpu.roll(tile, 96, 1), pltpu.roll(tile, 32, 1))
        turned = other * csf[:, 128:256]
        return tile * csf[:, 0:128] + (turned if forward else -turned)

    qf[:, qw:] = jnp.zeros((2 * tokens, qf.shape[1] - qw), F32)
    for part in range(2):
        got = dot_nn(n1[...], wq[part])
        qf[:, qcols * part : qcols * (part + 1)] = got[:, :qcols]
        kvf[:, kcols * part : kcols * (part + 1)] = got[:, qcols : qcols + kcols]
        kvf[:, kw + kcols * part : kw + kcols * (part + 1)] = got[:, qcols + kcols :]

    def turn_keys(forward):
        for t in range(kw // 128 + 1):
            tile = kvf[:, 128 * t : 128 * (t + 1)]
            kvf[:, 128 * t : 128 * (t + 1)] = jnp.where(
                128 * t + lane < kw, turn(tile, forward), tile
            )

    turn_keys(True)
    own_keys = pl.ds(off(ctx, tokens), tokens)
    for s in range(2):
        kv[s, own_keys] = kvf[s * tokens : (s + 1) * tokens].astype(BF16)
    r_kz, r_kx = net.slots(8), net.slots(8)

    def kv_part(s, k, hx):
        return kv.at[s, pl.ds(off(2 * zat(k) + flip(x, hx), tokens), tokens)]

    for s in range(2):
        part = kv_part(s, 0, 0)
        z_start(part, lambda k: part, r_kz + 4 * s)
        net.send(part, part, r_kx + 4 * s, dev(y, c, z, 1 - x))

    def pass_kv(s, k):
        part = kv_part(s, k, 0)
        net.recv(part, r_kz + 4 * s + k)
        if k == 2:
            z_relay(part, part, r_kz + 4 * s)
        net.send(part, part, r_kx + 4 * s + k, dev(y, c, z, 1 - x))

    def take_kv(s):
        for k in range(4):
            net.recv(kv_part(s, k, 1), r_kx + 4 * s + k)

    send_down()

    for t in range(qf.shape[1] // 128):
        qf[:, 128 * t : 128 * (t + 1)] = turn(qf[:, 128 * t : 128 * (t + 1)], True) * scale
    for s in range(2):
        for h in range(heads):
            q6[s * groups + h // per, (h % per) * tokens : (h % per + 1) * tokens] = qf[
                s * tokens : (s + 1) * tokens, HEAD_SIZE * h : HEAD_SIZE * (h + 1)
            ].astype(BF16)
    for k in range(1, 4):
        pass_kv(0, k)
    pass_kv(1, 1)
    pass_kv(1, 2)
    for zz in range(2):
        part = wok.at[2 * (1 - y), pl.ds(off(2 * zz + x, rows), rows)]
        net.recv(part, r_wo + zz * 8 + 2)
        net.send(part, part, r_wo + zz * 8 + 6, dev(y, c, z, 1 - x))
        part = wok.at[2 * y + 1, pl.ds(off(2 * zz + 1 - x, rows), rows)]
        net.recv(part, r_wo + zz * 8 + 5)
        net.send(part, part, r_wo + zz * 8 + 7, dev(1 - y, c, z, x))
    pass_ff(0)
    take_kv(0)

    def attend(s, g):
        kg = kv[s, :, HEAD_SIZE * g : HEAD_SIZE * (g + 1)]
        vg = kv[s, :, kw + HEAD_SIZE * g : kw + HEAD_SIZE * (g + 1)]
        scores = dot_nt(q6[s * groups + g], kg) + b2[s, 0:1, :]
        weights = jnp.exp(scores - jnp.max(scores, -1, keepdims=True))
        probs = (weights * (1.0 / jnp.sum(weights, -1, keepdims=True))).astype(BF16)
        p6[s * groups + g] = probs
        got = dot_nn(probs, vg).astype(BF16)
        o6[s * groups + g] = got
        for i in range(per):
            h = g * per + i
            ab[s * tokens : (s + 1) * tokens, HEAD_SIZE * h : HEAD_SIZE * (h + 1)] = got[
                i * tokens : (i + 1) * tokens
            ]

    attend(0, 0)
    pass_kv(1, 3)
    attend(0, 1)
    gather_pass(c8, r_c8, 1)
    attend(0, 2)
    pass_ff(1)
    take_kv(1)
    attend(1, 0)
    attend(1, 1)
    for cc in range(2):
        part = wd8.at[pl.ds(off(2 * y + cc, drows), drows)]
        net.recv(part, r_wd + cc)
        net.send(part, part, r_wy + cc, dev(1 - y, c, z, x))
    attend(1, 2)

    for hx, hy, cc in ((0, 0, 0), (0, 0, 1), (0, 1, 1), (1, 0, 0), (1, 1, 0), (1, 1, 1)):
        for zz in range(2):
            net.recv(
                wok.at[2 * flip(y, hy) + cc, pl.ds(off(2 * zz + flip(x, hx), rows), rows)],
                r_wo + zz * 8 + hx * 4 + hy * 2 + cc,
            )
    for part in range(4):
        got = dot_nn(ab[:, 0:qw], wok[part])
        for s in range(2):
            mp[s, :, qcols * part : qcols * (part + 1)] = got[s * tokens : (s + 1) * tokens]
    r_ml = net.slots(1)
    mp_sent = net.send(mp.at[1], ml, r_ml, partner)
    gather_pass(c8, r_c8, 2)
    gather_pass(c8, r_c8, 3)
    net.recv(ml, r_ml)
    mid[...] = tok[...].astype(F32) + mp[0] + ml[...]
    n8[0] = (normed(mid[...])[0] * grow[1:2]).astype(BF16)
    r_n8 = net.slots(8)
    gather_z(n8, r_n8)
    gather_x(n8, r_n8)

    net.recv(c8.at[1], r_c8 + 4)
    for h in range(1, 4):
        net.recv(c8.at[2 * h + 1], r_c8 + 4 + h)
    take_ff(0)
    take_ff(1)
    for cc in range(2):
        net.recv(wd8.at[pl.ds(off(2 * (1 - y) + cc, drows), drows)], r_wy + cc)

    all_tokens = 8 * tokens

    def feed(i):
        pair = slice(2 * i, 2 * i + 2)
        here = n8[pair].reshape(2 * tokens, width)
        grad_inner = dot_nn(c8[pair].reshape(2 * tokens, width), wd8[...])
        gate = dot_nn(here, wg8[0])
        up = dot_nn(here, wg8[1])
        sig = 1.0 / (1.0 + jnp.exp(-gate))
        silu = gate * sig
        dgate = (grad_inner * up * sig * (1.0 + gate * (1.0 - sig))).astype(BF16)
        dup = (grad_inner * silu).astype(BF16)
        at = 2 * tokens * i
        act[at : at + 2 * tokens] = (silu * up).astype(BF16)
        act[at + all_tokens : at + all_tokens + 2 * tokens] = dgate
        act[at + 2 * all_tokens : at + 2 * all_tokens + 2 * tokens] = dup
        pt[pair] = (dot_nt(dgate, wg8[0]) + dot_nt(dup, wg8[1])).astype(BF16).reshape(2, tokens, width)

    def reduce_start(part, land, slot, h):
        return net.send(part.at[2 * h + 1], land.at[h], slot + h, partner)

    def reduce_pass(part, land, out, land2, slot, h):
        net.recv(land.at[h], slot + h)
        out[h - 1] = (part[2 * h].astype(F32) + land[h].astype(F32)).astype(BF16)
        net.send(
            out.at[h - 1], land2.at[h - 1], slot + 4 + h,
            dev(y, c, zat(h % 2), flip(x, h // 2)),
        )

    def reduce_own(part, land, slot):
        net.recv(land.at[0], slot)
        return part[0].astype(F32) + land[0].astype(F32)

    def reduce_end(land2, slot):
        total = 0.0
        for h in range(1, 4):
            net.recv(land2.at[h - 1], slot + 4 + h)
            total = total + land2[h - 1].astype(F32)
        return total

    r_dn = net.slots(8)
    pt_sent = []
    net.recv(n8.at[1], r_n8 + 4)
    for h in range(4):
        if h:
            gather_pass(n8, r_n8, h)
            net.recv(n8.at[2 * h + 1], r_n8 + 4 + h)
        feed(h)
        pt_sent.append(reduce_start(pt, l1, r_dn, h))
        if h > 1:
            reduce_pass(pt, l1, s2, l2, r_dn, h - 1)
    reduce_pass(pt, l1, s2, l2, r_dn, 3)
    dmid[...] = reduce_own(pt, l1, r_dn)

    def flat(ref, i):
        return ref[:, :, pl.ds(off(i, 128), 128)].reshape(all_tokens, 128)

    def grad_gu(i, carry):
        left = flat(n8, i)
        at = pl.ds(off(i, 128), 128)
        ggu[0, at] = dot_tn(left, act[pl.ds(all_tokens, all_tokens)]).astype(BF16)
        ggu[1, at] = dot_tn(left, act[pl.ds(2 * all_tokens, all_tokens)]).astype(BF16)
        return carry

    def grad_d(i, carry):
        gdt[pl.ds(off(i, 128), 128)] = dot_tn(flat(c8, i), act[pl.ds(0, all_tokens)]).astype(BF16)
        return carry

    def feed_out(i, carry):
        got = dot_nt(act[pl.ds(off(i, 2 * tokens), 2 * tokens)], wd8[...])
        pt[pl.ds(2 * i, 2)] = got.astype(BF16).reshape(2, tokens, width)
        return carry

    r_gd, r_gz = net.slots(1), net.slots(4)
    half = 2 * drows
    lax.fori_loop(0, width // 128, grad_d, 0)
    net.send(gdt.at[pl.ds(off(1 - y, half), half)], lgd, r_gd, dev(1 - y, c, z, x))
    lax.fori_loop(0, width // 128, grad_gu, 0)
    for zt in range(4):
        at = pl.ds(2 * rows * zt, 2 * rows)
        net.send(
            ggu.at[:, at], lgu.at[:, at], r_gz + zt, dev(1 - y, c, z, x),
            only=jnp.logical_not(home),
        )

    total = dmid[...] + reduce_end(l2, r_dn)
    normed_two, inv_two = normed(mid[...])
    total = total * grow[1:2]
    dmid[...] = cot[...].astype(F32) + inv_two * (
        total - normed_two * jnp.mean(total * normed_two, -1, keepdims=True)
    )
    dmb[0] = dmid[...].astype(BF16)
    r_dm = net.slots(1)
    net.send(dmb.at[0], dmb.at[1], r_dm, partner)
    for finish in pt_sent:
        net.done(finish)
    lax.fori_loop(0, 4, feed_out, 0)
    r_out = net.slots(8)
    for h in range(4):
        reduce_start(pt, l1o, r_out, h)

    r_ld = net.slots(2)
    net.recv(lgd, r_gd)
    sgd[...] = (gdt[pl.ds(off(y, half), half)].astype(F32) + lgd[...].astype(F32)).astype(BF16)
    gd_z = 2 * (z_lo + c - 2 * z_lo * c) + c
    for cc in range(2):
        net.send(
            sgd.at[pl.ds(cc * drows, drows)], ld.at[z_hi], r_ld + z_hi, dev(y, cc, gd_z, x),
            is_self=jnp.logical_and(z == gd_z, c == cc),
        )
    net.recv(dmb.at[1], r_dm)

    for part in range(4):
        for s in range(2):
            dm4[part, s * tokens : (s + 1) * tokens] = dmb[s, :, qcols * part : qcols * (part + 1)]
    dattn = dot_nt(dm4[0], wok[0])
    for part in range(1, 4):
        dattn = dattn + dot_nt(dm4[part], wok[part])
    qf[:, 0:qw] = dattn
    for s in range(2):
        for h in range(heads):
            do6[s * groups + h // per, (h % per) * tokens : (h % per + 1) * tokens] = qf[
                s * tokens : (s + 1) * tokens, HEAD_SIZE * h : HEAD_SIZE * (h + 1)
            ].astype(BF16)
    attn_all = ab[:, 0:qw]
    for part in range(4):
        act[qw * part : qw * (part + 1), 0:qcols] = dot_tn(attn_all, dm4[part]).astype(BF16)
    r_gy, r_go = net.slots(2), net.slots(8)
    for cc in range(2):
        net.send(
            act.at[pl.ds(off(2 * (1 - y) + cc, qw), qw)], loy.at[cc], r_gy + cc, dev(1 - y, c, z, x)
        )

    def pass_go():
        for cc in range(2):
            net.recv(loy.at[cc], r_gy + cc)
            at = pl.ds(off(2 * y + cc, qw), qw)
            act[at] = (act[at].astype(F32) + loy[cc].astype(F32)).astype(BF16)
        for hx in (1, 0):
            for hc in range(2):
                for zz in range(2):
                    at = pl.multiple_of((2 * y + flip(c, hc)) * qw + (2 * zz + flip(x, hx)) * rows, rows)
                    src = act.at[pl.ds(at, rows)]
                    dst = lo.at[2 * c + zz, hx]
                    slot = r_go + (2 * c + zz) * 2 + hx
                    if hx + hc == 0:
                        net.keep(src, dst, slot)
                    else:
                        net.send(src, dst, slot, dev(y, flip(c, hc), z, flip(x, hx)))

    def attend_back(s, g):
        at = s * groups + g
        kg = kv[s, :, HEAD_SIZE * g : HEAD_SIZE * (g + 1)]
        vg = kv[s, :, kw + HEAD_SIZE * g : kw + HEAD_SIZE * (g + 1)]
        dout = do6[at]
        delta = jnp.sum(dout.astype(F32) * o6[at].astype(F32), -1, keepdims=True)
        dprob = dot_nt(dout, vg)
        dscore = (p6[at].astype(F32) * (dprob - delta)).astype(BF16)
        dquery = dot_nn(dscore, kg) * scale
        dkeys = dot_tn(q6[at], dscore)
        dvals = dot_tn(dout, p6[at])
        for t in range(n_ctx):
            cols = slice(t * tokens, (t + 1) * tokens)
            dkv[t, s, HEAD_SIZE * g : HEAD_SIZE * (g + 1)] = dkeys[:, cols].astype(BF16)
            dkv[t, s, kw + HEAD_SIZE * g : kw + HEAD_SIZE * (g + 1)] = dvals[:, cols].astype(BF16)
        for i in range(per):
            h = g * per + i
            qf[s * tokens : (s + 1) * tokens, HEAD_SIZE * h : HEAD_SIZE * (h + 1)] = dquery[
                i * tokens : (i + 1) * tokens
            ]

    r_dx, r_dz = net.slots(8), net.slots(8)

    def send_dkv(s):
        for k in (1, 2, 3, 0):
            net.send(
                dkv.at[2 * zat(k) + 1 - x, s], lx.at[k, s], r_dx + 4 * s + k, dev(y, c, z, 1 - x)
            )

    def pass_dkv(s):
        for k in range(1, 4):
            net.recv(lx.at[k, s], r_dx + 4 * s + k)
            sx[k - 1, s] = (dkv[2 * zat(k) + x, s].astype(F32) + lx[k, s].astype(F32)).astype(BF16)
            net.send(sx.at[k - 1, s], lkz.at[k - 1, s], r_dz + 4 * s + k, dev(y, c, zat(k), x))

    for g in range(groups):
        attend_back(0, g)
    send_dkv(0)
    attend_back(1, 0)
    attend_back(1, 1)
    pass_dkv(0)
    attend_back(1, 2)
    send_dkv(1)
    pass_go()
    for t in range(qf.shape[1] // 128):
        qf[:, 128 * t : 128 * (t + 1)] = turn(qf[:, 128 * t : 128 * (t + 1)], False)
    grad = dot_tn(n1[...], qf[:, 0:qw].astype(BF16)).astype(BF16)
    for t in range(n_ctx):
        p6[t // 2, (t % 2) * rows : (t % 2 + 1) * rows, 0:qw] = grad[rows * t : rows * (t + 1)]
    for part in range(2):
        dqk[part, :, 0:qcols] = qf[:, qcols * part : qcols * (part + 1)].astype(BF16)
    r_qy, r_qx, r_zq = net.slots(4), net.slots(4), net.slots(4)
    mine = c == y

    def send_grads(source, land, slot):
        for k in (1, 2, 3, 0):
            net.send(
                source(zat(k), slice(0, 2)), land.at[zat(k)], slot + k, dev(1 - y, c, z, x),
                only=jnp.logical_not(mine),
            )

    def add_y(source, land, slot, land_x, slot_x):
        for k in (1, 2, 3, 0):

            @pl.when(mine)
            def _():
                net.recv(land.at[zat(k)], slot + k)
                here = source(zat(k), slice(0, 2))
                here[...] = (here[...].astype(F32) + land[zat(k)].astype(F32)).astype(BF16)

            net.send(
                source(zat(k), 1 - x), land_x.at[k], slot_x + k, dev(y, c, z, 1 - x), only=mine
            )

    def add_x(source, land_x, slot_x, staged, arrived, slot_z):
        wide_part = arrived.shape[2]
        for k in (1, 2, 3, 0):

            @pl.when(mine)
            def _():
                net.recv(land_x.at[k], slot_x + k)
                staged[k] = (source(zat(k), x)[...].astype(F32) + land_x[k].astype(F32)).astype(BF16)

            for cc in range(2):
                first = cc * (staged.shape[2] - wide_part)
                src = staged.at[k, :, pl.ds(first, wide_part)]
                if k:
                    net.send(src, arrived.at[k], slot_z + k, dev(y, cc, zat(k), x), only=mine)
                else:

                    @pl.when(jnp.logical_and(mine, c == cc))
                    def _():
                        net.keep(src, arrived.at[k], slot_z)

                    net.send(
                        src, arrived.at[k], slot_z, dev(y, cc, z, x),
                        only=jnp.logical_and(mine, c != cc),
                    )

    def add_z(out, arrived, slot_z, staged):
        total = 0.0
        for k in (1, 2, 3, 0):
            net.recv(arrived.at[k], slot_z + k)
            total = total + arrived[k].astype(F32)
        count = out.shape[1]
        skip = count - (staged.shape[2] - arrived.shape[2])
        out[...] = jnp.where(c == 0, total[:, 0:count], total[:, skip : skip + count])

    def in_p6(zt, xt):
        at = pl.ds(0, 2 * rows) if isinstance(xt, slice) else pl.ds(off(xt, rows), rows)
        return p6.at[zt, at, pl.ds(0, qf.shape[1])]

    def in_wg8(zt, xt):
        at = pl.ds(off(zt, 2 * rows), 2 * rows) if isinstance(xt, slice) else pl.ds(off(2 * zt + xt, rows), rows)
        return wg8.at[0, at]

    send_grads(in_p6, lqy, r_qy)
    pass_dkv(1)
    r_gf = net.slots(4)
    for k in (3, 2, 1, 0):
        at = pl.ds(off(zat(k), 2 * rows), 2 * rows)

        @pl.when(home)
        def _():
            net.recv(lgu.at[:, at], r_gz + zat(k))
            ggu[:, at] = (ggu[:, at].astype(F32) + lgu[:, at].astype(F32)).astype(BF16)

        for hx in range(2):
            src = ggu.at[:, pl.ds(off(2 * zat(k) + flip(x, hx), rows), rows)]
            dst = lf.at[x, z_hi]
            slot = r_gf + x * 2 + z_hi
            if k + hx:
                net.send(src, dst, slot, dev(y, c, zat(k), flip(x, hx)), only=home)
            else:

                @pl.when(home)
                def _():
                    net.keep(src, dst, slot)

    for h in range(1, 4):
        reduce_pass(pt, l1o, s2o, l2o, r_out, h)
    mid[...] = mid[...] + reduce_own(pt, l1o, r_out)

    def attn_pass(land, out, staged, arrived, send_slot, slot, absolute):
        for k in (1, 2, 3, 0):
            at = zat(k) if absolute else k
            part = 0.0
            for h in range(2):
                net.recv(land.at[at, h], slot + at * 2 + h)
                part = part + land[at, h, :, 0 : out.shape[1]].astype(F32)
            if k == 0:
                out[...] = part
            else:
                staged[k - 1] = part.astype(BF16)
                net.send(staged.at[k - 1], arrived.at[k - 1], send_slot + k, dev(y, c, zat(k), x))

    def attn_end(out, arrived, slot):
        for k in range(1, 4):
            net.recv(arrived.at[k - 1], slot + k)
            out[...] = out[...] + arrived[k - 1].astype(F32)

    r_zo = net.slots(4)
    attn_pass(lo, o_o, so, lzo, r_zo, r_go, True)
    add_y(in_p6, lqy, r_qy, lqx, r_qx)

    for s in range(2):
        net.recv(lx.at[0, s], r_dx + 4 * s)
        total = dkv[2 * z + x, s].astype(F32) + lx[0, s].astype(F32)
        for k in range(1, 4):
            net.recv(lkz.at[k - 1, s], r_dz + 4 * s + k)
            total = total + lkz[k - 1, s].astype(F32)
        kvf[s * tokens : (s + 1) * tokens] = total.T
    turn_keys(False)
    for part in range(2):
        dqk[part, :, qcols : qcols + kcols] = kvf[:, kcols * part : kcols * (part + 1)].astype(BF16)
        dqk[part, :, qcols + kcols :] = kvf[:, kw + kcols * part : kw + kcols * (part + 1)].astype(BF16)
    for finish in ff_passed:
        net.done(finish)
    for part in range(2):
        wg8[0, :, 2 * kcols * part : 2 * kcols * (part + 1)] = dot_tn(
            n1[...], dqk[part, :, qcols:]
        ).astype(BF16)
    r_ky, r_kx2, r_zk = net.slots(4), net.slots(4), net.slots(4)
    send_grads(in_wg8, lky, r_ky)
    net.done(mp_sent)
    got = dot_nt(dqk[0], wq[0]) + dot_nt(dqk[1], wq[1])
    for s in range(2):
        mp[s] = got[s * tokens : (s + 1) * tokens]
    r_dn1 = net.slots(1)
    net.send(mp.at[1], ml, r_dn1, partner)
    add_x(in_p6, lqx, r_qx, sq, lzq, r_zq)
    add_y(in_wg8, lky, r_ky, lkx, r_kx2)
    net.recv(ml, r_dn1)
    total = mp[0] + ml[...]
    normed_one, inv_one = normed(tok[...])
    total = total * grow[0:1]
    o_ing[...] = (
        dmid[...]
        + inv_one * (total - normed_one * jnp.mean(total * normed_one, -1, keepdims=True))
    ).astype(BF16)
    add_x(in_wg8, lkx, r_kx2, sk, lzk, r_zk)

    o_out[...] = (mid[...] + reduce_end(l2o, r_out)).astype(BF16)
    gains = [0.0, 0.0]
    for h in range(2):
        for zh in range(2):
            net.recv(lf.at[h, zh], r_gf + h * 2 + zh)
        for m in range(2):
            got = lf[h, 0, m].astype(F32) + lf[h, 1, m].astype(F32)
            cols = slice(h * ff, (h + 1) * ff)
            (o_gate, o_up)[m][:, cols] = got
            gains[1] = gains[1] + jnp.sum(
                got * (wgate, wup)[m][:, cols].astype(F32), 1, keepdims=True
            )
    for zh in range(2):
        net.recv(ld.at[zh], r_ld + zh)
    o_d[...] = ld[0].astype(F32) + ld[1].astype(F32)
    attn_end(o_o, lzo, r_zo)
    add_z(o_q, lzq, r_zq, sq)
    gains[0] = jnp.sum(o_q[...] * wqkv[:, 0:qcols].astype(F32), 1, keepdims=True)
    add_z(kvg, lzk, r_zk, sk)
    gains[0] = gains[0] + jnp.sum(kvg[...] * wqkv[:, qcols:].astype(F32), 1, keepdims=True)
    o_k[...] = kvg[:, 0:kcols]
    o_v[...] = kvg[:, kcols:]
    column = lax.broadcasted_iota(jnp.int32, (rows, 128), 1)
    both = jnp.where(column == 0, gains[0], jnp.where(column == 1, gains[1], 0.0))
    sg[...] = both.T[0:8]
    r_lg = net.slots(4)
    for h in range(1, 4):
        net.send(sg, lg.at[h - 1], r_lg + h, dev(flip(y, h // 2), flip(c, h % 2), z, x))
    total = sg[...]
    for h in range(1, 4):
        net.recv(lg.at[h - 1], r_lg + h)
        total = total + lg[h - 1]
    total = total / gain[...]
    o_gain_one[...] = total[0:1]
    o_gain_two[...] = total[1:2]
    net.drain()


def hand_over(*refs):
    count = len(refs) // 2
    copies = [pltpu.make_async_copy(refs[i], refs[count + i], refs[-1].at[i]) for i in range(count)]
    for copy in copies:
        copy.start()
    for copy in copies:
        copy.wait()


def run_layer(n_ctx, tok, cot, pos, blk, gain_one, gain_two, wquery, wkey, wvalue, wo, wgate, wup, wdt):
    tokens, width = tok.shape
    rows, qcols = wquery.shape
    packed = qcols + 2 * wkey.shape[1]
    drows, ff = wdt.shape
    keys = n_ctx * tokens
    qw = 2 * qcols
    kw = packed - qcols
    groups = kw // HEAD_SIZE
    per = QUERY_HEADS // KEY_VALUE_HEADS
    stack = per * tokens
    wide = -(-qw // 128) * 128
    out_shape = [
        jax.ShapeDtypeStruct((tokens, width), BF16),
        jax.ShapeDtypeStruct((tokens, width), BF16),
        jax.ShapeDtypeStruct((1, rows), F32),
        jax.ShapeDtypeStruct((1, rows), F32),
        jax.ShapeDtypeStruct((rows, qcols), F32),
        jax.ShapeDtypeStruct((rows, kw // 2), F32),
        jax.ShapeDtypeStruct((rows, kw // 2), F32),
        jax.ShapeDtypeStruct((rows, qcols), F32),
        jax.ShapeDtypeStruct((rows, 2 * ff), F32),
        jax.ShapeDtypeStruct((rows, 2 * ff), F32),
        jax.ShapeDtypeStruct((drows, ff), F32),
    ]

    def vm(*shape, dtype=BF16):
        return pltpu.VMEM(shape, dtype)

    scratch = [
        vm(rows, packed),
        vm(8, rows, dtype=F32),
        vm(2 * tokens, 256, dtype=F32),
        vm(2, 8, keys, dtype=F32),
        vm(tokens, width),
        vm(n_ctx, 8, rows, dtype=F32),
        vm(8, width, dtype=F32),
        vm(3, rows, packed),
        vm(3, rows, qcols),
        vm(2, width, packed),
        vm(4, 4 * rows, qcols),
        vm(2, width, ff),
        vm(width, ff),
        vm(8, tokens, width),
        vm(8, tokens, width),
        vm(2 * tokens, width),
        vm(2 * tokens, wide, dtype=F32),
        vm(2 * tokens, 2 * kw, dtype=F32),
        vm(2, keys, 2 * kw),
        vm(2 * groups, stack, HEAD_SIZE),
        vm(2 * groups, stack, keys),
        vm(2 * groups, stack, HEAD_SIZE),
        vm(2 * tokens, wide),
        vm(2, tokens, width, dtype=F32),
        vm(tokens, width, dtype=F32),
        vm(tokens, width, dtype=F32),
        vm(tokens, width, dtype=F32),
        vm(2, tokens, width),
        vm(4, 2 * tokens, qcols),
        vm(2 * groups, stack, HEAD_SIZE),
        vm(24 * tokens, ff),
        vm(8, tokens, width),
        vm(4, tokens, width),
        vm(3, tokens, width),
        vm(3, tokens, width),
        vm(4, tokens, width),
        vm(3, tokens, width),
        vm(3, tokens, width),
        vm(2, width, ff),
        vm(2, width, ff),
        vm(2, 2, 2, rows, ff),
        vm(width, ff),
        vm(2 * drows, ff),
        vm(2 * drows, ff),
        vm(2, drows, ff),
        vm(2, qw, ff),
        vm(4, 2, rows, ff),
        vm(4, 2 * rows, wide),
        vm(4, rows, wide),
        vm(4, 2 * rows, ff),
        vm(4, rows, ff),
        vm(3, rows, qcols),
        vm(4, rows, wide),
        vm(4, rows, ff),
        vm(3, rows, qcols),
        vm(4, rows, ff),
        vm(4, rows, 256),
        vm(rows, kw, dtype=F32),
        vm(n_ctx, 2, 2 * kw, tokens),
        vm(4, 2, 2 * kw, tokens),
        vm(3, 2, 2 * kw, tokens),
        vm(3, 2, 2 * kw, tokens),
        vm(3, 8, rows, dtype=F32),
        vm(8, rows, dtype=F32),
        vm(2, 2 * tokens, packed),
        pltpu.SemaphoreType.DMA((N_SEM,)),
        pltpu.SemaphoreType.DMA((N_SEM,)),
    ]
    inside = pl.BlockSpec(memory_space=pltpu.VMEM)
    outs = pl.pallas_call(
        layer_kernel,
        out_shape=out_shape,
        in_specs=[inside] * 3 + [pl.BlockSpec(memory_space=pltpu.SMEM)] + [inside] * 9,
        out_specs=[inside] * len(out_shape),
        scratch_shapes=scratch,
        compiler_params=pltpu.CompilerParams(
            collective_id=0, has_side_effects=True, vmem_limit_bytes=VMEM_LIMIT
        ),
        name="layer",
    )(tok, cot, pos, blk, gain_one, gain_two, wquery, wkey, wvalue, wo, wgate, wup, wdt)
    anywhere = pl.BlockSpec(memory_space=pl.ANY)
    return pl.pallas_call(
        hand_over,
        out_shape=out_shape,
        in_specs=[inside] * len(out_shape),
        out_specs=[anywhere] * len(out_shape),
        scratch_shapes=[pltpu.SemaphoreType.DMA((len(out_shape),))],
        name="hand_over",
    )(*outs)


VMEM_LIMIT = 63 * 1024 * 1024


def on_device_plane(
    tokens, positions, block_sizes, attn_gain, w_query, w_key, w_value, w_out, mlp_gain,
    w_gate, w_up, w_down, cotangent,
):
    output, input_grad, g_one, g_two, g_q, g_k, g_v, g_o, g_gate, g_up, g_d = run_layer(
        lax.axis_size("ctx"), tokens[0], cotangent[0], positions, block_sizes, attn_gain,
        mlp_gain, w_query, w_key, w_value, w_out, w_gate, w_up, w_down.T,
    )
    return (
        output[None],
        input_grad[None],
        g_one[0],
        g_q,
        g_k,
        g_v,
        g_o,
        g_two[0],
        g_gate,
        g_up,
        g_d.T,
    )


def solution(mesh):
    placed = (
        P("dp", "ctx", None),
        P("dp", "ctx"),
        P("dp"),
        P("ctx"),
        P("ctx", "dp"),
        P("ctx", "dp"),
        P("ctx", "dp"),
        P("ctx", "dp"),
        P("ctx"),
        P("ctx", "dp"),
        P("ctx", "dp"),
        P("ctx", "dp"),
        P("dp", "ctx", None),
    )
    fits = mesh.shape["dp"] == 4 and mesh.shape["ctx"] == 8
    return jax.shard_map(
        on_device_plane if fits else on_device,
        mesh=mesh,
        in_specs=placed,
        out_specs=(
            P("dp", "ctx", None),
            P("dp", "ctx", None),
            P("ctx"),
            P("ctx", "dp"),
            P("ctx", "dp"),
            P("ctx", "dp"),
            P("ctx", "dp"),
            P("ctx"),
            P("ctx", "dp"),
            P("ctx", "dp"),
            P("ctx", "dp"),
        ),
        check_vma=False,
    )
```
